32 devices in a mesh: level: 2 (over x), row: 8 (over z, core), col: 2 (over y).
Axes of the slice: x: 2, y: 2, z: 4, core: 2. Of those that a mesh axis runs over, the one named last changes fastest.
Arguments:
- noise: bfloat16 [64, 512, 512], P('row', ('level', 'col')), may hold values from -6 to 6
- source: bfloat16 [64, 512, 512], P('row', ('level', 'col')), may hold values from -16 to 16
Outputs:
- fine_pressure: float32 [64, 512, 512], P('row', ('level', 'col'))
- coarse_pressure: float32 [32, 256, 256], P('row', ('level', 'col'))
The draws below stay inside these ranges and needn't reach their ends.
All inputs are finite; a program needn't handle non-finite values.
Results may differ from the reference program's by a relative error of at most 0.00035.
Values sent between devices are 32-bit elements; how exact they have to be, the bound alone decides.
No kernel may reach another device: no remote copies, remote signals or barrier semaphores. Data moves between devices by JAX's collectives and lax.ppermute only.
A program may use at most 256 MiB of HBM per device.

```python
import math
import jax
import jax.numpy as jnp

NF = 512
NZ = 64
NC = 256
NCZ = 32


def levels(stream_key, shape, pieces, low, largest):
    loudness, own = 1.0, jax.random.fold_in(stream_key, 6)
    for dim, blocks in pieces:
        draws = jnp.exp(jax.random.uniform(jax.random.fold_in(own, dim), (blocks,), jnp.float32, low / len(pieces), largest / len(pieces)))
        loudness = loudness * jnp.repeat(draws, shape[dim] // blocks).reshape([-1 if axis == dim else 1 for axis in range(len(shape))])
    return loudness


def scatter_about(stream_key, shape, width, reach, pieces=(), held_as=jnp.bfloat16):
    loudness = levels(stream_key, shape, pieces, -0.22, 0.18) if pieces else 1.0
    array = jax.random.normal(stream_key, shape, jnp.float32) * width * loudness
    return jnp.minimum(jnp.maximum(array, -reach), reach).astype(held_as)


def setup_inputs(seed: int = 0) -> dict:
    key_list = jax.random.split(jax.random.key(seed), 3)
    return {
        "noise": scatter_about(key_list[0], (NZ, NF, NF), 1.0, 6.0, ((0, 8), (1, 4))),
        "source": scatter_about(key_list[1], (NZ, NF, NF), 4.0, 16.0, ((0, 8), (1, 4))),
    }


JACOBI_WEIGHT = 2.0 / 3.0
CORRELATION = 0.2
FIELD_SCALE = 0.3
NEIGHBOUR_STEPS = ((1, 0, 0), (-1, 0, 0), (0, 1, 0), (0, -1, 0), (0, 0, 1), (0, 0, -1))


def signed_modes(index, length):
    return jnp.where(index < length // 2, index, index - length).astype(jnp.float32)


def amplitude(first_modes, second_modes, third_modes, first_edge, second_edge, third_edge):
    squared = first_modes * first_modes + second_modes * second_modes + third_modes * third_modes
    value = FIELD_SCALE / (1.0 + (2.0 * math.pi * CORRELATION) ** 2 * squared)
    edge = (jnp.abs(first_modes) == first_edge) | (jnp.abs(second_modes) == second_edge) | (jnp.abs(third_modes) == third_edge)
    return jnp.where(edge, 0.0, value)


def window(values, margin, offset):
    return values[margin + offset[0]: values.shape[0] - margin + offset[0],
                  margin + offset[1]: values.shape[1] - margin + offset[1],
                  margin + offset[2]: values.shape[2] - margin + offset[2]]


def face_weight(center, beside):
    return jnp.where(beside > 0.0, 0.5 * (center + beside), center)


def smooth_twice(kappa, source):
    no_shift = (0, 0, 0)
    center = window(kappa, 1, no_shift)
    faces = [face_weight(center, window(kappa, 1, offset)) for offset in NEIGHBOUR_STEPS]
    diagonal = faces[0] + faces[1] + faces[2] + faces[3] + faces[4] + faces[5]
    guarded = jnp.where(center > 0.0, diagonal, 1.0)
    first_sweep = JACOBI_WEIGHT * window(source, 1, no_shift) / guarded
    inner_first = window(first_sweep, 1, no_shift)
    inner_diagonal = window(diagonal, 1, no_shift)
    coupled = jnp.zeros_like(inner_first)
    for face_value, offset in zip(faces, NEIGHBOUR_STEPS):
        coupled = coupled + window(face_value, 1, no_shift) * window(first_sweep, 1, offset)
    residual = window(source, 2, no_shift) - inner_diagonal * inner_first + coupled
    return inner_first + JACOBI_WEIGHT * residual / inner_diagonal


def reference(noise, source):
    field = noise.astype(jnp.float32)
    spectrum = jnp.fft.rfftn(field)
    total_cells = float(NZ) * float(NF) * float(NF)
    slab_modes = signed_modes(jnp.arange(NZ, dtype=jnp.int32), NZ)
    fine_modes = signed_modes(jnp.arange(NF, dtype=jnp.int32), NF)
    third_fine = jnp.arange(NF // 2 + 1, dtype=jnp.int32).astype(jnp.float32)
    fine_scale = amplitude(slab_modes[:, None, None], fine_modes[None, :, None], third_fine[None, None, :], NZ / 2.0, NF / 2.0, NF / 2.0)
    fine_log = jnp.fft.irfftn(spectrum * fine_scale, s=(NZ, NF, NF)) * (total_cells ** 0.5)
    half_slab = NCZ // 2
    half_coarse = NC // 2
    band = jnp.concatenate([spectrum[:half_slab], spectrum[NZ - half_slab:]], axis=0)
    band = jnp.concatenate([band[:, :half_coarse], band[:, NF - half_coarse:]], axis=1)
    band = band[:, :, :half_coarse + 1]
    coarse_slab_modes = signed_modes(jnp.arange(NCZ, dtype=jnp.int32), NCZ)
    coarse_modes = signed_modes(jnp.arange(NC, dtype=jnp.int32), NC)
    third_coarse = jnp.arange(half_coarse + 1, dtype=jnp.int32).astype(jnp.float32)
    coarse_scale = amplitude(coarse_slab_modes[:, None, None], coarse_modes[None, :, None], third_coarse[None, None, :], NCZ / 2.0, NC / 2.0, NC / 2.0)
    coarse_cells = float(NCZ) * float(NC) * float(NC)
    coarse_log = jnp.fft.irfftn(band * coarse_scale, s=(NCZ, NC, NC)) * (coarse_cells / total_cells ** 0.5)
    fine_source = source.astype(jnp.float32)
    coarse_source = fine_source.reshape(NCZ, 2, NC, 2, NC, 2).mean(axis=(1, 3, 5))
    fine_pressure = smooth_twice(jnp.pad(jnp.exp(fine_log), 2), jnp.pad(fine_source, 2))
    coarse_pressure = smooth_twice(jnp.pad(jnp.exp(coarse_log), 2), jnp.pad(coarse_source, 2))
    return fine_pressure, coarse_pressure
```

```python
import functools
import math

import jax
import jax.numpy as jnp
import numpy as np
from jax import lax
from jax.experimental import pallas as pl
from jax.experimental.pallas import tpu as pltpu
from jax.sharding import PartitionSpec as P

JACOBI_WEIGHT = 2.0 / 3.0
CORRELATION = 0.2
FIELD_SCALE = 0.3
DECAY = (2.0 * math.pi * CORRELATION) ** 2
EVERY = ("row", "level", "col")
PLANE = ("level", "col")
MIB = 1 << 20
SUB, LANE = 8, 128


def two_parts(matrix):
    high = matrix.astype(jnp.bfloat16)
    low = (matrix - high.astype(np.float64)).astype(jnp.bfloat16)
    return high, low


def angles(rows, cols, length):
    return 2.0 * np.pi * (np.outer(rows, cols) % length) / length


def third_modes(devices, js):
    return np.array([[d + devices * j for j in js] for d in range(devices)])


def forward_third(length, devices, js):
    theta = angles(third_modes(devices, js).reshape(-1), np.arange(length), length)
    return np.stack([np.cos(theta), -np.sin(theta)], axis=1).reshape(-1, length)


def inverse_third(length, devices, js):
    theta = angles(third_modes(devices, js).reshape(-1), np.arange(length), length)
    return np.stack([np.cos(theta), -np.sin(theta)], axis=1).reshape(-1, length)


def second_table(length):
    theta = angles(np.arange(length), np.arange(length // 2), length)
    return np.concatenate([np.cos(theta), np.sin(theta)], axis=1)


def forward_first(length):
    theta = angles(np.arange(length), np.arange(length), length)
    cos, sin = np.cos(theta), np.sin(theta)
    return np.block([[cos, sin], [-sin, cos]])


def inverse_first(length):
    theta = angles(np.arange(length), np.arange(length), length)
    cos, sin = np.cos(theta), np.sin(theta)
    cos[:, length // 2] = 0.0
    sin[:, length // 2] = 0.0
    return np.block([[cos, -sin], [sin, cos]])


def inverse_first_coarse(length, rows):
    full = inverse_first(length)
    value = full.reshape(2, rows, length // rows, 2 * length)
    turned = np.concatenate([-full[length:], full[:length]]).reshape(value.shape)
    order = lambda x: x.transpose(1, 0, 2, 3).reshape(2 * length, 2 * length)
    return np.concatenate([order(value), order(turned)])


def second_coarse(length, groups):
    table = second_table(length).T
    span = length // groups
    out = np.zeros((2, length, groups, 2, span))
    for pair in range(2):
        out[pair, :, :, pair, :] = table.reshape(length, groups, span)
    return out.reshape(2 * length, 2 * length)


def third_coarse(length, devices, js):
    modes = third_modes(devices, js).reshape(devices, len(js) // 2, 2)
    theta = 2.0 * np.pi * (modes[..., None] * np.arange(length) % length) / length
    both = np.stack([np.cos(theta), -np.sin(theta)])
    return both.transpose(0, 2, 1, 3, 4).reshape(2 * (len(js) // 2) * devices, 2 * length)


def split(x):
    high = x.astype(jnp.bfloat16)
    return high, (x - high.astype(jnp.float32)).astype(jnp.bfloat16)


def dot(a, b):
    return lax.dot_general(a, b, (((1,), (0,)), ((), ())), preferred_element_type=jnp.float32)


def dot_t(a, b):
    return lax.dot_general(a, b, (((1,), (1,)), ((), ())), preferred_element_type=jnp.float32)


def dot3(a, b):
    (ah, al), (bh, bl) = a, b
    return dot(ah, bh) + (dot(ah, bl) + dot(al, bh))


def forward_kernel(planes, dh, dl, x, out):
    rows = dh.shape[0]
    for p in range(0, planes, 2):
        part = x[p * LANE : (p + 2) * LANE, :]
        value = dot_t(dh[...], part) + dot_t(dl[...], part)
        for h in range(2):
            out[pl.ds(p + h, rows, stride=SUB), :] = value[:, h * LANE : (h + 1) * LANE]


def middle_kernel(sizes, scale, b, csh, csl, fh, fl, ih, il, ch, cl, *rest):
    (first, second, rows, groups, js, low) = sizes
    if low:
        ich, icl, cch, ccl, out, zh, zl, y, oh, ol, qh, ql = rest
    else:
        out, zh, zl, y, oh, ol = rest
    q_count = 2 * js
    half = second // 2
    for q in range(q_count):
        for g in range(groups):
            for r in range(0, rows, 2):
                pair = jnp.concatenate([b[r * groups + g, q], b[(r + 1) * groups + g, q]], axis=0)
                high, rest_part = split(pair)
                at = q * first + r * SUB
                zh[at : at + 2 * SUB, g * LANE : (g + 1) * LANE] = high
                zl[at : at + 2 * SUB, g * LANE : (g + 1) * LANE] = rest_part
    y[...] = dot3((zh[...], zl[...]), (csh[...], csl[...]))
    mode0 = lax.broadcasted_iota(jnp.int32, (first, second), 0)
    mode0 = jnp.where(mode0 < first // 2, mode0, mode0 - first).astype(jnp.float32)
    lane = lax.broadcasted_iota(jnp.int32, (first, second), 1)
    mode1 = jnp.where(lane < half, lane, lane - half).astype(jnp.float32)
    base = 1.0 + DECAY * (mode0 * mode0 + mode1 * mode1)
    for j in range(js):
        top = j * 2 * first
        re, im = y[top : top + first, :], y[top + first : top + 2 * first, :]
        rc, rs, ic, isn = re[:, :half], re[:, half:], im[:, :half], im[:, half:]
        wave = jnp.concatenate(
            [
                jnp.concatenate([rc + isn, rc - isn], axis=1),
                jnp.concatenate([ic - rs, ic + rs], axis=1),
            ],
            axis=0,
        )
        spectrum = dot3((fh[...], fl[...]), split(wave))
        amp = jnp.where(lane == half, 0.0, scale[j, 1] / (base + scale[j, 0]))
        scaled = spectrum * jnp.concatenate([amp, amp], axis=0)
        field = dot3((ih[...], il[...]), split(scaled))
        plus, minus = field[:, :half], field[:, half:]
        even, odd = plus + minus, plus - minus
        operand = jnp.concatenate(
            [even, jnp.concatenate([-odd[first:], odd[:first]], axis=0)], axis=1
        )
        high, rest_part = split(operand)
        oh[top : top + 2 * first, :] = high
        ol[top : top + 2 * first, :] = rest_part
        if low:
            quarter = half // 2
            keep = first // 4
            kept = [
                scaled[at : at + keep, :]
                for at in (0, first - keep, first, 2 * first - keep)
            ]
            band = jnp.concatenate(kept, axis=0)
            band = jnp.concatenate([band[:, :quarter], band[:, half : half + quarter]], axis=1)
            field = dot3((ich[...], icl[...]), split(band))
            value, turned = field[:first], field[first:]
            operand = jnp.concatenate(
                [
                    value[:, :quarter] + value[:, quarter:],
                    turned[:, :quarter] - turned[:, quarter:],
                ],
                axis=1,
            )
            high, rest_part = split(operand)
            at_row, at_lane = (j // 2) * first, (j % 2) * half
            qh[at_row : at_row + first, at_lane : at_lane + half] = high
            ql[at_row : at_row + first, at_lane : at_lane + half] = rest_part
    y[...] = dot3((oh[...], ol[...]), (ch[...], cl[...]))
    for q in range(q_count):
        for r in range(rows):
            for g in range(groups):
                at = q * first + r * SUB
                out[r * groups + g, q] = y[at : at + SUB, g * LANE : (g + 1) * LANE]
    if low:
        coarse = dot3((qh[...], ql[...]), (cch[...], ccl[...]))
        for h in range(js // 2):
            for r in range(rows):
                for g in range(groups):
                    at = h * first + r * SUB
                    out[r * groups + g, q_count + h] = coarse[
                        at : at + SUB, g * LANE : (g + 1) * LANE
                    ]


def back_kernel(sizes, last, b, eh, el, *rest):
    (devices, q_count, tiles, planes) = sizes
    if last:
        before, out, lh, ll = rest
    else:
        out, lh, ll = rest
    for n in range(planes):
        if tiles == q_count:
            rows = b[pl.ds(n, devices * q_count, stride=SUB), :]
        else:
            rows = jnp.concatenate(
                [
                    b[pl.ds(s * tiles * SUB + n, q_count, stride=SUB), :]
                    for s in range(devices)
                ],
                axis=0,
            )
        high, rest_part = split(jnp.transpose(rows))
        lh[n * LANE : (n + 1) * LANE, :] = high
        ll[n * LANE : (n + 1) * LANE, :] = rest_part
    for p in range(0, planes, 2):
        at = slice(p * LANE, (p + 2) * LANE)
        value = dot3((lh[at, :], ll[at, :]), (eh[...], el[...]))
        if last:
            value = jnp.exp(value + before[at, :])
        out[at, :] = value


def coarse_back_kernel(sizes, b, eh, el, out, lh, ll):
    (devices, q_count, tiles, planes, length) = sizes
    halves = tiles - q_count
    for n in range(planes):
        rows = jnp.concatenate(
            [
                b[pl.ds((q_count + h) * SUB + c * planes + n, devices, stride=tiles * SUB), :]
                for c in range(2)
                for h in range(halves)
            ],
            axis=0,
        )
        high, rest_part = split(jnp.transpose(rows))
        lh[n * LANE : (n + 1) * LANE, :] = high
        ll[n * LANE : (n + 1) * LANE, :] = rest_part
    value = dot3((lh[...], ll[...]), (eh[...], el[...]))
    half = LANE // 2
    for n in range(planes):
        top = n * LANE
        part = value[top : top + half, :length] + value[top + half : top + LANE, length:]
        out[n * half : (n + 1) * half, :] = jnp.exp(part)


def mean_kernel(planes, pairs, x, out, held, summed):
    cells = x.shape[0] // planes
    half = cells // 2
    held[...] = dot(x[...], pairs[...])
    for n in range(planes // 2):
        top = 2 * n * cells
        for at in range(0, out.shape[1], LANE):
            lanes = slice(at, at + LANE)
            summed[...] = held[top : top + cells, lanes] + held[top + cells : top + 2 * cells, lanes]
            out[n * half : (n + 1) * half, lanes] = (
                summed[pl.ds(0, half, stride=2), :] + summed[pl.ds(1, half, stride=2), :]
            )


def beside(x, fill_edge):
    length = x.shape[1]
    lane = lax.broadcasted_iota(jnp.int32, x.shape, 1)
    left = pltpu.roll(x, 1, 1)
    right = pltpu.roll(x, length - 1, 1)
    if fill_edge:
        left = jnp.where(lane == 0, x, left)
        right = jnp.where(lane == length - 1, x, right)
    else:
        left = jnp.where(lane == 0, 0.0, left)
        right = jnp.where(lane == length - 1, 0.0, right)
    return left + right


def stencil_kernel(
    flags, kappa, k_lo, k_hi, k_left, k_right, f, f_lo, f_hi, f_left, f_right,
    out, ks, fs, us, ws, rs, sems,
):
    planes, cells, length = out.shape
    copies = [
        pltpu.make_async_copy(kappa, ks.at[2 : planes + 2, SUB : SUB + cells, :], sems.at[0]),
        pltpu.make_async_copy(k_lo, ks.at[0:2, SUB : SUB + cells, :], sems.at[1]),
        pltpu.make_async_copy(
            k_hi, ks.at[planes + 2 : planes + 4, SUB : SUB + cells, :], sems.at[2]
        ),
        pltpu.make_async_copy(f_lo, fs.at[0:1, SUB : SUB + cells, :], sems.at[3]),
        pltpu.make_async_copy(
            f_hi, fs.at[planes + 1 : planes + 2, SUB : SUB + cells, :], sems.at[4]
        ),
    ]
    for copy in copies:
        copy.start()
    end = SUB + cells
    for p in range(planes):
        fs[p + 1, SUB:end, :] = f[p].astype(jnp.float32)
        fs[p + 1, SUB - 1 : SUB, :] = f_left[p : p + 1, :]
        fs[p + 1, end : end + 1, :] = f_right[p : p + 1, :]
    for copy in copies:
        copy.wait()
    for p in range(planes + 2):
        ks[p + 1, SUB - 2 : SUB, :] = k_left[p]
        ks[p + 1, end : end + 2, :] = k_right[p]

    @pl.when(flags[0] == 1)
    def _():
        ks[1] = ks[2]

    @pl.when(flags[1] == 1)
    def _():
        ks[planes + 2] = ks[planes + 1]

    @pl.when(flags[2] == 1)
    def _():
        for p in range(planes + 4):
            ks[p, SUB - 1 : SUB, :] = ks[p, SUB : SUB + 1, :]

    @pl.when(flags[3] == 1)
    def _():
        for p in range(planes + 4):
            ks[p, end : end + 1, :] = ks[p, end - 1 : end, :]

    def first(p, carry):
        for top in range(0, cells + 2 * SUB, SUB):
            k = ks[p + 1, top : top + SUB, :]
            if top == 0:
                above = pltpu.roll(k, 1, 0)
            else:
                above = ks[p + 1, top - 1 : top + SUB - 1, :]
            if top == cells + SUB:
                below = pltpu.roll(k, SUB - 1, 0)
            else:
                below = ks[p + 1, top + 1 : top + SUB + 1, :]
            total = ks[p, top : top + SUB, :] + ks[p + 2, top : top + SUB, :]
            total = total + (above + below) + beside(k, True)
            scale = JACOBI_WEIGHT / (3.0 * k + 0.5 * total)
            u = fs[p, top : top + SUB, :] * scale
            us[p, top : top + SUB, :] = u
            ws[p, top : top + SUB, :] = k * u
            rs[p, top : top + SUB, :] = scale
        return carry

    lax.fori_loop(0, planes + 2, first, 0)

    def second(p, carry):
        for top in range(SUB, end, SUB):
            at = slice(top, top + SUB)
            sums = []
            for held in (us, ws):
                total = held[p, at, :] + held[p + 2, at, :]
                total = total + (
                    held[p + 1, top - 1 : top + SUB - 1, :]
                    + held[p + 1, top + 1 : top + SUB + 1, :]
                )
                sums.append(total + beside(held[p + 1, at, :], False))
            coupled = 0.5 * (ks[p + 2, at, :] * sums[0] + sums[1])
            out[p, top - SUB : top, :] = rs[p + 1, at, :] * (
                (2.0 - JACOBI_WEIGHT) * fs[p + 1, at, :] + coupled
            )
        return carry

    lax.fori_loop(0, planes, second, 0)


def call(kernel, out, operands, scratch, flops, specs=None, limit=48):
    moved = sum(x.size * x.dtype.itemsize for x in operands) + out.size * out.dtype.itemsize
    vmem = pl.BlockSpec(memory_space=pltpu.VMEM)
    return pl.pallas_call(
        kernel,
        out_shape=out,
        in_specs=specs or [vmem] * len(operands),
        out_specs=vmem,
        scratch_shapes=scratch,
        compiler_params=pltpu.CompilerParams(vmem_limit_bytes=limit * MIB),
        cost_estimate=pl.CostEstimate(flops=flops, bytes_accessed=moved, transcendentals=0),
    )(*operands)


def f32(*shape):
    return jax.ShapeDtypeStruct(shape, jnp.float32)


def halos(x, axis, dim, width):
    peers, length = lax.axis_size(axis), x.shape[dim]
    up = [(i, i + 1) for i in range(peers - 1)]
    down = [(j, i) for i, j in up]
    last = lax.slice_in_dim(x, length - width, length, axis=dim)
    leading = lax.slice_in_dim(x, 0, width, axis=dim)
    return lax.ppermute(last, axis, up), lax.ppermute(leading, axis, down)


def smooth(kappa, source, source_halo):
    planes, cells, length = kappa.shape
    row_at, rows = lax.axis_index("row"), lax.axis_size("row")
    group_at, groups = lax.axis_index(PLANE), lax.axis_size(PLANE)
    flags = jnp.stack(
        [row_at == 0, row_at == rows - 1, group_at == 0, group_at == groups - 1]
    ).astype(jnp.int32)
    k_lo, k_hi = halos(kappa, "row", 0, 2)
    first = jnp.concatenate([k_lo[1:, :2], kappa[:, :2], k_hi[:1, :2]], axis=0)
    last = jnp.concatenate([k_lo[1:, cells - 2 :], kappa[:, cells - 2 :], k_hi[:1, cells - 2 :]], axis=0)
    up = [(i, i + 1) for i in range(groups - 1)]
    k_left = lax.ppermute(last, PLANE, up)
    k_right = lax.ppermute(first, PLANE, [(j, i) for i, j in up])
    vmem = pl.BlockSpec(memory_space=pltpu.VMEM)
    anywhere = pl.BlockSpec(memory_space=pl.ANY)
    f_lo, f_hi, f_left, f_right = source_halo
    ext = cells + 2 * SUB
    wide = pltpu.VMEM((planes + 2, ext, length), jnp.float32)
    return call(
        stencil_kernel,
        f32(planes, cells, length),
        (flags, kappa, k_lo, k_hi, k_left, k_right, source, f_lo, f_hi, f_left, f_right),
        [
            pltpu.VMEM((planes + 4, ext, length), jnp.float32),
            wide, wide, wide, wide,
            pltpu.SemaphoreType.DMA((5,)),
        ],
        60 * kappa.size,
        [pl.BlockSpec(memory_space=pltpu.SMEM)]
        + [anywhere] * 3 + [vmem] * 3 + [anywhere] * 2 + [vmem] * 2,
    )


def source_edges(source):
    planes = source.shape[0]
    lo, hi = halos(source, "row", 0, 1)
    left, right = halos(source, PLANE, 1, 1)
    return lo, hi, left.reshape(planes, -1), right.reshape(planes, -1)


def fused_body(noise, source):
    rows, groups = lax.axis_size("row"), lax.axis_size(PLANE)
    devices = rows * groups
    planes, cells, length = noise.shape
    first, second = planes * rows, cells * groups
    bf16 = jnp.bfloat16
    held = length // 2 // devices
    chunks = [list(range(held // 2)), list(range(held // 2, held))]
    me = lax.axis_index(EVERY)
    norm = FIELD_SCALE * (float(first) * float(second) * float(length)) ** (-0.5)
    x = noise.reshape(planes * cells, length)

    arrived = []
    for js in chunks:
        count = 2 * len(js)
        table = two_parts(forward_third(length, devices, js))
        sent = call(
            functools.partial(forward_kernel, planes),
            f32(devices * count * SUB, LANE),
            (*table, x),
            [],
            4 * devices * count * length * planes * cells,
        )
        sent = sent.reshape(devices, count, SUB, LANE)
        arrived.append(lax.all_to_all(sent, EVERY, split_axis=0, concat_axis=0, tiled=True))

    pairs = np.zeros((length, length // 2), np.float32)
    pairs[np.arange(length), np.arange(length) // 2] = 0.125
    coarse_source = call(
        functools.partial(mean_kernel, planes),
        f32(planes * cells // 4, length // 2),
        (pairs.astype(bf16), source.reshape(planes * cells, length)),
        [
            pltpu.VMEM((planes * cells, length // 2), jnp.float32),
            pltpu.VMEM((cells, LANE), jnp.float32),
        ],
        planes * cells * length * length,
    ).reshape(planes // 2, cells // 2, length // 2)
    fine_edges = source_edges(source.astype(jnp.float32))
    coarse_edges = source_edges(coarse_source)

    table = two_parts(second_table(second))
    back_table = two_parts(second_table(second).T)
    outer = two_parts(forward_first(first)) + two_parts(inverse_first(first))
    coarse_outer = two_parts(inverse_first_coarse(first // 2, rows))
    coarse_table = two_parts(second_coarse(second // 2, groups))
    returned = []
    for at, js in enumerate(chunks):
        low = at == 0
        count = 2 * len(js)
        tiles = count + (len(js) // 2 if low else 0)
        modes = (me + devices * np.array(js)).astype(jnp.float32)
        weight = jnp.where(modes == 0.0, norm, 2.0 * norm).astype(jnp.float32)
        scale = jnp.stack([DECAY * modes * modes, weight], axis=1)
        operands = (scale, arrived[at], *table, *outer, *back_table)
        scratch = [
            pltpu.VMEM((count * first, second), bf16),
            pltpu.VMEM((count * first, second), bf16),
            pltpu.VMEM((count * first, second), jnp.float32),
            pltpu.VMEM((count * first, second), bf16),
            pltpu.VMEM((count * first, second), bf16),
        ]
        if low:
            operands += (*coarse_outer, *coarse_table)
            scratch += [pltpu.VMEM((len(js) // 2 * first, second), bf16)] * 2
        out = call(
            functools.partial(middle_kernel, (first, second, rows, groups, len(js), low)),
            f32(devices, tiles, SUB, LANE),
            operands,
            scratch,
            6 * 2 * count * first * second * (second + 2 * first),
            [pl.BlockSpec(memory_space=pltpu.SMEM)]
            + [pl.BlockSpec(memory_space=pltpu.VMEM)] * (len(operands) - 1),
        )
        returned.append(lax.all_to_all(out, EVERY, split_axis=0, concat_axis=0, tiled=True))

    fine = None
    for at, js in enumerate(chunks):
        count = 2 * len(js)
        tiles = returned[at].shape[1]
        last = at == len(chunks) - 1
        got = returned[at].reshape(devices * tiles * SUB, LANE)
        operands = (got, *two_parts(inverse_third(length, devices, js)))
        if last:
            operands += (fine,)
        fine = call(
            functools.partial(back_kernel, (devices, count, tiles, planes), last),
            f32(planes * cells, length),
            operands,
            [pltpu.VMEM((planes * cells, devices * count), bf16)] * 2,
            6 * planes * cells * devices * count * length,
        )
        if at == 0:
            coarse = call(
                functools.partial(
                    coarse_back_kernel, (devices, count, tiles, planes // 2, length // 2)
                ),
                f32(planes * cells // 4, length // 2),
                (got, *two_parts(third_coarse(length // 2, devices, js))),
                [pltpu.VMEM((planes // 2 * LANE, devices * count // 2), bf16)] * 2,
                6 * planes * cells // 4 * devices * count * length,
            ).reshape(coarse_source.shape)
            coarse_pressure = smooth(coarse, coarse_source, coarse_edges)
    fine_pressure = smooth(fine.reshape(noise.shape), source, fine_edges)
    return fine_pressure, coarse_pressure
NEIGHBOUR_STEPS = ((1, 0, 0), (-1, 0, 0), (0, 1, 0), (0, -1, 0), (0, 0, 1), (0, 0, -1))


def padded(x, sides, width):
    for axis, dim in sides:
        peers, length = (lax.axis_size(axis), x.shape[dim])
        up = [(i, (i + 1) % peers) for i in range(peers - 1)]
        down = [(j, i) for i, j in up]
        last = lax.slice_in_dim(x, length - width, length, axis=dim)
        leading = lax.slice_in_dim(x, 0, width, axis=dim)
        before = lax.ppermute(last, axis, up)
        after = lax.ppermute(leading, axis, down)
        x = jnp.concatenate([before, x, after], axis=dim)
    return x


def signed_modes(index, length):
    return jnp.where(index < length // 2, index, index - length).astype(jnp.float32)


def amplitude(first_modes, second_modes, third_modes, first_edge, second_edge, third_edge):
    squared = first_modes * first_modes + second_modes * second_modes + third_modes * third_modes
    value = FIELD_SCALE / (1.0 + (2.0 * math.pi * CORRELATION) ** 2 * squared)
    edge = (
        (jnp.abs(first_modes) == first_edge)
        | (jnp.abs(second_modes) == second_edge)
        | (jnp.abs(third_modes) == third_edge)
    )
    return jnp.where(edge, 0.0, value)


def phase_table(count_rows, count_cols, modulus, sign):
    left_index = jnp.arange(count_rows, dtype=jnp.int32)[:, None]
    right_index = jnp.arange(count_cols, dtype=jnp.int32)[None, :]
    angle = 2.0 * math.pi / modulus * (left_index * right_index % modulus).astype(jnp.float32)
    return (jnp.cos(angle), sign * jnp.sin(angle))


def split_length(length):
    outer_len = 2 ** ((length.bit_length() - 1) // 2)
    return (outer_len, length // outer_len)


def real_form(form, left_value, right_value):
    return jnp.einsum(form, left_value, right_value, precision=lax.Precision.HIGHEST)


def complex_form(form, left_real, left_imag, right_real, right_imag):
    real_part = real_form(form, left_real, right_real) - real_form(form, left_imag, right_imag)
    imag_part = real_form(form, left_real, right_imag) + real_form(form, left_imag, right_real)
    return (real_part, imag_part)


def merge_pair(values, out_form, first_letter):
    merge_at = out_form.index(first_letter)
    out_dims = list(values.shape)
    merged = (
        out_dims[:merge_at]
        + [out_dims[merge_at] * out_dims[merge_at + 1]]
        + out_dims[merge_at + 2 :]
    )
    return values.reshape(merged)


def forward_axis(real_part, imag_part, lead_form, out_form, kept_modes):
    length = real_part.shape[-1]
    outer_len, inner_len = split_length(length)
    split_shape = real_part.shape[:-1] + (outer_len, inner_len)
    outer_real, outer_imag = phase_table(outer_len, outer_len, outer_len, -1.0)
    twist_real, twist_imag = phase_table(outer_len, inner_len, length, -1.0)
    inner_real, inner_imag = phase_table(inner_len, kept_modes // outer_len, inner_len, -1.0)
    first_form = lead_form + "ab,ai->" + lead_form + "ib"
    split_real = real_part.reshape(split_shape)
    if imag_part is None:
        section_real = real_form(first_form, split_real, outer_real)
        section_imag = real_form(first_form, split_real, outer_imag)
    else:
        section_real, section_imag = complex_form(
            first_form, split_real, imag_part.reshape(split_shape), outer_real, outer_imag
        )
    turned_real = section_real * twist_real - section_imag * twist_imag
    turned_imag = section_real * twist_imag + section_imag * twist_real
    result_real, result_imag = complex_form(
        lead_form + "ib,bj->" + out_form, turned_real, turned_imag, inner_real, inner_imag
    )
    return (merge_pair(result_real, out_form, "j"), merge_pair(result_imag, out_form, "j"))


def inverse_axis(real_part, imag_part, length, lead_form, out_form, real_only):
    kept_modes = real_part.shape[-1]
    outer_len, inner_len = split_length(length)
    split_shape = real_part.shape[:-1] + (kept_modes // outer_len, outer_len)
    inner_real, inner_imag = phase_table(kept_modes // outer_len, inner_len, inner_len, 1.0)
    twist_real, twist_imag = phase_table(outer_len, inner_len, length, 1.0)
    outer_real, outer_imag = phase_table(outer_len, outer_len, outer_len, 1.0)
    section_real, section_imag = complex_form(
        lead_form + "ji,jb->" + lead_form + "ib",
        real_part.reshape(split_shape),
        imag_part.reshape(split_shape),
        inner_real,
        inner_imag,
    )
    turned_real = section_real * twist_real - section_imag * twist_imag
    turned_imag = section_real * twist_imag + section_imag * twist_real
    second_form = lead_form + "ib,ia->" + out_form
    if real_only:
        result = real_form(second_form, turned_real, outer_real) - real_form(
            second_form, turned_imag, outer_imag
        )
        return merge_pair(result, out_form, "a")
    result_real, result_imag = complex_form(
        second_form, turned_real, turned_imag, outer_real, outer_imag
    )
    return (merge_pair(result_real, out_form, "a"), merge_pair(result_imag, out_form, "a"))


def low_band(values, half_coarse, fine_len):
    return jnp.concatenate(
        [values[:, :, :half_coarse], values[:, :, fine_len - half_coarse :]], axis=2
    )


def window(values, margin, offset):
    return values[
        margin + offset[0] : values.shape[0] - margin + offset[0],
        margin + offset[1] : values.shape[1] - margin + offset[1],
        margin + offset[2] : values.shape[2] - margin + offset[2],
    ]


def face_weight(center, beside):
    return jnp.where(beside > 0.0, 0.5 * (center + beside), center)


def smooth_twice(kappa, source):
    no_shift = (0, 0, 0)
    center = window(kappa, 1, no_shift)
    faces = [face_weight(center, window(kappa, 1, offset)) for offset in NEIGHBOUR_STEPS]
    diagonal = faces[0] + faces[1] + faces[2] + faces[3] + faces[4] + faces[5]
    guarded = jnp.where(center > 0.0, diagonal, 1.0)
    first_sweep = JACOBI_WEIGHT * window(source, 1, no_shift) / guarded
    inner_first = window(first_sweep, 1, no_shift)
    inner_diagonal = window(diagonal, 1, no_shift)
    coupled = jnp.zeros_like(inner_first)
    for face_value, offset in zip(faces, NEIGHBOUR_STEPS):
        coupled = coupled + window(face_value, 1, no_shift) * window(first_sweep, 1, offset)
    residual = window(source, 2, no_shift) - inner_diagonal * inner_first + coupled
    return inner_first + JACOBI_WEIGHT * residual / inner_diagonal


def pad_depth(values):
    return jnp.pad(values, ((0, 0), (0, 0), (2, 2)))


def plain_body(noise, source):
    row_at = lax.axis_index("row")
    group_at = lax.axis_index(("level", "col"))
    fine_field = noise.astype(jnp.float32)
    fine_len = fine_field.shape[-1]
    coarse_len = fine_len // 2
    half_coarse = coarse_len // 2
    kept_modes = fine_len // 2
    real_part, imag_part = forward_axis(fine_field, None, "pq", "pjiq", kept_modes)
    real_part, imag_part = (
        lax.all_to_all(real_part, ("level", "col"), split_axis=1, concat_axis=2, tiled=True),
        lax.all_to_all(imag_part, ("level", "col"), split_axis=1, concat_axis=2, tiled=True),
    )
    real_part, imag_part = forward_axis(real_part, imag_part, "pq", "jiqp", fine_len)
    real_part, imag_part = (
        lax.all_to_all(real_part, "row", split_axis=0, concat_axis=2, tiled=True),
        lax.all_to_all(imag_part, "row", split_axis=0, concat_axis=2, tiled=True),
    )
    slab_len = real_part.shape[-1]
    coarse_slab = slab_len // 2
    half_slab = coarse_slab // 2
    real_part, imag_part = forward_axis(real_part, imag_part, "pq", "pqji", slab_len)
    second_count = real_part.shape[0]
    third_count = real_part.shape[1]
    wave_second = signed_modes(
        row_at * second_count + jnp.arange(second_count, dtype=jnp.int32), fine_len
    )[:, None, None]
    third_index = group_at * third_count + jnp.arange(third_count, dtype=jnp.int32)
    wave_third = signed_modes(third_index, fine_len)[None, :, None]
    spread = 2.0
    mirror_weight = jnp.where(third_index == 0, 1.0, spread).astype(jnp.float32)[None, :, None]
    norm_factor = (float(slab_len) * float(fine_len) * float(fine_len)) ** (-0.5)
    wave_first = signed_modes(jnp.arange(slab_len, dtype=jnp.int32), slab_len)[None, None, :]
    fine_scale = (
        amplitude(
            wave_second, wave_third, wave_first, fine_len / 2.0, fine_len / 2.0, slab_len / 2.0
        )
        * mirror_weight
        * norm_factor
    )
    coarse_first = signed_modes(jnp.arange(coarse_slab, dtype=jnp.int32), coarse_slab)[
        None, None, :
    ]
    coarse_scale = (
        amplitude(
            wave_second,
            wave_third,
            coarse_first,
            coarse_len / 2.0,
            coarse_len / 2.0,
            coarse_slab / 2.0,
        )
        * mirror_weight
        * norm_factor
    )
    coarse_real = low_band(real_part, half_slab, slab_len) * coarse_scale
    coarse_imag = low_band(imag_part, half_slab, slab_len) * coarse_scale
    fine_real, fine_imag = inverse_axis(
        real_part * fine_scale, imag_part * fine_scale, slab_len, "pq", "abqp", False
    )
    coarse_real, coarse_imag = inverse_axis(
        coarse_real, coarse_imag, coarse_slab, "pq", "abqp", False
    )
    fine_real, fine_imag, coarse_real, coarse_imag = (
        lax.all_to_all(fine_real, "row", split_axis=0, concat_axis=2, tiled=True),
        lax.all_to_all(fine_imag, "row", split_axis=0, concat_axis=2, tiled=True),
        lax.all_to_all(coarse_real, "row", split_axis=0, concat_axis=2, tiled=True),
        lax.all_to_all(coarse_imag, "row", split_axis=0, concat_axis=2, tiled=True),
    )
    coarse_real = low_band(coarse_real, half_coarse, fine_len)
    coarse_imag = low_band(coarse_imag, half_coarse, fine_len)
    fine_real, fine_imag = inverse_axis(fine_real, fine_imag, fine_len, "pq", "pabq", False)
    coarse_real, coarse_imag = inverse_axis(
        coarse_real, coarse_imag, coarse_len, "pq", "pabq", False
    )
    fine_real, fine_imag, coarse_real, coarse_imag = (
        lax.all_to_all(fine_real, ("level", "col"), split_axis=1, concat_axis=2, tiled=True),
        lax.all_to_all(fine_imag, ("level", "col"), split_axis=1, concat_axis=2, tiled=True),
        lax.all_to_all(coarse_real, ("level", "col"), split_axis=1, concat_axis=2, tiled=True),
        lax.all_to_all(coarse_imag, ("level", "col"), split_axis=1, concat_axis=2, tiled=True),
    )
    coarse_real = coarse_real[:, :, :half_coarse]
    coarse_imag = coarse_imag[:, :, :half_coarse]
    fine_log = inverse_axis(fine_real, fine_imag, fine_len, "pq", "pqab", True)
    coarse_log = inverse_axis(coarse_real, coarse_imag, coarse_len, "pq", "pqab", True)
    fine_kappa = jnp.exp(fine_log)
    coarse_kappa = jnp.exp(coarse_log)
    fine_source = source.astype(jnp.float32)
    coarse_rows = coarse_log.shape[0]
    coarse_cols = coarse_log.shape[1]
    coarse_source = fine_source.reshape(coarse_rows, 2, coarse_cols, 2, coarse_len, 2).mean(
        axis=(1, 3, 5)
    )
    fine_kappa, fine_source, coarse_kappa, coarse_source = (
        padded(fine_kappa, (("row", 0), (("level", "col"), 1)), 2),
        padded(fine_source, (("row", 0), (("level", "col"), 1)), 2),
        padded(coarse_kappa, (("row", 0), (("level", "col"), 1)), 2),
        padded(coarse_source, (("row", 0), (("level", "col"), 1)), 2),
    )
    fine_pressure = smooth_twice(pad_depth(fine_kappa), pad_depth(fine_source))
    coarse_pressure = smooth_twice(pad_depth(coarse_kappa), pad_depth(coarse_source))
    return (fine_pressure, coarse_pressure)


def body(noise, source):
    planes, cells, length = noise.shape
    devices = lax.axis_size(EVERY)
    held = length // 2 // devices
    if planes == SUB and cells == LANE and held % 4 == 0 and held > 0:
        return fused_body(noise, source)
    return plain_body(noise, source)


def solution(mesh):
    return jax.shard_map(
        body,
        mesh=mesh,
        in_specs=(P("row", ("level", "col"), None), P("row", ("level", "col"), None)),
        out_specs=(P("row", ("level", "col"), None), P("row", ("level", "col"), None)),
        check_vma=False,
    )
```

```python
import functools
import math

import jax
import jax.numpy as jnp
import numpy as np
from jax import lax
from jax.experimental import pallas as pl
from jax.experimental.pallas import tpu as pltpu
from jax.sharding import PartitionSpec as P

JACOBI_WEIGHT = 2.0 / 3.0
CORRELATION = 0.2
FIELD_SCALE = 0.3
DECAY = (2.0 * math.pi * CORRELATION) ** 2
EVERY = ("row", "level", "col")
PLANE = ("level", "col")
MIB = 1 << 20
SUB, LANE = 8, 128


def two_parts(matrix):
    high = matrix.astype(jnp.bfloat16)
    low = (matrix - high.astype(np.float64)).astype(jnp.bfloat16)
    return high, low


def angles(rows, cols, length):
    return 2.0 * np.pi * (np.outer(rows, cols) % length) / length


def third_modes(devices, js):
    return np.array([[d + devices * j for j in js] for d in range(devices)])


def forward_third(length, devices, js):
    theta = angles(third_modes(devices, js).reshape(-1), np.arange(length), length)
    return np.stack([np.cos(theta), -np.sin(theta)], axis=1).reshape(-1, length)


def inverse_third(length, devices, js):
    theta = angles(third_modes(devices, js).reshape(-1), np.arange(length), length)
    return np.stack([np.cos(theta), -np.sin(theta)], axis=1).reshape(-1, length)


def second_table(length):
    theta = angles(np.arange(length), np.arange(length // 2), length)
    return np.concatenate([np.cos(theta), np.sin(theta)], axis=1)


def forward_first(length):
    theta = angles(np.arange(length), np.arange(length), length)
    cos, sin = np.cos(theta), np.sin(theta)
    return np.block([[cos, sin], [-sin, cos]])


def inverse_first(length):
    theta = angles(np.arange(length), np.arange(length), length)
    cos, sin = np.cos(theta), np.sin(theta)
    cos[:, length // 2] = 0.0
    sin[:, length // 2] = 0.0
    return np.block([[cos, -sin], [sin, cos]])


def inverse_first_coarse(length, rows):
    full = inverse_first(length)
    value = full.reshape(2, rows, length // rows, 2 * length)
    turned = np.concatenate([-full[length:], full[:length]]).reshape(value.shape)
    order = lambda x: x.transpose(1, 0, 2, 3).reshape(2 * length, 2 * length)
    return np.concatenate([order(value), order(turned)])


def second_coarse(length, groups):
    table = second_table(length).T
    span = length // groups
    out = np.zeros((2, length, groups, 2, span))
    for pair in range(2):
        out[pair, :, :, pair, :] = table.reshape(length, groups, span)
    return out.reshape(2 * length, 2 * length)


def third_coarse(length, devices, js):
    modes = third_modes(devices, js).reshape(devices, len(js) // 2, 2)
    theta = 2.0 * np.pi * (modes[..., None] * np.arange(length) % length) / length
    both = np.stack([np.cos(theta), -np.sin(theta)])
    return both.transpose(0, 2, 1, 3, 4).reshape(2 * (len(js) // 2) * devices, 2 * length)


def split(x):
    high = x.astype(jnp.bfloat16)
    return high, (x - high.astype(jnp.float32)).astype(jnp.bfloat16)


def dot(a, b):
    return lax.dot_general(a, b, (((1,), (0,)), ((), ())), preferred_element_type=jnp.float32)


def dot_t(a, b):
    return lax.dot_general(a, b, (((1,), (1,)), ((), ())), preferred_element_type=jnp.float32)


def dot3(a, b):
    (ah, al), (bh, bl) = a, b
    return dot(ah, bh) + (dot(ah, bl) + dot(al, bh))


def load(pairs, sems):
    copies = [pltpu.make_async_copy(a, b, sems.at[i]) for i, (a, b) in enumerate(pairs)]
    for copy in copies:
        copy.start()
    return copies


def forward_kernel(planes, dh_hbm, dl_hbm, x_hbm, out, dh, dl, x, sems):
    rows = dh.shape[0]
    parts = [slice(p * LANE, (p + 2) * LANE) for p in range(0, planes, 2)]
    copies = load(
        [(dh_hbm, dh), (x_hbm.at[parts[0], :], x.at[parts[0], :]), (dl_hbm, dl)]
        + [(x_hbm.at[at, :], x.at[at, :]) for at in parts[1:]],
        sems,
    )
    for i, at in enumerate(parts):
        for copy in copies[:3] if i == 0 else [copies[i + 2]]:
            copy.wait()
        part = x[at, :]
        value = dot_t(dh[...], part) + dot_t(dl[...], part)
        for h in range(2):
            out[pl.ds(2 * i + h, rows, stride=SUB), :] = value[:, h * LANE : (h + 1) * LANE]


def middle_kernel(sizes, scale, b, *rest):
    (first, second, rows, groups, start, js, low) = sizes
    count = 12 if low else 8
    away, rest = rest[:count], rest[count:]
    out, near, rest = rest[0], rest[1 : 1 + count], rest[1 + count :]
    sems, zh, zl, y, oh, ol = rest[:6]
    copies = load(list(zip(away, near)), sems)
    csh, csl, fh, fl, ih, il, ch, cl = near[:8]
    if low:
        ich, icl, cch, ccl = near[8:]
        qh, ql = rest[6:]
    q_count = 2 * js
    half = second // 2
    for q in range(q_count):
        for g in range(groups):
            for r in range(0, rows, 2):
                at = r * groups + g
                pair = jnp.concatenate([b[at, start + q], b[at + groups, start + q]], axis=0)
                high, rest_part = split(pair)
                at = q * first + r * SUB
                zh[at : at + 2 * SUB, g * LANE : (g + 1) * LANE] = high
                zl[at : at + 2 * SUB, g * LANE : (g + 1) * LANE] = rest_part
    for copy in copies:
        copy.wait()
    y[...] = dot3((zh[...], zl[...]), (csh[...], csl[...]))
    mode0 = lax.broadcasted_iota(jnp.int32, (first, second), 0)
    mode0 = jnp.where(mode0 < first // 2, mode0, mode0 - first).astype(jnp.float32)
    lane = lax.broadcasted_iota(jnp.int32, (first, second), 1)
    mode1 = jnp.where(lane < half, lane, lane - half).astype(jnp.float32)
    base = 1.0 + DECAY * (mode0 * mode0 + mode1 * mode1)
    for j in range(js):
        top = j * 2 * first
        re, im = y[top : top + first, :], y[top + first : top + 2 * first, :]
        rc, rs, ic, isn = re[:, :half], re[:, half:], im[:, :half], im[:, half:]
        wave = jnp.concatenate(
            [
                jnp.concatenate([rc + isn, rc - isn], axis=1),
                jnp.concatenate([ic - rs, ic + rs], axis=1),
            ],
            axis=0,
        )
        spectrum = dot3((fh[...], fl[...]), split(wave))
        amp = jnp.where(lane == half, 0.0, scale[j, 1] / (base + scale[j, 0]))
        scaled = spectrum * jnp.concatenate([amp, amp], axis=0)
        field = dot3((ih[...], il[...]), split(scaled))
        plus, minus = field[:, :half], field[:, half:]
        even, odd = plus + minus, plus - minus
        operand = jnp.concatenate(
            [even, jnp.concatenate([-odd[first:], odd[:first]], axis=0)], axis=1
        )
        high, rest_part = split(operand)
        oh[top : top + 2 * first, :] = high
        ol[top : top + 2 * first, :] = rest_part
        if low:
            quarter = half // 2
            keep = first // 4
            kept = [
                scaled[at : at + keep, :]
                for at in (0, first - keep, first, 2 * first - keep)
            ]
            band = jnp.concatenate(kept, axis=0)
            band = jnp.concatenate([band[:, :quarter], band[:, half : half + quarter]], axis=1)
            field = dot3((ich[...], icl[...]), split(band))
            value, turned = field[:first], field[first:]
            operand = jnp.concatenate(
                [
                    value[:, :quarter] + value[:, quarter:],
                    turned[:, :quarter] - turned[:, quarter:],
                ],
                axis=1,
            )
            high, rest_part = split(operand)
            at_row, at_lane = (j // 2) * first, (j % 2) * half
            qh[at_row : at_row + first, at_lane : at_lane + half] = high
            ql[at_row : at_row + first, at_lane : at_lane + half] = rest_part
    y[...] = dot3((oh[...], ol[...]), (ch[...], cl[...]))
    for q in range(q_count):
        for r in range(rows):
            for g in range(groups):
                at = q * first + r * SUB
                out[r * groups + g, q] = y[at : at + SUB, g * LANE : (g + 1) * LANE]
    if low:
        coarse = dot3((qh[...], ql[...]), (cch[...], ccl[...]))
        for h in range(js // 2):
            for r in range(rows):
                for g in range(groups):
                    at = h * first + r * SUB
                    out[r * groups + g, q_count + h] = coarse[
                        at : at + SUB, g * LANE : (g + 1) * LANE
                    ]


def back_kernel(sizes, last, b, eh_hbm, el_hbm, *rest):
    (devices, q_count, tiles, planes) = sizes
    if last:
        before_hbm, out, lo, hi, eh, el, lh, ll, before, sems = rest
        copies = load([(eh_hbm, eh), (el_hbm, el), (before_hbm, before)], sems)
    else:
        out, eh, el, lh, ll, sems = rest
        copies = load([(eh_hbm, eh), (el_hbm, el)], sems)
    for n in range(planes):
        if tiles == q_count:
            rows = b[pl.ds(n, devices * q_count, stride=SUB), :]
        else:
            rows = jnp.concatenate(
                [
                    b[pl.ds(s * tiles * SUB + n, q_count, stride=SUB), :]
                    for s in range(devices)
                ],
                axis=0,
            )
        high, rest_part = split(jnp.transpose(rows))
        lh[n * LANE : (n + 1) * LANE, :] = high
        ll[n * LANE : (n + 1) * LANE, :] = rest_part
    for copy in copies:
        copy.wait()
    for p in range(0, planes, 2):
        at = slice(p * LANE, (p + 2) * LANE)
        value = dot3((lh[at, :], ll[at, :]), (eh[...], el[...]))
        if last:
            value = jnp.exp(value + before[at, :])
            if p == 0:
                lo[...] = value
            if p == planes - 2:
                hi[...] = value
        out[at, :] = value


def coarse_back_kernel(sizes, b, eh, el, out, lo, hi, lh, ll):
    (devices, q_count, tiles, planes, length) = sizes
    halves = tiles - q_count
    for n in range(planes):
        rows = jnp.concatenate(
            [
                b[pl.ds((q_count + h) * SUB + c * planes + n, devices, stride=tiles * SUB), :]
                for c in range(2)
                for h in range(halves)
            ],
            axis=0,
        )
        high, rest_part = split(jnp.transpose(rows))
        lh[n * LANE : (n + 1) * LANE, :] = high
        ll[n * LANE : (n + 1) * LANE, :] = rest_part
    value = dot3((lh[...], ll[...]), (eh[...], el[...]))
    half = LANE // 2
    for n in range(planes):
        top = n * LANE
        part = value[top : top + half, :length] + value[top + half : top + LANE, length:]
        part = jnp.exp(part)
        out[n * half : (n + 1) * half, :] = part
        if n < 2:
            lo[n * half : (n + 1) * half, :] = part
        if n >= planes - 2:
            hi[(n - planes + 2) * half : (n - planes + 3) * half, :] = part


def source_kernel(planes, pairs, x, out, lo, hi, left, right, held, summed):
    cells = x.shape[0] // planes
    length = x.shape[1]
    half, fourth = cells // 2, cells // 4
    held[...] = dot(x[...], pairs[...])
    for n in range(planes // 2):
        top = 2 * n * cells
        for at in range(0, out.shape[1], LANE):
            lanes = slice(at, at + LANE)
            summed[...] = held[top : top + cells, lanes] + held[top + cells : top + 2 * cells, lanes]
            out[n * half : (n + 1) * half, lanes] = (
                summed[pl.ds(0, half, stride=2), :] + summed[pl.ds(1, half, stride=2), :]
            )
    for edge, plane in ((lo, 0), (hi, planes - 1)):
        edge[:cells, :] = x[plane * cells : (plane + 1) * cells, :].astype(jnp.float32)
        at = plane // 2 * half
        edge[cells:, : length // 2] = out[at : at + fourth, :]
        edge[cells:, length // 2 :] = out[at + fourth : at + half, :]
    for edge, row in ((left, 0), (right, cells - 1)):
        edge[...] = jnp.zeros_like(edge)
        for n in range(planes):
            at = n * cells + (row // SUB * SUB)
            edge[n : n + 1, :] = x[at : at + SUB, :].astype(jnp.float32)[row % SUB : row % SUB + 1]
        for n in range(planes // 2):
            at = n * half + row // 2
            edge[SUB + n : SUB + n + 1, : length // 2] = out[at : at + 1, :]


def edge_kernel(kappa, k_lo, k_hi, first, last):
    planes, cells, _ = kappa.shape
    for n in range(planes + 2):
        held = k_lo.at[1] if n == 0 else k_hi.at[0] if n == planes + 1 else kappa.at[n - 1]
        first[n] = held[:2, :]
        last[n] = held[cells - 2 :, :]


def beside(x, fill_edge):
    length = x.shape[1]
    lane = lax.broadcasted_iota(jnp.int32, x.shape, 1)
    left = pltpu.roll(x, 1, 1)
    right = pltpu.roll(x, length - 1, 1)
    if fill_edge:
        left = jnp.where(lane == 0, x, left)
        right = jnp.where(lane == length - 1, x, right)
    else:
        left = jnp.where(lane == 0, 0.0, left)
        right = jnp.where(lane == length - 1, 0.0, right)
    return left + right


def stencil_kernel(
    fine, flags, kappa, k_lo, k_hi, f_lo, f_hi, k_left, k_right, f, f_left, f_right,
    out, ks, fs, us, ws, rs, sems,
):
    planes, cells, length = out.shape
    end = SUB + cells
    pairs = [
        (kappa, ks.at[2 : planes + 2, SUB:end, :]),
        (k_lo, ks.at[0:2, SUB:end, :]),
        (k_hi, ks.at[planes + 2 : planes + 4, SUB:end, :]),
    ]
    for edge, plane in ((f_lo, 0), (f_hi, planes + 1)):
        if fine:
            pairs.append((edge.at[:cells, :], fs.at[plane, SUB:end, :]))
        else:
            for h in range(2):
                at = SUB + h * cells // 2
                pairs.append(
                    (
                        edge.at[2 * cells :, h * length : (h + 1) * length],
                        fs.at[plane, at : at + cells // 2, :],
                    )
                )
    copies = load(pairs, sems)
    at = 0 if fine else SUB
    for p in range(planes):
        fs[p + 1, SUB:end, :] = f[p].astype(jnp.float32)
        fs[p + 1, SUB - 1 : SUB, :] = f_left[at + p : at + p + 1, :length]
        fs[p + 1, end : end + 1, :] = f_right[at + p : at + p + 1, :length]
    for copy in copies:
        copy.wait()
    for p in range(planes + 2):
        ks[p + 1, SUB - 2 : SUB, :] = k_left[p]
        ks[p + 1, end : end + 2, :] = k_right[p]

    @pl.when(flags[0] == 1)
    def _():
        ks[1] = ks[2]

    @pl.when(flags[1] == 1)
    def _():
        ks[planes + 2] = ks[planes + 1]

    @pl.when(flags[2] == 1)
    def _():
        for p in range(planes + 4):
            ks[p, SUB - 1 : SUB, :] = ks[p, SUB : SUB + 1, :]

    @pl.when(flags[3] == 1)
    def _():
        for p in range(planes + 4):
            ks[p, end : end + 1, :] = ks[p, end - 1 : end, :]

    def first(p, carry):
        for top in range(0, cells + 2 * SUB, SUB):
            k = ks[p + 1, top : top + SUB, :]
            if top == 0:
                above = pltpu.roll(k, 1, 0)
            else:
                above = ks[p + 1, top - 1 : top + SUB - 1, :]
            if top == cells + SUB:
                below = pltpu.roll(k, SUB - 1, 0)
            else:
                below = ks[p + 1, top + 1 : top + SUB + 1, :]
            total = ks[p, top : top + SUB, :] + ks[p + 2, top : top + SUB, :]
            total = total + (above + below) + beside(k, True)
            scale = JACOBI_WEIGHT / (3.0 * k + 0.5 * total)
            u = fs[p, top : top + SUB, :] * scale
            us[p, top : top + SUB, :] = u
            ws[p, top : top + SUB, :] = k * u
            rs[p, top : top + SUB, :] = scale
        return carry

    lax.fori_loop(0, planes + 2, first, 0)

    def second(p, carry):
        for top in range(SUB, end, SUB):
            at = slice(top, top + SUB)
            sums = []
            for held in (us, ws):
                total = held[p, at, :] + held[p + 2, at, :]
                total = total + (
                    held[p + 1, top - 1 : top + SUB - 1, :]
                    + held[p + 1, top + 1 : top + SUB + 1, :]
                )
                sums.append(total + beside(held[p + 1, at, :], False))
            coupled = 0.5 * (ks[p + 2, at, :] * sums[0] + sums[1])
            out[p, top - SUB : top, :] = rs[p + 1, at, :] * (
                (2.0 - JACOBI_WEIGHT) * fs[p + 1, at, :] + coupled
            )
        return carry

    lax.fori_loop(0, planes, second, 0)


SMEM = pl.BlockSpec(memory_space=pltpu.SMEM)
VMEM = pl.BlockSpec(memory_space=pltpu.VMEM)
AWAY = pl.BlockSpec(memory_space=pl.ANY)


def call(kernel, outs, operands, scratch, flops, specs, limit):
    many = isinstance(outs, (list, tuple))
    written = outs if many else [outs]
    moved = sum(x.size * x.dtype.itemsize for x in (*operands, *written))
    return pl.pallas_call(
        kernel,
        out_shape=outs,
        in_specs=specs,
        out_specs=[VMEM] * len(outs) if many else VMEM,
        scratch_shapes=scratch,
        compiler_params=pltpu.CompilerParams(vmem_limit_bytes=limit * MIB),
        cost_estimate=pl.CostEstimate(flops=flops, bytes_accessed=moved, transcendentals=0),
    )(*operands)


def f32(*shape):
    return jax.ShapeDtypeStruct(shape, jnp.float32)


def room(*arrays):
    return [pltpu.VMEM(x.shape, x.dtype) for x in arrays]


def chain(axis):
    up = [(i, i + 1) for i in range(lax.axis_size(axis) - 1)]
    return up, [(j, i) for i, j in up]


def swap(lo, hi, axis):
    up, down = chain(axis)
    return lax.ppermute(hi, axis, up), lax.ppermute(lo, axis, down)


def smooth(fine, flags, kappa, lo, hi, source, edges):
    planes, cells, length = source.shape
    kappa = kappa.reshape(source.shape)
    flat = (2, cells, length)
    k_lo, k_hi = swap(lo.reshape(flat), hi.reshape(flat), "row")
    first, last = call(
        edge_kernel,
        [f32(planes + 2, 2, length)] * 2,
        (kappa, k_lo, k_hi),
        [],
        kappa.size,
        [VMEM] * 3,
        16,
    )
    k_left, k_right = swap(first, last, PLANE)
    f_lo, f_hi, f_left, f_right = edges
    ext = cells + 2 * SUB
    wide = pltpu.VMEM((planes + 2, ext, length), jnp.float32)
    return call(
        functools.partial(stencil_kernel, fine),
        f32(planes, cells, length),
        (flags, kappa, k_lo, k_hi, f_lo, f_hi, k_left, k_right, source, f_left, f_right),
        [
            pltpu.VMEM((planes + 4, ext, length), jnp.float32),
            wide, wide, wide, wide,
            pltpu.SemaphoreType.DMA((7,)),
        ],
        60 * kappa.size,
        [SMEM] + [AWAY] * 5 + [VMEM] * 5,
        32,
    )


def fused_body(noise, source):
    rows, groups = lax.axis_size("row"), lax.axis_size(PLANE)
    devices = rows * groups
    planes, cells, length = noise.shape
    first, second = planes * rows, cells * groups
    bf16 = jnp.bfloat16
    held = length // 2 // devices
    chunks = [list(range(held // 2)), list(range(held // 2, held))]
    me = lax.axis_index(EVERY)
    row_at, group_at = lax.axis_index("row"), lax.axis_index(PLANE)
    flags = jnp.stack(
        [row_at == 0, row_at == rows - 1, group_at == 0, group_at == groups - 1]
    ).astype(jnp.int32)
    norm = FIELD_SCALE * (float(first) * float(second) * float(length)) ** (-0.5)
    flat = (planes * cells, length)

    table = two_parts(forward_third(length, devices, list(range(held))))
    sent = call(
        functools.partial(forward_kernel, planes),
        f32(length * SUB, LANE),
        (*table, noise.reshape(flat)),
        room(*table) + [pltpu.VMEM(flat, bf16), pltpu.SemaphoreType.DMA((2 + planes // 2,))],
        4 * length * length * planes * cells,
        [AWAY] * 3,
        16,
    )
    sent, source = lax.optimization_barrier((sent, source))
    sent = sent.reshape(devices, 2 * held, SUB, LANE)
    arrived = lax.all_to_all(sent, EVERY, split_axis=0, concat_axis=0, tiled=True)

    pairs = np.zeros((length, length // 2), np.float32)
    pairs[np.arange(length), np.arange(length) // 2] = 0.125
    level = f32(cells + cells // 4, length)
    side = f32(2 * SUB, length)
    coarse_source, *edges = call(
        functools.partial(source_kernel, planes),
        [f32(planes * cells // 4, length // 2), level, level, side, side],
        (pairs.astype(bf16), source.reshape(flat)),
        [
            pltpu.VMEM((planes * cells, length // 2), jnp.float32),
            pltpu.VMEM((cells, LANE), jnp.float32),
        ],
        planes * cells * length * length,
        [VMEM] * 2,
        16,
    )
    coarse_source = coarse_source.reshape(planes // 2, cells // 2, length // 2)
    edges = (*swap(*edges[:2], "row"), *swap(*edges[2:], PLANE))
    arrived, edges, coarse_source = lax.optimization_barrier((arrived, edges, coarse_source))

    outer = two_parts(forward_first(first)) + two_parts(inverse_first(first))
    tables = two_parts(second_table(second)) + outer + two_parts(second_table(second).T)
    coarse_tables = two_parts(inverse_first_coarse(first // 2, rows)) + two_parts(
        second_coarse(second // 2, groups)
    )
    returned = []
    for at, js in enumerate(chunks):
        low = at == 0
        count = 2 * len(js)
        tiles = count + (len(js) // 2 if low else 0)
        modes = (me + devices * np.array(js)).astype(jnp.float32)
        weight = jnp.where(modes == 0.0, norm, 2.0 * norm).astype(jnp.float32)
        scale = jnp.stack([DECAY * modes * modes, weight], axis=1)
        constants = tables + (coarse_tables if low else ())
        block = (count * first, second)
        scratch = room(*constants) + [
            pltpu.SemaphoreType.DMA((len(constants),)),
            pltpu.VMEM(block, bf16),
            pltpu.VMEM(block, bf16),
            pltpu.VMEM(block, jnp.float32),
            pltpu.VMEM(block, bf16),
            pltpu.VMEM(block, bf16),
        ]
        if low:
            scratch += [pltpu.VMEM((len(js) // 2 * first, second), bf16)] * 2
        sizes = (first, second, rows, groups, 2 * js[0], len(js), low)
        out = call(
            functools.partial(middle_kernel, sizes),
            f32(devices, tiles, SUB, LANE),
            (scale, arrived, *constants),
            scratch,
            6 * 2 * count * first * second * (second + 2 * first),
            [SMEM, VMEM] + [AWAY] * len(constants),
            24,
        )
        returned.append(lax.all_to_all(out, EVERY, split_axis=0, concat_axis=0, tiled=True))

    js = chunks[0]
    count, tiles = 2 * len(js), returned[0].shape[1]
    got = returned[0].reshape(devices * tiles * SUB, LANE)
    table = two_parts(third_coarse(length // 2, devices, js))
    coarse = f32(planes * cells // 4, length // 2)
    some = f32(cells, length // 2)
    coarse = call(
        functools.partial(coarse_back_kernel, (devices, count, tiles, planes // 2, length // 2)),
        [coarse, some, some],
        (got, *table),
        [pltpu.VMEM((planes // 2 * LANE, devices * count // 2), bf16)] * 2,
        6 * planes * cells // 4 * devices * count * length,
        [VMEM] * 3,
        16,
    )
    coarse_pressure = smooth(False, flags, *coarse, coarse_source, edges)
    table = two_parts(inverse_third(length, devices, js))
    scratch = [pltpu.VMEM((planes * cells, devices * count), bf16)] * 2
    partial = call(
        functools.partial(back_kernel, (devices, count, tiles, planes), False),
        f32(*flat),
        (got, *table),
        room(*table) + scratch + [pltpu.SemaphoreType.DMA((2,))],
        6 * planes * cells * devices * count * length,
        [VMEM] + [AWAY] * 2,
        24,
    )
    got, partial, coarse_pressure = lax.optimization_barrier(
        (returned[1], partial, coarse_pressure)
    )

    js = chunks[1]
    count, tiles = 2 * len(js), got.shape[1]
    table = two_parts(inverse_third(length, devices, js))
    scratch = [pltpu.VMEM((planes * cells, devices * count), bf16)] * 2
    some = f32(2 * cells, length)
    fine = call(
        functools.partial(back_kernel, (devices, count, tiles, planes), True),
        [f32(*flat), some, some],
        (got.reshape(devices * tiles * SUB, LANE), *table, partial),
        room(*table) + scratch + [pltpu.VMEM(flat, jnp.float32), pltpu.SemaphoreType.DMA((3,))],
        6 * planes * cells * devices * count * length,
        [VMEM] + [AWAY] * 3,
        24,
    )
    fine_pressure = smooth(True, flags, *fine, source, edges)
    return fine_pressure, coarse_pressure


NEIGHBOUR_STEPS = ((1, 0, 0), (-1, 0, 0), (0, 1, 0), (0, -1, 0), (0, 0, 1), (0, 0, -1))


def padded(x, sides, width):
    for axis, dim in sides:
        peers, length = (lax.axis_size(axis), x.shape[dim])
        up = [(i, (i + 1) % peers) for i in range(peers - 1)]
        down = [(j, i) for i, j in up]
        last = lax.slice_in_dim(x, length - width, length, axis=dim)
        leading = lax.slice_in_dim(x, 0, width, axis=dim)
        before = lax.ppermute(last, axis, up)
        after = lax.ppermute(leading, axis, down)
        x = jnp.concatenate([before, x, after], axis=dim)
    return x


def signed_modes(index, length):
    return jnp.where(index < length // 2, index, index - length).astype(jnp.float32)


def amplitude(first_modes, second_modes, third_modes, first_edge, second_edge, third_edge):
    squared = first_modes * first_modes + second_modes * second_modes + third_modes * third_modes
    value = FIELD_SCALE / (1.0 + (2.0 * math.pi * CORRELATION) ** 2 * squared)
    edge = (
        (jnp.abs(first_modes) == first_edge)
        | (jnp.abs(second_modes) == second_edge)
        | (jnp.abs(third_modes) == third_edge)
    )
    return jnp.where(edge, 0.0, value)


def phase_table(count_rows, count_cols, modulus, sign):
    left_index = jnp.arange(count_rows, dtype=jnp.int32)[:, None]
    right_index = jnp.arange(count_cols, dtype=jnp.int32)[None, :]
    angle = 2.0 * math.pi / modulus * (left_index * right_index % modulus).astype(jnp.float32)
    return (jnp.cos(angle), sign * jnp.sin(angle))


def split_length(length):
    outer_len = 2 ** ((length.bit_length() - 1) // 2)
    return (outer_len, length // outer_len)


def real_form(form, left_value, right_value):
    return jnp.einsum(form, left_value, right_value, precision=lax.Precision.HIGHEST)


def complex_form(form, left_real, left_imag, right_real, right_imag):
    real_part = real_form(form, left_real, right_real) - real_form(form, left_imag, right_imag)
    imag_part = real_form(form, left_real, right_imag) + real_form(form, left_imag, right_real)
    return (real_part, imag_part)


def merge_pair(values, out_form, first_letter):
    merge_at = out_form.index(first_letter)
    out_dims = list(values.shape)
    merged = (
        out_dims[:merge_at]
        + [out_dims[merge_at] * out_dims[merge_at + 1]]
        + out_dims[merge_at + 2 :]
    )
    return values.reshape(merged)


def forward_axis(real_part, imag_part, lead_form, out_form, kept_modes):
    length = real_part.shape[-1]
    outer_len, inner_len = split_length(length)
    split_shape = real_part.shape[:-1] + (outer_len, inner_len)
    outer_real, outer_imag = phase_table(outer_len, outer_len, outer_len, -1.0)
    twist_real, twist_imag = phase_table(outer_len, inner_len, length, -1.0)
    inner_real, inner_imag = phase_table(inner_len, kept_modes // outer_len, inner_len, -1.0)
    first_form = lead_form + "ab,ai->" + lead_form + "ib"
    split_real = real_part.reshape(split_shape)
    if imag_part is None:
        section_real = real_form(first_form, split_real, outer_real)
        section_imag = real_form(first_form, split_real, outer_imag)
    else:
        section_real, section_imag = complex_form(
            first_form, split_real, imag_part.reshape(split_shape), outer_real, outer_imag
        )
    turned_real = section_real * twist_real - section_imag * twist_imag
    turned_imag = section_real * twist_imag + section_imag * twist_real
    result_real, result_imag = complex_form(
        lead_form + "ib,bj->" + out_form, turned_real, turned_imag, inner_real, inner_imag
    )
    return (merge_pair(result_real, out_form, "j"), merge_pair(result_imag, out_form, "j"))


def inverse_axis(real_part, imag_part, length, lead_form, out_form, real_only):
    kept_modes = real_part.shape[-1]
    outer_len, inner_len = split_length(length)
    split_shape = real_part.shape[:-1] + (kept_modes // outer_len, outer_len)
    inner_real, inner_imag = phase_table(kept_modes // outer_len, inner_len, inner_len, 1.0)
    twist_real, twist_imag = phase_table(outer_len, inner_len, length, 1.0)
    outer_real, outer_imag = phase_table(outer_len, outer_len, outer_len, 1.0)
    section_real, section_imag = complex_form(
        lead_form + "ji,jb->" + lead_form + "ib",
        real_part.reshape(split_shape),
        imag_part.reshape(split_shape),
        inner_real,
        inner_imag,
    )
    turned_real = section_real * twist_real - section_imag * twist_imag
    turned_imag = section_real * twist_imag + section_imag * twist_real
    second_form = lead_form + "ib,ia->" + out_form
    if real_only:
        result = real_form(second_form, turned_real, outer_real) - real_form(
            second_form, turned_imag, outer_imag
        )
        return merge_pair(result, out_form, "a")
    result_real, result_imag = complex_form(
        second_form, turned_real, turned_imag, outer_real, outer_imag
    )
    return (merge_pair(result_real, out_form, "a"), merge_pair(result_imag, out_form, "a"))


def low_band(values, half_coarse, fine_len):
    return jnp.concatenate(
        [values[:, :, :half_coarse], values[:, :, fine_len - half_coarse :]], axis=2
    )


def window(values, margin, offset):
    return values[
        margin + offset[0] : values.shape[0] - margin + offset[0],
        margin + offset[1] : values.shape[1] - margin + offset[1],
        margin + offset[2] : values.shape[2] - margin + offset[2],
    ]


def face_weight(center, beside):
    return jnp.where(beside > 0.0, 0.5 * (center + beside), center)


def smooth_twice(kappa, source):
    no_shift = (0, 0, 0)
    center = window(kappa, 1, no_shift)
    faces = [face_weight(center, window(kappa, 1, offset)) for offset in NEIGHBOUR_STEPS]
    diagonal = faces[0] + faces[1] + faces[2] + faces[3] + faces[4] + faces[5]
    guarded = jnp.where(center > 0.0, diagonal, 1.0)
    first_sweep = JACOBI_WEIGHT * window(source, 1, no_shift) / guarded
    inner_first = window(first_sweep, 1, no_shift)
    inner_diagonal = window(diagonal, 1, no_shift)
    coupled = jnp.zeros_like(inner_first)
    for face_value, offset in zip(faces, NEIGHBOUR_STEPS):
        coupled = coupled + window(face_value, 1, no_shift) * window(first_sweep, 1, offset)
    residual = window(source, 2, no_shift) - inner_diagonal * inner_first + coupled
    return inner_first + JACOBI_WEIGHT * residual / inner_diagonal


def pad_depth(values):
    return jnp.pad(values, ((0, 0), (0, 0), (2, 2)))


def plain_body(noise, source):
    row_at = lax.axis_index("row")
    group_at = lax.axis_index(("level", "col"))
    fine_field = noise.astype(jnp.float32)
    fine_len = fine_field.shape[-1]
    coarse_len = fine_len // 2
    half_coarse = coarse_len // 2
    kept_modes = fine_len // 2
    real_part, imag_part = forward_axis(fine_field, None, "pq", "pjiq", kept_modes)
    real_part, imag_part = (
        lax.all_to_all(real_part, ("level", "col"), split_axis=1, concat_axis=2, tiled=True),
        lax.all_to_all(imag_part, ("level", "col"), split_axis=1, concat_axis=2, tiled=True),
    )
    real_part, imag_part = forward_axis(real_part, imag_part, "pq", "jiqp", fine_len)
    real_part, imag_part = (
        lax.all_to_all(real_part, "row", split_axis=0, concat_axis=2, tiled=True),
        lax.all_to_all(imag_part, "row", split_axis=0, concat_axis=2, tiled=True),
    )
    slab_len = real_part.shape[-1]
    coarse_slab = slab_len // 2
    half_slab = coarse_slab // 2
    real_part, imag_part = forward_axis(real_part, imag_part, "pq", "pqji", slab_len)
    second_count = real_part.shape[0]
    third_count = real_part.shape[1]
    wave_second = signed_modes(
        row_at * second_count + jnp.arange(second_count, dtype=jnp.int32), fine_len
    )[:, None, None]
    third_index = group_at * third_count + jnp.arange(third_count, dtype=jnp.int32)
    wave_third = signed_modes(third_index, fine_len)[None, :, None]
    spread = 2.0
    mirror_weight = jnp.where(third_index == 0, 1.0, spread).astype(jnp.float32)[None, :, None]
    norm_factor = (float(slab_len) * float(fine_len) * float(fine_len)) ** (-0.5)
    wave_first = signed_modes(jnp.arange(slab_len, dtype=jnp.int32), slab_len)[None, None, :]
    fine_scale = (
        amplitude(
            wave_second, wave_third, wave_first, fine_len / 2.0, fine_len / 2.0, slab_len / 2.0
        )
        * mirror_weight
        * norm_factor
    )
    coarse_first = signed_modes(jnp.arange(coarse_slab, dtype=jnp.int32), coarse_slab)[
        None, None, :
    ]
    coarse_scale = (
        amplitude(
            wave_second,
            wave_third,
            coarse_first,
            coarse_len / 2.0,
            coarse_len / 2.0,
            coarse_slab / 2.0,
        )
        * mirror_weight
        * norm_factor
    )
    coarse_real = low_band(real_part, half_slab, slab_len) * coarse_scale
    coarse_imag = low_band(imag_part, half_slab, slab_len) * coarse_scale
    fine_real, fine_imag = inverse_axis(
        real_part * fine_scale, imag_part * fine_scale, slab_len, "pq", "abqp", False
    )
    coarse_real, coarse_imag = inverse_axis(
        coarse_real, coarse_imag, coarse_slab, "pq", "abqp", False
    )
    fine_real, fine_imag, coarse_real, coarse_imag = (
        lax.all_to_all(fine_real, "row", split_axis=0, concat_axis=2, tiled=True),
        lax.all_to_all(fine_imag, "row", split_axis=0, concat_axis=2, tiled=True),
        lax.all_to_all(coarse_real, "row", split_axis=0, concat_axis=2, tiled=True),
        lax.all_to_all(coarse_imag, "row", split_axis=0, concat_axis=2, tiled=True),
    )
    coarse_real = low_band(coarse_real, half_coarse, fine_len)
    coarse_imag = low_band(coarse_imag, half_coarse, fine_len)
    fine_real, fine_imag = inverse_axis(fine_real, fine_imag, fine_len, "pq", "pabq", False)
    coarse_real, coarse_imag = inverse_axis(
        coarse_real, coarse_imag, coarse_len, "pq", "pabq", False
    )
    fine_real, fine_imag, coarse_real, coarse_imag = (
        lax.all_to_all(fine_real, ("level", "col"), split_axis=1, concat_axis=2, tiled=True),
        lax.all_to_all(fine_imag, ("level", "col"), split_axis=1, concat_axis=2, tiled=True),
        lax.all_to_all(coarse_real, ("level", "col"), split_axis=1, concat_axis=2, tiled=True),
        lax.all_to_all(coarse_imag, ("level", "col"), split_axis=1, concat_axis=2, tiled=True),
    )
    coarse_real = coarse_real[:, :, :half_coarse]
    coarse_imag = coarse_imag[:, :, :half_coarse]
    fine_log = inverse_axis(fine_real, fine_imag, fine_len, "pq", "pqab", True)
    coarse_log = inverse_axis(coarse_real, coarse_imag, coarse_len, "pq", "pqab", True)
    fine_kappa = jnp.exp(fine_log)
    coarse_kappa = jnp.exp(coarse_log)
    fine_source = source.astype(jnp.float32)
    coarse_rows = coarse_log.shape[0]
    coarse_cols = coarse_log.shape[1]
    coarse_source = fine_source.reshape(coarse_rows, 2, coarse_cols, 2, coarse_len, 2).mean(
        axis=(1, 3, 5)
    )
    fine_kappa, fine_source, coarse_kappa, coarse_source = (
        padded(fine_kappa, (("row", 0), (("level", "col"), 1)), 2),
        padded(fine_source, (("row", 0), (("level", "col"), 1)), 2),
        padded(coarse_kappa, (("row", 0), (("level", "col"), 1)), 2),
        padded(coarse_source, (("row", 0), (("level", "col"), 1)), 2),
    )
    fine_pressure = smooth_twice(pad_depth(fine_kappa), pad_depth(fine_source))
    coarse_pressure = smooth_twice(pad_depth(coarse_kappa), pad_depth(coarse_source))
    return (fine_pressure, coarse_pressure)


def body(noise, source):
    planes, cells, length = noise.shape
    devices = lax.axis_size(EVERY)
    held = length // 2 // devices
    if planes == SUB and cells == LANE and held % 4 == 0 and held > 0:
        return fused_body(noise, source)
    return plain_body(noise, source)


def solution(mesh):
    return jax.shard_map(
        body,
        mesh=mesh,
        in_specs=(P("row", ("level", "col"), None), P("row", ("level", "col"), None)),
        out_specs=(P("row", ("level", "col"), None), P("row", ("level", "col"), None)),
        check_vma=False,
    )
```

```python
import functools
import math

import jax
import jax.numpy as jnp
import numpy as np
from jax import lax
from jax.experimental import pallas as pl
from jax.experimental.pallas import tpu as pltpu
from jax.sharding import PartitionSpec as P

JACOBI_WEIGHT = 2.0 / 3.0
CORRELATION = 0.2
FIELD_SCALE = 0.3
DECAY = (2.0 * math.pi * CORRELATION) ** 2
EVERY = ("row", "level", "col")
PLANE = ("level", "col")
MIB = 1 << 20
SUB, LANE = 8, 128
PIECES = 4


def two_parts(matrix):
    high = matrix.astype(jnp.bfloat16)
    low = (matrix - high.astype(np.float64)).astype(jnp.bfloat16)
    return high, low


def angles(rows, cols, length):
    return 2.0 * np.pi * (np.outer(rows, cols) % length) / length


def third_modes(devices, js):
    return np.array([[d + devices * j for j in js] for d in range(devices)])


def forward_third(length, devices, js):
    theta = angles(third_modes(devices, js).reshape(-1), np.arange(length), length)
    return np.stack([np.cos(theta), -np.sin(theta)], axis=1).reshape(-1, length)


def inverse_third(length, devices, js):
    theta = angles(third_modes(devices, js).reshape(-1), np.arange(length), length)
    return np.stack([np.cos(theta), -np.sin(theta)], axis=1).reshape(-1, length)


def second_table(length):
    theta = angles(np.arange(length), np.arange(length // 2), length)
    return np.concatenate([np.cos(theta), np.sin(theta)], axis=1)


def forward_first(length):
    theta = angles(np.arange(length), np.arange(length), length)
    cos, sin = np.cos(theta), np.sin(theta)
    return np.block([[cos, sin], [-sin, cos]])


def inverse_first(length):
    theta = angles(np.arange(length), np.arange(length), length)
    cos, sin = np.cos(theta), np.sin(theta)
    cos[:, length // 2] = 0.0
    sin[:, length // 2] = 0.0
    return np.block([[cos, -sin], [sin, cos]])


def inverse_first_coarse(length, rows):
    full = inverse_first(length)
    value = full.reshape(2, rows, length // rows, 2 * length)
    turned = np.concatenate([-full[length:], full[:length]]).reshape(value.shape)
    order = lambda x: x.transpose(1, 0, 2, 3).reshape(2 * length, 2 * length)
    return np.concatenate([order(value), order(turned)])


def second_coarse(length, groups):
    table = second_table(length).T
    span = length // groups
    out = np.zeros((2, length, groups, 2, span))
    for pair in range(2):
        out[pair, :, :, pair, :] = table.reshape(length, groups, span)
    return out.reshape(2 * length, 2 * length)


def third_coarse(length, devices, js):
    modes = third_modes(devices, js).reshape(devices, len(js) // 2, 2)
    theta = 2.0 * np.pi * (modes[..., None] * np.arange(length) % length) / length
    both = np.stack([np.cos(theta), -np.sin(theta)])
    return both.transpose(0, 2, 1, 3, 4).reshape(2 * (len(js) // 2) * devices, 2 * length)


def split(x):
    high = x.astype(jnp.bfloat16)
    return high, (x - high.astype(jnp.float32)).astype(jnp.bfloat16)


def dot(a, b):
    return lax.dot_general(a, b, (((1,), (0,)), ((), ())), preferred_element_type=jnp.float32)


def dot_t(a, b):
    return lax.dot_general(a, b, (((1,), (1,)), ((), ())), preferred_element_type=jnp.float32)


def dot3(a, b):
    (ah, al), (bh, bl) = a, b
    return dot(ah, bh) + (dot(ah, bl) + dot(al, bh))


def load(pairs, sems):
    copies = [pltpu.make_async_copy(a, b, sems.at[i]) for i, (a, b) in enumerate(pairs)]
    for copy in copies:
        copy.start()
    return copies


def send(pairs, sems, first):
    copies = [pltpu.make_async_copy(a, b, sems.at[first + i]) for i, (a, b) in enumerate(pairs)]
    for copy in copies:
        copy.start()
    return copies


def forward_kernel(planes, dh_hbm, dl_hbm, x_hbm, out_hbm, dh, dl, x, out, sems):
    rows = dh.shape[0]
    step = rows // PIECES
    parts = [slice(i * step, (i + 1) * step) for i in range(PIECES)]
    copies = load(
        [(x_hbm, x)]
        + [
            pair
            for at in parts
            for pair in ((dh_hbm.at[at, :], dh.at[at, :]), (dl_hbm.at[at, :], dl.at[at, :]))
        ],
        sems,
    )
    count = len(copies)
    copies[0].wait()
    for i, at in enumerate(parts):
        copies[2 * i + 1].wait()
        copies[2 * i + 2].wait()
        value = dot_t(dh[at, :], x[...]) + dot_t(dl[at, :], x[...])
        for n in range(planes):
            out[pl.ds(i * step * SUB + n, step, stride=SUB), :] = value[
                :, n * LANE : (n + 1) * LANE
            ]
        tall = slice(i * step * SUB, (i + 1) * step * SUB)
        copies += send([(out.at[tall, :], out_hbm.at[tall, :])], sems, count + i)
    for copy in copies[count:]:
        copy.wait()


def middle_kernel(sizes, scale, b, *rest):
    (first, second, rows, groups, js, low) = sizes
    count = 12
    away, out_hbm, near, rest = rest[:count], rest[count], rest[count + 1 : 2 * count + 1], rest[2 * count + 1 :]
    out, sems, zh, zl, y, oh, ol, qh, ql = rest
    copies = load(list(zip(away, near)), sems)
    csh, csl, fh, fl, ih, il, ch, cl, ich, icl, cch, ccl = near
    q_count = 2 * js
    half = second // 2
    for q in range(q_count):
        for g in range(groups):
            for r in range(0, rows, 2):
                at = r * groups + g
                pair = jnp.concatenate([b[at, q], b[at + groups, q]], axis=0)
                high, rest_part = split(pair)
                at = q * first + r * SUB
                zh[at : at + 2 * SUB, g * LANE : (g + 1) * LANE] = high
                zl[at : at + 2 * SUB, g * LANE : (g + 1) * LANE] = rest_part
    for copy in copies:
        copy.wait()
    wide = 4 * first
    for top in range(0, q_count * first, wide):
        at = slice(top, top + wide)
        y[at, :] = dot3((zh[at, :], zl[at, :]), (csh[...], csl[...]))
    mode0 = lax.broadcasted_iota(jnp.int32, (first, second), 0)
    mode0 = jnp.where(mode0 < first // 2, mode0, mode0 - first).astype(jnp.float32)
    lane = lax.broadcasted_iota(jnp.int32, (first, second), 1)
    mode1 = jnp.where(lane < half, lane, lane - half).astype(jnp.float32)
    base = 1.0 + DECAY * (mode0 * mode0 + mode1 * mode1)
    for j in range(js):
        top = j * 2 * first
        re, im = y[top : top + first, :], y[top + first : top + 2 * first, :]
        rc, rs, ic, isn = re[:, :half], re[:, half:], im[:, :half], im[:, half:]
        wave = jnp.concatenate(
            [
                jnp.concatenate([rc + isn, rc - isn], axis=1),
                jnp.concatenate([ic - rs, ic + rs], axis=1),
            ],
            axis=0,
        )
        spectrum = dot3((fh[...], fl[...]), split(wave))
        amp = jnp.where(lane == half, 0.0, scale[j, 1] / (base + scale[j, 0]))
        scaled = spectrum * jnp.concatenate([amp, amp], axis=0)
        field = dot3((ih[...], il[...]), split(scaled))
        plus, minus = field[:, :half], field[:, half:]
        even, odd = plus + minus, plus - minus
        operand = jnp.concatenate(
            [even, jnp.concatenate([-odd[first:], odd[:first]], axis=0)], axis=1
        )
        high, rest_part = split(operand)
        oh[top : top + 2 * first, :] = high
        ol[top : top + 2 * first, :] = rest_part
        if j < low:
            quarter = half // 2
            keep = first // 4
            kept = [
                scaled[at : at + keep, :]
                for at in (0, first - keep, first, 2 * first - keep)
            ]
            band = jnp.concatenate(kept, axis=0)
            band = jnp.concatenate([band[:, :quarter], band[:, half : half + quarter]], axis=1)
            field = dot3((ich[...], icl[...]), split(band))
            value, turned = field[:first], field[first:]
            operand = jnp.concatenate(
                [
                    value[:, :quarter] + value[:, quarter:],
                    turned[:, :quarter] - turned[:, quarter:],
                ],
                axis=1,
            )
            high, rest_part = split(operand)
            at_row, at_lane = (j // 2) * first, (j % 2) * half
            qh[at_row : at_row + first, at_lane : at_lane + half] = high
            ql[at_row : at_row + first, at_lane : at_lane + half] = rest_part
    copies = []

    def give(value, start):
        tiles = value.shape[0] // first
        for q in range(tiles):
            for r in range(rows):
                for g in range(groups):
                    at = q * first + r * SUB
                    out[r * groups + g, start + q] = value[
                        at : at + SUB, g * LANE : (g + 1) * LANE
                    ]
        at = slice(start, start + tiles)
        copies.extend(send([(out.at[:, at], out_hbm.at[:, at])], sems, len(copies)))

    give(dot3((qh[...], ql[...]), (cch[...], ccl[...])), q_count)
    for top in range(0, q_count * first, wide):
        at = slice(top, top + wide)
        give(dot3((oh[at, :], ol[at, :]), (ch[...], cl[...])), top // first)
    for copy in copies:
        copy.wait()


def back_kernel(sizes, b, *rest):
    (devices, q_count, tiles, planes, length) = sizes
    away, outs, near, (lh, ll, mh, ml, sems) = rest[:4], rest[4:8], rest[8:12], rest[12:]
    out, coarse, lo, hi = outs
    copies = load(list(zip(away, near)), sems)
    eh, el, ceh, cel = near
    cells = LANE
    for n in range(planes):
        rows = jnp.concatenate(
            [b[pl.ds(s * tiles * SUB + n, q_count, stride=SUB), :] for s in range(devices)],
            axis=0,
        )
        high, rest_part = split(jnp.transpose(rows))
        lh[n * LANE : (n + 1) * LANE, :] = high
        ll[n * LANE : (n + 1) * LANE, :] = rest_part
    halves = tiles - q_count
    coarse_planes = planes // 2
    for n in range(coarse_planes):
        rows = jnp.concatenate(
            [
                b[pl.ds((q_count + h) * SUB + c * coarse_planes + n, devices, stride=tiles * SUB), :]
                for c in range(2)
                for h in range(halves)
            ],
            axis=0,
        )
        high, rest_part = split(jnp.transpose(rows))
        mh[n * LANE : (n + 1) * LANE, :] = high
        ml[n * LANE : (n + 1) * LANE, :] = rest_part
    for copy in copies:
        copy.wait()
    for p in range(0, planes, 2):
        at = slice(p * cells, (p + 2) * cells)
        value = jnp.exp(dot3((lh[at, :], ll[at, :]), (eh[...], el[...])))
        if p == 0:
            lo[: 2 * cells, :] = value
        if p == planes - 2:
            hi[: 2 * cells, :] = value
        out[at, :] = value
    value = dot3((mh[...], ml[...]), (ceh[...], cel[...]))
    half, fourth, short = cells // 2, cells // 4, length // 2
    for n in range(coarse_planes):
        top = n * cells
        part = value[top : top + half, :short] + value[top + half : top + cells, short:]
        part = jnp.exp(part)
        coarse[n * half : (n + 1) * half, :] = part
        for edge, start in ((lo, 0), (hi, coarse_planes - 2)):
            if start <= n < start + 2:
                top = 2 * cells + (n - start) * fourth
                edge[top : top + fourth, :short] = part[:fourth]
                edge[top : top + fourth, short:] = part[fourth:]


def source_kernel(planes, pairs, x, out, lo, hi, left, right, held, summed):
    cells = x.shape[0] // planes
    length = x.shape[1]
    half, fourth = cells // 2, cells // 4
    held[...] = dot(x[...], pairs[...])
    for n in range(planes // 2):
        top = 2 * n * cells
        for at in range(0, out.shape[1], LANE):
            lanes = slice(at, at + LANE)
            summed[...] = held[top : top + cells, lanes] + held[top + cells : top + 2 * cells, lanes]
            out[n * half : (n + 1) * half, lanes] = (
                summed[pl.ds(0, half, stride=2), :] + summed[pl.ds(1, half, stride=2), :]
            )
    for edge, plane in ((lo, 0), (hi, planes - 1)):
        edge[:cells, :] = x[plane * cells : (plane + 1) * cells, :].astype(jnp.float32)
        at = plane // 2 * half
        edge[cells:, : length // 2] = out[at : at + fourth, :]
        edge[cells:, length // 2 :] = out[at + fourth : at + half, :]
    for edge, row in ((left, 0), (right, cells - 1)):
        edge[...] = jnp.zeros_like(edge)
        for n in range(planes):
            at = n * cells + (row // SUB * SUB)
            edge[n : n + 1, :] = x[at : at + SUB, :].astype(jnp.float32)[row % SUB : row % SUB + 1]
        for n in range(planes // 2):
            at = n * half + row // 2
            edge[SUB + n : SUB + n + 1, : length // 2] = out[at : at + 1, :]


def edge_kernel(kappa, coarse, k_lo, k_hi, first, last):
    planes, cells, _ = kappa.shape
    coarse_planes, half, short = coarse.shape
    fourth = half // 2
    for n in range(planes + 2):
        if n == 0:
            held = k_lo.at[cells : 2 * cells, :]
        elif n == planes + 1:
            held = k_hi.at[:cells, :]
        else:
            held = kappa.at[n - 1]
        first[n] = held[:2, :]
        last[n] = held[cells - 2 :, :]
    for n in range(coarse_planes + 2):
        at = planes + 2 + n
        if 0 < n < coarse_planes + 1:
            top, bottom = coarse[n - 1, :2, :], coarse[n - 1, half - 2 :, :]
        else:
            held, start = (k_lo, 2 * cells + fourth) if n == 0 else (k_hi, 2 * cells)
            top = held[start : start + 2, :short]
            bottom = held[start + fourth - 2 : start + fourth, short:]
        first[at, :, :short] = top
        last[at, :, :short] = bottom
        first[at, :, short:] = jnp.zeros((2, short), jnp.float32)
        last[at, :, short:] = jnp.zeros((2, short), jnp.float32)


def beside(x, fill_edge):
    length = x.shape[1]
    lane = lax.broadcasted_iota(jnp.int32, x.shape, 1)
    left = pltpu.roll(x, 1, 1)
    right = pltpu.roll(x, length - 1, 1)
    if fill_edge:
        left = jnp.where(lane == 0, x, left)
        right = jnp.where(lane == length - 1, x, right)
    else:
        left = jnp.where(lane == 0, 0.0, left)
        right = jnp.where(lane == length - 1, 0.0, right)
    return left + right


def stencil_kernel(
    fine, flags, kappa, k_lo, k_hi, f_lo, f_hi, k_left, k_right, f, f_left, f_right,
    out, ks, fs, us, ws, rs, sems,
):
    planes, cells, length = out.shape
    end = SUB + cells
    pairs = [(kappa, ks.at[2 : planes + 2, SUB:end, :])]

    def place(edge, row, held, plane):
        if fine:
            pairs.append((edge.at[row : row + cells, :], held.at[plane, SUB:end, :]))
            return
        half = cells // 2
        for h in range(2):
            at = SUB + h * half
            pairs.append(
                (
                    edge.at[row : row + half, h * length : (h + 1) * length],
                    held.at[plane, at : at + half, :],
                )
            )

    for i in range(2):
        row = i * cells if fine else 4 * cells + i * cells // 2
        place(k_lo, row, ks, i)
        place(k_hi, row, ks, planes + 2 + i)
    row = 0 if fine else 2 * cells
    place(f_lo, row, fs, 0)
    place(f_hi, row, fs, planes + 1)
    copies = load(pairs, sems)
    at = 0 if fine else SUB
    for p in range(planes):
        fs[p + 1, SUB:end, :] = f[p].astype(jnp.float32)
        fs[p + 1, SUB - 1 : SUB, :] = f_left[at + p : at + p + 1, :length]
        fs[p + 1, end : end + 1, :] = f_right[at + p : at + p + 1, :length]
    at = 0 if fine else 2 * planes + 2
    for p in range(planes + 2):
        ks[p + 1, SUB - 2 : SUB, :] = k_left[at + p, :, :length]
        ks[p + 1, end : end + 2, :] = k_right[at + p, :, :length]
    for copy in copies:
        copy.wait()

    @pl.when(flags[0] == 1)
    def _():
        ks[1] = ks[2]

    @pl.when(flags[1] == 1)
    def _():
        ks[planes + 2] = ks[planes + 1]

    @pl.when(flags[2] == 1)
    def _():
        for p in range(planes + 4):
            ks[p, SUB - 1 : SUB, :] = ks[p, SUB : SUB + 1, :]

    @pl.when(flags[3] == 1)
    def _():
        for p in range(planes + 4):
            ks[p, end : end + 1, :] = ks[p, end - 1 : end, :]

    def first(p, carry):
        for top in range(0, cells + 2 * SUB, SUB):
            k = ks[p + 1, top : top + SUB, :]
            if top == 0:
                above = pltpu.roll(k, 1, 0)
            else:
                above = ks[p + 1, top - 1 : top + SUB - 1, :]
            if top == cells + SUB:
                below = pltpu.roll(k, SUB - 1, 0)
            else:
                below = ks[p + 1, top + 1 : top + SUB + 1, :]
            total = ks[p, top : top + SUB, :] + ks[p + 2, top : top + SUB, :]
            total = total + (above + below) + beside(k, True)
            scale = JACOBI_WEIGHT / (3.0 * k + 0.5 * total)
            u = fs[p, top : top + SUB, :] * scale
            us[p, top : top + SUB, :] = u
            ws[p, top : top + SUB, :] = k * u
            rs[p, top : top + SUB, :] = scale
        return carry

    lax.fori_loop(0, planes + 2, first, 0)

    def second(p, carry):
        for top in range(SUB, end, SUB):
            at = slice(top, top + SUB)
            sums = []
            for held in (us, ws):
                total = held[p, at, :] + held[p + 2, at, :]
                total = total + (
                    held[p + 1, top - 1 : top + SUB - 1, :]
                    + held[p + 1, top + 1 : top + SUB + 1, :]
                )
                sums.append(total + beside(held[p + 1, at, :], False))
            coupled = 0.5 * (ks[p + 2, at, :] * sums[0] + sums[1])
            out[p, top - SUB : top, :] = rs[p + 1, at, :] * (
                (2.0 - JACOBI_WEIGHT) * fs[p + 1, at, :] + coupled
            )
        return carry

    lax.fori_loop(0, planes, second, 0)


SMEM = pl.BlockSpec(memory_space=pltpu.SMEM)
VMEM = pl.BlockSpec(memory_space=pltpu.VMEM)
AWAY = pl.BlockSpec(memory_space=pltpu.HBM)
ANY = pl.BlockSpec(memory_space=pl.ANY)


def call(kernel, outs, operands, scratch, flops, specs, limit):
    many = isinstance(outs, (list, tuple))
    written = outs if many else [outs]
    moved = sum(math.prod(x.shape) * x.dtype.itemsize for x in (*operands, *written))
    operands = [
        pltpu.with_memory_space_constraint(x, pltpu.HBM) if spec is AWAY else x
        for x, spec in zip(operands, specs)
    ]
    out_specs = [VMEM if isinstance(x, jax.ShapeDtypeStruct) else AWAY for x in written]
    return pl.pallas_call(
        kernel,
        out_shape=outs,
        in_specs=specs,
        out_specs=out_specs if many else out_specs[0],
        scratch_shapes=scratch,
        compiler_params=pltpu.CompilerParams(vmem_limit_bytes=limit * MIB),
        cost_estimate=pl.CostEstimate(flops=flops, bytes_accessed=moved, transcendentals=0),
    )(*operands)


def f32(*shape):
    return jax.ShapeDtypeStruct(shape, jnp.float32)


def room(*arrays):
    return [pltpu.VMEM(x.shape, x.dtype) for x in arrays]


def chain(axis):
    up = [(i, i + 1) for i in range(lax.axis_size(axis) - 1)]
    return up, [(j, i) for i, j in up]


def swap(lo, hi, axis):
    up, down = chain(axis)
    return lax.ppermute(hi, axis, up), lax.ppermute(lo, axis, down)


def smooth(fine, flags, kappa, halo, source, edges):
    planes, cells, length = source.shape
    k_lo, k_hi, k_left, k_right = halo
    f_lo, f_hi, f_left, f_right = edges
    ext = cells + 2 * SUB
    wide = pltpu.VMEM((planes + 2, ext, length), jnp.float32)
    return call(
        functools.partial(stencil_kernel, fine),
        f32(planes, cells, length),
        (flags, kappa, k_lo, k_hi, f_lo, f_hi, k_left, k_right, source, f_left, f_right),
        [
            pltpu.VMEM((planes + 4, ext, length), jnp.float32),
            wide, wide, wide, wide,
            pltpu.SemaphoreType.DMA((13,)),
        ],
        60 * kappa.size,
        [SMEM] + [ANY] * 5 + [VMEM] * 5,
        32,
    )


def fused_body(noise, source):
    rows, groups = lax.axis_size("row"), lax.axis_size(PLANE)
    devices = rows * groups
    planes, cells, length = noise.shape
    first, second = planes * rows, cells * groups
    bf16 = jnp.bfloat16
    held = length // 2 // devices
    js = list(range(held))
    low = held // 2
    me = lax.axis_index(EVERY)
    row_at, group_at = lax.axis_index("row"), lax.axis_index(PLANE)
    flags = jnp.stack(
        [row_at == 0, row_at == rows - 1, group_at == 0, group_at == groups - 1]
    ).astype(jnp.int32)
    norm = FIELD_SCALE * (float(first) * float(second) * float(length)) ** (-0.5)
    flat = (planes * cells, length)

    table = two_parts(forward_third(length, devices, js))
    shape = (length * SUB, LANE)
    sent = call(
        functools.partial(forward_kernel, planes),
        pltpu.HBM(shape, jnp.float32),
        (*table, noise.reshape(flat)),
        room(*table)
        + [
            pltpu.VMEM(flat, bf16),
            pltpu.VMEM(shape, jnp.float32),
            pltpu.SemaphoreType.DMA((1 + 3 * PIECES,)),
        ],
        4 * length * length * planes * cells,
        [AWAY] * 3,
        16,
    )
    sent, source = lax.optimization_barrier((sent, source))
    sent = sent.reshape(devices, 2 * held, SUB, LANE)
    arrived = lax.all_to_all(sent, EVERY, split_axis=0, concat_axis=0, tiled=True)

    pairs = np.zeros((length, length // 2), np.float32)
    pairs[np.arange(length), np.arange(length) // 2] = 0.125
    level = f32(cells + cells // 4, length)
    side = f32(2 * SUB, length)
    coarse_source, *edges = call(
        functools.partial(source_kernel, planes),
        [f32(planes * cells // 4, length // 2), level, level, side, side],
        (pairs.astype(bf16), source.reshape(flat)),
        [
            pltpu.VMEM((planes * cells, length // 2), jnp.float32),
            pltpu.VMEM((cells, LANE), jnp.float32),
        ],
        planes * cells * length * length,
        [VMEM] * 2,
        16,
    )
    coarse_source = coarse_source.reshape(planes // 2, cells // 2, length // 2)
    edges = (*swap(*edges[:2], "row"), *swap(*edges[2:], PLANE))
    arrived, edges, coarse_source = lax.optimization_barrier((arrived, edges, coarse_source))

    constants = (
        two_parts(second_table(second))
        + two_parts(forward_first(first))
        + two_parts(inverse_first(first))
        + two_parts(second_table(second).T)
        + two_parts(inverse_first_coarse(first // 2, rows))
        + two_parts(second_coarse(second // 2, groups))
    )
    tiles = 2 * held + low // 2
    modes = (me + devices * np.array(js)).astype(jnp.float32)
    weight = jnp.where(modes == 0.0, norm, 2.0 * norm).astype(jnp.float32)
    scale = jnp.stack([DECAY * modes * modes, weight], axis=1)
    block = (2 * held * first, second)
    shape = (devices, tiles, SUB, LANE)
    out = call(
        functools.partial(middle_kernel, (first, second, rows, groups, held, low)),
        pltpu.HBM(shape, jnp.float32),
        (scale, arrived, *constants),
        room(*constants)
        + [
            pltpu.VMEM(shape, jnp.float32),
            pltpu.SemaphoreType.DMA((len(constants),)),
            pltpu.VMEM(block, bf16),
            pltpu.VMEM(block, bf16),
            pltpu.VMEM(block, jnp.float32),
            pltpu.VMEM(block, bf16),
            pltpu.VMEM(block, bf16),
            pltpu.VMEM((low // 2 * first, second), bf16),
            pltpu.VMEM((low // 2 * first, second), bf16),
        ],
        6 * 2 * 2 * held * first * second * (second + 2 * first),
        [SMEM, VMEM] + [AWAY] * len(constants),
        32,
    )
    got = lax.all_to_all(out, EVERY, split_axis=0, concat_axis=0, tiled=True)

    constants = two_parts(inverse_third(length, devices, js)) + two_parts(
        third_coarse(length // 2, devices, js[:low])
    )
    edge = f32(2 * cells + cells // 2, length)
    fine, coarse, lo, hi = call(
        functools.partial(back_kernel, (devices, 2 * held, tiles, planes, length)),
        [f32(*flat), f32(planes * cells // 4, length // 2), edge, edge],
        (got.reshape(devices * tiles * SUB, LANE), *constants),
        room(*constants)
        + [pltpu.VMEM((planes * cells, devices * 2 * held), bf16)] * 2
        + [pltpu.VMEM((planes // 2 * LANE, devices * low), bf16)] * 2
        + [pltpu.SemaphoreType.DMA((4,))],
        6 * planes * cells * length * length,
        [VMEM] + [AWAY] * 4,
        24,
    )
    fine, coarse = fine.reshape(source.shape), coarse.reshape(coarse_source.shape)
    k_lo, k_hi = swap(lo, hi, "row")
    side = f32(planes + planes // 2 + 4, 2, length)
    left, right = call(
        edge_kernel, [side, side], (fine, coarse, k_lo, k_hi), [], fine.size, [VMEM] * 4, 16
    )
    halo = (k_lo, k_hi, *swap(left, right, PLANE))
    fine_pressure = smooth(True, flags, fine, halo, source, edges)
    coarse_pressure = smooth(False, flags, coarse, halo, coarse_source, edges)
    return fine_pressure, coarse_pressure


NEIGHBOUR_STEPS = ((1, 0, 0), (-1, 0, 0), (0, 1, 0), (0, -1, 0), (0, 0, 1), (0, 0, -1))


def padded(x, sides, width):
    for axis, dim in sides:
        peers, length = (lax.axis_size(axis), x.shape[dim])
        up = [(i, (i + 1) % peers) for i in range(peers - 1)]
        down = [(j, i) for i, j in up]
        last = lax.slice_in_dim(x, length - width, length, axis=dim)
        leading = lax.slice_in_dim(x, 0, width, axis=dim)
        before = lax.ppermute(last, axis, up)
        after = lax.ppermute(leading, axis, down)
        x = jnp.concatenate([before, x, after], axis=dim)
    return x


def signed_modes(index, length):
    return jnp.where(index < length // 2, index, index - length).astype(jnp.float32)


def amplitude(first_modes, second_modes, third_modes, first_edge, second_edge, third_edge):
    squared = first_modes * first_modes + second_modes * second_modes + third_modes * third_modes
    value = FIELD_SCALE / (1.0 + (2.0 * math.pi * CORRELATION) ** 2 * squared)
    edge = (
        (jnp.abs(first_modes) == first_edge)
        | (jnp.abs(second_modes) == second_edge)
        | (jnp.abs(third_modes) == third_edge)
    )
    return jnp.where(edge, 0.0, value)


def phase_table(count_rows, count_cols, modulus, sign):
    left_index = jnp.arange(count_rows, dtype=jnp.int32)[:, None]
    right_index = jnp.arange(count_cols, dtype=jnp.int32)[None, :]
    angle = 2.0 * math.pi / modulus * (left_index * right_index % modulus).astype(jnp.float32)
    return (jnp.cos(angle), sign * jnp.sin(angle))


def split_length(length):
    outer_len = 2 ** ((length.bit_length() - 1) // 2)
    return (outer_len, length // outer_len)


def real_form(form, left_value, right_value):
    return jnp.einsum(form, left_value, right_value, precision=lax.Precision.HIGHEST)


def complex_form(form, left_real, left_imag, right_real, right_imag):
    real_part = real_form(form, left_real, right_real) - real_form(form, left_imag, right_imag)
    imag_part = real_form(form, left_real, right_imag) + real_form(form, left_imag, right_real)
    return (real_part, imag_part)


def merge_pair(values, out_form, first_letter):
    merge_at = out_form.index(first_letter)
    out_dims = list(values.shape)
    merged = (
        out_dims[:merge_at]
        + [out_dims[merge_at] * out_dims[merge_at + 1]]
        + out_dims[merge_at + 2 :]
    )
    return values.reshape(merged)


def forward_axis(real_part, imag_part, lead_form, out_form, kept_modes):
    length = real_part.shape[-1]
    outer_len, inner_len = split_length(length)
    split_shape = real_part.shape[:-1] + (outer_len, inner_len)
    outer_real, outer_imag = phase_table(outer_len, outer_len, outer_len, -1.0)
    twist_real, twist_imag = phase_table(outer_len, inner_len, length, -1.0)
    inner_real, inner_imag = phase_table(inner_len, kept_modes // outer_len, inner_len, -1.0)
    first_form = lead_form + "ab,ai->" + lead_form + "ib"
    split_real = real_part.reshape(split_shape)
    if imag_part is None:
        section_real = real_form(first_form, split_real, outer_real)
        section_imag = real_form(first_form, split_real, outer_imag)
    else:
        section_real, section_imag = complex_form(
            first_form, split_real, imag_part.reshape(split_shape), outer_real, outer_imag
        )
    turned_real = section_real * twist_real - section_imag * twist_imag
    turned_imag = section_real * twist_imag + section_imag * twist_real
    result_real, result_imag = complex_form(
        lead_form + "ib,bj->" + out_form, turned_real, turned_imag, inner_real, inner_imag
    )
    return (merge_pair(result_real, out_form, "j"), merge_pair(result_imag, out_form, "j"))


def inverse_axis(real_part, imag_part, length, lead_form, out_form, real_only):
    kept_modes = real_part.shape[-1]
    outer_len, inner_len = split_length(length)
    split_shape = real_part.shape[:-1] + (kept_modes // outer_len, outer_len)
    inner_real, inner_imag = phase_table(kept_modes // outer_len, inner_len, inner_len, 1.0)
    twist_real, twist_imag = phase_table(outer_len, inner_len, length, 1.0)
    outer_real, outer_imag = phase_table(outer_len, outer_len, outer_len, 1.0)
    section_real, section_imag = complex_form(
        lead_form + "ji,jb->" + lead_form + "ib",
        real_part.reshape(split_shape),
        imag_part.reshape(split_shape),
        inner_real,
        inner_imag,
    )
    turned_real = section_real * twist_real - section_imag * twist_imag
    turned_imag = section_real * twist_imag + section_imag * twist_real
    second_form = lead_form + "ib,ia->" + out_form
    if real_only:
        result = real_form(second_form, turned_real, outer_real) - real_form(
            second_form, turned_imag, outer_imag
        )
        return merge_pair(result, out_form, "a")
    result_real, result_imag = complex_form(
        second_form, turned_real, turned_imag, outer_real, outer_imag
    )
    return (merge_pair(result_real, out_form, "a"), merge_pair(result_imag, out_form, "a"))


def low_band(values, half_coarse, fine_len):
    return jnp.concatenate(
        [values[:, :, :half_coarse], values[:, :, fine_len - half_coarse :]], axis=2
    )


def window(values, margin, offset):
    return values[
        margin + offset[0] : values.shape[0] - margin + offset[0],
        margin + offset[1] : values.shape[1] - margin + offset[1],
        margin + offset[2] : values.shape[2] - margin + offset[2],
    ]


def face_weight(center, beside):
    return jnp.where(beside > 0.0, 0.5 * (center + beside), center)


def smooth_twice(kappa, source):
    no_shift = (0, 0, 0)
    center = window(kappa, 1, no_shift)
    faces = [face_weight(center, window(kappa, 1, offset)) for offset in NEIGHBOUR_STEPS]
    diagonal = faces[0] + faces[1] + faces[2] + faces[3] + faces[4] + faces[5]
    guarded = jnp.where(center > 0.0, diagonal, 1.0)
    first_sweep = JACOBI_WEIGHT * window(source, 1, no_shift) / guarded
    inner_first = window(first_sweep, 1, no_shift)
    inner_diagonal = window(diagonal, 1, no_shift)
    coupled = jnp.zeros_like(inner_first)
    for face_value, offset in zip(faces, NEIGHBOUR_STEPS):
        coupled = coupled + window(face_value, 1, no_shift) * window(first_sweep, 1, offset)
    residual = window(source, 2, no_shift) - inner_diagonal * inner_first + coupled
    return inner_first + JACOBI_WEIGHT * residual / inner_diagonal


def pad_depth(values):
    return jnp.pad(values, ((0, 0), (0, 0), (2, 2)))


def plain_body(noise, source):
    row_at = lax.axis_index("row")
    group_at = lax.axis_index(("level", "col"))
    fine_field = noise.astype(jnp.float32)
    fine_len = fine_field.shape[-1]
    coarse_len = fine_len // 2
    half_coarse = coarse_len // 2
    kept_modes = fine_len // 2
    real_part, imag_part = forward_axis(fine_field, None, "pq", "pjiq", kept_modes)
    real_part, imag_part = (
        lax.all_to_all(real_part, ("level", "col"), split_axis=1, concat_axis=2, tiled=True),
        lax.all_to_all(imag_part, ("level", "col"), split_axis=1, concat_axis=2, tiled=True),
    )
    real_part, imag_part = forward_axis(real_part, imag_part, "pq", "jiqp", fine_len)
    real_part, imag_part = (
        lax.all_to_all(real_part, "row", split_axis=0, concat_axis=2, tiled=True),
        lax.all_to_all(imag_part, "row", split_axis=0, concat_axis=2, tiled=True),
    )
    slab_len = real_part.shape[-1]
    coarse_slab = slab_len // 2
    half_slab = coarse_slab // 2
    real_part, imag_part = forward_axis(real_part, imag_part, "pq", "pqji", slab_len)
    second_count = real_part.shape[0]
    third_count = real_part.shape[1]
    wave_second = signed_modes(
        row_at * second_count + jnp.arange(second_count, dtype=jnp.int32), fine_len
    )[:, None, None]
    third_index = group_at * third_count + jnp.arange(third_count, dtype=jnp.int32)
    wave_third = signed_modes(third_index, fine_len)[None, :, None]
    spread = 2.0
    mirror_weight = jnp.where(third_index == 0, 1.0, spread).astype(jnp.float32)[None, :, None]
    norm_factor = (float(slab_len) * float(fine_len) * float(fine_len)) ** (-0.5)
    wave_first = signed_modes(jnp.arange(slab_len, dtype=jnp.int32), slab_len)[None, None, :]
    fine_scale = (
        amplitude(
            wave_second, wave_third, wave_first, fine_len / 2.0, fine_len / 2.0, slab_len / 2.0
        )
        * mirror_weight
        * norm_factor
    )
    coarse_first = signed_modes(jnp.arange(coarse_slab, dtype=jnp.int32), coarse_slab)[
        None, None, :
    ]
    coarse_scale = (
        amplitude(
            wave_second,
            wave_third,
            coarse_first,
            coarse_len / 2.0,
            coarse_len / 2.0,
            coarse_slab / 2.0,
        )
        * mirror_weight
        * norm_factor
    )
    coarse_real = low_band(real_part, half_slab, slab_len) * coarse_scale
    coarse_imag = low_band(imag_part, half_slab, slab_len) * coarse_scale
    fine_real, fine_imag = inverse_axis(
        real_part * fine_scale, imag_part * fine_scale, slab_len, "pq", "abqp", False
    )
    coarse_real, coarse_imag = inverse_axis(
        coarse_real, coarse_imag, coarse_slab, "pq", "abqp", False
    )
    fine_real, fine_imag, coarse_real, coarse_imag = (
        lax.all_to_all(fine_real, "row", split_axis=0, concat_axis=2, tiled=True),
        lax.all_to_all(fine_imag, "row", split_axis=0, concat_axis=2, tiled=True),
        lax.all_to_all(coarse_real, "row", split_axis=0, concat_axis=2, tiled=True),
        lax.all_to_all(coarse_imag, "row", split_axis=0, concat_axis=2, tiled=True),
    )
    coarse_real = low_band(coarse_real, half_coarse, fine_len)
    coarse_imag = low_band(coarse_imag, half_coarse, fine_len)
    fine_real, fine_imag = inverse_axis(fine_real, fine_imag, fine_len, "pq", "pabq", False)
    coarse_real, coarse_imag = inverse_axis(
        coarse_real, coarse_imag, coarse_len, "pq", "pabq", False
    )
    fine_real, fine_imag, coarse_real, coarse_imag = (
        lax.all_to_all(fine_real, ("level", "col"), split_axis=1, concat_axis=2, tiled=True),
        lax.all_to_all(fine_imag, ("level", "col"), split_axis=1, concat_axis=2, tiled=True),
        lax.all_to_all(coarse_real, ("level", "col"), split_axis=1, concat_axis=2, tiled=True),
        lax.all_to_all(coarse_imag, ("level", "col"), split_axis=1, concat_axis=2, tiled=True),
    )
    coarse_real = coarse_real[:, :, :half_coarse]
    coarse_imag = coarse_imag[:, :, :half_coarse]
    fine_log = inverse_axis(fine_real, fine_imag, fine_len, "pq", "pqab", True)
    coarse_log = inverse_axis(coarse_real, coarse_imag, coarse_len, "pq", "pqab", True)
    fine_kappa = jnp.exp(fine_log)
    coarse_kappa = jnp.exp(coarse_log)
    fine_source = source.astype(jnp.float32)
    coarse_rows = coarse_log.shape[0]
    coarse_cols = coarse_log.shape[1]
    coarse_source = fine_source.reshape(coarse_rows, 2, coarse_cols, 2, coarse_len, 2).mean(
        axis=(1, 3, 5)
    )
    fine_kappa, fine_source, coarse_kappa, coarse_source = (
        padded(fine_kappa, (("row", 0), (("level", "col"), 1)), 2),
        padded(fine_source, (("row", 0), (("level", "col"), 1)), 2),
        padded(coarse_kappa, (("row", 0), (("level", "col"), 1)), 2),
        padded(coarse_source, (("row", 0), (("level", "col"), 1)), 2),
    )
    fine_pressure = smooth_twice(pad_depth(fine_kappa), pad_depth(fine_source))
    coarse_pressure = smooth_twice(pad_depth(coarse_kappa), pad_depth(coarse_source))
    return (fine_pressure, coarse_pressure)


def body(noise, source):
    planes, cells, length = noise.shape
    devices = lax.axis_size(EVERY)
    held = length // 2 // devices
    if planes == SUB and cells == LANE and held % 4 == 0 and held > 0:
        return fused_body(noise, source)
    return plain_body(noise, source)


def solution(mesh):
    return jax.shard_map(
        body,
        mesh=mesh,
        in_specs=(P("row", ("level", "col"), None), P("row", ("level", "col"), None)),
        out_specs=(P("row", ("level", "col"), None), P("row", ("level", "col"), None)),
        check_vma=False,
    )
```

```python
import functools
import math

import jax
import jax.numpy as jnp
import numpy as np
from jax import lax
from jax.experimental import pallas as pl
from jax.experimental.pallas import tpu as pltpu
from jax.sharding import PartitionSpec as P

JACOBI_WEIGHT = 2.0 / 3.0
CORRELATION = 0.2
FIELD_SCALE = 0.3
DECAY = (2.0 * math.pi * CORRELATION) ** 2
EVERY = ("row", "level", "col")
PLANE = ("level", "col")
MIB = 1 << 20
SUB, LANE = 8, 128


def two_parts(matrix):
    high = matrix.astype(jnp.bfloat16)
    low = (matrix - high.astype(np.float64)).astype(jnp.bfloat16)
    return high, low


def angles(rows, cols, length):
    return 2.0 * np.pi * (np.outer(rows, cols) % length) / length


def third_modes(devices, js):
    return np.array([[d + devices * j for j in js] for d in range(devices)])


def forward_third(length, devices, js):
    theta = angles(third_modes(devices, js).reshape(-1), np.arange(length), length)
    return np.stack([np.cos(theta), -np.sin(theta)], axis=1).reshape(-1, length)


def inverse_third(length, devices, js):
    modes = third_modes(devices, js).reshape(devices // 2, 2, len(js)).transpose(1, 0, 2)
    theta = 2.0 * np.pi * (modes[..., None] * np.arange(length // 2) % length) / length
    both = np.stack([np.cos(theta), -np.sin(theta)], axis=3)
    return both.reshape(2, -1, length // 2)


def second_modes(length):
    return np.arange(length // 2).reshape(-1, 2).T


def second_table(length):
    theta = second_modes(length)[:, None, :] * np.arange(length // 2)[None, :, None]
    theta = 2.0 * np.pi * (theta % length) / length
    return np.concatenate([np.cos(theta), np.sin(theta)], axis=2)


def forward_first(length):
    theta = angles(np.arange(length), np.arange(length), length)
    cos, sin = np.cos(theta), np.sin(theta)
    return np.block([[cos, sin], [-sin, cos]])


def inverse_first(length):
    theta = angles(np.arange(length), np.arange(length), length)
    cos, sin = np.cos(theta), np.sin(theta)
    cos[:, length // 2] = 0.0
    sin[:, length // 2] = 0.0
    return np.block([[cos, -sin], [sin, cos]])


def inverse_first_coarse(length, rows):
    full = inverse_first(length)
    value = full.reshape(2, rows, length // rows, 2 * length)
    turned = np.concatenate([-full[length:], full[:length]]).reshape(value.shape)
    order = lambda x: x.transpose(1, 0, 2, 3).reshape(2 * length, 2 * length)
    return np.concatenate([order(value), order(turned)])


def second_coarse(length, groups):
    theta = angles(second_modes(length).reshape(-1), np.arange(length), length)
    table = np.concatenate([np.cos(theta), np.sin(theta)])
    span = length // groups
    out = np.zeros((2, length, groups, 2, span))
    for pair in range(2):
        out[pair, :, :, pair, :] = table.reshape(length, groups, span)
    return out.reshape(2 * length, 2 * length)


def third_coarse(length, devices, js):
    modes = third_modes(devices, js).reshape(devices, len(js) // 2, 2)
    theta = 2.0 * np.pi * (modes[..., None] * np.arange(length) % length) / length
    both = np.stack([np.cos(theta), -np.sin(theta)])
    return both.transpose(0, 2, 1, 3, 4).reshape(2 * (len(js) // 2) * devices, 2 * length)


def split(x):
    high = x.astype(jnp.bfloat16)
    return high, (x - high.astype(jnp.float32)).astype(jnp.bfloat16)


def dot(a, b):
    return lax.dot_general(a, b, (((1,), (0,)), ((), ())), preferred_element_type=jnp.float32)


def dot_t(a, b):
    return lax.dot_general(a, b, (((1,), (1,)), ((), ())), preferred_element_type=jnp.float32)


def dot3(a, b):
    (ah, al), (bh, bl) = a, b
    return dot(ah, bh) + (dot(ah, bl) + dot(al, bh))


def load(pairs, sems):
    copies = [pltpu.make_async_copy(a, b, sems.at[i]) for i, (a, b) in enumerate(pairs)]
    for copy in copies:
        copy.start()
    return copies


def send(pairs, sems, first):
    copies = [pltpu.make_async_copy(a, b, sems.at[first + i]) for i, (a, b) in enumerate(pairs)]
    for copy in copies:
        copy.start()
    return copies


def forward_kernel(planes, d_hbm, x_hbm, out_hbm, d, x, out, sems):
    rows = d.shape[0] // 2
    parts = [slice(p * LANE, (p + 2) * LANE) for p in range(0, planes, 2)]
    copies = load([(d_hbm, d)] + [(x_hbm.at[at, :], x.at[at, :]) for at in parts], sems)
    copies[0].wait()
    for i, at in enumerate(parts):
        copies[i + 1].wait()
        value = dot_t(d[...], x[at, :])
        value = value[:rows] + value[rows:]
        for h in range(2):
            out[pl.ds(2 * i + h, rows, stride=SUB), :] = value[:, h * LANE : (h + 1) * LANE]
    for copy in send([(out, out_hbm)], sems, 0):
        copy.wait()


def middle_kernel(sizes, scale, b, *rest):
    (first, second, rows, groups, js, low) = sizes
    count = 12
    away, out_hbm, near, rest = rest[:count], rest[count], rest[count + 1 : 2 * count + 1], rest[2 * count + 1 :]
    out, sems, zh, zl, y, oh, ol, qh, ql = rest
    copies = load(list(zip(away, near)), sems)
    csh, csl, fh, fl, ih, il, ch, cl, ich, icl, cch, ccl = near
    q_count = 2 * js
    half, quarter = second // 2, second // 4
    for q in range(q_count):
        for g in range(groups // 2):
            for r in range(0, rows, 2):
                at = r * groups + g
                near_half = jnp.concatenate([b[at, q], b[at + groups, q]], axis=0)
                at += groups // 2
                far_half = jnp.concatenate([b[at, q], b[at + groups, q]], axis=0)
                at = slice(q * first + r * SUB, q * first + (r + 2) * SUB)
                lanes = slice(g * LANE, (g + 1) * LANE)
                zh[0, at, lanes], zl[0, at, lanes] = split(near_half + far_half)
                zh[1, at, lanes], zl[1, at, lanes] = split(near_half - far_half)
    for copy in copies:
        copy.wait()
    wide = 8 * first
    for top in range(0, q_count * first, wide):
        at = slice(top, top + wide)
        for parity in range(2):
            y[parity, at, :] = dot3(
                (zh[parity, at, :], zl[parity, at, :]), (csh[parity], csl[parity])
            )
    mode0 = lax.broadcasted_iota(jnp.int32, (first, second), 0)
    mode0 = jnp.where(mode0 < first // 2, mode0, mode0 - first).astype(jnp.float32)
    lane = lax.broadcasted_iota(jnp.int32, (first, second), 1)
    mode1 = jnp.where(lane < half, lane, lane - half)
    mode1 = jnp.where(mode1 < quarter, 2 * mode1, 2 * (mode1 - quarter) + 1).astype(jnp.float32)
    base = 1.0 + DECAY * (mode0 * mode0 + mode1 * mode1)
    for j in range(js):
        top = j * 2 * first
        re, im = slice(top, top + first), slice(top + first, top + 2 * first)
        cos, sin = slice(0, quarter), slice(quarter, half)
        whole = lambda part, lanes: jnp.concatenate(
            [y[0, part, lanes], y[1, part, lanes]], axis=1
        )
        rc, rs, ic, isn = whole(re, cos), whole(re, sin), whole(im, cos), whole(im, sin)
        wave = jnp.concatenate(
            [
                jnp.concatenate([rc + isn, rc - isn], axis=1),
                jnp.concatenate([ic - rs, ic + rs], axis=1),
            ],
            axis=0,
        )
        spectrum = dot3((fh[...], fl[...]), split(wave))
        amp = jnp.where(lane == half, 0.0, scale[j, 1] / (base + scale[j, 0]))
        scaled = spectrum * jnp.concatenate([amp, amp], axis=0)
        field = dot3((ih[...], il[...]), split(scaled))
        plus, minus = field[:, :half], field[:, half:]
        even, odd = plus + minus, plus - minus
        odd = jnp.concatenate([-odd[first:], odd[:first]], axis=0)
        at = slice(top, top + 2 * first)
        for parity, lanes in enumerate((cos, sin)):
            operand = jnp.concatenate([even[:, lanes], odd[:, lanes]], axis=1)
            oh[parity, at, :], ol[parity, at, :] = split(operand)
        if j < low:
            keep = first // 4
            kept = [
                scaled[at : at + keep, :]
                for at in (0, first - keep, first, 2 * first - keep)
            ]
            band = jnp.concatenate(kept, axis=0)
            low_lane = lax.broadcasted_iota(jnp.int32, (first, quarter), 1) < quarter // 2
            pieces = []
            for at in (0, half):
                upper = pltpu.roll(band[:, at + quarter : at + half], quarter // 2, 1)
                pieces.append(jnp.where(low_lane, band[:, at : at + quarter], upper))
            band = jnp.concatenate(pieces, axis=1)
            field = dot3((ich[...], icl[...]), split(band))
            value, turned = field[:first], field[first:]
            operand = jnp.concatenate(
                [
                    value[:, :quarter] + value[:, quarter:],
                    turned[:, :quarter] - turned[:, quarter:],
                ],
                axis=1,
            )
            at = slice(j // 2 * first, (j // 2 + 1) * first)
            lanes = slice(j % 2 * half, (j % 2 + 1) * half)
            qh[at, lanes], ql[at, lanes] = split(operand)
    copies = []

    def give(value, start):
        tiles = value.shape[0] // first
        for q in range(tiles):
            for r in range(rows):
                for g in range(groups):
                    at = q * first + r * SUB
                    out[r * groups + g, start + q] = value[
                        at : at + SUB, g * LANE : (g + 1) * LANE
                    ]
        at = slice(start, start + tiles)
        copies.extend(send([(out.at[:, at], out_hbm.at[:, at])], sems, len(copies)))

    give(dot3((qh[...], ql[...]), (cch[...], ccl[...])), q_count)
    for top in range(0, q_count * first, wide):
        at = slice(top, top + wide)
        even, odd = (
            dot3((oh[parity, at, :], ol[parity, at, :]), (ch[parity], cl[parity]))
            for parity in range(2)
        )
        give(jnp.concatenate([even + odd, even - odd], axis=1), top // first)
    for copy in copies:
        copy.wait()


def back_kernel(sizes, b, *rest):
    (devices, q_count, tiles, planes, length) = sizes
    away, outs, near, (lh, ll, mh, ml, sems) = rest[:4], rest[4:8], rest[8:12], rest[12:]
    out, coarse, lo, hi = outs
    copies = load(list(zip(away, near)), sems)
    eh, el, ceh, cel = near
    cells = LANE
    for n in range(planes):
        for parity in range(2):
            rows = jnp.concatenate(
                [
                    b[pl.ds(s * tiles * SUB + n, q_count, stride=SUB), :]
                    for s in range(parity, devices, 2)
                ],
                axis=0,
            )
            at = slice(n * LANE, (n + 1) * LANE)
            lh[parity, at, :], ll[parity, at, :] = split(jnp.transpose(rows))
    halves = tiles - q_count
    coarse_planes = planes // 2
    for n in range(coarse_planes):
        rows = jnp.concatenate(
            [
                b[pl.ds((q_count + h) * SUB + c * coarse_planes + n, devices, stride=tiles * SUB), :]
                for c in range(2)
                for h in range(halves)
            ],
            axis=0,
        )
        high, rest_part = split(jnp.transpose(rows))
        mh[n * LANE : (n + 1) * LANE, :] = high
        ml[n * LANE : (n + 1) * LANE, :] = rest_part
    for copy in copies:
        copy.wait()
    for p in range(0, planes, 2):
        at = slice(p * cells, (p + 2) * cells)
        even, odd = (
            dot3((lh[parity, at, :], ll[parity, at, :]), (eh[parity], el[parity]))
            for parity in range(2)
        )
        value = jnp.exp(jnp.concatenate([even + odd, even - odd], axis=1))
        if p == 0:
            lo[: 2 * cells, :] = value
        if p == planes - 2:
            hi[: 2 * cells, :] = value
        out[at, :] = value
    value = dot3((mh[...], ml[...]), (ceh[...], cel[...]))
    half, fourth, short = cells // 2, cells // 4, length // 2
    for n in range(coarse_planes):
        top = n * cells
        part = value[top : top + half, :short] + value[top + half : top + cells, short:]
        part = jnp.exp(part)
        coarse[n * half : (n + 1) * half, :] = part
        for edge, start in ((lo, 0), (hi, coarse_planes - 2)):
            if start <= n < start + 2:
                top = 2 * cells + (n - start) * fourth
                edge[top : top + fourth, :short] = part[:fourth]
                edge[top : top + fourth, short:] = part[fourth:]


def source_kernel(planes, pairs, x, out, lo, hi, left, right, held, summed):
    cells = x.shape[0] // planes
    length = x.shape[1]
    half, fourth = cells // 2, cells // 4
    held[...] = dot(x[...], pairs[...])
    for n in range(planes // 2):
        top = 2 * n * cells
        for at in range(0, out.shape[1], LANE):
            lanes = slice(at, at + LANE)
            summed[...] = held[top : top + cells, lanes] + held[top + cells : top + 2 * cells, lanes]
            out[n * half : (n + 1) * half, lanes] = (
                summed[pl.ds(0, half, stride=2), :] + summed[pl.ds(1, half, stride=2), :]
            )
    for edge, plane in ((lo, 0), (hi, planes - 1)):
        edge[:cells, :] = x[plane * cells : (plane + 1) * cells, :].astype(jnp.float32)
        at = plane // 2 * half
        edge[cells:, : length // 2] = out[at : at + fourth, :]
        edge[cells:, length // 2 :] = out[at + fourth : at + half, :]
    for edge, row in ((left, 0), (right, cells - 1)):
        edge[...] = jnp.zeros_like(edge)
        for n in range(planes):
            at = n * cells + (row // SUB * SUB)
            edge[n : n + 1, :] = x[at : at + SUB, :].astype(jnp.float32)[row % SUB : row % SUB + 1]
        for n in range(planes // 2):
            at = n * half + row // 2
            edge[SUB + n : SUB + n + 1, : length // 2] = out[at : at + 1, :]


def edge_kernel(kappa, coarse, k_lo, k_hi, first, last):
    planes, cells, _ = kappa.shape
    coarse_planes, half, short = coarse.shape
    fourth = half // 2
    for n in range(planes + 2):
        if n == 0:
            held = k_lo.at[cells : 2 * cells, :]
        elif n == planes + 1:
            held = k_hi.at[:cells, :]
        else:
            held = kappa.at[n - 1]
        first[n] = held[:2, :]
        last[n] = held[cells - 2 :, :]
    for n in range(coarse_planes + 2):
        at = planes + 2 + n
        if 0 < n < coarse_planes + 1:
            top, bottom = coarse[n - 1, :2, :], coarse[n - 1, half - 2 :, :]
        else:
            held, start = (k_lo, 2 * cells + fourth) if n == 0 else (k_hi, 2 * cells)
            top = held[start : start + 2, :short]
            bottom = held[start + fourth - 2 : start + fourth, short:]
        first[at, :, :short] = top
        last[at, :, :short] = bottom
        first[at, :, short:] = jnp.zeros((2, short), jnp.float32)
        last[at, :, short:] = jnp.zeros((2, short), jnp.float32)


def beside(parts, ends):
    lane = lax.broadcasted_iota(jnp.int32, parts[0].shape, 1)
    ahead = [pltpu.roll(x, 1, 1) for x in parts]
    behind = [pltpu.roll(x, LANE - 1, 1) for x in parts]
    sums = []
    for i in range(len(parts)):
        left = jnp.where(lane == 0, ahead[i - 1] if i else ends[0], ahead[i])
        right = jnp.where(
            lane == LANE - 1, behind[i + 1] if i + 1 < len(parts) else ends[1], behind[i]
        )
        sums.append(left + right)
    return sums


def stencil_kernel(
    fine, flags, kappa, k_lo, k_hi, f_lo, f_hi, k_left, k_right, f, f_left, f_right,
    out, ks, fs, us, ws, rs, sems,
):
    planes, cells, length = out.shape
    end = SUB + cells
    pairs = [(kappa, ks.at[2 : planes + 2, SUB:end, :])]

    def place(edge, row, held, plane):
        if fine:
            pairs.append((edge.at[row : row + cells, :], held.at[plane, SUB:end, :]))
            return
        half = cells // 2
        for h in range(2):
            at = SUB + h * half
            pairs.append(
                (
                    edge.at[row : row + half, h * length : (h + 1) * length],
                    held.at[plane, at : at + half, :],
                )
            )

    for i in range(2):
        row = i * cells if fine else 4 * cells + i * cells // 2
        place(k_lo, row, ks, i)
        place(k_hi, row, ks, planes + 2 + i)
    row = 0 if fine else 2 * cells
    place(f_lo, row, fs, 0)
    place(f_hi, row, fs, planes + 1)
    copies = load(pairs, sems)
    at = 0 if fine else SUB
    for p in range(planes):
        fs[p + 1, SUB:end, :] = f[p].astype(jnp.float32)
        fs[p + 1, SUB - 1 : SUB, :] = f_left[at + p : at + p + 1, :length]
        fs[p + 1, end : end + 1, :] = f_right[at + p : at + p + 1, :length]
    at = 0 if fine else 2 * planes + 2
    for p in range(planes + 2):
        ks[p + 1, SUB - 2 : SUB, :] = k_left[at + p, :, :length]
        ks[p + 1, end : end + 2, :] = k_right[at + p, :, :length]
    for copy in copies:
        copy.wait()

    @pl.when(flags[0] == 1)
    def _():
        ks[1] = ks[2]

    @pl.when(flags[1] == 1)
    def _():
        ks[planes + 2] = ks[planes + 1]

    @pl.when(flags[2] == 1)
    def _():
        for p in range(planes + 4):
            ks[p, SUB - 1 : SUB, :] = ks[p, SUB : SUB + 1, :]

    @pl.when(flags[3] == 1)
    def _():
        for p in range(planes + 4):
            ks[p, end : end + 1, :] = ks[p, end - 1 : end, :]

    lanes = [slice(at, at + LANE) for at in range(0, length, LANE)]

    def first(p, carry):
        for top in range(0, cells + 2 * SUB, SUB):
            at = slice(top, top + SUB)
            parts = [ks[p + 1, at, x] for x in lanes]
            for k, both, x in zip(parts, beside(parts, (parts[0], parts[-1])), lanes):
                if top == 0:
                    above = pltpu.roll(k, 1, 0)
                else:
                    above = ks[p + 1, top - 1 : top + SUB - 1, x]
                if top == cells + SUB:
                    below = pltpu.roll(k, SUB - 1, 0)
                else:
                    below = ks[p + 1, top + 1 : top + SUB + 1, x]
                total = (ks[p, at, x] + ks[p + 2, at, x]) + (above + below) + both
                scale = JACOBI_WEIGHT / (6.0 * k + total)
                u = fs[p, at, x] * (2.0 * scale)
                us[p, at, x] = u
                ws[p, at, x] = k * u
                rs[p, at, x] = scale
        return carry

    lax.fori_loop(0, planes + 2, first, 0)

    def second(p, carry):
        for top in range(SUB, end, SUB):
            at = slice(top, top + SUB)
            sums = []
            for held in (us, ws):
                parts = [held[p + 1, at, x] for x in lanes]
                sums.append(
                    [
                        both
                        + (held[p, at, x] + held[p + 2, at, x])
                        + (
                            held[p + 1, top - 1 : top + SUB - 1, x]
                            + held[p + 1, top + 1 : top + SUB + 1, x]
                        )
                        for both, x in zip(beside(parts, (0.0, 0.0)), lanes)
                    ]
                )
            for i, x in enumerate(lanes):
                coupled = ks[p + 2, at, x] * sums[0][i] + sums[1][i]
                out[p, top - SUB : top, x] = (2.0 - JACOBI_WEIGHT) * us[
                    p + 1, at, x
                ] + rs[p + 1, at, x] * coupled
        return carry

    lax.fori_loop(0, planes, second, 0)


SMEM = pl.BlockSpec(memory_space=pltpu.SMEM)
VMEM = pl.BlockSpec(memory_space=pltpu.VMEM)
AWAY = pl.BlockSpec(memory_space=pltpu.HBM)
ANY = pl.BlockSpec(memory_space=pl.ANY)


def call(kernel, outs, operands, scratch, flops, specs, limit):
    many = isinstance(outs, (list, tuple))
    written = outs if many else [outs]
    moved = sum(math.prod(x.shape) * x.dtype.itemsize for x in (*operands, *written))
    operands = [
        pltpu.with_memory_space_constraint(x, pltpu.HBM) if spec is AWAY else x
        for x, spec in zip(operands, specs)
    ]
    out_specs = [VMEM if isinstance(x, jax.ShapeDtypeStruct) else AWAY for x in written]
    return pl.pallas_call(
        kernel,
        out_shape=outs,
        in_specs=specs,
        out_specs=out_specs if many else out_specs[0],
        scratch_shapes=scratch,
        compiler_params=pltpu.CompilerParams(vmem_limit_bytes=limit * MIB),
        cost_estimate=pl.CostEstimate(flops=flops, bytes_accessed=moved, transcendentals=0),
    )(*operands)


def f32(*shape):
    return jax.ShapeDtypeStruct(shape, jnp.float32)


def room(*arrays):
    return [pltpu.VMEM(x.shape, x.dtype) for x in arrays]


def chain(axis):
    up = [(i, i + 1) for i in range(lax.axis_size(axis) - 1)]
    return up, [(j, i) for i, j in up]


def swap(lo, hi, axis):
    up, down = chain(axis)
    return lax.ppermute(hi, axis, up), lax.ppermute(lo, axis, down)


def smooth(fine, flags, kappa, halo, source, edges):
    planes, cells, length = source.shape
    k_lo, k_hi, k_left, k_right = halo
    f_lo, f_hi, f_left, f_right = edges
    ext = cells + 2 * SUB
    wide = pltpu.VMEM((planes + 2, ext, length), jnp.float32)
    return call(
        functools.partial(stencil_kernel, fine),
        f32(planes, cells, length),
        (flags, kappa, k_lo, k_hi, f_lo, f_hi, k_left, k_right, source, f_left, f_right),
        [
            pltpu.VMEM((planes + 4, ext, length), jnp.float32),
            wide, wide, wide, wide,
            pltpu.SemaphoreType.DMA((13,)),
        ],
        60 * kappa.size,
        [SMEM] + [ANY] * 5 + [VMEM] * 5,
        32,
    )


def fused_body(noise, source):
    rows, groups = lax.axis_size("row"), lax.axis_size(PLANE)
    devices = rows * groups
    planes, cells, length = noise.shape
    first, second = planes * rows, cells * groups
    bf16 = jnp.bfloat16
    held = length // 2 // devices
    js = list(range(held))
    low = held // 2
    me = lax.axis_index(EVERY)
    row_at, group_at = lax.axis_index("row"), lax.axis_index(PLANE)
    flags = jnp.stack(
        [row_at == 0, row_at == rows - 1, group_at == 0, group_at == groups - 1]
    ).astype(jnp.int32)
    norm = FIELD_SCALE * (float(first) * float(second) * float(length)) ** (-0.5)
    flat = (planes * cells, length)

    table = np.concatenate(two_parts(forward_third(length, devices, js)))
    shape = (length * SUB, LANE)
    sent = call(
        functools.partial(forward_kernel, planes),
        pltpu.HBM(shape, jnp.float32),
        (table, noise.reshape(flat)),
        room(table)
        + [
            pltpu.VMEM(flat, bf16),
            pltpu.VMEM(shape, jnp.float32),
            pltpu.SemaphoreType.DMA((1 + planes // 2,)),
        ],
        4 * length * length * planes * cells,
        [AWAY] * 2,
        16,
    )
    sent, source = lax.optimization_barrier((sent, source))
    sent = sent.reshape(devices, 2 * held, SUB, LANE)
    arrived = lax.all_to_all(sent, EVERY, split_axis=0, concat_axis=0, tiled=True)

    pairs = np.zeros((length, length // 2), np.float32)
    pairs[np.arange(length), np.arange(length) // 2] = 0.125
    level = f32(cells + cells // 4, length)
    side = f32(2 * SUB, length)
    coarse_source, *edges = call(
        functools.partial(source_kernel, planes),
        [f32(planes * cells // 4, length // 2), level, level, side, side],
        (pairs.astype(bf16), source.reshape(flat)),
        [
            pltpu.VMEM((planes * cells, length // 2), jnp.float32),
            pltpu.VMEM((cells, LANE), jnp.float32),
        ],
        planes * cells * length * length,
        [VMEM] * 2,
        16,
    )
    coarse_source = coarse_source.reshape(planes // 2, cells // 2, length // 2)
    edges = (*swap(*edges[:2], "row"), *swap(*edges[2:], PLANE))
    arrived, edges, coarse_source = lax.optimization_barrier((arrived, edges, coarse_source))

    constants = (
        two_parts(second_table(second))
        + two_parts(forward_first(first))
        + two_parts(inverse_first(first))
        + two_parts(second_table(second).transpose(0, 2, 1))
        + two_parts(inverse_first_coarse(first // 2, rows))
        + two_parts(second_coarse(second // 2, groups))
    )
    tiles = 2 * held + low // 2
    modes = (me + devices * np.array(js)).astype(jnp.float32)
    weight = jnp.where(modes == 0.0, norm, 2.0 * norm).astype(jnp.float32)
    scale = jnp.stack([DECAY * modes * modes, weight], axis=1)
    block = (2, 2 * held * first, second // 2)
    shape = (devices, tiles, SUB, LANE)
    out = call(
        functools.partial(middle_kernel, (first, second, rows, groups, held, low)),
        pltpu.HBM(shape, jnp.float32),
        (scale, arrived, *constants),
        room(*constants)
        + [
            pltpu.VMEM(shape, jnp.float32),
            pltpu.SemaphoreType.DMA((len(constants),)),
            pltpu.VMEM(block, bf16),
            pltpu.VMEM(block, bf16),
            pltpu.VMEM(block, jnp.float32),
            pltpu.VMEM(block, bf16),
            pltpu.VMEM(block, bf16),
            pltpu.VMEM((low // 2 * first, second), bf16),
            pltpu.VMEM((low // 2 * first, second), bf16),
        ],
        6 * 2 * 2 * held * first * second * (second + 2 * first),
        [SMEM, VMEM] + [AWAY] * len(constants),
        32,
    )
    got = lax.all_to_all(out, EVERY, split_axis=0, concat_axis=0, tiled=True)

    constants = two_parts(inverse_third(length, devices, js)) + two_parts(
        third_coarse(length // 2, devices, js[:low])
    )
    edge = f32(2 * cells + cells // 2, length)
    fine, coarse, lo, hi = call(
        functools.partial(back_kernel, (devices, 2 * held, tiles, planes, length)),
        [f32(*flat), f32(planes * cells // 4, length // 2), edge, edge],
        (got.reshape(devices * tiles * SUB, LANE), *constants),
        room(*constants)
        + [pltpu.VMEM((2, planes * cells, devices * held), bf16)] * 2
        + [pltpu.VMEM((planes // 2 * LANE, devices * low), bf16)] * 2
        + [pltpu.SemaphoreType.DMA((4,))],
        6 * planes * cells * length * length,
        [VMEM] + [AWAY] * 4,
        24,
    )
    fine, coarse = fine.reshape(source.shape), coarse.reshape(coarse_source.shape)
    k_lo, k_hi = swap(lo, hi, "row")
    side = f32(planes + planes // 2 + 4, 2, length)
    left, right = call(
        edge_kernel, [side, side], (fine, coarse, k_lo, k_hi), [], fine.size, [VMEM] * 4, 16
    )
    halo = (k_lo, k_hi, *swap(left, right, PLANE))
    fine_pressure = smooth(True, flags, fine, halo, source, edges)
    coarse_pressure = smooth(False, flags, coarse, halo, coarse_source, edges)
    return fine_pressure, coarse_pressure


NEIGHBOUR_STEPS = ((1, 0, 0), (-1, 0, 0), (0, 1, 0), (0, -1, 0), (0, 0, 1), (0, 0, -1))


def padded(x, sides, width):
    for axis, dim in sides:
        peers, length = (lax.axis_size(axis), x.shape[dim])
        up = [(i, (i + 1) % peers) for i in range(peers - 1)]
        down = [(j, i) for i, j in up]
        last = lax.slice_in_dim(x, length - width, length, axis=dim)
        leading = lax.slice_in_dim(x, 0, width, axis=dim)
        before = lax.ppermute(last, axis, up)
        after = lax.ppermute(leading, axis, down)
        x = jnp.concatenate([before, x, after], axis=dim)
    return x


def signed_modes(index, length):
    return jnp.where(index < length // 2, index, index - length).astype(jnp.float32)


def amplitude(first_modes, second_modes, third_modes, first_edge, second_edge, third_edge):
    squared = first_modes * first_modes + second_modes * second_modes + third_modes * third_modes
    value = FIELD_SCALE / (1.0 + (2.0 * math.pi * CORRELATION) ** 2 * squared)
    edge = (
        (jnp.abs(first_modes) == first_edge)
        | (jnp.abs(second_modes) == second_edge)
        | (jnp.abs(third_modes) == third_edge)
    )
    return jnp.where(edge, 0.0, value)


def phase_table(count_rows, count_cols, modulus, sign):
    left_index = jnp.arange(count_rows, dtype=jnp.int32)[:, None]
    right_index = jnp.arange(count_cols, dtype=jnp.int32)[None, :]
    angle = 2.0 * math.pi / modulus * (left_index * right_index % modulus).astype(jnp.float32)
    return (jnp.cos(angle), sign * jnp.sin(angle))


def split_length(length):
    outer_len = 2 ** ((length.bit_length() - 1) // 2)
    return (outer_len, length // outer_len)


def real_form(form, left_value, right_value):
    return jnp.einsum(form, left_value, right_value, precision=lax.Precision.HIGHEST)


def complex_form(form, left_real, left_imag, right_real, right_imag):
    real_part = real_form(form, left_real, right_real) - real_form(form, left_imag, right_imag)
    imag_part = real_form(form, left_real, right_imag) + real_form(form, left_imag, right_real)
    return (real_part, imag_part)


def merge_pair(values, out_form, first_letter):
    merge_at = out_form.index(first_letter)
    out_dims = list(values.shape)
    merged = (
        out_dims[:merge_at]
        + [out_dims[merge_at] * out_dims[merge_at + 1]]
        + out_dims[merge_at + 2 :]
    )
    return values.reshape(merged)


def forward_axis(real_part, imag_part, lead_form, out_form, kept_modes):
    length = real_part.shape[-1]
    outer_len, inner_len = split_length(length)
    split_shape = real_part.shape[:-1] + (outer_len, inner_len)
    outer_real, outer_imag = phase_table(outer_len, outer_len, outer_len, -1.0)
    twist_real, twist_imag = phase_table(outer_len, inner_len, length, -1.0)
    inner_real, inner_imag = phase_table(inner_len, kept_modes // outer_len, inner_len, -1.0)
    first_form = lead_form + "ab,ai->" + lead_form + "ib"
    split_real = real_part.reshape(split_shape)
    if imag_part is None:
        section_real = real_form(first_form, split_real, outer_real)
        section_imag = real_form(first_form, split_real, outer_imag)
    else:
        section_real, section_imag = complex_form(
            first_form, split_real, imag_part.reshape(split_shape), outer_real, outer_imag
        )
    turned_real = section_real * twist_real - section_imag * twist_imag
    turned_imag = section_real * twist_imag + section_imag * twist_real
    result_real, result_imag = complex_form(
        lead_form + "ib,bj->" + out_form, turned_real, turned_imag, inner_real, inner_imag
    )
    return (merge_pair(result_real, out_form, "j"), merge_pair(result_imag, out_form, "j"))


def inverse_axis(real_part, imag_part, length, lead_form, out_form, real_only):
    kept_modes = real_part.shape[-1]
    outer_len, inner_len = split_length(length)
    split_shape = real_part.shape[:-1] + (kept_modes // outer_len, outer_len)
    inner_real, inner_imag = phase_table(kept_modes // outer_len, inner_len, inner_len, 1.0)
    twist_real, twist_imag = phase_table(outer_len, inner_len, length, 1.0)
    outer_real, outer_imag = phase_table(outer_len, outer_len, outer_len, 1.0)
    section_real, section_imag = complex_form(
        lead_form + "ji,jb->" + lead_form + "ib",
        real_part.reshape(split_shape),
        imag_part.reshape(split_shape),
        inner_real,
        inner_imag,
    )
    turned_real = section_real * twist_real - section_imag * twist_imag
    turned_imag = section_real * twist_imag + section_imag * twist_real
    second_form = lead_form + "ib,ia->" + out_form
    if real_only:
        result = real_form(second_form, turned_real, outer_real) - real_form(
            second_form, turned_imag, outer_imag
        )
        return merge_pair(result, out_form, "a")
    result_real, result_imag = complex_form(
        second_form, turned_real, turned_imag, outer_real, outer_imag
    )
    return (merge_pair(result_real, out_form, "a"), merge_pair(result_imag, out_form, "a"))


def low_band(values, half_coarse, fine_len):
    return jnp.concatenate(
        [values[:, :, :half_coarse], values[:, :, fine_len - half_coarse :]], axis=2
    )


def window(values, margin, offset):
    return values[
        margin + offset[0] : values.shape[0] - margin + offset[0],
        margin + offset[1] : values.shape[1] - margin + offset[1],
        margin + offset[2] : values.shape[2] - margin + offset[2],
    ]


def face_weight(center, beside):
    return jnp.where(beside > 0.0, 0.5 * (center + beside), center)


def smooth_twice(kappa, source):
    no_shift = (0, 0, 0)
    center = window(kappa, 1, no_shift)
    faces = [face_weight(center, window(kappa, 1, offset)) for offset in NEIGHBOUR_STEPS]
    diagonal = faces[0] + faces[1] + faces[2] + faces[3] + faces[4] + faces[5]
    guarded = jnp.where(center > 0.0, diagonal, 1.0)
    first_sweep = JACOBI_WEIGHT * window(source, 1, no_shift) / guarded
    inner_first = window(first_sweep, 1, no_shift)
    inner_diagonal = window(diagonal, 1, no_shift)
    coupled = jnp.zeros_like(inner_first)
    for face_value, offset in zip(faces, NEIGHBOUR_STEPS):
        coupled = coupled + window(face_value, 1, no_shift) * window(first_sweep, 1, offset)
    residual = window(source, 2, no_shift) - inner_diagonal * inner_first + coupled
    return inner_first + JACOBI_WEIGHT * residual / inner_diagonal


def pad_depth(values):
    return jnp.pad(values, ((0, 0), (0, 0), (2, 2)))


def plain_body(noise, source):
    row_at = lax.axis_index("row")
    group_at = lax.axis_index(("level", "col"))
    fine_field = noise.astype(jnp.float32)
    fine_len = fine_field.shape[-1]
    coarse_len = fine_len // 2
    half_coarse = coarse_len // 2
    kept_modes = fine_len // 2
    real_part, imag_part = forward_axis(fine_field, None, "pq", "pjiq", kept_modes)
    real_part, imag_part = (
        lax.all_to_all(real_part, ("level", "col"), split_axis=1, concat_axis=2, tiled=True),
        lax.all_to_all(imag_part, ("level", "col"), split_axis=1, concat_axis=2, tiled=True),
    )
    real_part, imag_part = forward_axis(real_part, imag_part, "pq", "jiqp", fine_len)
    real_part, imag_part = (
        lax.all_to_all(real_part, "row", split_axis=0, concat_axis=2, tiled=True),
        lax.all_to_all(imag_part, "row", split_axis=0, concat_axis=2, tiled=True),
    )
    slab_len = real_part.shape[-1]
    coarse_slab = slab_len // 2
    half_slab = coarse_slab // 2
    real_part, imag_part = forward_axis(real_part, imag_part, "pq", "pqji", slab_len)
    second_count = real_part.shape[0]
    third_count = real_part.shape[1]
    wave_second = signed_modes(
        row_at * second_count + jnp.arange(second_count, dtype=jnp.int32), fine_len
    )[:, None, None]
    third_index = group_at * third_count + jnp.arange(third_count, dtype=jnp.int32)
    wave_third = signed_modes(third_index, fine_len)[None, :, None]
    spread = 2.0
    mirror_weight = jnp.where(third_index == 0, 1.0, spread).astype(jnp.float32)[None, :, None]
    norm_factor = (float(slab_len) * float(fine_len) * float(fine_len)) ** (-0.5)
    wave_first = signed_modes(jnp.arange(slab_len, dtype=jnp.int32), slab_len)[None, None, :]
    fine_scale = (
        amplitude(
            wave_second, wave_third, wave_first, fine_len / 2.0, fine_len / 2.0, slab_len / 2.0
        )
        * mirror_weight
        * norm_factor
    )
    coarse_first = signed_modes(jnp.arange(coarse_slab, dtype=jnp.int32), coarse_slab)[
        None, None, :
    ]
    coarse_scale = (
        amplitude(
            wave_second,
            wave_third,
            coarse_first,
            coarse_len / 2.0,
            coarse_len / 2.0,
            coarse_slab / 2.0,
        )
        * mirror_weight
        * norm_factor
    )
    coarse_real = low_band(real_part, half_slab, slab_len) * coarse_scale
    coarse_imag = low_band(imag_part, half_slab, slab_len) * coarse_scale
    fine_real, fine_imag = inverse_axis(
        real_part * fine_scale, imag_part * fine_scale, slab_len, "pq", "abqp", False
    )
    coarse_real, coarse_imag = inverse_axis(
        coarse_real, coarse_imag, coarse_slab, "pq", "abqp", False
    )
    fine_real, fine_imag, coarse_real, coarse_imag = (
        lax.all_to_all(fine_real, "row", split_axis=0, concat_axis=2, tiled=True),
        lax.all_to_all(fine_imag, "row", split_axis=0, concat_axis=2, tiled=True),
        lax.all_to_all(coarse_real, "row", split_axis=0, concat_axis=2, tiled=True),
        lax.all_to_all(coarse_imag, "row", split_axis=0, concat_axis=2, tiled=True),
    )
    coarse_real = low_band(coarse_real, half_coarse, fine_len)
    coarse_imag = low_band(coarse_imag, half_coarse, fine_len)
    fine_real, fine_imag = inverse_axis(fine_real, fine_imag, fine_len, "pq", "pabq", False)
    coarse_real, coarse_imag = inverse_axis(
        coarse_real, coarse_imag, coarse_len, "pq", "pabq", False
    )
    fine_real, fine_imag, coarse_real, coarse_imag = (
        lax.all_to_all(fine_real, ("level", "col"), split_axis=1, concat_axis=2, tiled=True),
        lax.all_to_all(fine_imag, ("level", "col"), split_axis=1, concat_axis=2, tiled=True),
        lax.all_to_all(coarse_real, ("level", "col"), split_axis=1, concat_axis=2, tiled=True),
        lax.all_to_all(coarse_imag, ("level", "col"), split_axis=1, concat_axis=2, tiled=True),
    )
    coarse_real = coarse_real[:, :, :half_coarse]
    coarse_imag = coarse_imag[:, :, :half_coarse]
    fine_log = inverse_axis(fine_real, fine_imag, fine_len, "pq", "pqab", True)
    coarse_log = inverse_axis(coarse_real, coarse_imag, coarse_len, "pq", "pqab", True)
    fine_kappa = jnp.exp(fine_log)
    coarse_kappa = jnp.exp(coarse_log)
    fine_source = source.astype(jnp.float32)
    coarse_rows = coarse_log.shape[0]
    coarse_cols = coarse_log.shape[1]
    coarse_source = fine_source.reshape(coarse_rows, 2, coarse_cols, 2, coarse_len, 2).mean(
        axis=(1, 3, 5)
    )
    fine_kappa, fine_source, coarse_kappa, coarse_source = (
        padded(fine_kappa, (("row", 0), (("level", "col"), 1)), 2),
        padded(fine_source, (("row", 0), (("level", "col"), 1)), 2),
        padded(coarse_kappa, (("row", 0), (("level", "col"), 1)), 2),
        padded(coarse_source, (("row", 0), (("level", "col"), 1)), 2),
    )
    fine_pressure = smooth_twice(pad_depth(fine_kappa), pad_depth(fine_source))
    coarse_pressure = smooth_twice(pad_depth(coarse_kappa), pad_depth(coarse_source))
    return (fine_pressure, coarse_pressure)


def body(noise, source):
    planes, cells, length = noise.shape
    devices = lax.axis_size(EVERY)
    held = length // 2 // devices
    if planes == SUB and cells == LANE and held % 4 == 0 and held > 0:
        return fused_body(noise, source)
    return plain_body(noise, source)


def solution(mesh):
    return jax.shard_map(
        body,
        mesh=mesh,
        in_specs=(P("row", ("level", "col"), None), P("row", ("level", "col"), None)),
        out_specs=(P("row", ("level", "col"), None), P("row", ("level", "col"), None)),
        check_vma=False,
    )
```

```python
import functools
import math

import jax
import jax.numpy as jnp
import numpy as np
from jax import lax
from jax.experimental import pallas as pl
from jax.experimental.pallas import tpu as pltpu
from jax.sharding import PartitionSpec as P

JACOBI_WEIGHT = 2.0 / 3.0
CORRELATION = 0.2
FIELD_SCALE = 0.3
DECAY = (2.0 * math.pi * CORRELATION) ** 2
EVERY = ("row", "level", "col")
PLANE = ("level", "col")
MIB = 1 << 20
SUB, LANE = 8, 128
HALO = 4


def two_parts(matrix):
    high = matrix.astype(jnp.bfloat16)
    low = (matrix - high.astype(np.float64)).astype(jnp.bfloat16)
    return high, low


def angles(rows, cols, length):
    return 2.0 * np.pi * (np.outer(rows, cols) % length) / length


def third_modes(devices, js):
    return np.array([[d + devices * j for j in js] for d in range(devices)])


def forward_third(length, devices, js):
    theta = angles(third_modes(devices, js).reshape(-1), np.arange(length), length)
    return np.stack([np.cos(theta), -np.sin(theta)], axis=1).reshape(-1, length)


def inverse_third(length, devices, js):
    modes = third_modes(devices, js).reshape(devices // 2, 2, len(js)).transpose(1, 0, 2)
    theta = 2.0 * np.pi * (modes[..., None] * np.arange(length // 2) % length) / length
    both = np.stack([np.cos(theta), -np.sin(theta)], axis=3)
    return both.reshape(2, -1, length // 2)


def second_modes(length):
    return np.arange(length // 2).reshape(-1, 2).T


def second_table(length):
    theta = second_modes(length)[:, None, :] * np.arange(length // 2)[None, :, None]
    theta = 2.0 * np.pi * (theta % length) / length
    return np.concatenate([np.cos(theta), np.sin(theta)], axis=2)


def forward_first(length):
    theta = angles(np.arange(length), np.arange(length), length)
    cos, sin = np.cos(theta), np.sin(theta)
    return np.block([[cos, sin], [-sin, cos]])


def inverse_first(length):
    theta = angles(np.arange(length), np.arange(length), length)
    cos, sin = np.cos(theta), np.sin(theta)
    cos[:, length // 2] = 0.0
    sin[:, length // 2] = 0.0
    return np.block([[cos, -sin], [sin, cos]])


def inverse_first_coarse(length, rows):
    full = inverse_first(length)
    value = full.reshape(2, rows, length // rows, 2 * length)
    turned = np.concatenate([-full[length:], full[:length]]).reshape(value.shape)
    order = lambda x: x.transpose(1, 0, 2, 3).reshape(2 * length, 2 * length)
    return np.concatenate([order(value), order(turned)])


def second_coarse(length, groups):
    theta = angles(second_modes(length).reshape(-1), np.arange(length), length)
    table = np.concatenate([np.cos(theta), np.sin(theta)])
    span = length // groups
    out = np.zeros((2, length, groups, 2, span))
    for pair in range(2):
        out[pair, :, :, pair, :] = table.reshape(length, groups, span)
    return out.reshape(2 * length, 2 * length)


def third_coarse(length, devices, js):
    modes = third_modes(devices, js).reshape(devices, len(js) // 2, 2)
    theta = 2.0 * np.pi * (modes[..., None] * np.arange(length) % length) / length
    both = np.stack([np.cos(theta), -np.sin(theta)])
    return both.transpose(0, 2, 1, 3, 4).reshape(2 * (len(js) // 2) * devices, 2 * length)


def third_coarse_halo(length, devices, js):
    modes = np.repeat(third_modes(devices, js).reshape(-1), HALO)
    theta = angles(modes, np.arange(length), length)
    return np.concatenate([np.cos(theta), -np.sin(theta)], axis=1)


def split(x):
    high = x.astype(jnp.bfloat16)
    return high, (x - high.astype(jnp.float32)).astype(jnp.bfloat16)


def dot(a, b):
    return lax.dot_general(a, b, (((1,), (0,)), ((), ())), preferred_element_type=jnp.float32)


def dot_t(a, b):
    return lax.dot_general(a, b, (((1,), (1,)), ((), ())), preferred_element_type=jnp.float32)


def dot3(a, b):
    (ah, al), (bh, bl) = a, b
    return dot(ah, bh) + (dot(ah, bl) + dot(al, bh))


def load(pairs, sems):
    copies = [pltpu.make_async_copy(a, b, sems.at[i]) for i, (a, b) in enumerate(pairs)]
    for copy in copies:
        copy.start()
    return copies


def send(pairs, sems, first):
    copies = [pltpu.make_async_copy(a, b, sems.at[first + i]) for i, (a, b) in enumerate(pairs)]
    for copy in copies:
        copy.start()
    return copies


def forward_kernel(planes, d_hbm, x_hbm, out_hbm, d, x, out, sems):
    rows = d.shape[0] // 2
    parts = [slice(p * LANE, (p + 2) * LANE) for p in range(0, planes, 2)]
    copies = load([(d_hbm, d)] + [(x_hbm.at[at, :], x.at[at, :]) for at in parts], sems)
    copies[0].wait()
    for i, at in enumerate(parts):
        copies[i + 1].wait()
        value = dot_t(d[...], x[at, :])
        value = value[:rows] + value[rows:]
        for h in range(2):
            out[pl.ds(2 * i + h, rows, stride=SUB), :] = value[:, h * LANE : (h + 1) * LANE]
    for copy in send([(out, out_hbm)], sems, 0):
        copy.wait()


def middle_kernel(sizes, scale, b, *rest):
    (first, second, rows, groups, js, low) = sizes
    count = 12
    away, out_hbm, near, rest = rest[:count], rest[count], rest[count + 1 : 2 * count + 1], rest[2 * count + 1 :]
    out, sems, zh, zl, y, oh, ol, qh, ql = rest
    copies = load(list(zip(away, near)), sems)
    csh, csl, fh, fl, ih, il, ch, cl, ich, icl, cch, ccl = near
    q_count = 2 * js
    half, quarter = second // 2, second // 4
    for q in range(q_count):
        for g in range(groups // 2):
            for r in range(0, rows, 2):
                at = r * groups + g
                near_half = jnp.concatenate([b[at, q], b[at + groups, q]], axis=0)
                at += groups // 2
                far_half = jnp.concatenate([b[at, q], b[at + groups, q]], axis=0)
                at = slice(q * first + r * SUB, q * first + (r + 2) * SUB)
                lanes = slice(g * LANE, (g + 1) * LANE)
                zh[0, at, lanes], zl[0, at, lanes] = split(near_half + far_half)
                zh[1, at, lanes], zl[1, at, lanes] = split(near_half - far_half)
    for copy in copies:
        copy.wait()
    wide = 8 * first
    for top in range(0, q_count * first, wide):
        at = slice(top, top + wide)
        for parity in range(2):
            y[parity, at, :] = dot3(
                (zh[parity, at, :], zl[parity, at, :]), (csh[parity], csl[parity])
            )
    mode0 = lax.broadcasted_iota(jnp.int32, (first, second), 0)
    mode0 = jnp.where(mode0 < first // 2, mode0, mode0 - first).astype(jnp.float32)
    lane = lax.broadcasted_iota(jnp.int32, (first, second), 1)
    mode1 = jnp.where(lane < half, lane, lane - half)
    mode1 = jnp.where(mode1 < quarter, 2 * mode1, 2 * (mode1 - quarter) + 1).astype(jnp.float32)
    base = 1.0 + DECAY * (mode0 * mode0 + mode1 * mode1)
    for j in range(js):
        top = j * 2 * first
        re, im = slice(top, top + first), slice(top + first, top + 2 * first)
        cos, sin = slice(0, quarter), slice(quarter, half)
        whole = lambda part, lanes: jnp.concatenate(
            [y[0, part, lanes], y[1, part, lanes]], axis=1
        )
        rc, rs, ic, isn = whole(re, cos), whole(re, sin), whole(im, cos), whole(im, sin)
        wave = jnp.concatenate(
            [
                jnp.concatenate([rc + isn, rc - isn], axis=1),
                jnp.concatenate([ic - rs, ic + rs], axis=1),
            ],
            axis=0,
        )
        spectrum = dot3((fh[...], fl[...]), split(wave))
        amp = jnp.where(lane == half, 0.0, scale[j, 1] / (base + scale[j, 0]))
        scaled = spectrum * jnp.concatenate([amp, amp], axis=0)
        field = dot3((ih[...], il[...]), split(scaled))
        plus, minus = field[:, :half], field[:, half:]
        even, odd = plus + minus, plus - minus
        odd = jnp.concatenate([-odd[first:], odd[:first]], axis=0)
        at = slice(top, top + 2 * first)
        for parity, lanes in enumerate((cos, sin)):
            operand = jnp.concatenate([even[:, lanes], odd[:, lanes]], axis=1)
            oh[parity, at, :], ol[parity, at, :] = split(operand)
        if j < low:
            keep = first // 4
            kept = [
                scaled[at : at + keep, :]
                for at in (0, first - keep, first, 2 * first - keep)
            ]
            band = jnp.concatenate(kept, axis=0)
            low_lane = lax.broadcasted_iota(jnp.int32, (first, quarter), 1) < quarter // 2
            pieces = []
            for at in (0, half):
                upper = pltpu.roll(band[:, at + quarter : at + half], quarter // 2, 1)
                pieces.append(jnp.where(low_lane, band[:, at : at + quarter], upper))
            band = jnp.concatenate(pieces, axis=1)
            field = dot3((ich[...], icl[...]), split(band))
            value, turned = field[:first], field[first:]
            operand = jnp.concatenate(
                [
                    value[:, :quarter] + value[:, quarter:],
                    turned[:, :quarter] - turned[:, quarter:],
                ],
                axis=1,
            )
            at = slice(j // 2 * first, (j // 2 + 1) * first)
            lanes = slice(j % 2 * half, (j % 2 + 1) * half)
            qh[at, lanes], ql[at, lanes] = split(operand)
    copies = []
    lane = lax.broadcasted_iota(jnp.int32, (SUB, LANE), 1)
    extra = q_count + low // 2

    def leave(start, stop):
        at = slice(start, stop)
        copies.extend(send([(out.at[:, at], out_hbm.at[:, at])], sems, len(copies)))

    def give(value, start):
        tiles = value.shape[0] // first
        for q in range(tiles):
            for r in range(rows):
                for g in range(groups):
                    at = q * first + r * SUB
                    out[r * groups + g, start + q] = value[
                        at : at + SUB, g * LANE : (g + 1) * LANE
                    ]
        leave(start, start + tiles)

    def halo_columns(value, start, held):
        tiles = value.shape[0] // first
        for r in range(rows):
            for g in range(groups):
                total = held[r, g]
                left = max(g - 1, 0) * LANE
                right = min(g + 1, groups - 1) * LANE
                for q in range(tiles):
                    at = slice(q * first + r * SUB, q * first + (r + 1) * SUB)
                    both = jnp.where(
                        lane < LANE // 2,
                        value[at, right : right + LANE],
                        value[at, left : left + LANE],
                    )
                    to = HALO * (start + q)
                    both = pltpu.roll(both, (to + 2) % LANE, 1)
                    total = jnp.where((lane >= to) & (lane < to + HALO), both, total)
                held[r, g] = total

    def coarse_columns(value, held):
        half_lane = LANE // 2
        for j in range(low):
            for r in range(rows):
                at = slice(j // 2 * first + r * SUB, j // 2 * first + (r + 1) * SUB)
                shift = HALO * j + 2 - j % 2 * half_lane
                to = half_lane + HALO * j
                for g in range(groups):
                    left = max(g - 1, 0) * LANE
                    right = min(g + 1, groups - 1) * LANE
                    left = pltpu.roll(value[at, left : left + LANE], shift % LANE, 1)
                    right = pltpu.roll(
                        value[at, right : right + LANE], (shift + half_lane) % LANE, 1
                    )
                    total = jnp.where((lane >= to) & (lane < to + 2), left, held[r, g])
                    held[r, g] = jnp.where(
                        (lane >= to + 2) & (lane < to + HALO), right, total
                    )

    columns = {
        (r, g): jnp.zeros((SUB, LANE), jnp.float32) for r in range(rows) for g in range(groups)
    }
    coarse = dot3((qh[...], ql[...]), (cch[...], ccl[...]))
    give(coarse, q_count)
    coarse_columns(coarse, columns)
    for top in range(0, q_count * first, wide):
        at = slice(top, top + wide)
        even, odd = (
            dot3((oh[parity, at, :], ol[parity, at, :]), (ch[parity], cl[parity]))
            for parity in range(2)
        )
        value = jnp.concatenate([even + odd, even - odd], axis=1)
        give(value, top // first)
        halo_columns(value, top // first, columns)
    for (r, g), total in columns.items():
        out[r * groups + g, extra] = total
    leave(extra, extra + 1)
    for copy in copies:
        copy.wait()


def back_kernel(sizes, b, *rest):
    (devices, q_count, low, tiles, planes, length) = sizes
    away, outs, near, (lh, ll, mh, ml, sems) = rest[:8], rest[8:13], rest[13:21], rest[21:]
    out, coarse, lo, hi, side = outs
    copies = load(list(zip(away, near)), sems)
    eh, el, ceh, cel, wh, wl, cwh, cwl = near
    cells, short = LANE, length // 2
    for n in range(planes):
        for parity in range(2):
            rows = jnp.concatenate(
                [
                    b[pl.ds(s * tiles * SUB + n, q_count, stride=SUB), :]
                    for s in range(parity, devices, 2)
                ],
                axis=0,
            )
            at = slice(n * LANE, (n + 1) * LANE)
            lh[parity, at, :], ll[parity, at, :] = split(jnp.transpose(rows))
    halves = low // 2
    coarse_planes = planes // 2
    for n in range(coarse_planes):
        rows = jnp.concatenate(
            [
                b[pl.ds((q_count + h) * SUB + c * coarse_planes + n, devices, stride=tiles * SUB), :]
                for c in range(2)
                for h in range(halves)
            ],
            axis=0,
        )
        at = slice(n * LANE, (n + 1) * LANE)
        mh[at, :], ml[at, :] = split(jnp.transpose(rows))

    for copy in copies[:4]:
        copy.wait()
    for p in range(0, planes, 2):
        at = slice(p * cells, (p + 2) * cells)
        even, odd = (
            dot3((lh[parity, at, :], ll[parity, at, :]), (eh[parity], el[parity]))
            for parity in range(2)
        )
        value = jnp.exp(jnp.concatenate([even + odd, even - odd], axis=1))
        if p == 0:
            lo[: 2 * cells, :] = value
        if p == planes - 2:
            hi[: 2 * cells, :] = value
        out[at, :] = value
    value = dot3((mh[...], ml[...]), (ceh[...], cel[...]))
    half, fourth = cells // 2, cells // 4
    for n in range(coarse_planes):
        top = n * cells
        part = value[top : top + half, :short] + value[top + half : top + cells, short:]
        part = jnp.exp(part)
        coarse[n * half : (n + 1) * half, :] = part
        for edge, start in ((lo, 0), (hi, coarse_planes - 2)):
            if start <= n < start + 2:
                top = 2 * cells + (n - start) * fourth
                edge[top : top + fourth, :short] = part[:fourth]
                edge[top : top + fourth, short:] = part[fourth:]

    lane = lax.broadcasted_iota(jnp.int32, (SUB, LANE), 1)
    tile = lambda s: b[(s * tiles + tiles - 1) * SUB : (s + 1) * tiles * SUB, :]

    def spread(parts):
        return jnp.concatenate(
            [
                jnp.concatenate(
                    [jnp.where(lane % HALO == h, part, 0.0) for part in parts], axis=1
                )
                for h in range(HALO)
            ],
            axis=0,
        )

    for copy in copies[4:]:
        copy.wait()
    half_lane = LANE // 2
    results = []
    for parity in range(2):
        parts = [
            jnp.where(lane < half_lane, tile(s), pltpu.roll(tile(s + 2), half_lane, 1))
            for s in range(parity, devices, 4)
        ]
        results.append(dot3(split(spread(parts)), (wh[parity], wl[parity])))
    even, odd = results
    value = jnp.exp(jnp.concatenate([even + odd, even - odd], axis=1))
    side[: HALO * planes, :] = value
    width = HALO * low
    fit = LANE // width
    parts = []
    for s in range(0, devices, fit):
        part = jnp.zeros((SUB, LANE), jnp.float32)
        for i in range(fit):
            moved = pltpu.roll(tile(s + i), (i * width - half_lane) % LANE, 1)
            part = jnp.where((lane >= i * width) & (lane < (i + 1) * width), moved, part)
        parts.append(part)
    whole = dot3(split(spread(parts)), (cwh[...], cwl[...]))
    side[HALO * planes :, short:] = jnp.zeros((HALO * coarse_planes, short), jnp.float32)
    after = 2 * cells + 2 * fourth
    for h in range(HALO):
        top = h * SUB
        part = whole[top : top + coarse_planes, :short] + whole[top + coarse_planes : top + SUB, short:]
        part = jnp.exp(part)
        at = HALO * planes + h * coarse_planes
        side[at : at + coarse_planes, :short] = part
        for edge, fine_at, coarse_at in ((lo, 0, 0), (hi, planes - 2, coarse_planes - 2)):
            for i in range(2):
                at = h * planes + fine_at + i
                to = after + i * HALO + h
                edge[to : to + 1, :] = value[at : at + 1, :]
                to += 2 * HALO
                at = coarse_at + i
                edge[to : to + 1, :short] = part[at : at + 1, :]
                edge[to : to + 1, short:] = jnp.zeros((1, short), jnp.float32)


def source_kernel(planes, pairs, x, out, lo, hi, left, right, held, summed):
    cells = x.shape[0] // planes
    length = x.shape[1]
    half, fourth = cells // 2, cells // 4
    held[...] = dot(x[...], pairs[...])
    for n in range(planes // 2):
        top = 2 * n * cells
        for at in range(0, out.shape[1], LANE):
            lanes = slice(at, at + LANE)
            summed[...] = held[top : top + cells, lanes] + held[top + cells : top + 2 * cells, lanes]
            out[n * half : (n + 1) * half, lanes] = (
                summed[pl.ds(0, half, stride=2), :] + summed[pl.ds(1, half, stride=2), :]
            )
    for edge, plane in ((lo, 0), (hi, planes - 1)):
        edge[:cells, :] = x[plane * cells : (plane + 1) * cells, :].astype(jnp.float32)
        at = plane // 2 * half
        edge[cells:, : length // 2] = out[at : at + fourth, :]
        edge[cells:, length // 2 :] = out[at + fourth : at + half, :]
    for edge, row in ((left, 0), (right, cells - 1)):
        edge[...] = jnp.zeros_like(edge)
        for n in range(planes):
            at = n * cells + (row // SUB * SUB)
            edge[n : n + 1, :] = x[at : at + SUB, :].astype(jnp.float32)[row % SUB : row % SUB + 1]
        for n in range(planes // 2):
            at = n * half + row // 2
            edge[SUB + n : SUB + n + 1, : length // 2] = out[at : at + 1, :]


def beside(parts, ends):
    lane = lax.broadcasted_iota(jnp.int32, parts[0].shape, 1)
    ahead = [pltpu.roll(x, 1, 1) for x in parts]
    behind = [pltpu.roll(x, LANE - 1, 1) for x in parts]
    sums = []
    for i in range(len(parts)):
        left = jnp.where(lane == 0, ahead[i - 1] if i else ends[0], ahead[i])
        right = jnp.where(
            lane == LANE - 1, behind[i + 1] if i + 1 < len(parts) else ends[1], behind[i]
        )
        sums.append(left + right)
    return sums


def first_sweep(ks, fs, us, ws, rs, k_at, f_at, to, ext, length):
    lanes = [slice(at, at + LANE) for at in range(0, length, LANE)]
    for top in range(0, ext, SUB):
        at = slice(top, top + SUB)
        parts = [ks[k_at, at, x] for x in lanes]
        for k, both, x in zip(parts, beside(parts, (parts[0], parts[-1])), lanes):
            if top == 0:
                above = pltpu.roll(k, 1, 0)
            else:
                above = ks[k_at, top - 1 : top + SUB - 1, x]
            if top == ext - SUB:
                below = pltpu.roll(k, SUB - 1, 0)
            else:
                below = ks[k_at, top + 1 : top + SUB + 1, x]
            total = (ks[k_at - 1, at, x] + ks[k_at + 1, at, x]) + (above + below) + both
            scale = JACOBI_WEIGHT / (6.0 * k + total)
            u = fs[f_at, at, x] * (2.0 * scale)
            us[to, at, x] = u
            ws[to, at, x] = k * u
            rs[to, at, x] = scale


def second_sweep(ks, us, ws, rs, k_at, u_at, out, to, ext, length):
    lanes = [slice(at, at + LANE) for at in range(0, length, LANE)]
    for top in range(SUB, ext - SUB, SUB):
        at = slice(top, top + SUB)
        sums = []
        for held in (us, ws):
            parts = [held[u_at, at, x] for x in lanes]
            sums.append(
                [
                    both
                    + (held[u_at - 1, at, x] + held[u_at + 1, at, x])
                    + (
                        held[u_at, top - 1 : top + SUB - 1, x]
                        + held[u_at, top + 1 : top + SUB + 1, x]
                    )
                    for both, x in zip(beside(parts, (0.0, 0.0)), lanes)
                ]
            )
        for i, x in enumerate(lanes):
            coupled = ks[k_at, at, x] * sums[0][i] + sums[1][i]
            out[to, top - SUB : top, x] = (2.0 - JACOBI_WEIGHT) * us[u_at, at, x] + rs[
                u_at, at, x
            ] * coupled


def fill_sides(flags, ks, at):
    end = ks.shape[1] - SUB

    @pl.when(flags[2] == 1)
    def _():
        for p in at:
            ks[p, SUB - 1 : SUB, :] = ks[p, SUB : SUB + 1, :]

    @pl.when(flags[3] == 1)
    def _():
        for p in at:
            ks[p, end : end + 1, :] = ks[p, end - 1 : end, :]


def put_source(fs, to, plane, left, right, row, length):
    end = fs.shape[1] - SUB
    fs[to, SUB:end, :] = plane.astype(jnp.float32)
    fs[to, SUB - 1 : SUB, :] = left[row : row + 1, :length]
    fs[to, end : end + 1, :] = right[row : row + 1, :length]


def inner_level(fine, flags, kappa, side, f, f_left, f_right, out_hbm, keep_hbm, scratch):
    ks, fs, us, ws, rs, out, sems = scratch
    planes, cells, length = kappa.shape
    ext, end = cells + 2 * SUB, cells + SUB
    row = 0 if fine else HALO * 2 * planes
    source_row = 0 if fine else SUB
    for p in range(planes):
        ks[p, SUB:end, :] = kappa[p]
        for h, to in enumerate((SUB - 2, SUB - 1, end, end + 1)):
            at = row + h * planes + p
            ks[p, to : to + 1, :] = side[at : at + 1, :length]
    fill_sides(flags, ks, range(planes))
    for p in range(1, planes - 1):
        put_source(fs, p, f[p], f_left, f_right, source_row + p, length)

    def first(p, carry):
        first_sweep(ks, fs, us, ws, rs, p, p, p, ext, length)
        return carry

    lax.fori_loop(1, planes - 1, first, 0)
    pairs = []
    for group, at in enumerate((1, planes - 3)):
        pairs.append((us.at[at : at + 2], keep_hbm.at[5 * group : 5 * group + 2]))
        pairs.append((ws.at[at : at + 2], keep_hbm.at[5 * group + 2 : 5 * group + 4]))
        own = 1 if group == 0 else planes - 2
        pairs.append((rs.at[own], keep_hbm.at[5 * group + 4]))
    copies = send(pairs, sems, 0)
    if planes > 4:

        def second(p, carry):
            second_sweep(ks, us, ws, rs, p, p, out, p, ext, length)
            return carry

        lax.fori_loop(2, planes - 2, second, 0)
        at = slice(2, planes - 2)
        copies += send([(out.at[at], out_hbm.at[at])], sems, len(copies))
    return copies


def inner_kernel(
    flags, kappa, coarse, side, f, cf, f_left, f_right, out_hbm, keep_hbm, ckeep_hbm, *scratch
):
    half = len(scratch) // 2
    copies = inner_level(
        True, flags, kappa, side, f, f_left, f_right, out_hbm, keep_hbm, scratch[:half]
    )
    copies += inner_level(
        False, flags, coarse, side, cf, f_left, f_right, None, ckeep_hbm, scratch[half:]
    )
    for copy in copies:
        copy.wait()


def outer_level(
    fine, flags, kappa, f, keep_hbm, k_edges, f_edges, f_left, f_right, out_hbm, scratch
):
    ks, fs, us, ws, rs, out, sems = scratch
    planes, cells, length = kappa.shape
    ext, end = cells + 2 * SUB, cells + SUB
    half = cells // 2
    fine_cells = cells if fine else 2 * cells
    pairs = []
    for group in range(2):
        at, to = 5 * group, 4 * group + 2 * (1 - group)
        pairs.append((keep_hbm.at[at : at + 2], us.at[to : to + 2]))
        pairs.append((keep_hbm.at[at + 2 : at + 4], ws.at[to : to + 2]))
        pairs.append((keep_hbm.at[at + 4], rs.at[2 if group == 0 else 5]))
    copies = load(pairs, sems)

    def place(held, to, edge, row):
        if fine:
            held[to, SUB:end, :] = edge[row : row + cells, :]
        else:
            held[to, SUB : SUB + half, :] = edge[row : row + half, :length]
            held[to, SUB + half : end, :] = edge[row : row + half, length:]

    after = 2 * fine_cells + fine_cells // 2 + (0 if fine else 2 * HALO)
    for group, edge in enumerate(k_edges):
        for i in range(2):
            row = i * cells if fine else 2 * fine_cells + i * half
            to = 4 * group + 2 * group + i
            place(ks, to, edge, row)
            for h, at in enumerate((SUB - 2, SUB - 1, end, end + 1)):
                row = after + i * HALO + h
                ks[to, at : at + 1, :] = edge[row : row + 1, :length]
            ks[4 * group + 2 * (1 - group) + i, SUB:end, :] = kappa[
                i if group == 0 else planes - 2 + i
            ]
    source_row = 0 if fine else SUB
    for group, edge in enumerate(f_edges):
        place(fs, 3 * group, edge, 0 if fine else fine_cells)
        own = 0 if group == 0 else planes - 1
        put_source(fs, 1 + group, f[own], f_left, f_right, source_row + own, length)
    return copies


def outer_kernel(flags, kappa, coarse, side, f, cf, keep, ckeep, *rest):
    (k_lo, k_hi, f_lo, f_hi, f_left, f_right, _, out, cout), scratch = rest[:9], rest[9:]
    half = len(scratch) // 2
    levels = []
    for fine in (True, False):
        held = scratch[:half] if fine else scratch[half:]
        own, source, kept = (kappa, f, keep) if fine else (coarse, cf, ckeep)
        copies = outer_level(
            fine, flags, own, source, kept, (k_lo, k_hi), (f_lo, f_hi), f_left, f_right, None, held
        )
        levels.append((fine, own, held, copies, out if fine else cout))
    sent = []
    for fine, own, (ks, fs, us, ws, rs, done, sems), copies, target in levels:
        planes, cells, length = own.shape
        ext, end = cells + 2 * SUB, cells + SUB
        row = 0 if fine else HALO * 2 * planes
        for group in range(2):
            for i in range(2):
                p = i if group == 0 else planes - 2 + i
                to = 4 * group + 2 * (1 - group) + i
                for h, at in enumerate((SUB - 2, SUB - 1, end, end + 1)):
                    ks[to, at : at + 1, :] = side[
                        row + h * planes + p : row + h * planes + p + 1, :length
                    ]

        @pl.when(flags[0] == 1)
        def _():
            ks[1] = ks[2]

        @pl.when(flags[1] == 1)
        def _():
            ks[6] = ks[5]

        fill_sides(flags, ks, range(8))

        def first(i, carry):
            k_at = jnp.where(i < 2, i + 1, i + 3)
            to = jnp.where(i < 2, i, i + 4)
            first_sweep(ks, fs, us, ws, rs, k_at, i, to, ext, length)
            return carry

        lax.fori_loop(0, 4, first, 0)
        for copy in copies:
            copy.wait()

        def second(i, carry):
            second_sweep(
                ks, us, ws, rs, i + 2, jnp.where(i < 2, i + 1, i + 3), done, i, ext, length
            )
            return carry

        lax.fori_loop(0, 4, second, 0)
        sent += send(
            [
                (done.at[0:2], target.at[0:2]),
                (done.at[2:4], target.at[planes - 2 : planes]),
            ],
            sems,
            6,
        )
    for copy in sent:
        copy.wait()


SMEM = pl.BlockSpec(memory_space=pltpu.SMEM)
VMEM = pl.BlockSpec(memory_space=pltpu.VMEM)
AWAY = pl.BlockSpec(memory_space=pltpu.HBM)
ANY = pl.BlockSpec(memory_space=pl.ANY)


def call(kernel, outs, operands, scratch, flops, specs, limit, out_specs=None, aliases=None):
    many = isinstance(outs, (list, tuple))
    written = outs if many else [outs]
    moved = sum(math.prod(x.shape) * x.dtype.itemsize for x in (*operands, *written))
    operands = [
        pltpu.with_memory_space_constraint(x, pltpu.HBM) if spec is AWAY else x
        for x, spec in zip(operands, specs)
    ]
    out_specs = out_specs or [
        VMEM if isinstance(x, jax.ShapeDtypeStruct) else AWAY for x in written
    ]
    return pl.pallas_call(
        kernel,
        out_shape=outs,
        in_specs=specs,
        out_specs=out_specs if many else out_specs[0],
        scratch_shapes=scratch,
        input_output_aliases=aliases or {},
        compiler_params=pltpu.CompilerParams(vmem_limit_bytes=limit * MIB),
        cost_estimate=pl.CostEstimate(flops=flops, bytes_accessed=moved, transcendentals=0),
    )(*operands)


def f32(*shape):
    return jax.ShapeDtypeStruct(shape, jnp.float32)


def room(*arrays):
    return [pltpu.VMEM(x.shape, x.dtype) for x in arrays]


def chain(axis):
    up = [(i, i + 1) for i in range(lax.axis_size(axis) - 1)]
    return up, [(j, i) for i, j in up]


def swap(lo, hi, axis):
    up, down = chain(axis)
    return lax.ppermute(hi, axis, up), lax.ppermute(lo, axis, down)


def level_scratch(shape, k_planes, f_planes, out_planes):
    planes, cells, length = shape
    wide = lambda n: pltpu.VMEM((n, cells + 2 * SUB, length), jnp.float32)
    return [
        wide(k_planes),
        wide(f_planes),
        wide(k_planes),
        wide(k_planes),
        wide(k_planes),
        pltpu.VMEM((out_planes, cells, length), jnp.float32),
        pltpu.SemaphoreType.DMA((8,)),
    ]


def fused_body(noise, source):
    rows, groups = lax.axis_size("row"), lax.axis_size(PLANE)
    devices = rows * groups
    planes, cells, length = noise.shape
    first, second = planes * rows, cells * groups
    bf16 = jnp.bfloat16
    held = length // 2 // devices
    js = list(range(held))
    low = held // 2
    me = lax.axis_index(EVERY)
    row_at, group_at = lax.axis_index("row"), lax.axis_index(PLANE)
    flags = jnp.stack(
        [row_at == 0, row_at == rows - 1, group_at == 0, group_at == groups - 1]
    ).astype(jnp.int32)
    norm = FIELD_SCALE * (float(first) * float(second) * float(length)) ** (-0.5)
    flat = (planes * cells, length)

    table = np.concatenate(two_parts(forward_third(length, devices, js)))
    shape = (length * SUB, LANE)
    sent = call(
        functools.partial(forward_kernel, planes),
        pltpu.HBM(shape, jnp.float32),
        (table, noise.reshape(flat)),
        room(table)
        + [
            pltpu.VMEM(flat, bf16),
            pltpu.VMEM(shape, jnp.float32),
            pltpu.SemaphoreType.DMA((1 + planes // 2,)),
        ],
        4 * length * length * planes * cells,
        [AWAY] * 2,
        16,
    )
    sent, source = lax.optimization_barrier((sent, source))
    sent = sent.reshape(devices, 2 * held, SUB, LANE)
    arrived = lax.all_to_all(sent, EVERY, split_axis=0, concat_axis=0, tiled=True)

    pairs = np.zeros((length, length // 2), np.float32)
    pairs[np.arange(length), np.arange(length) // 2] = 0.125
    level = f32(cells + cells // 4, length)
    side = f32(2 * SUB, length)
    coarse_source, *edges = call(
        functools.partial(source_kernel, planes),
        [f32(planes * cells // 4, length // 2), level, level, side, side],
        (pairs.astype(bf16), source.reshape(flat)),
        [
            pltpu.VMEM((planes * cells, length // 2), jnp.float32),
            pltpu.VMEM((cells, LANE), jnp.float32),
        ],
        planes * cells * length * length,
        [VMEM] * 2,
        16,
    )
    coarse_source = coarse_source.reshape(planes // 2, cells // 2, length // 2)
    edges = (*swap(*edges[:2], "row"), *swap(*edges[2:], PLANE))
    arrived, edges, coarse_source = lax.optimization_barrier((arrived, edges, coarse_source))

    constants = (
        two_parts(second_table(second))
        + two_parts(forward_first(first))
        + two_parts(inverse_first(first))
        + two_parts(second_table(second).transpose(0, 2, 1))
        + two_parts(inverse_first_coarse(first // 2, rows))
        + two_parts(second_coarse(second // 2, groups))
    )
    tiles = 2 * held + low // 2 + 1
    modes = (me + devices * np.array(js)).astype(jnp.float32)
    weight = jnp.where(modes == 0.0, norm, 2.0 * norm).astype(jnp.float32)
    scale = jnp.stack([DECAY * modes * modes, weight], axis=1)
    block = (2, 2 * held * first, second // 2)
    shape = (devices, tiles, SUB, LANE)
    out = call(
        functools.partial(middle_kernel, (first, second, rows, groups, held, low)),
        pltpu.HBM(shape, jnp.float32),
        (scale, arrived, *constants),
        room(*constants)
        + [
            pltpu.VMEM(shape, jnp.float32),
            pltpu.SemaphoreType.DMA((len(constants),)),
            pltpu.VMEM(block, bf16),
            pltpu.VMEM(block, bf16),
            pltpu.VMEM(block, jnp.float32),
            pltpu.VMEM(block, bf16),
            pltpu.VMEM(block, bf16),
            pltpu.VMEM((low // 2 * first, second), bf16),
            pltpu.VMEM((low // 2 * first, second), bf16),
        ],
        6 * 2 * 2 * held * first * second * (second + 2 * first),
        [SMEM, VMEM] + [AWAY] * len(constants),
        32,
    )
    got = lax.all_to_all(out, EVERY, split_axis=0, concat_axis=0, tiled=True)

    third = inverse_third(length, devices, js)
    constants = (
        two_parts(third)
        + two_parts(third_coarse(length // 2, devices, js[:low]))
        + two_parts(np.repeat(third, HALO, axis=1))
        + two_parts(third_coarse_halo(length // 2, devices, js[:low]))
    )
    edge = f32(2 * cells + cells // 2 + 4 * HALO, length)
    side = f32(HALO * planes * 3 // 2, length)
    fine, coarse, lo, hi, side = call(
        functools.partial(back_kernel, (devices, 2 * held, low, tiles, planes, length)),
        [f32(*flat), f32(planes * cells // 4, length // 2), edge, edge, side],
        (got.reshape(devices * tiles * SUB, LANE), *constants),
        room(*constants)
        + [pltpu.VMEM((2, planes * cells, devices * held), bf16)] * 2
        + [pltpu.VMEM((planes // 2 * LANE, devices * low), bf16)] * 2
        + [pltpu.SemaphoreType.DMA((8,))],
        6 * planes * cells * length * length,
        [VMEM] + [AWAY] * 8,
        28,
    )
    fine, coarse = fine.reshape(source.shape), coarse.reshape(coarse_source.shape)
    k_lo, k_hi = swap(lo, hi, "row")
    f_lo, f_hi, f_left, f_right = edges
    kept = lambda x: jax.ShapeDtypeStruct((10, x.shape[1] + 2 * SUB, x.shape[2]), jnp.float32)
    own = (flags, fine, coarse, side, source, coarse_source)
    inner, keep, coarse_keep = call(
        inner_kernel,
        [pltpu.HBM(fine.shape, jnp.float32), kept(fine), kept(coarse)],
        (*own, f_left, f_right),
        level_scratch(fine.shape, planes, planes, planes)
        + level_scratch(coarse.shape, planes // 2, planes // 2, planes // 2),
        30 * fine.size,
        [SMEM] + [VMEM] * 7,
        32,
        [AWAY, ANY, ANY],
    )
    return call(
        outer_kernel,
        [pltpu.HBM(fine.shape, jnp.float32), pltpu.HBM(coarse.shape, jnp.float32)],
        (*own, keep, coarse_keep, k_lo, k_hi, f_lo, f_hi, f_left, f_right, inner),
        level_scratch(fine.shape, 8, 4, 4) + level_scratch(coarse.shape, 8, 4, 4),
        30 * fine.size,
        [SMEM] + [VMEM] * 5 + [ANY] * 2 + [VMEM] * 6 + [AWAY],
        32,
        [AWAY] * 2,
        {14: 0},
    )


NEIGHBOUR_STEPS = ((1, 0, 0), (-1, 0, 0), (0, 1, 0), (0, -1, 0), (0, 0, 1), (0, 0, -1))


def padded(x, sides, width):
    for axis, dim in sides:
        peers, length = (lax.axis_size(axis), x.shape[dim])
        up = [(i, (i + 1) % peers) for i in range(peers - 1)]
        down = [(j, i) for i, j in up]
        last = lax.slice_in_dim(x, length - width, length, axis=dim)
        leading = lax.slice_in_dim(x, 0, width, axis=dim)
        before = lax.ppermute(last, axis, up)
        after = lax.ppermute(leading, axis, down)
        x = jnp.concatenate([before, x, after], axis=dim)
    return x


def signed_modes(index, length):
    return jnp.where(index < length // 2, index, index - length).astype(jnp.float32)


def amplitude(first_modes, second_modes, third_modes, first_edge, second_edge, third_edge):
    squared = first_modes * first_modes + second_modes * second_modes + third_modes * third_modes
    value = FIELD_SCALE / (1.0 + (2.0 * math.pi * CORRELATION) ** 2 * squared)
    edge = (
        (jnp.abs(first_modes) == first_edge)
        | (jnp.abs(second_modes) == second_edge)
        | (jnp.abs(third_modes) == third_edge)
    )
    return jnp.where(edge, 0.0, value)


def phase_table(count_rows, count_cols, modulus, sign):
    left_index = jnp.arange(count_rows, dtype=jnp.int32)[:, None]
    right_index = jnp.arange(count_cols, dtype=jnp.int32)[None, :]
    angle = 2.0 * math.pi / modulus * (left_index * right_index % modulus).astype(jnp.float32)
    return (jnp.cos(angle), sign * jnp.sin(angle))


def split_length(length):
    outer_len = 2 ** ((length.bit_length() - 1) // 2)
    return (outer_len, length // outer_len)


def real_form(form, left_value, right_value):
    return jnp.einsum(form, left_value, right_value, precision=lax.Precision.HIGHEST)


def complex_form(form, left_real, left_imag, right_real, right_imag):
    real_part = real_form(form, left_real, right_real) - real_form(form, left_imag, right_imag)
    imag_part = real_form(form, left_real, right_imag) + real_form(form, left_imag, right_real)
    return (real_part, imag_part)


def merge_pair(values, out_form, first_letter):
    merge_at = out_form.index(first_letter)
    out_dims = list(values.shape)
    merged = (
        out_dims[:merge_at]
        + [out_dims[merge_at] * out_dims[merge_at + 1]]
        + out_dims[merge_at + 2 :]
    )
    return values.reshape(merged)


def forward_axis(real_part, imag_part, lead_form, out_form, kept_modes):
    length = real_part.shape[-1]
    outer_len, inner_len = split_length(length)
    split_shape = real_part.shape[:-1] + (outer_len, inner_len)
    outer_real, outer_imag = phase_table(outer_len, outer_len, outer_len, -1.0)
    twist_real, twist_imag = phase_table(outer_len, inner_len, length, -1.0)
    inner_real, inner_imag = phase_table(inner_len, kept_modes // outer_len, inner_len, -1.0)
    first_form = lead_form + "ab,ai->" + lead_form + "ib"
    split_real = real_part.reshape(split_shape)
    if imag_part is None:
        section_real = real_form(first_form, split_real, outer_real)
        section_imag = real_form(first_form, split_real, outer_imag)
    else:
        section_real, section_imag = complex_form(
            first_form, split_real, imag_part.reshape(split_shape), outer_real, outer_imag
        )
    turned_real = section_real * twist_real - section_imag * twist_imag
    turned_imag = section_real * twist_imag + section_imag * twist_real
    result_real, result_imag = complex_form(
        lead_form + "ib,bj->" + out_form, turned_real, turned_imag, inner_real, inner_imag
    )
    return (merge_pair(result_real, out_form, "j"), merge_pair(result_imag, out_form, "j"))


def inverse_axis(real_part, imag_part, length, lead_form, out_form, real_only):
    kept_modes = real_part.shape[-1]
    outer_len, inner_len = split_length(length)
    split_shape = real_part.shape[:-1] + (kept_modes // outer_len, outer_len)
    inner_real, inner_imag = phase_table(kept_modes // outer_len, inner_len, inner_len, 1.0)
    twist_real, twist_imag = phase_table(outer_len, inner_len, length, 1.0)
    outer_real, outer_imag = phase_table(outer_len, outer_len, outer_len, 1.0)
    section_real, section_imag = complex_form(
        lead_form + "ji,jb->" + lead_form + "ib",
        real_part.reshape(split_shape),
        imag_part.reshape(split_shape),
        inner_real,
        inner_imag,
    )
    turned_real = section_real * twist_real - section_imag * twist_imag
    turned_imag = section_real * twist_imag + section_imag * twist_real
    second_form = lead_form + "ib,ia->" + out_form
    if real_only:
        result = real_form(second_form, turned_real, outer_real) - real_form(
            second_form, turned_imag, outer_imag
        )
        return merge_pair(result, out_form, "a")
    result_real, result_imag = complex_form(
        second_form, turned_real, turned_imag, outer_real, outer_imag
    )
    return (merge_pair(result_real, out_form, "a"), merge_pair(result_imag, out_form, "a"))


def low_band(values, half_coarse, fine_len):
    return jnp.concatenate(
        [values[:, :, :half_coarse], values[:, :, fine_len - half_coarse :]], axis=2
    )


def window(values, margin, offset):
    return values[
        margin + offset[0] : values.shape[0] - margin + offset[0],
        margin + offset[1] : values.shape[1] - margin + offset[1],
        margin + offset[2] : values.shape[2] - margin + offset[2],
    ]


def face_weight(center, beside):
    return jnp.where(beside > 0.0, 0.5 * (center + beside), center)


def smooth_twice(kappa, source):
    no_shift = (0, 0, 0)
    center = window(kappa, 1, no_shift)
    faces = [face_weight(center, window(kappa, 1, offset)) for offset in NEIGHBOUR_STEPS]
    diagonal = faces[0] + faces[1] + faces[2] + faces[3] + faces[4] + faces[5]
    guarded = jnp.where(center > 0.0, diagonal, 1.0)
    first_sweep = JACOBI_WEIGHT * window(source, 1, no_shift) / guarded
    inner_first = window(first_sweep, 1, no_shift)
    inner_diagonal = window(diagonal, 1, no_shift)
    coupled = jnp.zeros_like(inner_first)
    for face_value, offset in zip(faces, NEIGHBOUR_STEPS):
        coupled = coupled + window(face_value, 1, no_shift) * window(first_sweep, 1, offset)
    residual = window(source, 2, no_shift) - inner_diagonal * inner_first + coupled
    return inner_first + JACOBI_WEIGHT * residual / inner_diagonal


def pad_depth(values):
    return jnp.pad(values, ((0, 0), (0, 0), (2, 2)))


def plain_body(noise, source):
    row_at = lax.axis_index("row")
    group_at = lax.axis_index(("level", "col"))
    fine_field = noise.astype(jnp.float32)
    fine_len = fine_field.shape[-1]
    coarse_len = fine_len // 2
    half_coarse = coarse_len // 2
    kept_modes = fine_len // 2
    real_part, imag_part = forward_axis(fine_field, None, "pq", "pjiq", kept_modes)
    real_part, imag_part = (
        lax.all_to_all(real_part, ("level", "col"), split_axis=1, concat_axis=2, tiled=True),
        lax.all_to_all(imag_part, ("level", "col"), split_axis=1, concat_axis=2, tiled=True),
    )
    real_part, imag_part = forward_axis(real_part, imag_part, "pq", "jiqp", fine_len)
    real_part, imag_part = (
        lax.all_to_all(real_part, "row", split_axis=0, concat_axis=2, tiled=True),
        lax.all_to_all(imag_part, "row", split_axis=0, concat_axis=2, tiled=True),
    )
    slab_len = real_part.shape[-1]
    coarse_slab = slab_len // 2
    half_slab = coarse_slab // 2
    real_part, imag_part = forward_axis(real_part, imag_part, "pq", "pqji", slab_len)
    second_count = real_part.shape[0]
    third_count = real_part.shape[1]
    wave_second = signed_modes(
        row_at * second_count + jnp.arange(second_count, dtype=jnp.int32), fine_len
    )[:, None, None]
    third_index = group_at * third_count + jnp.arange(third_count, dtype=jnp.int32)
    wave_third = signed_modes(third_index, fine_len)[None, :, None]
    spread = 2.0
    mirror_weight = jnp.where(third_index == 0, 1.0, spread).astype(jnp.float32)[None, :, None]
    norm_factor = (float(slab_len) * float(fine_len) * float(fine_len)) ** (-0.5)
    wave_first = signed_modes(jnp.arange(slab_len, dtype=jnp.int32), slab_len)[None, None, :]
    fine_scale = (
        amplitude(
            wave_second, wave_third, wave_first, fine_len / 2.0, fine_len / 2.0, slab_len / 2.0
        )
        * mirror_weight
        * norm_factor
    )
    coarse_first = signed_modes(jnp.arange(coarse_slab, dtype=jnp.int32), coarse_slab)[
        None, None, :
    ]
    coarse_scale = (
        amplitude(
            wave_second,
            wave_third,
            coarse_first,
            coarse_len / 2.0,
            coarse_len / 2.0,
            coarse_slab / 2.0,
        )
        * mirror_weight
        * norm_factor
    )
    coarse_real = low_band(real_part, half_slab, slab_len) * coarse_scale
    coarse_imag = low_band(imag_part, half_slab, slab_len) * coarse_scale
    fine_real, fine_imag = inverse_axis(
        real_part * fine_scale, imag_part * fine_scale, slab_len, "pq", "abqp", False
    )
    coarse_real, coarse_imag = inverse_axis(
        coarse_real, coarse_imag, coarse_slab, "pq", "abqp", False
    )
    fine_real, fine_imag, coarse_real, coarse_imag = (
        lax.all_to_all(fine_real, "row", split_axis=0, concat_axis=2, tiled=True),
        lax.all_to_all(fine_imag, "row", split_axis=0, concat_axis=2, tiled=True),
        lax.all_to_all(coarse_real, "row", split_axis=0, concat_axis=2, tiled=True),
        lax.all_to_all(coarse_imag, "row", split_axis=0, concat_axis=2, tiled=True),
    )
    coarse_real = low_band(coarse_real, half_coarse, fine_len)
    coarse_imag = low_band(coarse_imag, half_coarse, fine_len)
    fine_real, fine_imag = inverse_axis(fine_real, fine_imag, fine_len, "pq", "pabq", False)
    coarse_real, coarse_imag = inverse_axis(
        coarse_real, coarse_imag, coarse_len, "pq", "pabq", False
    )
    fine_real, fine_imag, coarse_real, coarse_imag = (
        lax.all_to_all(fine_real, ("level", "col"), split_axis=1, concat_axis=2, tiled=True),
        lax.all_to_all(fine_imag, ("level", "col"), split_axis=1, concat_axis=2, tiled=True),
        lax.all_to_all(coarse_real, ("level", "col"), split_axis=1, concat_axis=2, tiled=True),
        lax.all_to_all(coarse_imag, ("level", "col"), split_axis=1, concat_axis=2, tiled=True),
    )
    coarse_real = coarse_real[:, :, :half_coarse]
    coarse_imag = coarse_imag[:, :, :half_coarse]
    fine_log = inverse_axis(fine_real, fine_imag, fine_len, "pq", "pqab", True)
    coarse_log = inverse_axis(coarse_real, coarse_imag, coarse_len, "pq", "pqab", True)
    fine_kappa = jnp.exp(fine_log)
    coarse_kappa = jnp.exp(coarse_log)
    fine_source = source.astype(jnp.float32)
    coarse_rows = coarse_log.shape[0]
    coarse_cols = coarse_log.shape[1]
    coarse_source = fine_source.reshape(coarse_rows, 2, coarse_cols, 2, coarse_len, 2).mean(
        axis=(1, 3, 5)
    )
    fine_kappa, fine_source, coarse_kappa, coarse_source = (
        padded(fine_kappa, (("row", 0), (("level", "col"), 1)), 2),
        padded(fine_source, (("row", 0), (("level", "col"), 1)), 2),
        padded(coarse_kappa, (("row", 0), (("level", "col"), 1)), 2),
        padded(coarse_source, (("row", 0), (("level", "col"), 1)), 2),
    )
    fine_pressure = smooth_twice(pad_depth(fine_kappa), pad_depth(fine_source))
    coarse_pressure = smooth_twice(pad_depth(coarse_kappa), pad_depth(coarse_source))
    return (fine_pressure, coarse_pressure)


def body(noise, source):
    planes, cells, length = noise.shape
    devices = lax.axis_size(EVERY)
    held = length // 2 // devices
    if planes == SUB and cells == LANE and held % 4 == 0 and held > 0:
        return fused_body(noise, source)
    return plain_body(noise, source)


def solution(mesh):
    return jax.shard_map(
        body,
        mesh=mesh,
        in_specs=(P("row", ("level", "col"), None), P("row", ("level", "col"), None)),
        out_specs=(P("row", ("level", "col"), None), P("row", ("level", "col"), None)),
        check_vma=False,
    )
```

```python
import functools
import math

import jax
import jax.numpy as jnp
import numpy as np
from jax import lax
from jax.experimental import pallas as pl
from jax.experimental.pallas import tpu as pltpu
from jax.sharding import PartitionSpec as P

JACOBI_WEIGHT = 2.0 / 3.0
CORRELATION = 0.2
FIELD_SCALE = 0.3
DECAY = (2.0 * math.pi * CORRELATION) ** 2
EVERY = ("row", "level", "col")
PLANE = ("level", "col")
MIB = 1 << 20
SUB, LANE = 8, 128
HALO = 4


def two_parts(matrix):
    high = matrix.astype(jnp.bfloat16)
    low = (matrix - high.astype(np.float64)).astype(jnp.bfloat16)
    return high, low


def angles(rows, cols, length):
    return 2.0 * np.pi * (np.outer(rows, cols) % length) / length


def third_modes(devices, js):
    return np.array([[d + devices * j for j in js] for d in range(devices)])


def forward_third(length, devices, js):
    theta = angles(third_modes(devices, js).reshape(-1), np.arange(length), length)
    return np.stack([np.cos(theta), -np.sin(theta)], axis=1).reshape(-1, length)


def inverse_third(length, devices, js):
    modes = third_modes(devices, js).reshape(devices // 2, 2, len(js)).transpose(1, 0, 2)
    theta = 2.0 * np.pi * (modes[..., None] * np.arange(length // 2) % length) / length
    both = np.stack([np.cos(theta), -np.sin(theta)], axis=3)
    return both.reshape(2, -1, length // 2)


def second_modes(length):
    return np.arange(length // 2).reshape(-1, 2).T


def second_table(length):
    theta = second_modes(length)[:, None, :] * np.arange(length // 2)[None, :, None]
    theta = 2.0 * np.pi * (theta % length) / length
    return np.concatenate([np.cos(theta), np.sin(theta)], axis=2)


def forward_first(length):
    theta = angles(np.arange(length), np.arange(length), length)
    cos, sin = np.cos(theta), np.sin(theta)
    return np.block([[cos, sin], [-sin, cos]])


def inverse_first(length):
    theta = angles(np.arange(length), np.arange(length), length)
    cos, sin = np.cos(theta), np.sin(theta)
    cos[:, length // 2] = 0.0
    sin[:, length // 2] = 0.0
    return np.block([[cos, -sin], [sin, cos]])


def inverse_first_coarse(length, rows):
    full = inverse_first(length)
    value = full.reshape(2, rows, length // rows, 2 * length)
    turned = np.concatenate([-full[length:], full[:length]]).reshape(value.shape)
    order = lambda x: x.transpose(1, 0, 2, 3).reshape(2 * length, 2 * length)
    return np.concatenate([order(value), order(turned)])


def second_coarse(length, groups):
    theta = angles(second_modes(length).reshape(-1), np.arange(length), length)
    table = np.concatenate([np.cos(theta), np.sin(theta)])
    span = length // groups
    out = np.zeros((2, length, groups, 2, span))
    for pair in range(2):
        out[pair, :, :, pair, :] = table.reshape(length, groups, span)
    return out.reshape(2 * length, 2 * length)


def third_coarse(length, devices, js):
    modes = third_modes(devices, js).reshape(devices, len(js) // 2, 2)
    theta = 2.0 * np.pi * (modes[..., None] * np.arange(length) % length) / length
    both = np.stack([np.cos(theta), -np.sin(theta)])
    return both.transpose(0, 2, 1, 3, 4).reshape(2 * (len(js) // 2) * devices, 2 * length)


def third_coarse_halo(length, devices, js):
    modes = np.repeat(third_modes(devices, js).reshape(-1), HALO)
    theta = angles(modes, np.arange(length), length)
    return np.concatenate([np.cos(theta), -np.sin(theta)], axis=1)


def split(x):
    high = x.astype(jnp.bfloat16)
    return high, (x - high.astype(jnp.float32)).astype(jnp.bfloat16)


def dot(a, b):
    return lax.dot_general(a, b, (((1,), (0,)), ((), ())), preferred_element_type=jnp.float32)


def dot_t(a, b):
    return lax.dot_general(a, b, (((1,), (1,)), ((), ())), preferred_element_type=jnp.float32)


def dot3(a, b):
    (ah, al), (bh, bl) = a, b
    return dot(ah, bh) + (dot(ah, bl) + dot(al, bh))


def load(pairs, sems):
    copies = [pltpu.make_async_copy(a, b, sems.at[i]) for i, (a, b) in enumerate(pairs)]
    for copy in copies:
        copy.start()
    return copies


def send(pairs, sems, first):
    copies = [pltpu.make_async_copy(a, b, sems.at[first + i]) for i, (a, b) in enumerate(pairs)]
    for copy in copies:
        copy.start()
    return copies


def forward_kernel(planes, d_hbm, x_hbm, out_hbm, d, x, out, sems):
    pieces, rows = d.shape[0], d.shape[1] // 2
    parts = [slice(p * LANE, (p + 2) * LANE) for p in range(0, planes, 2)]
    pairs = [(x_hbm.at[at, :], x.at[at, :]) for at in parts]
    copies = load([(d_hbm.at[0], d.at[0])] + pairs + [(d_hbm.at[i], d.at[i]) for i in range(1, pieces)], sems)
    sent = []
    copies[0].wait()
    for piece in range(pieces):
        if piece:
            copies[len(parts) + piece].wait()
        for i, at in enumerate(parts):
            if piece == 0:
                copies[i + 1].wait()
            value = dot_t(d[piece], x[at, :])
            value = value[:rows] + value[rows:]
            for h in range(2):
                out[pl.ds(piece * rows * SUB + 2 * i + h, rows, stride=SUB), :] = value[
                    :, h * LANE : (h + 1) * LANE
                ]
        tall = slice(piece * rows * SUB, (piece + 1) * rows * SUB)
        sent += send([(out.at[tall, :], out_hbm.at[tall, :])], sems, len(copies) + piece)
    for copy in sent:
        copy.wait()


def middle_kernel(sizes, scale, b, *rest):
    (first, second, rows, groups, js, low) = sizes
    count = 12
    away, out_hbm, near, rest = rest[:count], rest[count], rest[count + 1 : 2 * count + 1], rest[2 * count + 1 :]
    out, sems, zh, zl, y, oh, ol, qh, ql = rest
    copies = load(list(zip(away, near)), sems)
    csh, csl, fh, fl, ih, il, ich, icl, cch, ccl, ch, cl = near
    q_count = 2 * js
    half, quarter = second // 2, second // 4
    for q in range(q_count):
        for g in range(groups // 2):
            for r in range(0, rows, 2):
                at = r * groups + g
                near_half = jnp.concatenate([b[at, q], b[at + groups, q]], axis=0)
                at += groups // 2
                far_half = jnp.concatenate([b[at, q], b[at + groups, q]], axis=0)
                at = slice(q * first + r * SUB, q * first + (r + 2) * SUB)
                lanes = slice(g * LANE, (g + 1) * LANE)
                zh[0, at, lanes], zl[0, at, lanes] = split(near_half + far_half)
                zh[1, at, lanes], zl[1, at, lanes] = split(near_half - far_half)
    for copy in copies[:8]:
        copy.wait()
    wide = 8 * first
    for top in range(0, q_count * first, wide):
        at = slice(top, top + wide)
        for parity in range(2):
            y[parity, at, :] = dot3(
                (zh[parity, at, :], zl[parity, at, :]), (csh[parity], csl[parity])
            )
    mode0 = lax.broadcasted_iota(jnp.int32, (first, second), 0)
    mode0 = jnp.where(mode0 < first // 2, mode0, mode0 - first).astype(jnp.float32)
    lane = lax.broadcasted_iota(jnp.int32, (first, second), 1)
    mode1 = jnp.where(lane < half, lane, lane - half)
    mode1 = jnp.where(mode1 < quarter, 2 * mode1, 2 * (mode1 - quarter) + 1).astype(jnp.float32)
    base = 1.0 + DECAY * (mode0 * mode0 + mode1 * mode1)
    for j in range(js):
        top = j * 2 * first
        re, im = slice(top, top + first), slice(top + first, top + 2 * first)
        cos, sin = slice(0, quarter), slice(quarter, half)
        whole = lambda part, lanes: jnp.concatenate(
            [y[0, part, lanes], y[1, part, lanes]], axis=1
        )
        rc, rs, ic, isn = whole(re, cos), whole(re, sin), whole(im, cos), whole(im, sin)
        wave = jnp.concatenate(
            [
                jnp.concatenate([rc + isn, rc - isn], axis=1),
                jnp.concatenate([ic - rs, ic + rs], axis=1),
            ],
            axis=0,
        )
        spectrum = dot3((fh[...], fl[...]), split(wave))
        amp = jnp.where(lane == half, 0.0, scale[j, 1] / (base + scale[j, 0]))
        scaled = spectrum * jnp.concatenate([amp, amp], axis=0)
        field = dot3((ih[...], il[...]), split(scaled))
        plus, minus = field[:, :half], field[:, half:]
        even, odd = plus + minus, plus - minus
        odd = jnp.concatenate([-odd[first:], odd[:first]], axis=0)
        at = slice(top, top + 2 * first)
        for parity, lanes in enumerate((cos, sin)):
            operand = jnp.concatenate([even[:, lanes], odd[:, lanes]], axis=1)
            oh[parity, at, :], ol[parity, at, :] = split(operand)
        if j < low:
            keep = first // 4
            kept = [
                scaled[at : at + keep, :]
                for at in (0, first - keep, first, 2 * first - keep)
            ]
            band = jnp.concatenate(kept, axis=0)
            low_lane = lax.broadcasted_iota(jnp.int32, (first, quarter), 1) < quarter // 2
            pieces = []
            for at in (0, half):
                upper = pltpu.roll(band[:, at + quarter : at + half], quarter // 2, 1)
                pieces.append(jnp.where(low_lane, band[:, at : at + quarter], upper))
            band = jnp.concatenate(pieces, axis=1)
            field = dot3((ich[...], icl[...]), split(band))
            value, turned = field[:first], field[first:]
            operand = jnp.concatenate(
                [
                    value[:, :quarter] + value[:, quarter:],
                    turned[:, :quarter] - turned[:, quarter:],
                ],
                axis=1,
            )
            at = slice(j // 2 * first, (j // 2 + 1) * first)
            lanes = slice(j % 2 * half, (j % 2 + 1) * half)
            qh[at, lanes], ql[at, lanes] = split(operand)
    for copy in copies[8:]:
        copy.wait()
    copies = []
    wide = 4 * first
    lane = lax.broadcasted_iota(jnp.int32, (SUB, LANE), 1)
    extra = q_count + low // 2

    def leave(start, stop):
        at = slice(start, stop)
        copies.extend(send([(out.at[:, at], out_hbm.at[:, at])], sems, len(copies)))

    def give(value, start):
        tiles = value.shape[0] // first
        for q in range(tiles):
            for r in range(rows):
                for g in range(groups):
                    at = q * first + r * SUB
                    out[r * groups + g, start + q] = value[
                        at : at + SUB, g * LANE : (g + 1) * LANE
                    ]
        leave(start, start + tiles)

    def halo_columns(value, start, held):
        tiles = value.shape[0] // first
        for r in range(rows):
            for g in range(groups):
                total = held[r, g]
                left = max(g - 1, 0) * LANE
                right = min(g + 1, groups - 1) * LANE
                for q in range(tiles):
                    at = slice(q * first + r * SUB, q * first + (r + 1) * SUB)
                    both = jnp.where(
                        lane < LANE // 2,
                        value[at, right : right + LANE],
                        value[at, left : left + LANE],
                    )
                    to = HALO * (start + q)
                    both = pltpu.roll(both, (to + 2) % LANE, 1)
                    total = jnp.where((lane >= to) & (lane < to + HALO), both, total)
                held[r, g] = total

    def coarse_columns(value, held):
        half_lane = LANE // 2
        for j in range(low):
            for r in range(rows):
                at = slice(j // 2 * first + r * SUB, j // 2 * first + (r + 1) * SUB)
                shift = HALO * j + 2 - j % 2 * half_lane
                to = half_lane + HALO * j
                for g in range(groups):
                    left = max(g - 1, 0) * LANE
                    right = min(g + 1, groups - 1) * LANE
                    left = pltpu.roll(value[at, left : left + LANE], shift % LANE, 1)
                    right = pltpu.roll(
                        value[at, right : right + LANE], (shift + half_lane) % LANE, 1
                    )
                    total = jnp.where((lane >= to) & (lane < to + 2), left, held[r, g])
                    held[r, g] = jnp.where(
                        (lane >= to + 2) & (lane < to + HALO), right, total
                    )

    columns = {
        (r, g): jnp.zeros((SUB, LANE), jnp.float32) for r in range(rows) for g in range(groups)
    }
    coarse = dot3((qh[...], ql[...]), (cch[...], ccl[...]))
    give(coarse, q_count)
    coarse_columns(coarse, columns)
    for top in range(0, q_count * first, wide):
        at = slice(top, top + wide)
        even, odd = (
            dot3((oh[parity, at, :], ol[parity, at, :]), (ch[parity], cl[parity]))
            for parity in range(2)
        )
        value = jnp.concatenate([even + odd, even - odd], axis=1)
        give(value, top // first)
        halo_columns(value, top // first, columns)
    for (r, g), total in columns.items():
        out[r * groups + g, extra] = total
    leave(extra, extra + 1)
    for copy in copies:
        copy.wait()


def back_kernel(sizes, b, *rest):
    (devices, q_count, low, tiles, planes, length) = sizes
    away, outs, near, (lh, ll, mh, ml, sems) = rest[:8], rest[8:13], rest[13:21], rest[21:]
    out, coarse, lo, hi, side = outs
    copies = load(list(zip(away, near)), sems)
    eh, el, ceh, cel, wh, wl, cwh, cwl = near
    cells, short = LANE, length // 2
    for n in range(planes):
        for parity in range(2):
            rows = jnp.concatenate(
                [
                    b[pl.ds(s * tiles * SUB + n, q_count, stride=SUB), :]
                    for s in range(parity, devices, 2)
                ],
                axis=0,
            )
            at = slice(n * LANE, (n + 1) * LANE)
            lh[parity, at, :], ll[parity, at, :] = split(jnp.transpose(rows))
    halves = low // 2
    coarse_planes = planes // 2
    for n in range(coarse_planes):
        rows = jnp.concatenate(
            [
                b[pl.ds((q_count + h) * SUB + c * coarse_planes + n, devices, stride=tiles * SUB), :]
                for c in range(2)
                for h in range(halves)
            ],
            axis=0,
        )
        at = slice(n * LANE, (n + 1) * LANE)
        mh[at, :], ml[at, :] = split(jnp.transpose(rows))

    for copy in copies[:4]:
        copy.wait()
    for p in range(0, planes, 2):
        at = slice(p * cells, (p + 2) * cells)
        even, odd = (
            dot3((lh[parity, at, :], ll[parity, at, :]), (eh[parity], el[parity]))
            for parity in range(2)
        )
        value = jnp.exp(jnp.concatenate([even + odd, even - odd], axis=1))
        if p == 0:
            lo[: 2 * cells, :] = value
        if p == planes - 2:
            hi[: 2 * cells, :] = value
        out[at, :] = value
    value = dot3((mh[...], ml[...]), (ceh[...], cel[...]))
    half, fourth = cells // 2, cells // 4
    for n in range(coarse_planes):
        top = n * cells
        part = value[top : top + half, :short] + value[top + half : top + cells, short:]
        part = jnp.exp(part)
        coarse[n * half : (n + 1) * half, :] = part
        for edge, start in ((lo, 0), (hi, coarse_planes - 2)):
            if start <= n < start + 2:
                top = 2 * cells + (n - start) * fourth
                edge[top : top + fourth, :short] = part[:fourth]
                edge[top : top + fourth, short:] = part[fourth:]

    lane = lax.broadcasted_iota(jnp.int32, (SUB, LANE), 1)
    tile = lambda s: b[(s * tiles + tiles - 1) * SUB : (s + 1) * tiles * SUB, :]

    def spread(parts):
        return jnp.concatenate(
            [
                jnp.concatenate(
                    [jnp.where(lane % HALO == h, part, 0.0) for part in parts], axis=1
                )
                for h in range(HALO)
            ],
            axis=0,
        )

    for copy in copies[4:]:
        copy.wait()
    half_lane = LANE // 2
    results = []
    for parity in range(2):
        parts = [
            jnp.where(lane < half_lane, tile(s), pltpu.roll(tile(s + 2), half_lane, 1))
            for s in range(parity, devices, 4)
        ]
        results.append(dot3(split(spread(parts)), (wh[parity], wl[parity])))
    even, odd = results
    value = jnp.exp(jnp.concatenate([even + odd, even - odd], axis=1))
    side[: HALO * planes, :] = value
    width = HALO * low
    fit = LANE // width
    parts = []
    for s in range(0, devices, fit):
        part = jnp.zeros((SUB, LANE), jnp.float32)
        for i in range(fit):
            moved = pltpu.roll(tile(s + i), (i * width - half_lane) % LANE, 1)
            part = jnp.where((lane >= i * width) & (lane < (i + 1) * width), moved, part)
        parts.append(part)
    whole = dot3(split(spread(parts)), (cwh[...], cwl[...]))
    side[HALO * planes :, short:] = jnp.zeros((HALO * coarse_planes, short), jnp.float32)
    after = 2 * cells + 2 * fourth
    for h in range(HALO):
        top = h * SUB
        part = whole[top : top + coarse_planes, :short] + whole[top + coarse_planes : top + SUB, short:]
        part = jnp.exp(part)
        at = HALO * planes + h * coarse_planes
        side[at : at + coarse_planes, :short] = part
        for edge, fine_at, coarse_at in ((lo, 0, 0), (hi, planes - 2, coarse_planes - 2)):
            for i in range(2):
                at = h * planes + fine_at + i
                to = after + i * HALO + h
                edge[to : to + 1, :] = value[at : at + 1, :]
                to += 2 * HALO
                at = coarse_at + i
                edge[to : to + 1, :short] = part[at : at + 1, :]
                edge[to : to + 1, short:] = jnp.zeros((1, short), jnp.float32)


def source_kernel(planes, pairs, x, out, lo, hi, left, right, held, summed):
    cells = x.shape[0] // planes
    length = x.shape[1]
    half, fourth = cells // 2, cells // 4
    held[...] = dot(x[...], pairs[...])
    for n in range(planes // 2):
        top = 2 * n * cells
        for at in range(0, out.shape[1], LANE):
            lanes = slice(at, at + LANE)
            summed[...] = held[top : top + cells, lanes] + held[top + cells : top + 2 * cells, lanes]
            out[n * half : (n + 1) * half, lanes] = (
                summed[pl.ds(0, half, stride=2), :] + summed[pl.ds(1, half, stride=2), :]
            )
    for edge, plane in ((lo, 0), (hi, planes - 1)):
        edge[:cells, :] = x[plane * cells : (plane + 1) * cells, :].astype(jnp.float32)
        at = plane // 2 * half
        edge[cells:, : length // 2] = out[at : at + fourth, :]
        edge[cells:, length // 2 :] = out[at + fourth : at + half, :]
    for edge, row in ((left, 0), (right, cells - 1)):
        edge[...] = jnp.zeros_like(edge)
        for n in range(planes):
            at = n * cells + (row // SUB * SUB)
            edge[n : n + 1, :] = x[at : at + SUB, :].astype(jnp.float32)[row % SUB : row % SUB + 1]
        for n in range(planes // 2):
            at = n * half + row // 2
            edge[SUB + n : SUB + n + 1, : length // 2] = out[at : at + 1, :]


def beside(parts, ends):
    lane = lax.broadcasted_iota(jnp.int32, parts[0].shape, 1)
    ahead = [pltpu.roll(x, 1, 1) for x in parts]
    behind = [pltpu.roll(x, LANE - 1, 1) for x in parts]
    sums = []
    for i in range(len(parts)):
        left = jnp.where(lane == 0, ahead[i - 1] if i else ends[0], ahead[i])
        right = jnp.where(
            lane == LANE - 1, behind[i + 1] if i + 1 < len(parts) else ends[1], behind[i]
        )
        sums.append(left + right)
    return sums


def first_sweep(ks, fs, us, ws, rs, k_at, f_at, to):
    _, tiles, ext, _ = ks.shape
    for top in range(0, ext, SUB):
        at = slice(top, top + SUB)
        parts = [ks[k_at, x, at, :] for x in range(tiles)]
        for x, both in enumerate(beside(parts, (parts[0], parts[-1]))):
            k = parts[x]
            if top == 0:
                above = pltpu.roll(k, 1, 0)
            else:
                above = ks[k_at, x, top - 1 : top + SUB - 1, :]
            if top == ext - SUB:
                below = pltpu.roll(k, SUB - 1, 0)
            else:
                below = ks[k_at, x, top + 1 : top + SUB + 1, :]
            total = (ks[k_at - 1, x, at, :] + ks[k_at + 1, x, at, :]) + (above + below) + both
            scale = JACOBI_WEIGHT / (6.0 * k + total)
            u = fs[f_at, x, at, :] * (2.0 * scale)
            us[to, x, at, :] = u
            ws[to, x, at, :] = k * u
            rs[to, x, at, :] = scale


def second_sweep(ks, us, ws, rs, k_at, u_at, out, to):
    _, tiles, ext, _ = ks.shape
    for top in range(SUB, ext - SUB, SUB):
        at = slice(top, top + SUB)
        sums = []
        for held in (us, ws):
            parts = [held[u_at, x, at, :] for x in range(tiles)]
            sums.append(
                [
                    both
                    + (held[u_at - 1, x, at, :] + held[u_at + 1, x, at, :])
                    + (
                        held[u_at, x, top - 1 : top + SUB - 1, :]
                        + held[u_at, x, top + 1 : top + SUB + 1, :]
                    )
                    for x, both in enumerate(beside(parts, (0.0, 0.0)))
                ]
            )
        for x in range(tiles):
            coupled = ks[k_at, x, at, :] * sums[0][x] + sums[1][x]
            out[to, top - SUB : top, x * LANE : (x + 1) * LANE] = (2.0 - JACOBI_WEIGHT) * us[
                u_at, x, at, :
            ] + rs[u_at, x, at, :] * coupled


def put_rows(held, to, at, rows):
    for x in range(held.shape[1]):
        held[to, x, at : at + rows.shape[0], :] = rows[:, x * LANE : (x + 1) * LANE]


def fill_sides(flags, ks, at):
    end = ks.shape[2] - SUB

    @pl.when(flags[2] == 1)
    def _():
        for p in at:
            ks[p, :, SUB - 1 : SUB, :] = ks[p, :, SUB : SUB + 1, :]

    @pl.when(flags[3] == 1)
    def _():
        for p in at:
            ks[p, :, end : end + 1, :] = ks[p, :, end - 1 : end, :]


def put_source(fs, to, plane, left, right, row, length):
    put_rows(fs, to, SUB, plane.astype(jnp.float32))
    put_rows(fs, to, SUB - 1, left[row : row + 1, :length])
    put_rows(fs, to, fs.shape[2] - SUB, right[row : row + 1, :length])


def inner_level(fine, flags, kappa, side, f, f_left, f_right, out_hbm, keep_hbm, scratch):
    ks, fs, us, ws, rs, out, sems = scratch
    planes, cells, length = kappa.shape
    end = cells + SUB
    row = 0 if fine else HALO * 2 * planes
    source_row = 0 if fine else SUB
    for p in range(planes):
        put_rows(ks, p, SUB, kappa[p])
        for h, to in enumerate((SUB - 2, SUB - 1, end, end + 1)):
            at = row + h * planes + p
            put_rows(ks, p, to, side[at : at + 1, :length])
    fill_sides(flags, ks, range(planes))
    for p in range(1, planes - 1):
        put_source(fs, p, f[p], f_left, f_right, source_row + p, length)

    def first(p, carry):
        first_sweep(ks, fs, us, ws, rs, p, p, p)
        return carry

    lax.fori_loop(1, planes - 1, first, 0)
    pairs = []
    for group, at in enumerate((1, planes - 3)):
        pairs.append((us.at[at : at + 2], keep_hbm.at[5 * group : 5 * group + 2]))
        pairs.append((ws.at[at : at + 2], keep_hbm.at[5 * group + 2 : 5 * group + 4]))
        own = 1 if group == 0 else planes - 2
        pairs.append((rs.at[own], keep_hbm.at[5 * group + 4]))
    copies = send(pairs, sems, 0)
    if planes > 4:

        def second(p, carry):
            second_sweep(ks, us, ws, rs, p, p, out, p)
            return carry

        lax.fori_loop(2, planes - 2, second, 0)
        at = slice(2, planes - 2)
        copies += send([(out.at[at], out_hbm.at[at])], sems, len(copies))
    return copies


def inner_kernel(
    flags, kappa, coarse, side, f, cf, f_left, f_right, out_hbm, keep_hbm, ckeep_hbm, *scratch
):
    half = len(scratch) // 2
    copies = inner_level(
        True, flags, kappa, side, f, f_left, f_right, out_hbm, keep_hbm, scratch[:half]
    )
    copies += inner_level(
        False, flags, coarse, side, cf, f_left, f_right, None, ckeep_hbm, scratch[half:]
    )
    for copy in copies:
        copy.wait()


def outer_level(
    fine, flags, kappa, f, keep_hbm, k_edges, f_edges, f_left, f_right, out_hbm, scratch
):
    ks, fs, us, ws, rs, out, sems = scratch
    planes, cells, length = kappa.shape
    end = cells + SUB
    half = cells // 2
    fine_cells = cells if fine else 2 * cells
    pairs = []
    for group in range(2):
        at, to = 5 * group, 4 * group + 2 * (1 - group)
        pairs.append((keep_hbm.at[at : at + 2], us.at[to : to + 2]))
        pairs.append((keep_hbm.at[at + 2 : at + 4], ws.at[to : to + 2]))
        pairs.append((keep_hbm.at[at + 4], rs.at[2 if group == 0 else 5]))
    copies = load(pairs, sems)

    def place(held, to, edge, row):
        if fine:
            put_rows(held, to, SUB, edge[row : row + cells, :])
        else:
            put_rows(held, to, SUB, edge[row : row + half, :length])
            put_rows(held, to, SUB + half, edge[row : row + half, length:])

    after = 2 * fine_cells + fine_cells // 2 + (0 if fine else 2 * HALO)
    for group, edge in enumerate(k_edges):
        for i in range(2):
            row = i * cells if fine else 2 * fine_cells + i * half
            to = 4 * group + 2 * group + i
            place(ks, to, edge, row)
            for h, at in enumerate((SUB - 2, SUB - 1, end, end + 1)):
                row = after + i * HALO + h
                put_rows(ks, to, at, edge[row : row + 1, :length])
            own = i if group == 0 else planes - 2 + i
            put_rows(ks, 4 * group + 2 * (1 - group) + i, SUB, kappa[own])
    source_row = 0 if fine else SUB
    for group, edge in enumerate(f_edges):
        place(fs, 3 * group, edge, 0 if fine else fine_cells)
        own = 0 if group == 0 else planes - 1
        put_source(fs, 1 + group, f[own], f_left, f_right, source_row + own, length)
    return copies


def outer_kernel(flags, kappa, coarse, side, f, cf, keep, ckeep, *rest):
    (k_lo, k_hi, f_lo, f_hi, f_left, f_right, _, out, cout), scratch = rest[:9], rest[9:]
    half = len(scratch) // 2
    levels = []
    for fine in (True, False):
        held = scratch[:half] if fine else scratch[half:]
        own, source, kept = (kappa, f, keep) if fine else (coarse, cf, ckeep)
        copies = outer_level(
            fine, flags, own, source, kept, (k_lo, k_hi), (f_lo, f_hi), f_left, f_right, None, held
        )
        levels.append((fine, own, held, copies, out if fine else cout))
    sent = []
    for fine, own, (ks, fs, us, ws, rs, done, sems), copies, target in levels:
        planes, cells, length = own.shape
        end = cells + SUB
        row = 0 if fine else HALO * 2 * planes
        for group in range(2):
            for i in range(2):
                p = i if group == 0 else planes - 2 + i
                to = 4 * group + 2 * (1 - group) + i
                for h, at in enumerate((SUB - 2, SUB - 1, end, end + 1)):
                    here = row + h * planes + p
                    put_rows(ks, to, at, side[here : here + 1, :length])

        @pl.when(flags[0] == 1)
        def _():
            ks[1] = ks[2]

        @pl.when(flags[1] == 1)
        def _():
            ks[6] = ks[5]

        fill_sides(flags, ks, range(8))

        def first(i, carry):
            k_at = jnp.where(i < 2, i + 1, i + 3)
            to = jnp.where(i < 2, i, i + 4)
            first_sweep(ks, fs, us, ws, rs, k_at, i, to)
            return carry

        lax.fori_loop(0, 4, first, 0)
        for copy in copies:
            copy.wait()

        def second(i, carry):
            second_sweep(
                ks, us, ws, rs, i + 2, jnp.where(i < 2, i + 1, i + 3), done, i
            )
            return carry

        lax.fori_loop(0, 4, second, 0)
        sent += send(
            [
                (done.at[0:2], target.at[0:2]),
                (done.at[2:4], target.at[planes - 2 : planes]),
            ],
            sems,
            6,
        )
    for copy in sent:
        copy.wait()


SMEM = pl.BlockSpec(memory_space=pltpu.SMEM)
VMEM = pl.BlockSpec(memory_space=pltpu.VMEM)
AWAY = pl.BlockSpec(memory_space=pltpu.HBM)
ANY = pl.BlockSpec(memory_space=pl.ANY)


def call(kernel, outs, operands, scratch, flops, specs, limit, out_specs=None, aliases=None):
    many = isinstance(outs, (list, tuple))
    written = outs if many else [outs]
    moved = sum(math.prod(x.shape) * x.dtype.itemsize for x in (*operands, *written))
    operands = [
        pltpu.with_memory_space_constraint(x, pltpu.HBM) if spec is AWAY else x
        for x, spec in zip(operands, specs)
    ]
    out_specs = out_specs or [
        VMEM if isinstance(x, jax.ShapeDtypeStruct) else AWAY for x in written
    ]
    return pl.pallas_call(
        kernel,
        out_shape=outs,
        in_specs=specs,
        out_specs=out_specs if many else out_specs[0],
        scratch_shapes=scratch,
        input_output_aliases=aliases or {},
        compiler_params=pltpu.CompilerParams(vmem_limit_bytes=limit * MIB),
        cost_estimate=pl.CostEstimate(flops=flops, bytes_accessed=moved, transcendentals=0),
    )(*operands)


def f32(*shape):
    return jax.ShapeDtypeStruct(shape, jnp.float32)


def room(*arrays):
    return [pltpu.VMEM(x.shape, x.dtype) for x in arrays]


def chain(axis):
    up = [(i, i + 1) for i in range(lax.axis_size(axis) - 1)]
    return up, [(j, i) for i, j in up]


def swap(lo, hi, axis):
    up, down = chain(axis)
    return lax.ppermute(hi, axis, up), lax.ppermute(lo, axis, down)


def level_scratch(shape, k_planes, f_planes, out_planes):
    planes, cells, length = shape
    wide = lambda n: pltpu.VMEM((n, length // LANE, cells + 2 * SUB, LANE), jnp.float32)
    return [
        wide(k_planes),
        wide(f_planes),
        wide(k_planes),
        wide(k_planes),
        wide(k_planes),
        pltpu.VMEM((out_planes, cells, length), jnp.float32),
        pltpu.SemaphoreType.DMA((8,)),
    ]


def fused_body(noise, source):
    rows, groups = lax.axis_size("row"), lax.axis_size(PLANE)
    devices = rows * groups
    planes, cells, length = noise.shape
    first, second = planes * rows, cells * groups
    bf16 = jnp.bfloat16
    held = length // 2 // devices
    js = list(range(held))
    low = held // 2
    me = lax.axis_index(EVERY)
    row_at, group_at = lax.axis_index("row"), lax.axis_index(PLANE)
    flags = jnp.stack(
        [row_at == 0, row_at == rows - 1, group_at == 0, group_at == groups - 1]
    ).astype(jnp.int32)
    norm = FIELD_SCALE * (float(first) * float(second) * float(length)) ** (-0.5)
    flat = (planes * cells, length)

    pieces = 2
    table = [x.reshape(pieces, -1, length) for x in two_parts(forward_third(length, devices, js))]
    table = np.concatenate(table, axis=1)
    shape = (length * SUB, LANE)
    sent = call(
        functools.partial(forward_kernel, planes),
        pltpu.HBM(shape, jnp.float32),
        (table, noise.reshape(flat)),
        room(table)
        + [
            pltpu.VMEM(flat, bf16),
            pltpu.VMEM(shape, jnp.float32),
            pltpu.SemaphoreType.DMA((2 * pieces + planes // 2,)),
        ],
        4 * length * length * planes * cells,
        [AWAY] * 2,
        12,
    )
    sent, source = lax.optimization_barrier((sent, source))
    sent = sent.reshape(devices, 2 * held, SUB, LANE)
    arrived = lax.all_to_all(sent, EVERY, split_axis=0, concat_axis=0, tiled=True)

    pairs = np.zeros((length, length // 2), np.float32)
    pairs[np.arange(length), np.arange(length) // 2] = 0.125
    level = f32(cells + cells // 4, length)
    side = f32(2 * SUB, length)
    coarse_source, *edges = call(
        functools.partial(source_kernel, planes),
        [f32(planes * cells // 4, length // 2), level, level, side, side],
        (pairs.astype(bf16), source.reshape(flat)),
        [
            pltpu.VMEM((planes * cells, length // 2), jnp.float32),
            pltpu.VMEM((cells, LANE), jnp.float32),
        ],
        planes * cells * length * length,
        [VMEM] * 2,
        12,
    )
    coarse_source = coarse_source.reshape(planes // 2, cells // 2, length // 2)
    edges = (*swap(*edges[:2], "row"), *swap(*edges[2:], PLANE))
    arrived, edges, coarse_source = lax.optimization_barrier((arrived, edges, coarse_source))

    constants = (
        two_parts(second_table(second))
        + two_parts(forward_first(first))
        + two_parts(inverse_first(first))
        + two_parts(inverse_first_coarse(first // 2, rows))
        + two_parts(second_coarse(second // 2, groups))
        + two_parts(second_table(second).transpose(0, 2, 1))
    )
    tiles = 2 * held + low // 2 + 1
    modes = (me + devices * np.array(js)).astype(jnp.float32)
    weight = jnp.where(modes == 0.0, norm, 2.0 * norm).astype(jnp.float32)
    scale = jnp.stack([DECAY * modes * modes, weight], axis=1)
    block = (2, 2 * held * first, second // 2)
    shape = (devices, tiles, SUB, LANE)
    out = call(
        functools.partial(middle_kernel, (first, second, rows, groups, held, low)),
        pltpu.HBM(shape, jnp.float32),
        (scale, arrived, *constants),
        room(*constants)
        + [
            pltpu.VMEM(shape, jnp.float32),
            pltpu.SemaphoreType.DMA((len(constants),)),
            pltpu.VMEM(block, bf16),
            pltpu.VMEM(block, bf16),
            pltpu.VMEM(block, jnp.float32),
            pltpu.VMEM(block, bf16),
            pltpu.VMEM(block, bf16),
            pltpu.VMEM((low // 2 * first, second), bf16),
            pltpu.VMEM((low // 2 * first, second), bf16),
        ],
        6 * 2 * 2 * held * first * second * (second + 2 * first),
        [SMEM, VMEM] + [AWAY] * len(constants),
        22,
    )
    got = lax.all_to_all(out, EVERY, split_axis=0, concat_axis=0, tiled=True)

    third = inverse_third(length, devices, js)
    constants = (
        two_parts(third)
        + two_parts(third_coarse(length // 2, devices, js[:low]))
        + two_parts(np.repeat(third, HALO, axis=1))
        + two_parts(third_coarse_halo(length // 2, devices, js[:low]))
    )
    edge = f32(2 * cells + cells // 2 + 4 * HALO, length)
    side = f32(HALO * planes * 3 // 2, length)
    fine, coarse, lo, hi, side = call(
        functools.partial(back_kernel, (devices, 2 * held, low, tiles, planes, length)),
        [f32(*flat), f32(planes * cells // 4, length // 2), edge, edge, side],
        (got.reshape(devices * tiles * SUB, LANE), *constants),
        room(*constants)
        + [pltpu.VMEM((2, planes * cells, devices * held), bf16)] * 2
        + [pltpu.VMEM((planes // 2 * LANE, devices * low), bf16)] * 2
        + [pltpu.SemaphoreType.DMA((8,))],
        6 * planes * cells * length * length,
        [VMEM] + [AWAY] * 8,
        18,
    )
    fine, coarse = fine.reshape(source.shape), coarse.reshape(coarse_source.shape)
    k_lo, k_hi = swap(lo, hi, "row")
    f_lo, f_hi, f_left, f_right = edges
    kept = lambda x: f32(10, x.shape[2] // LANE, x.shape[1] + 2 * SUB, LANE)
    own = (flags, fine, coarse, side, source, coarse_source)
    inner, keep, coarse_keep = call(
        inner_kernel,
        [pltpu.HBM(fine.shape, jnp.float32), kept(fine), kept(coarse)],
        (*own, f_left, f_right),
        level_scratch(fine.shape, planes, planes, planes)
        + level_scratch(coarse.shape, planes // 2, planes // 2, planes // 2),
        30 * fine.size,
        [SMEM] + [VMEM] * 7,
        22,
        [AWAY, ANY, ANY],
    )
    return call(
        outer_kernel,
        [pltpu.HBM(fine.shape, jnp.float32), pltpu.HBM(coarse.shape, jnp.float32)],
        (*own, keep, coarse_keep, k_lo, k_hi, f_lo, f_hi, f_left, f_right, inner),
        level_scratch(fine.shape, 8, 4, 4) + level_scratch(coarse.shape, 8, 4, 4),
        30 * fine.size,
        [SMEM] + [VMEM] * 5 + [ANY] * 2 + [VMEM] * 6 + [AWAY],
        22,
        [AWAY] * 2,
        {14: 0},
    )


NEIGHBOUR_STEPS = ((1, 0, 0), (-1, 0, 0), (0, 1, 0), (0, -1, 0), (0, 0, 1), (0, 0, -1))


def padded(x, sides, width):
    for axis, dim in sides:
        peers, length = (lax.axis_size(axis), x.shape[dim])
        up = [(i, (i + 1) % peers) for i in range(peers - 1)]
        down = [(j, i) for i, j in up]
        last = lax.slice_in_dim(x, length - width, length, axis=dim)
        leading = lax.slice_in_dim(x, 0, width, axis=dim)
        before = lax.ppermute(last, axis, up)
        after = lax.ppermute(leading, axis, down)
        x = jnp.concatenate([before, x, after], axis=dim)
    return x


def signed_modes(index, length):
    return jnp.where(index < length // 2, index, index - length).astype(jnp.float32)


def amplitude(first_modes, second_modes, third_modes, first_edge, second_edge, third_edge):
    squared = first_modes * first_modes + second_modes * second_modes + third_modes * third_modes
    value = FIELD_SCALE / (1.0 + (2.0 * math.pi * CORRELATION) ** 2 * squared)
    edge = (
        (jnp.abs(first_modes) == first_edge)
        | (jnp.abs(second_modes) == second_edge)
        | (jnp.abs(third_modes) == third_edge)
    )
    return jnp.where(edge, 0.0, value)


def phase_table(count_rows, count_cols, modulus, sign):
    left_index = jnp.arange(count_rows, dtype=jnp.int32)[:, None]
    right_index = jnp.arange(count_cols, dtype=jnp.int32)[None, :]
    angle = 2.0 * math.pi / modulus * (left_index * right_index % modulus).astype(jnp.float32)
    return (jnp.cos(angle), sign * jnp.sin(angle))


def split_length(length):
    outer_len = 2 ** ((length.bit_length() - 1) // 2)
    return (outer_len, length // outer_len)


def real_form(form, left_value, right_value):
    return jnp.einsum(form, left_value, right_value, precision=lax.Precision.HIGHEST)


def complex_form(form, left_real, left_imag, right_real, right_imag):
    real_part = real_form(form, left_real, right_real) - real_form(form, left_imag, right_imag)
    imag_part = real_form(form, left_real, right_imag) + real_form(form, left_imag, right_real)
    return (real_part, imag_part)


def merge_pair(values, out_form, first_letter):
    merge_at = out_form.index(first_letter)
    out_dims = list(values.shape)
    merged = (
        out_dims[:merge_at]
        + [out_dims[merge_at] * out_dims[merge_at + 1]]
        + out_dims[merge_at + 2 :]
    )
    return values.reshape(merged)


def forward_axis(real_part, imag_part, lead_form, out_form, kept_modes):
    length = real_part.shape[-1]
    outer_len, inner_len = split_length(length)
    split_shape = real_part.shape[:-1] + (outer_len, inner_len)
    outer_real, outer_imag = phase_table(outer_len, outer_len, outer_len, -1.0)
    twist_real, twist_imag = phase_table(outer_len, inner_len, length, -1.0)
    inner_real, inner_imag = phase_table(inner_len, kept_modes // outer_len, inner_len, -1.0)
    first_form = lead_form + "ab,ai->" + lead_form + "ib"
    split_real = real_part.reshape(split_shape)
    if imag_part is None:
        section_real = real_form(first_form, split_real, outer_real)
        section_imag = real_form(first_form, split_real, outer_imag)
    else:
        section_real, section_imag = complex_form(
            first_form, split_real, imag_part.reshape(split_shape), outer_real, outer_imag
        )
    turned_real = section_real * twist_real - section_imag * twist_imag
    turned_imag = section_real * twist_imag + section_imag * twist_real
    result_real, result_imag = complex_form(
        lead_form + "ib,bj->" + out_form, turned_real, turned_imag, inner_real, inner_imag
    )
    return (merge_pair(result_real, out_form, "j"), merge_pair(result_imag, out_form, "j"))


def inverse_axis(real_part, imag_part, length, lead_form, out_form, real_only):
    kept_modes = real_part.shape[-1]
    outer_len, inner_len = split_length(length)
    split_shape = real_part.shape[:-1] + (kept_modes // outer_len, outer_len)
    inner_real, inner_imag = phase_table(kept_modes // outer_len, inner_len, inner_len, 1.0)
    twist_real, twist_imag = phase_table(outer_len, inner_len, length, 1.0)
    outer_real, outer_imag = phase_table(outer_len, outer_len, outer_len, 1.0)
    section_real, section_imag = complex_form(
        lead_form + "ji,jb->" + lead_form + "ib",
        real_part.reshape(split_shape),
        imag_part.reshape(split_shape),
        inner_real,
        inner_imag,
    )
    turned_real = section_real * twist_real - section_imag * twist_imag
    turned_imag = section_real * twist_imag + section_imag * twist_real
    second_form = lead_form + "ib,ia->" + out_form
    if real_only:
        result = real_form(second_form, turned_real, outer_real) - real_form(
            second_form, turned_imag, outer_imag
        )
        return merge_pair(result, out_form, "a")
    result_real, result_imag = complex_form(
        second_form, turned_real, turned_imag, outer_real, outer_imag
    )
    return (merge_pair(result_real, out_form, "a"), merge_pair(result_imag, out_form, "a"))


def low_band(values, half_coarse, fine_len):
    return jnp.concatenate(
        [values[:, :, :half_coarse], values[:, :, fine_len - half_coarse :]], axis=2
    )


def window(values, margin, offset):
    return values[
        margin + offset[0] : values.shape[0] - margin + offset[0],
        margin + offset[1] : values.shape[1] - margin + offset[1],
        margin + offset[2] : values.shape[2] - margin + offset[2],
    ]


def face_weight(center, beside):
    return jnp.where(beside > 0.0, 0.5 * (center + beside), center)


def smooth_twice(kappa, source):
    no_shift = (0, 0, 0)
    center = window(kappa, 1, no_shift)
    faces = [face_weight(center, window(kappa, 1, offset)) for offset in NEIGHBOUR_STEPS]
    diagonal = faces[0] + faces[1] + faces[2] + faces[3] + faces[4] + faces[5]
    guarded = jnp.where(center > 0.0, diagonal, 1.0)
    first_sweep = JACOBI_WEIGHT * window(source, 1, no_shift) / guarded
    inner_first = window(first_sweep, 1, no_shift)
    inner_diagonal = window(diagonal, 1, no_shift)
    coupled = jnp.zeros_like(inner_first)
    for face_value, offset in zip(faces, NEIGHBOUR_STEPS):
        coupled = coupled + window(face_value, 1, no_shift) * window(first_sweep, 1, offset)
    residual = window(source, 2, no_shift) - inner_diagonal * inner_first + coupled
    return inner_first + JACOBI_WEIGHT * residual / inner_diagonal


def pad_depth(values):
    return jnp.pad(values, ((0, 0), (0, 0), (2, 2)))


def plain_body(noise, source):
    row_at = lax.axis_index("row")
    group_at = lax.axis_index(("level", "col"))
    fine_field = noise.astype(jnp.float32)
    fine_len = fine_field.shape[-1]
    coarse_len = fine_len // 2
    half_coarse = coarse_len // 2
    kept_modes = fine_len // 2
    real_part, imag_part = forward_axis(fine_field, None, "pq", "pjiq", kept_modes)
    real_part, imag_part = (
        lax.all_to_all(real_part, ("level", "col"), split_axis=1, concat_axis=2, tiled=True),
        lax.all_to_all(imag_part, ("level", "col"), split_axis=1, concat_axis=2, tiled=True),
    )
    real_part, imag_part = forward_axis(real_part, imag_part, "pq", "jiqp", fine_len)
    real_part, imag_part = (
        lax.all_to_all(real_part, "row", split_axis=0, concat_axis=2, tiled=True),
        lax.all_to_all(imag_part, "row", split_axis=0, concat_axis=2, tiled=True),
    )
    slab_len = real_part.shape[-1]
    coarse_slab = slab_len // 2
    half_slab = coarse_slab // 2
    real_part, imag_part = forward_axis(real_part, imag_part, "pq", "pqji", slab_len)
    second_count = real_part.shape[0]
    third_count = real_part.shape[1]
    wave_second = signed_modes(
        row_at * second_count + jnp.arange(second_count, dtype=jnp.int32), fine_len
    )[:, None, None]
    third_index = group_at * third_count + jnp.arange(third_count, dtype=jnp.int32)
    wave_third = signed_modes(third_index, fine_len)[None, :, None]
    spread = 2.0
    mirror_weight = jnp.where(third_index == 0, 1.0, spread).astype(jnp.float32)[None, :, None]
    norm_factor = (float(slab_len) * float(fine_len) * float(fine_len)) ** (-0.5)
    wave_first = signed_modes(jnp.arange(slab_len, dtype=jnp.int32), slab_len)[None, None, :]
    fine_scale = (
        amplitude(
            wave_second, wave_third, wave_first, fine_len / 2.0, fine_len / 2.0, slab_len / 2.0
        )
        * mirror_weight
        * norm_factor
    )
    coarse_first = signed_modes(jnp.arange(coarse_slab, dtype=jnp.int32), coarse_slab)[
        None, None, :
    ]
    coarse_scale = (
        amplitude(
            wave_second,
            wave_third,
            coarse_first,
            coarse_len / 2.0,
            coarse_len / 2.0,
            coarse_slab / 2.0,
        )
        * mirror_weight
        * norm_factor
    )
    coarse_real = low_band(real_part, half_slab, slab_len) * coarse_scale
    coarse_imag = low_band(imag_part, half_slab, slab_len) * coarse_scale
    fine_real, fine_imag = inverse_axis(
        real_part * fine_scale, imag_part * fine_scale, slab_len, "pq", "abqp", False
    )
    coarse_real, coarse_imag = inverse_axis(
        coarse_real, coarse_imag, coarse_slab, "pq", "abqp", False
    )
    fine_real, fine_imag, coarse_real, coarse_imag = (
        lax.all_to_all(fine_real, "row", split_axis=0, concat_axis=2, tiled=True),
        lax.all_to_all(fine_imag, "row", split_axis=0, concat_axis=2, tiled=True),
        lax.all_to_all(coarse_real, "row", split_axis=0, concat_axis=2, tiled=True),
        lax.all_to_all(coarse_imag, "row", split_axis=0, concat_axis=2, tiled=True),
    )
    coarse_real = low_band(coarse_real, half_coarse, fine_len)
    coarse_imag = low_band(coarse_imag, half_coarse, fine_len)
    fine_real, fine_imag = inverse_axis(fine_real, fine_imag, fine_len, "pq", "pabq", False)
    coarse_real, coarse_imag = inverse_axis(
        coarse_real, coarse_imag, coarse_len, "pq", "pabq", False
    )
    fine_real, fine_imag, coarse_real, coarse_imag = (
        lax.all_to_all(fine_real, ("level", "col"), split_axis=1, concat_axis=2, tiled=True),
        lax.all_to_all(fine_imag, ("level", "col"), split_axis=1, concat_axis=2, tiled=True),
        lax.all_to_all(coarse_real, ("level", "col"), split_axis=1, concat_axis=2, tiled=True),
        lax.all_to_all(coarse_imag, ("level", "col"), split_axis=1, concat_axis=2, tiled=True),
    )
    coarse_real = coarse_real[:, :, :half_coarse]
    coarse_imag = coarse_imag[:, :, :half_coarse]
    fine_log = inverse_axis(fine_real, fine_imag, fine_len, "pq", "pqab", True)
    coarse_log = inverse_axis(coarse_real, coarse_imag, coarse_len, "pq", "pqab", True)
    fine_kappa = jnp.exp(fine_log)
    coarse_kappa = jnp.exp(coarse_log)
    fine_source = source.astype(jnp.float32)
    coarse_rows = coarse_log.shape[0]
    coarse_cols = coarse_log.shape[1]
    coarse_source = fine_source.reshape(coarse_rows, 2, coarse_cols, 2, coarse_len, 2).mean(
        axis=(1, 3, 5)
    )
    fine_kappa, fine_source, coarse_kappa, coarse_source = (
        padded(fine_kappa, (("row", 0), (("level", "col"), 1)), 2),
        padded(fine_source, (("row", 0), (("level", "col"), 1)), 2),
        padded(coarse_kappa, (("row", 0), (("level", "col"), 1)), 2),
        padded(coarse_source, (("row", 0), (("level", "col"), 1)), 2),
    )
    fine_pressure = smooth_twice(pad_depth(fine_kappa), pad_depth(fine_source))
    coarse_pressure = smooth_twice(pad_depth(coarse_kappa), pad_depth(coarse_source))
    return (fine_pressure, coarse_pressure)


def body(noise, source):
    planes, cells, length = noise.shape
    devices = lax.axis_size(EVERY)
    held = length // 2 // devices
    if planes == SUB and cells == LANE and held % 4 == 0 and held > 0:
        return fused_body(noise, source)
    return plain_body(noise, source)


def solution(mesh):
    return jax.shard_map(
        body,
        mesh=mesh,
        in_specs=(P("row", ("level", "col"), None), P("row", ("level", "col"), None)),
        out_specs=(P("row", ("level", "col"), None), P("row", ("level", "col"), None)),
        check_vma=False,
    )
```

```python
import functools
import math

import jax
import jax.numpy as jnp
import numpy as np
from jax import lax
from jax.experimental import pallas as pl
from jax.experimental.pallas import tpu as pltpu
from jax.sharding import PartitionSpec as P

JACOBI_WEIGHT = 2.0 / 3.0
CORRELATION = 0.2
FIELD_SCALE = 0.3
DECAY = (2.0 * math.pi * CORRELATION) ** 2
EVERY = ("row", "level", "col")
PLANE = ("level", "col")
MIB = 1 << 20
SUB, LANE = 8, 128
HALO = 4


def two_parts(matrix):
    high = matrix.astype(jnp.bfloat16)
    low = (matrix - high.astype(np.float64)).astype(jnp.bfloat16)
    return high, low


def angles(rows, cols, length):
    return 2.0 * np.pi * (np.outer(rows, cols) % length) / length


def third_modes(devices, js):
    return np.array([[d + devices * j for j in js] for d in range(devices)])


def forward_third(length, devices, js):
    theta = angles(third_modes(devices, js).reshape(-1), np.arange(length), length)
    return np.stack([np.cos(theta), -np.sin(theta)], axis=1).reshape(-1, length)


def inverse_third(length, devices, js):
    modes = third_modes(devices, js).reshape(devices // 2, 2, len(js)).transpose(1, 0, 2)
    theta = 2.0 * np.pi * (modes[..., None] * np.arange(length // 2) % length) / length
    both = np.stack([np.cos(theta), -np.sin(theta)], axis=3)
    return both.reshape(2, -1, length // 2)


def second_modes(length):
    return np.arange(length // 2).reshape(-1, 2).T


def second_table(length):
    theta = second_modes(length)[:, None, :] * np.arange(length // 2)[None, :, None]
    theta = 2.0 * np.pi * (theta % length) / length
    return np.concatenate([np.cos(theta), np.sin(theta)], axis=2)


def forward_first(length):
    theta = angles(np.arange(length), np.arange(length), length)
    cos, sin = np.cos(theta), np.sin(theta)
    return np.block([[cos, sin], [-sin, cos]])


def inverse_first(length):
    theta = angles(np.arange(length), np.arange(length), length)
    cos, sin = np.cos(theta), np.sin(theta)
    cos[:, length // 2] = 0.0
    sin[:, length // 2] = 0.0
    return np.block([[cos, -sin], [sin, cos]])


def inverse_first_coarse(length, rows):
    full = inverse_first(length)
    value = full.reshape(2, rows, length // rows, 2 * length)
    turned = np.concatenate([-full[length:], full[:length]]).reshape(value.shape)
    order = lambda x: x.transpose(1, 0, 2, 3).reshape(2 * length, 2 * length)
    return np.concatenate([order(value), order(turned)])


def second_coarse(length, groups):
    theta = angles(second_modes(length).reshape(-1), np.arange(length), length)
    table = np.concatenate([np.cos(theta), np.sin(theta)])
    span = length // groups
    out = np.zeros((2, length, groups, 2, span))
    for pair in range(2):
        out[pair, :, :, pair, :] = table.reshape(length, groups, span)
    return out.reshape(2 * length, 2 * length)


def third_coarse(length, devices, js):
    modes = third_modes(devices, js).reshape(devices, len(js) // 2, 2)
    theta = 2.0 * np.pi * (modes[..., None] * np.arange(length) % length) / length
    both = np.stack([np.cos(theta), -np.sin(theta)])
    return both.transpose(0, 2, 1, 3, 4).reshape(2 * (len(js) // 2) * devices, 2 * length)


def third_coarse_halo(length, devices, js):
    modes = np.repeat(third_modes(devices, js).reshape(-1), HALO)
    theta = angles(modes, np.arange(length), length)
    return np.concatenate([np.cos(theta), -np.sin(theta)], axis=1)


def split(x):
    high = x.astype(jnp.bfloat16)
    return high, (x - high.astype(jnp.float32)).astype(jnp.bfloat16)


def dot(a, b):
    return lax.dot_general(a, b, (((1,), (0,)), ((), ())), preferred_element_type=jnp.float32)


def dot_t(a, b):
    return lax.dot_general(a, b, (((1,), (1,)), ((), ())), preferred_element_type=jnp.float32)


def dot3(a, b):
    (ah, al), (bh, bl) = a, b
    return dot(ah, bh) + (dot(ah, bl) + dot(al, bh))


def load(pairs, sems):
    copies = [pltpu.make_async_copy(a, b, sems.at[i]) for i, (a, b) in enumerate(pairs)]
    for copy in copies:
        copy.start()
    return copies


def send(pairs, sems, first):
    copies = [pltpu.make_async_copy(a, b, sems.at[first + i]) for i, (a, b) in enumerate(pairs)]
    for copy in copies:
        copy.start()
    return copies


def forward_kernel(planes, d_hbm, x_hbm, out_hbm, d, x, out, sems):
    pieces, rows = d.shape[0], d.shape[1] // 2
    parts = [slice(p * LANE, (p + 2) * LANE) for p in range(0, planes, 2)]
    pairs = [(x_hbm.at[at, :], x.at[at, :]) for at in parts]
    copies = load([(d_hbm.at[0], d.at[0])] + pairs + [(d_hbm.at[i], d.at[i]) for i in range(1, pieces)], sems)
    sent = []
    copies[0].wait()
    for piece in range(pieces):
        if piece:
            copies[len(parts) + piece].wait()
        for i, at in enumerate(parts):
            if piece == 0:
                copies[i + 1].wait()
            value = dot_t(d[piece], x[at, :])
            value = value[:rows] + value[rows:]
            for h in range(2):
                out[pl.ds(piece * rows * SUB + 2 * i + h, rows, stride=SUB), :] = value[
                    :, h * LANE : (h + 1) * LANE
                ]
        tall = slice(piece * rows * SUB, (piece + 1) * rows * SUB)
        sent += send([(out.at[tall, :], out_hbm.at[tall, :])], sems, len(copies) + piece)
    for copy in sent:
        copy.wait()


def middle_kernel(sizes, scale, b, *rest):
    (first, second, rows, groups, js, low) = sizes
    count = 12
    away, out_hbm, near, rest = rest[:count], rest[count], rest[count + 1 : 2 * count + 1], rest[2 * count + 1 :]
    out, sems, zh, zl, y, oh, ol, qh, ql = rest
    copies = load(list(zip(away, near)), sems)
    csh, csl, fh, fl, ih, il, ich, icl, cch, ccl, ch, cl = near
    q_count = 2 * js
    half, quarter = second // 2, second // 4
    for q in range(q_count):
        for g in range(groups // 2):
            for r in range(0, rows, 2):
                at = r * groups + g
                near_half = jnp.concatenate([b[at, q], b[at + groups, q]], axis=0)
                at += groups // 2
                far_half = jnp.concatenate([b[at, q], b[at + groups, q]], axis=0)
                at = slice(q * first + r * SUB, q * first + (r + 2) * SUB)
                lanes = slice(g * LANE, (g + 1) * LANE)
                zh[0, at, lanes], zl[0, at, lanes] = split(near_half + far_half)
                zh[1, at, lanes], zl[1, at, lanes] = split(near_half - far_half)
    for copy in copies[:8]:
        copy.wait()
    wide = 8 * first
    for top in range(0, q_count * first, wide):
        at = slice(top, top + wide)
        for parity in range(2):
            y[parity, at, :] = dot3(
                (zh[parity, at, :], zl[parity, at, :]), (csh[parity], csl[parity])
            )
    mode0 = lax.broadcasted_iota(jnp.int32, (first, second), 0)
    mode0 = jnp.where(mode0 < first // 2, mode0, mode0 - first).astype(jnp.float32)
    lane = lax.broadcasted_iota(jnp.int32, (first, second), 1)
    mode1 = jnp.where(lane < half, lane, lane - half)
    mode1 = jnp.where(mode1 < quarter, 2 * mode1, 2 * (mode1 - quarter) + 1).astype(jnp.float32)
    base = 1.0 + DECAY * (mode0 * mode0 + mode1 * mode1)
    for j in range(js):
        top = j * 2 * first
        re, im = slice(top, top + first), slice(top + first, top + 2 * first)
        cos, sin = slice(0, quarter), slice(quarter, half)
        whole = lambda part, lanes: jnp.concatenate(
            [y[0, part, lanes], y[1, part, lanes]], axis=1
        )
        rc, rs, ic, isn = whole(re, cos), whole(re, sin), whole(im, cos), whole(im, sin)
        wave = jnp.concatenate(
            [
                jnp.concatenate([rc + isn, rc - isn], axis=1),
                jnp.concatenate([ic - rs, ic + rs], axis=1),
            ],
            axis=0,
        )
        spectrum = dot3((fh[...], fl[...]), split(wave))
        amp = jnp.where(lane == half, 0.0, scale[j, 1] / (base + scale[j, 0]))
        scaled = spectrum * jnp.concatenate([amp, amp], axis=0)
        field = dot3((ih[...], il[...]), split(scaled))
        plus, minus = field[:, :half], field[:, half:]
        even, odd = plus + minus, plus - minus
        odd = jnp.concatenate([-odd[first:], odd[:first]], axis=0)
        at = slice(top, top + 2 * first)
        for parity, lanes in enumerate((cos, sin)):
            operand = jnp.concatenate([even[:, lanes], odd[:, lanes]], axis=1)
            oh[parity, at, :], ol[parity, at, :] = split(operand)
        if j < low:
            keep = first // 4
            kept = [
                scaled[at : at + keep, :]
                for at in (0, first - keep, first, 2 * first - keep)
            ]
            band = jnp.concatenate(kept, axis=0)
            low_lane = lax.broadcasted_iota(jnp.int32, (first, quarter), 1) < quarter // 2
            pieces = []
            for at in (0, half):
                upper = pltpu.roll(band[:, at + quarter : at + half], quarter // 2, 1)
                pieces.append(jnp.where(low_lane, band[:, at : at + quarter], upper))
            band = jnp.concatenate(pieces, axis=1)
            field = dot3((ich[...], icl[...]), split(band))
            value, turned = field[:first], field[first:]
            operand = jnp.concatenate(
                [
                    value[:, :quarter] + value[:, quarter:],
                    turned[:, :quarter] - turned[:, quarter:],
                ],
                axis=1,
            )
            at = slice(j // 2 * first, (j // 2 + 1) * first)
            lanes = slice(j % 2 * half, (j % 2 + 1) * half)
            qh[at, lanes], ql[at, lanes] = split(operand)
    for copy in copies[8:]:
        copy.wait()
    copies = []
    wide = 4 * first
    lane = lax.broadcasted_iota(jnp.int32, (SUB, LANE), 1)
    extra = q_count + low // 2

    def leave(start, stop):
        at = slice(start, stop)
        copies.extend(send([(out.at[:, at], out_hbm.at[:, at])], sems, len(copies)))

    def give(value, start):
        tiles = value.shape[0] // first
        for q in range(tiles):
            for r in range(rows):
                for g in range(groups):
                    at = q * first + r * SUB
                    out[r * groups + g, start + q] = value[
                        at : at + SUB, g * LANE : (g + 1) * LANE
                    ]
        leave(start, start + tiles)

    def halo_columns(value, start, held):
        tiles = value.shape[0] // first
        for r in range(rows):
            for g in range(groups):
                total = held[r, g]
                left = max(g - 1, 0) * LANE
                right = min(g + 1, groups - 1) * LANE
                for q in range(tiles):
                    at = slice(q * first + r * SUB, q * first + (r + 1) * SUB)
                    both = jnp.where(
                        lane < LANE // 2,
                        value[at, right : right + LANE],
                        value[at, left : left + LANE],
                    )
                    to = HALO * (start + q)
                    both = pltpu.roll(both, (to + 2) % LANE, 1)
                    total = jnp.where((lane >= to) & (lane < to + HALO), both, total)
                held[r, g] = total

    def coarse_columns(value, held):
        half_lane = LANE // 2
        for j in range(low):
            for r in range(rows):
                at = slice(j // 2 * first + r * SUB, j // 2 * first + (r + 1) * SUB)
                shift = HALO * j + 2 - j % 2 * half_lane
                to = half_lane + HALO * j
                for g in range(groups):
                    left = max(g - 1, 0) * LANE
                    right = min(g + 1, groups - 1) * LANE
                    left = pltpu.roll(value[at, left : left + LANE], shift % LANE, 1)
                    right = pltpu.roll(
                        value[at, right : right + LANE], (shift + half_lane) % LANE, 1
                    )
                    total = jnp.where((lane >= to) & (lane < to + 2), left, held[r, g])
                    held[r, g] = jnp.where(
                        (lane >= to + 2) & (lane < to + HALO), right, total
                    )

    columns = {
        (r, g): jnp.zeros((SUB, LANE), jnp.float32) for r in range(rows) for g in range(groups)
    }
    coarse = dot3((qh[...], ql[...]), (cch[...], ccl[...]))
    give(coarse, q_count)
    coarse_columns(coarse, columns)
    for top in range(0, q_count * first, wide):
        at = slice(top, top + wide)
        even, odd = (
            dot3((oh[parity, at, :], ol[parity, at, :]), (ch[parity], cl[parity]))
            for parity in range(2)
        )
        value = jnp.concatenate([even + odd, even - odd], axis=1)
        give(value, top // first)
        halo_columns(value, top // first, columns)
    for (r, g), total in columns.items():
        out[r * groups + g, extra] = total
    leave(extra, extra + 1)
    for copy in copies:
        copy.wait()


def back_kernel(sizes, b, *rest):
    (devices, q_count, low, tiles, planes, length) = sizes
    away, (own, lo_hbm, hi_hbm), rest = rest[:8], rest[8:11], rest[11:]
    near, (lo, hi, lh, ll, mh, ml, sems) = rest[:8], rest[8:]
    copies = load(list(zip(away, near)), sems)
    eh, el, ceh, cel, wh, wl, cwh, cwl = near
    cells, short = LANE, length // 2
    halves, coarse_planes = low // 2, planes // 2
    half, fourth = cells // 2, cells // 4
    ext, coarse_ext = cells + 2 * SUB, half + 2 * SUB
    fine_rows = 2 * (length // LANE) * ext
    ends = ((lo, lambda n, count: 1 - n), (hi, lambda n, count: n - count + 2))

    def put(edge, slot, start, height, at, value):
        for x in range(value.shape[1] // LANE):
            to = start + (slot * (value.shape[1] // LANE) + x) * height + at
            edge[to : to + value.shape[0], :] = value[:, x * LANE : (x + 1) * LANE]

    for n in (0, 1, planes - 2, planes - 1, *range(2, planes - 2)):
        for parity in range(2):
            rows = jnp.concatenate(
                [
                    b[pl.ds(s * tiles * SUB + n, q_count, stride=SUB), :]
                    for s in range(parity, devices, 2)
                ],
                axis=0,
            )
            at = slice(n * LANE, (n + 1) * LANE)
            lh[parity, at, :], ll[parity, at, :] = split(jnp.transpose(rows))
    for n in range(coarse_planes):
        rows = jnp.concatenate(
            [
                b[pl.ds((q_count + h) * SUB + c * coarse_planes + n, devices, stride=tiles * SUB), :]
                for c in range(2)
                for h in range(halves)
            ],
            axis=0,
        )
        at = slice(n * LANE, (n + 1) * LANE)
        mh[at, :], ml[at, :] = split(jnp.transpose(rows))

    for copy in copies[:4]:
        copy.wait()

    def pair(p):
        at = slice(p * cells, (p + 2) * cells)
        even, odd = (
            dot3((lh[parity, at, :], ll[parity, at, :]), (eh[parity], el[parity]))
            for parity in range(2)
        )
        value = jnp.exp(jnp.concatenate([even + odd, even - odd], axis=1))
        own[at, :] = value
        return value

    for (edge, slot), p in zip(ends, (0, planes - 2)):
        value = pair(p)
        for n in range(2):
            put(edge, slot(p + n, planes), 0, ext, SUB, value[n * cells : (n + 1) * cells])
    value = dot3((mh[...], ml[...]), (ceh[...], cel[...]))
    for n in range(coarse_planes):
        top = n * cells
        part = value[top : top + half, :short] + value[top + half : top + cells, short:]
        part = jnp.exp(part)
        at = planes * cells + n * fourth
        own[at : at + fourth, :short] = part[:fourth]
        own[at : at + fourth, short:] = part[fourth:]
        for edge, slot in ends:
            if 0 <= slot(n, coarse_planes) < 2:
                put(edge, slot(n, coarse_planes), fine_rows, coarse_ext, SUB, part)

    lane = lax.broadcasted_iota(jnp.int32, (SUB, LANE), 1)
    tile = lambda s: b[(s * tiles + tiles - 1) * SUB : (s + 1) * tiles * SUB, :]

    def spread(parts):
        return jnp.concatenate(
            [
                jnp.concatenate(
                    [jnp.where(lane % HALO == h, part, 0.0) for part in parts], axis=1
                )
                for h in range(HALO)
            ],
            axis=0,
        )

    for copy in copies[4:]:
        copy.wait()
    half_lane = LANE // 2
    results = []
    for parity in range(2):
        parts = [
            jnp.where(lane < half_lane, tile(s), pltpu.roll(tile(s + 2), half_lane, 1))
            for s in range(parity, devices, 4)
        ]
        results.append(dot3(split(spread(parts)), (wh[parity], wl[parity])))
    even, odd = results
    value = jnp.exp(jnp.concatenate([even + odd, even - odd], axis=1))
    side = planes * cells + coarse_planes * fourth
    own[side : side + HALO * planes, :] = value
    width = HALO * low
    fit = LANE // width
    parts = []
    for s in range(0, devices, fit):
        part = jnp.zeros((SUB, LANE), jnp.float32)
        for i in range(fit):
            moved = pltpu.roll(tile(s + i), (i * width - half_lane) % LANE, 1)
            part = jnp.where((lane >= i * width) & (lane < (i + 1) * width), moved, part)
        parts.append(part)
    whole = dot3(split(spread(parts)), (cwh[...], cwl[...]))
    side += HALO * planes
    own[side:, short:] = jnp.zeros((HALO * coarse_planes, short), jnp.float32)
    for h in range(HALO):
        top = h * SUB
        part = whole[top : top + coarse_planes, :short] + whole[top + coarse_planes : top + SUB, short:]
        part = jnp.exp(part)
        at = side + h * coarse_planes
        own[at : at + coarse_planes, :short] = part
        for edge, slot in ends:
            for n in range(planes):
                if 0 <= slot(n, planes) < 2:
                    at = h * planes + n
                    put(
                        edge, slot(n, planes), 0, ext, halo_row(h, cells), value[at : at + 1, :]
                    )
            for n in range(coarse_planes):
                if 0 <= slot(n, coarse_planes) < 2:
                    put(
                        edge,
                        slot(n, coarse_planes),
                        fine_rows,
                        coarse_ext,
                        halo_row(h, half),
                        part[n : n + 1, :],
                    )
    sent = send([(lo, lo_hbm), (hi, hi_hbm)], sems, 0)
    for p in range(2, planes - 2, 2):
        pair(p)
    for copy in sent:
        copy.wait()


def halo_row(h, cells):
    return SUB - 2 + h if h < 2 else SUB + cells + h - 2


def source_kernel(planes, pairs, x, out, lo, hi, left, right, held, summed):
    cells = x.shape[0] // planes
    length = x.shape[1]
    half, fourth = cells // 2, cells // 4
    held[...] = dot(x[...], pairs[...])
    for n in range(planes // 2):
        top = 2 * n * cells
        for at in range(0, out.shape[1], LANE):
            lanes = slice(at, at + LANE)
            summed[...] = held[top : top + cells, lanes] + held[top + cells : top + 2 * cells, lanes]
            out[n * half : (n + 1) * half, lanes] = (
                summed[pl.ds(0, half, stride=2), :] + summed[pl.ds(1, half, stride=2), :]
            )
    for edge, plane in ((lo, 0), (hi, planes - 1)):
        edge[:cells, :] = x[plane * cells : (plane + 1) * cells, :].astype(jnp.float32)
        at = plane // 2 * half
        edge[cells:, : length // 2] = out[at : at + fourth, :]
        edge[cells:, length // 2 :] = out[at + fourth : at + half, :]
    for edge, row in ((left, 0), (right, cells - 1)):
        edge[...] = jnp.zeros_like(edge)
        for n in range(planes):
            at = n * cells + (row // SUB * SUB)
            edge[n : n + 1, :] = x[at : at + SUB, :].astype(jnp.float32)[row % SUB : row % SUB + 1]
        for n in range(planes // 2):
            at = n * half + row // 2
            edge[SUB + n : SUB + n + 1, : length // 2] = out[at : at + 1, :]


def beside(parts, ends):
    lane = lax.broadcasted_iota(jnp.int32, parts[0].shape, 1)
    ahead = [pltpu.roll(x, 1, 1) for x in parts]
    behind = [pltpu.roll(x, LANE - 1, 1) for x in parts]
    sums = []
    for i in range(len(parts)):
        left = jnp.where(lane == 0, ahead[i - 1] if i else ends[0], ahead[i])
        right = jnp.where(
            lane == LANE - 1, behind[i + 1] if i + 1 < len(parts) else ends[1], behind[i]
        )
        sums.append(left + right)
    return sums


def first_sweep(tiles, ext, mid, lower, upper, f, store):
    for top in range(0, ext, SUB):
        end = top + SUB
        parts = [mid(x, top, end) for x in range(tiles)]
        for x, both in enumerate(beside(parts, (parts[0], parts[-1]))):
            k = parts[x]
            above = pltpu.roll(k, 1, 0) if top == 0 else mid(x, top - 1, end - 1)
            below = pltpu.roll(k, SUB - 1, 0) if end == ext else mid(x, top + 1, end + 1)
            total = (lower(x, top, end) + upper(x, top, end)) + (above + below) + both
            scale = JACOBI_WEIGHT / (6.0 * k + total)
            u = f(x, top, end) * (2.0 * scale)
            store(x, top, end, u, k * u, scale)


def second_sweep(tiles, ext, k, u, w, r, store):
    for top in range(SUB, ext - SUB, SUB):
        end = top + SUB
        sums = []
        for lower, mid, upper in (u, w):
            parts = [mid(x, top, end) for x in range(tiles)]
            sums.append(
                [
                    both
                    + (lower(x, top, end) + upper(x, top, end))
                    + (mid(x, top - 1, end - 1) + mid(x, top + 1, end + 1))
                    for x, both in enumerate(beside(parts, (0.0, 0.0)))
                ]
            )
        for x in range(tiles):
            coupled = k(x, top, end) * sums[0][x] + sums[1][x]
            value = (2.0 - JACOBI_WEIGHT) * u[1](x, top, end) + r(x, top, end) * coupled
            store(x, top, end, value)


def plane_of(held, *at):
    return lambda x, top, end: held[(*at, x, slice(top, end), slice(None))]


def put_rows(held, to, at, rows):
    for x in range(held.shape[1]):
        held[to, x, at : at + rows.shape[0], :] = rows[:, x * LANE : (x + 1) * LANE]


def repeat_sides(flags, held, at):
    end = held.shape[-2] - SUB

    @pl.when(flags[2] == 1)
    def _():
        for p in at:
            held[(*p, slice(None), slice(SUB - 1, SUB))] = held[(*p, slice(None), slice(SUB, SUB + 1))]

    @pl.when(flags[3] == 1)
    def _():
        for p in at:
            held[(*p, slice(None), slice(end, end + 1))] = held[
                (*p, slice(None), slice(end - 1, end))
            ]


def put_block(fine, held, to, source, row, cells, length):
    if fine:
        put_rows(held, to, SUB, source[row : row + cells, :])
    else:
        half = cells // 2
        put_rows(held, to, SUB, source[row : row + half, :length])
        put_rows(held, to, SUB + half, source[row : row + half, length:])


def inner_level(fine, sizes, flags, own, f, edges, sides, out_hbm, keeps, scratch):
    ks, fs, us, ws, rs, out, sems = scratch
    keep_k, keep_f, keep_u, keep_w, keep_r = keeps
    planes, cells, length = sizes
    ext, tiles = cells + 2 * SUB, length // LANE
    fine_planes, fine_cells = (planes, cells) if fine else (2 * planes, 2 * cells)
    block = 0 if fine else fine_planes * fine_cells
    height = cells if fine else cells // 2
    side = fine_planes * fine_cells * 9 // 8 + (0 if fine else HALO * fine_planes)
    for p in range(planes):
        put_block(fine, ks, p, own, block + p * height, cells, length)
        for h in range(HALO):
            at = side + h * planes + p
            put_rows(ks, p, halo_row(h, cells), own[at : at + 1, :length])
    repeat_sides(flags, ks, [(p,) for p in range(planes)])
    source_row = 0 if fine else SUB
    for p in range(planes):
        put_rows(fs, p + 1, SUB, f[p].astype(jnp.float32))
        for held, row in zip(sides, (SUB - 1, SUB + cells)):
            at = source_row + p
            put_rows(fs, p + 1, row, held[at : at + 1, :length])
    for edge, to in zip(edges, (0, planes + 1)):
        put_block(fine, fs, to, edge, 0 if fine else fine_cells, cells, length)
    ends = ((0, 1), (planes - 1, planes - 2))
    pairs = []
    for group, at in enumerate(ends):
        pairs += [(ks.at[p], keep_k.at[group, i]) for i, p in enumerate(at)]
        around = (0, 1) if group == 0 else (planes + 1, planes)
        pairs += [(fs.at[p], keep_f.at[group, i]) for i, p in enumerate(around)]
    copies = send(pairs, sems, 0)

    def first(p, carry):
        def store(x, top, end, u, w, r):
            at = (p, x, slice(top, end))
            us[at], ws[at], rs[at] = u, w, r

        near = [plane_of(ks, p + i) for i in (0, -1, 1)]
        first_sweep(tiles, ext, *near, plane_of(fs, p + 1), store)
        return carry

    lax.fori_loop(1, planes - 1, first, 0)
    pairs = []
    for group, at in enumerate(((1, 2), (planes - 2, planes - 3))):
        pairs += [(us.at[p], keep_u.at[group, i]) for i, p in enumerate(at)]
        pairs += [(ws.at[p], keep_w.at[group, i]) for i, p in enumerate(at)]
        pairs.append((rs.at[at[0]], keep_r.at[group]))
    copies += send(pairs, sems, len(copies))
    if planes > 4:

        def second(p, carry):
            def store(x, top, end, value):
                out[p, top - SUB : end - SUB, x * LANE : (x + 1) * LANE] = value

            u, w = ([plane_of(held, p + i) for i in (-1, 0, 1)] for held in (us, ws))
            second_sweep(tiles, ext, plane_of(ks, p), u, w, plane_of(rs, p), store)
            return carry

        lax.fori_loop(2, planes - 2, second, 0)
        at = slice(2, planes - 2)
        copies += send([(out.at[at], out_hbm.at[at])], sems, len(copies))
    return copies


def inner_kernel(sizes, flags, own, f, cf, *rest):
    away, out_hbm, rest = rest[:4], rest[4], rest[5:]
    keeps, coarse_keeps, rest = rest[:5], rest[5:10], rest[10:]
    near, sems, scratch = rest[:4], rest[4], rest[5:]
    for copy in load(list(zip(away, near)), sems):
        copy.wait()
    edges, sides = near[:2], near[2:]
    planes, cells, length = sizes
    coarse = tuple(n // 2 for n in sizes)
    half = len(scratch) // 2
    copies = inner_level(True, sizes, flags, own, f, edges, sides, out_hbm, keeps, scratch[:half])
    copies += inner_level(
        False, coarse, flags, own, cf, edges, sides, None, coarse_keeps, scratch[half:]
    )
    for copy in copies:
        copy.wait()


def outer_kernel(sizes, flags, *rest):
    keeps, coarse_keeps, (k_lo, k_hi, _, out, coarse_out), rest = (
        rest[:5],
        rest[5:10],
        rest[10:15],
        rest[15:],
    )
    scratch = (rest[:6], rest[6:])
    levels = (sizes, tuple(n // 2 for n in sizes))
    waits, start = [], 0
    for (planes, cells, length), (halo, *_, sems) in zip(levels, scratch):
        count = halo.shape[1]
        at = slice(start, start + count)
        waits.append(load([(k_lo.at[at, :], halo.at[0]), (k_hi.at[at, :], halo.at[1])], sems))
        start += count
    sent = []
    for size, held, kept, copies, target in zip(
        levels, scratch, (keeps, coarse_keeps), waits, (out, coarse_out)
    ):
        planes, cells, length = size
        ext, tiles = cells + 2 * SUB, length // LANE
        halo, us, ws, rs, done, sems = held
        keep_k, keep_f, keep_u, keep_w, keep_r = kept
        for copy in copies:
            copy.wait()
        for group in range(2):

            @pl.when(flags[group] == 1)
            def _():
                for x in range(tiles):
                    at = (tiles + x) * ext
                    halo[group, at : at + ext, :] = keep_k[group, 0, x]

        for flag, to, source in ((2, SUB - 1, SUB), (3, ext - SUB, ext - SUB - 1)):

            @pl.when(flags[flag] == 1)
            def _():
                for group in range(2):
                    for x in range(tiles):
                        at = (tiles + x) * ext
                        halo[group, at + to : at + to + 1, :] = halo[
                            group, at + source : at + source + 1, :
                        ]

        def both_ends(group, carry):
            def halo_plane(slot):
                def get(x, top, end):
                    at = (slot * tiles + x) * ext
                    return halo[group, at + top : at + end, :]

                return get

            own = [plane_of(keep_k, group, i) for i in range(2)]
            new_u = [plane_of(us, group, i) for i in range(2)]
            new_w = [plane_of(ws, group, i) for i in range(2)]
            old_u = [plane_of(keep_u, group, i) for i in range(2)]
            old_w = [plane_of(keep_w, group, i) for i in range(2)]
            around = ((halo_plane(1), halo_plane(0), own[0]), (own[0], halo_plane(1), own[1]))
            for i, near in enumerate(around):

                def store(x, top, end, u, w, r):
                    at = (group, i, x, slice(top, end))
                    us[at], ws[at] = u, w
                    if i == 1:
                        rs[group, x, top:end, :] = r

                first_sweep(tiles, ext, *near, plane_of(keep_f, group, i), store)
            u = (new_u[0], new_u[1], old_u[0], old_u[1])
            w = (new_w[0], new_w[1], old_w[0], old_w[1])
            for i, r in enumerate((rs, keep_r)):

                def store(x, top, end, value):
                    done[group, i, top - SUB : end - SUB, x * LANE : (x + 1) * LANE] = value

                second_sweep(
                    tiles, ext, own[i], u[i : i + 3], w[i : i + 3], plane_of(r, group), store
                )
            return carry

        lax.fori_loop(0, 2, both_ends, 0)
        pairs = [
            (done.at[group, i], target.at[p])
            for group, at in enumerate(((0, 1), (planes - 1, planes - 2)))
            for i, p in enumerate(at)
        ]
        sent += send(pairs, sems, 0)
    for copy in sent:
        copy.wait()


SMEM = pl.BlockSpec(memory_space=pltpu.SMEM)
VMEM = pl.BlockSpec(memory_space=pltpu.VMEM)
AWAY = pl.BlockSpec(memory_space=pltpu.HBM)
ANY = pl.BlockSpec(memory_space=pl.ANY)


def call(kernel, outs, operands, scratch, flops, specs, limit, out_specs=None, aliases=None):
    many = isinstance(outs, (list, tuple))
    written = outs if many else [outs]
    moved = sum(math.prod(x.shape) * x.dtype.itemsize for x in (*operands, *written))
    operands = [
        pltpu.with_memory_space_constraint(x, pltpu.HBM) if spec is AWAY else x
        for x, spec in zip(operands, specs)
    ]
    out_specs = out_specs or [
        VMEM if isinstance(x, jax.ShapeDtypeStruct) else AWAY for x in written
    ]
    return pl.pallas_call(
        kernel,
        out_shape=outs,
        in_specs=specs,
        out_specs=out_specs if many else out_specs[0],
        scratch_shapes=scratch,
        input_output_aliases=aliases or {},
        compiler_params=pltpu.CompilerParams(vmem_limit_bytes=limit * MIB),
        cost_estimate=pl.CostEstimate(flops=flops, bytes_accessed=moved, transcendentals=0),
    )(*operands)


def f32(*shape):
    return jax.ShapeDtypeStruct(shape, jnp.float32)


def room(*arrays):
    return [pltpu.VMEM(x.shape, x.dtype) for x in arrays]


def chain(axis):
    up = [(i, i + 1) for i in range(lax.axis_size(axis) - 1)]
    return up, [(j, i) for i, j in up]


def swap(lo, hi, axis):
    up, down = chain(axis)
    return lax.ppermute(hi, axis, up), lax.ppermute(lo, axis, down)


def held_planes(size, *count):
    planes, cells, length = size
    return f32(*count, length // LANE, cells + 2 * SUB, LANE)


def inner_scratch(size):
    planes = size[0]
    return room(
        held_planes(size, planes),
        held_planes(size, planes + 2),
        *[held_planes(size, planes)] * 3,
        f32(*size),
    ) + [pltpu.SemaphoreType.DMA((20,))]


def outer_scratch(size):
    planes, cells, length = size
    return room(
        f32(2, 2 * (length // LANE) * (cells + 2 * SUB), LANE),
        held_planes(size, 2, 2),
        held_planes(size, 2, 2),
        held_planes(size, 2),
        f32(2, 2, cells, length),
    ) + [pltpu.SemaphoreType.DMA((4,))]


def fused_body(noise, source):
    rows, groups = lax.axis_size("row"), lax.axis_size(PLANE)
    devices = rows * groups
    planes, cells, length = noise.shape
    first, second = planes * rows, cells * groups
    bf16 = jnp.bfloat16
    held = length // 2 // devices
    js = list(range(held))
    low = held // 2
    me = lax.axis_index(EVERY)
    row_at, group_at = lax.axis_index("row"), lax.axis_index(PLANE)
    flags = jnp.stack(
        [row_at == 0, row_at == rows - 1, group_at == 0, group_at == groups - 1]
    ).astype(jnp.int32)
    norm = FIELD_SCALE * (float(first) * float(second) * float(length)) ** (-0.5)
    flat = (planes * cells, length)

    pieces = 2
    table = [x.reshape(pieces, -1, length) for x in two_parts(forward_third(length, devices, js))]
    table = np.concatenate(table, axis=1)
    shape = (length * SUB, LANE)
    sent = call(
        functools.partial(forward_kernel, planes),
        pltpu.HBM(shape, jnp.float32),
        (table, noise.reshape(flat)),
        room(table)
        + [
            pltpu.VMEM(flat, bf16),
            pltpu.VMEM(shape, jnp.float32),
            pltpu.SemaphoreType.DMA((2 * pieces + planes // 2,)),
        ],
        4 * length * length * planes * cells,
        [AWAY] * 2,
        12,
    )
    sent, source = lax.optimization_barrier((sent, source))
    sent = sent.reshape(devices, 2 * held, SUB, LANE)
    arrived = lax.all_to_all(sent, EVERY, split_axis=0, concat_axis=0, tiled=True)

    pairs = np.zeros((length, length // 2), np.float32)
    pairs[np.arange(length), np.arange(length) // 2] = 0.125
    level = f32(cells + cells // 4, length)
    side = f32(2 * SUB, length)
    coarse_source, *edges = call(
        functools.partial(source_kernel, planes),
        [f32(planes * cells // 4, length // 2), level, level, side, side],
        (pairs.astype(bf16), source.reshape(flat)),
        [
            pltpu.VMEM((planes * cells, length // 2), jnp.float32),
            pltpu.VMEM((cells, LANE), jnp.float32),
        ],
        planes * cells * length * length,
        [VMEM] * 2,
        12,
    )
    coarse_source = coarse_source.reshape(planes // 2, cells // 2, length // 2)
    edges = (*swap(*edges[:2], "row"), *swap(*edges[2:], PLANE))
    arrived, edges, coarse_source = lax.optimization_barrier((arrived, edges, coarse_source))

    constants = (
        two_parts(second_table(second))
        + two_parts(forward_first(first))
        + two_parts(inverse_first(first))
        + two_parts(inverse_first_coarse(first // 2, rows))
        + two_parts(second_coarse(second // 2, groups))
        + two_parts(second_table(second).transpose(0, 2, 1))
    )
    tiles = 2 * held + low // 2 + 1
    modes = (me + devices * np.array(js)).astype(jnp.float32)
    weight = jnp.where(modes == 0.0, norm, 2.0 * norm).astype(jnp.float32)
    scale = jnp.stack([DECAY * modes * modes, weight], axis=1)
    block = (2, 2 * held * first, second // 2)
    shape = (devices, tiles, SUB, LANE)
    out = call(
        functools.partial(middle_kernel, (first, second, rows, groups, held, low)),
        pltpu.HBM(shape, jnp.float32),
        (scale, arrived, *constants),
        room(*constants)
        + [
            pltpu.VMEM(shape, jnp.float32),
            pltpu.SemaphoreType.DMA((len(constants),)),
            pltpu.VMEM(block, bf16),
            pltpu.VMEM(block, bf16),
            pltpu.VMEM(block, jnp.float32),
            pltpu.VMEM(block, bf16),
            pltpu.VMEM(block, bf16),
            pltpu.VMEM((low // 2 * first, second), bf16),
            pltpu.VMEM((low // 2 * first, second), bf16),
        ],
        6 * 2 * 2 * held * first * second * (second + 2 * first),
        [SMEM, VMEM] + [AWAY] * len(constants),
        22,
    )
    got = lax.all_to_all(out, EVERY, split_axis=0, concat_axis=0, tiled=True)

    third = inverse_third(length, devices, js)
    constants = (
        two_parts(third)
        + two_parts(third_coarse(length // 2, devices, js[:low]))
        + two_parts(np.repeat(third, HALO, axis=1))
        + two_parts(third_coarse_halo(length // 2, devices, js[:low]))
    )
    size, coarse_size = noise.shape, coarse_source.shape
    ext, coarse_ext = cells + 2 * SUB, cells // 2 + 2 * SUB
    edge = (2 * (length // LANE * ext + length // 2 // LANE * coarse_ext), LANE)
    own, lo, hi = call(
        functools.partial(back_kernel, (devices, 2 * held, low, tiles, planes, length)),
        [
            f32(planes * cells * 9 // 8 + HALO * planes * 3 // 2, length),
            pltpu.HBM(edge, jnp.float32),
            pltpu.HBM(edge, jnp.float32),
        ],
        (got.reshape(devices * tiles * SUB, LANE), *constants),
        room(*constants, f32(*edge), f32(*edge))
        + [pltpu.VMEM((2, planes * cells, devices * held), bf16)] * 2
        + [pltpu.VMEM((planes // 2 * LANE, devices * low), bf16)] * 2
        + [pltpu.SemaphoreType.DMA((8,))],
        6 * planes * cells * length * length,
        [VMEM] + [AWAY] * 8,
        20,
    )
    k_lo, k_hi = swap(lo, hi, "row")
    kept = [
        x
        for s in (size, coarse_size)
        for x in [held_planes(s, 2, 2)] * 4 + [held_planes(s, 2)]
    ]
    inner, *kept = call(
        functools.partial(inner_kernel, size),
        [pltpu.HBM(size, jnp.float32), *kept],
        (flags, own, source, coarse_source, *edges),
        room(*edges)
        + [pltpu.SemaphoreType.DMA((4,))]
        + inner_scratch(size)
        + inner_scratch(coarse_size),
        30 * source.size,
        [SMEM] + [VMEM] * 3 + [ANY] * 4,
        26,
    )
    return call(
        functools.partial(outer_kernel, size),
        [pltpu.HBM(size, jnp.float32), pltpu.HBM(coarse_size, jnp.float32)],
        (flags, *kept, k_lo, k_hi, inner),
        outer_scratch(size) + outer_scratch(coarse_size),
        30 * source.size,
        [SMEM] + [VMEM] * 10 + [ANY] * 2 + [AWAY],
        20,
        None,
        {13: 0},
    )


NEIGHBOUR_STEPS = ((1, 0, 0), (-1, 0, 0), (0, 1, 0), (0, -1, 0), (0, 0, 1), (0, 0, -1))


def padded(x, sides, width):
    for axis, dim in sides:
        peers, length = (lax.axis_size(axis), x.shape[dim])
        up = [(i, (i + 1) % peers) for i in range(peers - 1)]
        down = [(j, i) for i, j in up]
        last = lax.slice_in_dim(x, length - width, length, axis=dim)
        leading = lax.slice_in_dim(x, 0, width, axis=dim)
        before = lax.ppermute(last, axis, up)
        after = lax.ppermute(leading, axis, down)
        x = jnp.concatenate([before, x, after], axis=dim)
    return x


def signed_modes(index, length):
    return jnp.where(index < length // 2, index, index - length).astype(jnp.float32)


def amplitude(first_modes, second_modes, third_modes, first_edge, second_edge, third_edge):
    squared = first_modes * first_modes + second_modes * second_modes + third_modes * third_modes
    value = FIELD_SCALE / (1.0 + (2.0 * math.pi * CORRELATION) ** 2 * squared)
    edge = (
        (jnp.abs(first_modes) == first_edge)
        | (jnp.abs(second_modes) == second_edge)
        | (jnp.abs(third_modes) == third_edge)
    )
    return jnp.where(edge, 0.0, value)


def phase_table(count_rows, count_cols, modulus, sign):
    left_index = jnp.arange(count_rows, dtype=jnp.int32)[:, None]
    right_index = jnp.arange(count_cols, dtype=jnp.int32)[None, :]
    angle = 2.0 * math.pi / modulus * (left_index * right_index % modulus).astype(jnp.float32)
    return (jnp.cos(angle), sign * jnp.sin(angle))


def split_length(length):
    outer_len = 2 ** ((length.bit_length() - 1) // 2)
    return (outer_len, length // outer_len)


def real_form(form, left_value, right_value):
    return jnp.einsum(form, left_value, right_value, precision=lax.Precision.HIGHEST)


def complex_form(form, left_real, left_imag, right_real, right_imag):
    real_part = real_form(form, left_real, right_real) - real_form(form, left_imag, right_imag)
    imag_part = real_form(form, left_real, right_imag) + real_form(form, left_imag, right_real)
    return (real_part, imag_part)


def merge_pair(values, out_form, first_letter):
    merge_at = out_form.index(first_letter)
    out_dims = list(values.shape)
    merged = (
        out_dims[:merge_at]
        + [out_dims[merge_at] * out_dims[merge_at + 1]]
        + out_dims[merge_at + 2 :]
    )
    return values.reshape(merged)


def forward_axis(real_part, imag_part, lead_form, out_form, kept_modes):
    length = real_part.shape[-1]
    outer_len, inner_len = split_length(length)
    split_shape = real_part.shape[:-1] + (outer_len, inner_len)
    outer_real, outer_imag = phase_table(outer_len, outer_len, outer_len, -1.0)
    twist_real, twist_imag = phase_table(outer_len, inner_len, length, -1.0)
    inner_real, inner_imag = phase_table(inner_len, kept_modes // outer_len, inner_len, -1.0)
    first_form = lead_form + "ab,ai->" + lead_form + "ib"
    split_real = real_part.reshape(split_shape)
    if imag_part is None:
        section_real = real_form(first_form, split_real, outer_real)
        section_imag = real_form(first_form, split_real, outer_imag)
    else:
        section_real, section_imag = complex_form(
            first_form, split_real, imag_part.reshape(split_shape), outer_real, outer_imag
        )
    turned_real = section_real * twist_real - section_imag * twist_imag
    turned_imag = section_real * twist_imag + section_imag * twist_real
    result_real, result_imag = complex_form(
        lead_form + "ib,bj->" + out_form, turned_real, turned_imag, inner_real, inner_imag
    )
    return (merge_pair(result_real, out_form, "j"), merge_pair(result_imag, out_form, "j"))


def inverse_axis(real_part, imag_part, length, lead_form, out_form, real_only):
    kept_modes = real_part.shape[-1]
    outer_len, inner_len = split_length(length)
    split_shape = real_part.shape[:-1] + (kept_modes // outer_len, outer_len)
    inner_real, inner_imag = phase_table(kept_modes // outer_len, inner_len, inner_len, 1.0)
    twist_real, twist_imag = phase_table(outer_len, inner_len, length, 1.0)
    outer_real, outer_imag = phase_table(outer_len, outer_len, outer_len, 1.0)
    section_real, section_imag = complex_form(
        lead_form + "ji,jb->" + lead_form + "ib",
        real_part.reshape(split_shape),
        imag_part.reshape(split_shape),
        inner_real,
        inner_imag,
    )
    turned_real = section_real * twist_real - section_imag * twist_imag
    turned_imag = section_real * twist_imag + section_imag * twist_real
    second_form = lead_form + "ib,ia->" + out_form
    if real_only:
        result = real_form(second_form, turned_real, outer_real) - real_form(
            second_form, turned_imag, outer_imag
        )
        return merge_pair(result, out_form, "a")
    result_real, result_imag = complex_form(
        second_form, turned_real, turned_imag, outer_real, outer_imag
    )
    return (merge_pair(result_real, out_form, "a"), merge_pair(result_imag, out_form, "a"))


def low_band(values, half_coarse, fine_len):
    return jnp.concatenate(
        [values[:, :, :half_coarse], values[:, :, fine_len - half_coarse :]], axis=2
    )


def window(values, margin, offset):
    return values[
        margin + offset[0] : values.shape[0] - margin + offset[0],
        margin + offset[1] : values.shape[1] - margin + offset[1],
        margin + offset[2] : values.shape[2] - margin + offset[2],
    ]


def face_weight(center, beside):
    return jnp.where(beside > 0.0, 0.5 * (center + beside), center)


def smooth_twice(kappa, source):
    no_shift = (0, 0, 0)
    center = window(kappa, 1, no_shift)
    faces = [face_weight(center, window(kappa, 1, offset)) for offset in NEIGHBOUR_STEPS]
    diagonal = faces[0] + faces[1] + faces[2] + faces[3] + faces[4] + faces[5]
    guarded = jnp.where(center > 0.0, diagonal, 1.0)
    first_sweep = JACOBI_WEIGHT * window(source, 1, no_shift) / guarded
    inner_first = window(first_sweep, 1, no_shift)
    inner_diagonal = window(diagonal, 1, no_shift)
    coupled = jnp.zeros_like(inner_first)
    for face_value, offset in zip(faces, NEIGHBOUR_STEPS):
        coupled = coupled + window(face_value, 1, no_shift) * window(first_sweep, 1, offset)
    residual = window(source, 2, no_shift) - inner_diagonal * inner_first + coupled
    return inner_first + JACOBI_WEIGHT * residual / inner_diagonal


def pad_depth(values):
    return jnp.pad(values, ((0, 0), (0, 0), (2, 2)))


def plain_body(noise, source):
    row_at = lax.axis_index("row")
    group_at = lax.axis_index(("level", "col"))
    fine_field = noise.astype(jnp.float32)
    fine_len = fine_field.shape[-1]
    coarse_len = fine_len // 2
    half_coarse = coarse_len // 2
    kept_modes = fine_len // 2
    real_part, imag_part = forward_axis(fine_field, None, "pq", "pjiq", kept_modes)
    real_part, imag_part = (
        lax.all_to_all(real_part, ("level", "col"), split_axis=1, concat_axis=2, tiled=True),
        lax.all_to_all(imag_part, ("level", "col"), split_axis=1, concat_axis=2, tiled=True),
    )
    real_part, imag_part = forward_axis(real_part, imag_part, "pq", "jiqp", fine_len)
    real_part, imag_part = (
        lax.all_to_all(real_part, "row", split_axis=0, concat_axis=2, tiled=True),
        lax.all_to_all(imag_part, "row", split_axis=0, concat_axis=2, tiled=True),
    )
    slab_len = real_part.shape[-1]
    coarse_slab = slab_len // 2
    half_slab = coarse_slab // 2
    real_part, imag_part = forward_axis(real_part, imag_part, "pq", "pqji", slab_len)
    second_count = real_part.shape[0]
    third_count = real_part.shape[1]
    wave_second = signed_modes(
        row_at * second_count + jnp.arange(second_count, dtype=jnp.int32), fine_len
    )[:, None, None]
    third_index = group_at * third_count + jnp.arange(third_count, dtype=jnp.int32)
    wave_third = signed_modes(third_index, fine_len)[None, :, None]
    spread = 2.0
    mirror_weight = jnp.where(third_index == 0, 1.0, spread).astype(jnp.float32)[None, :, None]
    norm_factor = (float(slab_len) * float(fine_len) * float(fine_len)) ** (-0.5)
    wave_first = signed_modes(jnp.arange(slab_len, dtype=jnp.int32), slab_len)[None, None, :]
    fine_scale = (
        amplitude(
            wave_second, wave_third, wave_first, fine_len / 2.0, fine_len / 2.0, slab_len / 2.0
        )
        * mirror_weight
        * norm_factor
    )
    coarse_first = signed_modes(jnp.arange(coarse_slab, dtype=jnp.int32), coarse_slab)[
        None, None, :
    ]
    coarse_scale = (
        amplitude(
            wave_second,
            wave_third,
            coarse_first,
            coarse_len / 2.0,
            coarse_len / 2.0,
            coarse_slab / 2.0,
        )
        * mirror_weight
        * norm_factor
    )
    coarse_real = low_band(real_part, half_slab, slab_len) * coarse_scale
    coarse_imag = low_band(imag_part, half_slab, slab_len) * coarse_scale
    fine_real, fine_imag = inverse_axis(
        real_part * fine_scale, imag_part * fine_scale, slab_len, "pq", "abqp", False
    )
    coarse_real, coarse_imag = inverse_axis(
        coarse_real, coarse_imag, coarse_slab, "pq", "abqp", False
    )
    fine_real, fine_imag, coarse_real, coarse_imag = (
        lax.all_to_all(fine_real, "row", split_axis=0, concat_axis=2, tiled=True),
        lax.all_to_all(fine_imag, "row", split_axis=0, concat_axis=2, tiled=True),
        lax.all_to_all(coarse_real, "row", split_axis=0, concat_axis=2, tiled=True),
        lax.all_to_all(coarse_imag, "row", split_axis=0, concat_axis=2, tiled=True),
    )
    coarse_real = low_band(coarse_real, half_coarse, fine_len)
    coarse_imag = low_band(coarse_imag, half_coarse, fine_len)
    fine_real, fine_imag = inverse_axis(fine_real, fine_imag, fine_len, "pq", "pabq", False)
    coarse_real, coarse_imag = inverse_axis(
        coarse_real, coarse_imag, coarse_len, "pq", "pabq", False
    )
    fine_real, fine_imag, coarse_real, coarse_imag = (
        lax.all_to_all(fine_real, ("level", "col"), split_axis=1, concat_axis=2, tiled=True),
        lax.all_to_all(fine_imag, ("level", "col"), split_axis=1, concat_axis=2, tiled=True),
        lax.all_to_all(coarse_real, ("level", "col"), split_axis=1, concat_axis=2, tiled=True),
        lax.all_to_all(coarse_imag, ("level", "col"), split_axis=1, concat_axis=2, tiled=True),
    )
    coarse_real = coarse_real[:, :, :half_coarse]
    coarse_imag = coarse_imag[:, :, :half_coarse]
    fine_log = inverse_axis(fine_real, fine_imag, fine_len, "pq", "pqab", True)
    coarse_log = inverse_axis(coarse_real, coarse_imag, coarse_len, "pq", "pqab", True)
    fine_kappa = jnp.exp(fine_log)
    coarse_kappa = jnp.exp(coarse_log)
    fine_source = source.astype(jnp.float32)
    coarse_rows = coarse_log.shape[0]
    coarse_cols = coarse_log.shape[1]
    coarse_source = fine_source.reshape(coarse_rows, 2, coarse_cols, 2, coarse_len, 2).mean(
        axis=(1, 3, 5)
    )
    fine_kappa, fine_source, coarse_kappa, coarse_source = (
        padded(fine_kappa, (("row", 0), (("level", "col"), 1)), 2),
        padded(fine_source, (("row", 0), (("level", "col"), 1)), 2),
        padded(coarse_kappa, (("row", 0), (("level", "col"), 1)), 2),
        padded(coarse_source, (("row", 0), (("level", "col"), 1)), 2),
    )
    fine_pressure = smooth_twice(pad_depth(fine_kappa), pad_depth(fine_source))
    coarse_pressure = smooth_twice(pad_depth(coarse_kappa), pad_depth(coarse_source))
    return (fine_pressure, coarse_pressure)


def body(noise, source):
    planes, cells, length = noise.shape
    devices = lax.axis_size(EVERY)
    held = length // 2 // devices
    if planes == SUB and cells == LANE and held % 4 == 0 and held > 0:
        return fused_body(noise, source)
    return plain_body(noise, source)


def solution(mesh):
    return jax.shard_map(
        body,
        mesh=mesh,
        in_specs=(P("row", ("level", "col"), None), P("row", ("level", "col"), None)),
        out_specs=(P("row", ("level", "col"), None), P("row", ("level", "col"), None)),
        check_vma=False,
    )
```

```python
import functools
import math

import jax
import jax.numpy as jnp
import numpy as np
from jax import lax
from jax.experimental import pallas as pl
from jax.experimental.pallas import tpu as pltpu
from jax.sharding import PartitionSpec as P

JACOBI_WEIGHT = 2.0 / 3.0
CORRELATION = 0.2
FIELD_SCALE = 0.3
DECAY = (2.0 * math.pi * CORRELATION) ** 2
EVERY = ("row", "level", "col")
PLANE = ("level", "col")
MIB = 1 << 20
SUB, LANE = 8, 128
HALO = 4


def two_parts(matrix):
    high = matrix.astype(jnp.bfloat16)
    low = (matrix - high.astype(np.float64)).astype(jnp.bfloat16)
    return high, low


def angles(rows, cols, length):
    return 2.0 * np.pi * (np.outer(rows, cols) % length) / length


def third_modes(devices, js):
    return np.array([[d + devices * j for j in js] for d in range(devices)])


def forward_third(length, devices, js):
    theta = angles(third_modes(devices, js).reshape(-1), np.arange(length), length)
    return np.stack([np.cos(theta), -np.sin(theta)], axis=1).reshape(-1, length)


def inverse_third(length, devices, js):
    modes = third_modes(devices, js).reshape(devices // 2, 2, len(js)).transpose(1, 0, 2)
    theta = 2.0 * np.pi * (modes[..., None] * np.arange(length // 2) % length) / length
    both = np.stack([np.cos(theta), -np.sin(theta)], axis=3)
    return both.reshape(2, -1, length // 2)


def second_modes(length):
    return np.arange(length // 2).reshape(-1, 2).T


def second_table(length):
    theta = second_modes(length)[:, None, :] * np.arange(length // 2)[None, :, None]
    theta = 2.0 * np.pi * (theta % length) / length
    return np.concatenate([np.cos(theta), np.sin(theta)], axis=2)


def forward_first(length):
    theta = angles(np.arange(length), np.arange(length), length)
    cos, sin = np.cos(theta), np.sin(theta)
    return np.block([[cos, sin], [-sin, cos]])


def inverse_first(length):
    theta = angles(np.arange(length), np.arange(length), length)
    cos, sin = np.cos(theta), np.sin(theta)
    cos[:, length // 2] = 0.0
    sin[:, length // 2] = 0.0
    return np.block([[cos, -sin], [sin, cos]])


def inverse_first_coarse(length, rows):
    full = inverse_first(length)
    value = full.reshape(2, rows, length // rows, 2 * length)
    turned = np.concatenate([-full[length:], full[:length]]).reshape(value.shape)
    order = lambda x: x.transpose(1, 0, 2, 3).reshape(2 * length, 2 * length)
    return np.concatenate([order(value), order(turned)])


def second_coarse(length, groups):
    theta = angles(second_modes(length).reshape(-1), np.arange(length), length)
    table = np.concatenate([np.cos(theta), np.sin(theta)])
    span = length // groups
    out = np.zeros((2, length, groups, 2, span))
    for pair in range(2):
        out[pair, :, :, pair, :] = table.reshape(length, groups, span)
    return out.reshape(2 * length, 2 * length)


def third_coarse(length, devices, js):
    modes = third_modes(devices, js).reshape(devices, len(js) // 2, 2)
    theta = 2.0 * np.pi * (modes[..., None] * np.arange(length) % length) / length
    both = np.stack([np.cos(theta), -np.sin(theta)])
    return both.transpose(0, 2, 1, 3, 4).reshape(2 * (len(js) // 2) * devices, 2 * length)


def third_coarse_halo(length, devices, js):
    modes = np.repeat(third_modes(devices, js).reshape(-1), HALO)
    theta = angles(modes, np.arange(length), length)
    return np.concatenate([np.cos(theta), -np.sin(theta)], axis=1)


def split(x):
    high = x.astype(jnp.bfloat16)
    return high, (x - high.astype(jnp.float32)).astype(jnp.bfloat16)


def dot(a, b):
    return lax.dot_general(a, b, (((1,), (0,)), ((), ())), preferred_element_type=jnp.float32)


def dot_t(a, b):
    return lax.dot_general(a, b, (((1,), (1,)), ((), ())), preferred_element_type=jnp.float32)


def dot3(a, b):
    (ah, al), (bh, bl) = a, b
    return dot(ah, bh) + (dot(ah, bl) + dot(al, bh))


def load(pairs, sems):
    copies = [pltpu.make_async_copy(a, b, sems.at[i]) for i, (a, b) in enumerate(pairs)]
    for copy in copies:
        copy.start()
    return copies


def send(pairs, sems, first):
    copies = [pltpu.make_async_copy(a, b, sems.at[first + i]) for i, (a, b) in enumerate(pairs)]
    for copy in copies:
        copy.start()
    return copies


def forward_kernel(planes, d_hbm, x_hbm, out_hbm, d, x, out, sems):
    pieces, rows = d.shape[0], d.shape[1] // 2
    parts = [slice(p * LANE, (p + 2) * LANE) for p in range(0, planes, 2)]
    pairs = [(x_hbm.at[at, :], x.at[at, :]) for at in parts]
    copies = load([(d_hbm.at[0], d.at[0])] + pairs + [(d_hbm.at[i], d.at[i]) for i in range(1, pieces)], sems)
    sent = []
    copies[0].wait()
    for piece in range(pieces):
        if piece:
            copies[len(parts) + piece].wait()
        for i, at in enumerate(parts):
            if piece == 0:
                copies[i + 1].wait()
            value = dot_t(d[piece], x[at, :])
            value = value[:rows] + value[rows:]
            for h in range(2):
                out[pl.ds(piece * rows * SUB + 2 * i + h, rows, stride=SUB), :] = value[
                    :, h * LANE : (h + 1) * LANE
                ]
        tall = slice(piece * rows * SUB, (piece + 1) * rows * SUB)
        sent += send([(out.at[tall, :], out_hbm.at[tall, :])], sems, len(copies) + piece)
    for copy in sent:
        copy.wait()


def middle_kernel(sizes, scale, b, *rest):
    (first, second, rows, groups, js, low) = sizes
    count = 12
    away, out_hbm, near, rest = rest[:count], rest[count], rest[count + 1 : 2 * count + 1], rest[2 * count + 1 :]
    out, sems, zh, zl, y, oh, ol, qh, ql = rest
    copies = load(list(zip(away, near)), sems)
    csh, csl, fh, fl, ih, il, ich, icl, cch, ccl, ch, cl = near
    q_count = 2 * js
    half, quarter = second // 2, second // 4
    for q in range(q_count):
        for g in range(groups // 2):
            for r in range(0, rows, 2):
                at = r * groups + g
                near_half = jnp.concatenate([b[at, q], b[at + groups, q]], axis=0)
                at += groups // 2
                far_half = jnp.concatenate([b[at, q], b[at + groups, q]], axis=0)
                at = slice(q * first + r * SUB, q * first + (r + 2) * SUB)
                lanes = slice(g * LANE, (g + 1) * LANE)
                zh[0, at, lanes], zl[0, at, lanes] = split(near_half + far_half)
                zh[1, at, lanes], zl[1, at, lanes] = split(near_half - far_half)
    for copy in copies[:8]:
        copy.wait()
    wide = 8 * first
    for top in range(0, q_count * first, wide):
        at = slice(top, top + wide)
        for parity in range(2):
            y[parity, at, :] = dot3(
                (zh[parity, at, :], zl[parity, at, :]), (csh[parity], csl[parity])
            )
    mode0 = lax.broadcasted_iota(jnp.int32, (first, second), 0)
    mode0 = jnp.where(mode0 < first // 2, mode0, mode0 - first).astype(jnp.float32)
    lane = lax.broadcasted_iota(jnp.int32, (first, second), 1)
    mode1 = jnp.where(lane < half, lane, lane - half)
    mode1 = jnp.where(mode1 < quarter, 2 * mode1, 2 * (mode1 - quarter) + 1).astype(jnp.float32)
    base = 1.0 + DECAY * (mode0 * mode0 + mode1 * mode1)
    for j in range(js):
        top = j * 2 * first
        re, im = slice(top, top + first), slice(top + first, top + 2 * first)
        cos, sin = slice(0, quarter), slice(quarter, half)
        whole = lambda part, lanes: jnp.concatenate(
            [y[0, part, lanes], y[1, part, lanes]], axis=1
        )
        rc, rs, ic, isn = whole(re, cos), whole(re, sin), whole(im, cos), whole(im, sin)
        wave = jnp.concatenate(
            [
                jnp.concatenate([rc + isn, rc - isn], axis=1),
                jnp.concatenate([ic - rs, ic + rs], axis=1),
            ],
            axis=0,
        )
        spectrum = dot3((fh[...], fl[...]), split(wave))
        amp = jnp.where(lane == half, 0.0, scale[j, 1] / (base + scale[j, 0]))
        scaled = spectrum * jnp.concatenate([amp, amp], axis=0)
        field = dot3((ih[...], il[...]), split(scaled))
        plus, minus = field[:, :half], field[:, half:]
        even, odd = plus + minus, plus - minus
        odd = jnp.concatenate([-odd[first:], odd[:first]], axis=0)
        at = slice(top, top + 2 * first)
        for parity, lanes in enumerate((cos, sin)):
            operand = jnp.concatenate([even[:, lanes], odd[:, lanes]], axis=1)
            oh[parity, at, :], ol[parity, at, :] = split(operand)
        if j < low:
            keep = first // 4
            kept = [
                scaled[at : at + keep, :]
                for at in (0, first - keep, first, 2 * first - keep)
            ]
            band = jnp.concatenate(kept, axis=0)
            low_lane = lax.broadcasted_iota(jnp.int32, (first, quarter), 1) < quarter // 2
            pieces = []
            for at in (0, half):
                upper = pltpu.roll(band[:, at + quarter : at + half], quarter // 2, 1)
                pieces.append(jnp.where(low_lane, band[:, at : at + quarter], upper))
            band = jnp.concatenate(pieces, axis=1)
            field = dot3((ich[...], icl[...]), split(band))
            value, turned = field[:first], field[first:]
            operand = jnp.concatenate(
                [
                    value[:, :quarter] + value[:, quarter:],
                    turned[:, :quarter] - turned[:, quarter:],
                ],
                axis=1,
            )
            at = slice(j // 2 * first, (j // 2 + 1) * first)
            lanes = slice(j % 2 * half, (j % 2 + 1) * half)
            qh[at, lanes], ql[at, lanes] = split(operand)
    for copy in copies[8:]:
        copy.wait()
    copies = []
    wide = 4 * first
    lane = lax.broadcasted_iota(jnp.int32, (SUB, LANE), 1)
    extra = q_count + low // 2

    def leave(start, stop):
        at = slice(start, stop)
        copies.extend(send([(out.at[:, at], out_hbm.at[:, at])], sems, len(copies)))

    def give(value, start):
        tiles = value.shape[0] // first
        for q in range(tiles):
            for r in range(rows):
                for g in range(groups):
                    at = q * first + r * SUB
                    out[r * groups + g, start + q] = value[
                        at : at + SUB, g * LANE : (g + 1) * LANE
                    ]
        leave(start, start + tiles)

    def halo_columns(value, start, held):
        tiles = value.shape[0] // first
        for r in range(rows):
            for g in range(groups):
                total = held[r, g]
                left = max(g - 1, 0) * LANE
                right = min(g + 1, groups - 1) * LANE
                for q in range(tiles):
                    at = slice(q * first + r * SUB, q * first + (r + 1) * SUB)
                    both = jnp.where(
                        lane < LANE // 2,
                        value[at, right : right + LANE],
                        value[at, left : left + LANE],
                    )
                    to = HALO * (start + q)
                    both = pltpu.roll(both, (to + 2) % LANE, 1)
                    total = jnp.where((lane >= to) & (lane < to + HALO), both, total)
                held[r, g] = total

    def coarse_columns(value, held):
        half_lane = LANE // 2
        for j in range(low):
            for r in range(rows):
                at = slice(j // 2 * first + r * SUB, j // 2 * first + (r + 1) * SUB)
                shift = HALO * j + 2 - j % 2 * half_lane
                to = half_lane + HALO * j
                for g in range(groups):
                    left = max(g - 1, 0) * LANE
                    right = min(g + 1, groups - 1) * LANE
                    left = pltpu.roll(value[at, left : left + LANE], shift % LANE, 1)
                    right = pltpu.roll(
                        value[at, right : right + LANE], (shift + half_lane) % LANE, 1
                    )
                    total = jnp.where((lane >= to) & (lane < to + 2), left, held[r, g])
                    held[r, g] = jnp.where(
                        (lane >= to + 2) & (lane < to + HALO), right, total
                    )

    columns = {
        (r, g): jnp.zeros((SUB, LANE), jnp.float32) for r in range(rows) for g in range(groups)
    }
    coarse = dot3((qh[...], ql[...]), (cch[...], ccl[...]))
    give(coarse, q_count)
    coarse_columns(coarse, columns)
    for top in range(0, q_count * first, wide):
        at = slice(top, top + wide)
        even, odd = (
            dot3((oh[parity, at, :], ol[parity, at, :]), (ch[parity], cl[parity]))
            for parity in range(2)
        )
        value = jnp.concatenate([even + odd, even - odd], axis=1)
        give(value, top // first)
        halo_columns(value, top // first, columns)
    for (r, g), total in columns.items():
        out[r * groups + g, extra] = total
    leave(extra, extra + 1)
    for copy in copies:
        copy.wait()


def back_kernel(sizes, flags, b, *rest):
    (devices, q_count, low, tiles, planes, length) = sizes
    away, (ks, cks, lo, hi), rest = rest[:8], rest[8:12], rest[12:]
    near, (lh, ll, mh, ml, sems) = rest[:8], rest[8:]
    copies = load(list(zip(away, near)), sems)
    eh, el, ceh, cel, wh, wl, cwh, cwl = near
    cells, short = LANE, length // 2
    halves, coarse_planes = low // 2, planes // 2
    half = cells // 2
    for n in (0, 1, planes - 2, planes - 1, *range(2, planes - 2)):
        for parity in range(2):
            rows = jnp.concatenate(
                [
                    b[pl.ds(s * tiles * SUB + n, q_count, stride=SUB), :]
                    for s in range(parity, devices, 2)
                ],
                axis=0,
            )
            at = slice(n * LANE, (n + 1) * LANE)
            lh[parity, at, :], ll[parity, at, :] = split(jnp.transpose(rows))
    for n in range(coarse_planes):
        rows = jnp.concatenate(
            [
                b[pl.ds((q_count + h) * SUB + c * coarse_planes + n, devices, stride=tiles * SUB), :]
                for c in range(2)
                for h in range(halves)
            ],
            axis=0,
        )
        at = slice(n * LANE, (n + 1) * LANE)
        mh[at, :], ml[at, :] = split(jnp.transpose(rows))

    for copy in copies[:4]:
        copy.wait()

    def pair(p):
        at = slice(p * cells, (p + 2) * cells)
        even, odd = (
            dot3((lh[parity, at, :], ll[parity, at, :]), (eh[parity], el[parity]))
            for parity in range(2)
        )
        value = jnp.exp(jnp.concatenate([even + odd, even - odd], axis=1))
        for n in range(2):
            put_rows(ks, p + n, SUB, value[n * cells : (n + 1) * cells])

    pair(0)
    pair(planes - 2)
    value = dot3((mh[...], ml[...]), (ceh[...], cel[...]))
    for n in range(coarse_planes):
        top = n * cells
        part = value[top : top + half, :short] + value[top + half : top + cells, short:]
        part = jnp.exp(part)
        put_rows(cks, n, SUB, part)

    lane = lax.broadcasted_iota(jnp.int32, (SUB, LANE), 1)
    tile = lambda s: b[(s * tiles + tiles - 1) * SUB : (s + 1) * tiles * SUB, :]

    def spread(parts):
        return jnp.concatenate(
            [
                jnp.concatenate(
                    [jnp.where(lane % HALO == h, part, 0.0) for part in parts], axis=1
                )
                for h in range(HALO)
            ],
            axis=0,
        )

    for copy in copies[4:]:
        copy.wait()
    half_lane = LANE // 2
    results = []
    for parity in range(2):
        parts = [
            jnp.where(lane < half_lane, tile(s), pltpu.roll(tile(s + 2), half_lane, 1))
            for s in range(parity, devices, 4)
        ]
        results.append(dot3(split(spread(parts)), (wh[parity], wl[parity])))
    even, odd = results
    value = jnp.exp(jnp.concatenate([even + odd, even - odd], axis=1))
    for h in range(HALO):
        for n in range(planes):
            at = h * planes + n
            put_rows(ks, n, halo_row(h, cells), value[at : at + 1, :])
    width = HALO * low
    fit = LANE // width
    parts = []
    for s in range(0, devices, fit):
        part = jnp.zeros((SUB, LANE), jnp.float32)
        for i in range(fit):
            moved = pltpu.roll(tile(s + i), (i * width - half_lane) % LANE, 1)
            part = jnp.where((lane >= i * width) & (lane < (i + 1) * width), moved, part)
        parts.append(part)
    whole = dot3(split(spread(parts)), (cwh[...], cwl[...]))
    for h in range(HALO):
        top = h * SUB
        part = whole[top : top + coarse_planes, :short] + whole[top + coarse_planes : top + SUB, short:]
        part = jnp.exp(part)
        for n in range(coarse_planes):
            put_rows(cks, n, halo_row(h, half), part[n : n + 1, :])
    repeat_sides(flags, cks, [(n,) for n in range(coarse_planes)])
    edge_planes = (0, 1, planes - 2, planes - 1)
    repeat_sides(flags, ks, [(n,) for n in edge_planes])
    sent = []
    for edge, of in ((lo, lambda count: (1, 0)), (hi, lambda count: (count - 2, count - 1))):
        at = 0
        for held in (ks, cks):
            ext = held.shape[2]
            for n in of(held.shape[0]):
                for x in range(held.shape[1]):
                    sent += send([(held.at[n, x], edge.at[at : at + ext, :])], sems, 8 + len(sent))
                    at += ext
    for p in range(2, planes - 2, 2):
        pair(p)
    repeat_sides(flags, ks, [(n,) for n in range(2, planes - 2)])
    for copy in sent:
        copy.wait()


def halo_row(h, cells):
    return SUB - 2 + h if h < 2 else SUB + cells + h - 2


def source_kernel(planes, pairs, x, out, lo, hi, left, right, held, summed):
    cells = x.shape[0] // planes
    length = x.shape[1]
    half, fourth = cells // 2, cells // 4
    held[...] = dot(x[...], pairs[...])
    for n in range(planes // 2):
        top = 2 * n * cells
        for at in range(0, out.shape[1], LANE):
            lanes = slice(at, at + LANE)
            summed[...] = held[top : top + cells, lanes] + held[top + cells : top + 2 * cells, lanes]
            out[n * half : (n + 1) * half, lanes] = (
                summed[pl.ds(0, half, stride=2), :] + summed[pl.ds(1, half, stride=2), :]
            )
    for edge, plane in ((lo, 0), (hi, planes - 1)):
        edge[:cells, :] = x[plane * cells : (plane + 1) * cells, :].astype(jnp.float32)
        at = plane // 2 * half
        edge[cells:, : length // 2] = out[at : at + fourth, :]
        edge[cells:, length // 2 :] = out[at + fourth : at + half, :]
    for edge, row in ((left, 0), (right, cells - 1)):
        edge[...] = jnp.zeros_like(edge)
        for n in range(planes):
            at = n * cells + (row // SUB * SUB)
            edge[n : n + 1, :] = x[at : at + SUB, :].astype(jnp.float32)[row % SUB : row % SUB + 1]
        for n in range(planes // 2):
            at = n * half + row // 2
            edge[SUB + n : SUB + n + 1, : length // 2] = out[at : at + 1, :]


def beside(parts, ends):
    lane = lax.broadcasted_iota(jnp.int32, parts[0].shape, 1)
    ahead = [pltpu.roll(x, 1, 1) for x in parts]
    behind = [pltpu.roll(x, LANE - 1, 1) for x in parts]
    sums = []
    for i in range(len(parts)):
        left = jnp.where(lane == 0, ahead[i - 1] if i else ends[0], ahead[i])
        right = jnp.where(
            lane == LANE - 1, behind[i + 1] if i + 1 < len(parts) else ends[1], behind[i]
        )
        sums.append(left + right)
    return sums


def first_sweep(tiles, ext, mid, lower, upper, f, store):
    for top in range(0, ext, SUB):
        end = top + SUB
        parts = [mid(x, top, end) for x in range(tiles)]
        for x, both in enumerate(beside(parts, (parts[0], parts[-1]))):
            k = parts[x]
            above = pltpu.roll(k, 1, 0) if top == 0 else mid(x, top - 1, end - 1)
            below = pltpu.roll(k, SUB - 1, 0) if end == ext else mid(x, top + 1, end + 1)
            total = (lower(x, top, end) + upper(x, top, end)) + (above + below) + both
            scale = JACOBI_WEIGHT / (6.0 * k + total)
            u = f(x, top, end) * (2.0 * scale)
            store(x, top, end, u, k * u, scale)


def second_sweep(tiles, ext, k, u, w, r, store):
    for top in range(SUB, ext - SUB, SUB):
        end = top + SUB
        sums = []
        for lower, mid, upper in (u, w):
            parts = [mid(x, top, end) for x in range(tiles)]
            sums.append(
                [
                    both
                    + (lower(x, top, end) + upper(x, top, end))
                    + (mid(x, top - 1, end - 1) + mid(x, top + 1, end + 1))
                    for x, both in enumerate(beside(parts, (0.0, 0.0)))
                ]
            )
        for x in range(tiles):
            coupled = k(x, top, end) * sums[0][x] + sums[1][x]
            value = (2.0 - JACOBI_WEIGHT) * u[1](x, top, end) + r(x, top, end) * coupled
            store(x, top, end, value)


def plane_of(held, *at):
    return lambda x, top, end: held[(*at, x, slice(top, end), slice(None))]


def put_rows(held, to, at, rows):
    for x in range(held.shape[1]):
        held[to, x, at : at + rows.shape[0], :] = rows[:, x * LANE : (x + 1) * LANE]


def repeat_sides(flags, held, at):
    end = held.shape[-2] - SUB

    @pl.when(flags[2] == 1)
    def _():
        for p in at:
            held[(*p, slice(None), slice(SUB - 1, SUB))] = held[(*p, slice(None), slice(SUB, SUB + 1))]

    @pl.when(flags[3] == 1)
    def _():
        for p in at:
            held[(*p, slice(None), slice(end, end + 1))] = held[
                (*p, slice(None), slice(end - 1, end))
            ]


def put_block(fine, held, to, source, row, cells, length):
    if fine:
        put_rows(held, to, SUB, source[row : row + cells, :])
    else:
        half = cells // 2
        put_rows(held, to, SUB, source[row : row + half, :length])
        put_rows(held, to, SUB + half, source[row : row + half, length:])


def layout_kernel(sizes, *rest):
    away, outs, near, sems = rest[:6], rest[6:10], rest[10:16], rest[16]
    for copy in load(list(zip(away, near)), sems):
        copy.wait()
    source, coarse_source, *edges = near
    sides = edges[2:]
    for fine, inner, outer in ((True, *outs[:2]), (False, *outs[2:])):
        planes, cells, length = sizes if fine else [n // 2 for n in sizes]
        f = source if fine else coarse_source
        source_row = 0 if fine else SUB

        def plane(held, to, p):
            put_rows(held, to, SUB, f[p].astype(jnp.float32))
            for side, row in zip(sides, (SUB - 1, SUB + cells)):
                at = source_row + p
                put_rows(held, to, row, side[at : at + 1, :length])

        for p in range(1, planes - 1):
            plane(inner, p - 1, p)
        for group, p in enumerate((0, planes - 1)):
            row = 0 if fine else 2 * cells
            put_block(fine, outer.at[group], 0, edges[group], row, cells, length)
            plane(outer.at[group], 1, p)


def inner_level(sizes, ks, fs, us, ws, rs):
    planes, _, length = sizes
    tiles, ext = ks.shape[1:3]

    def first(p, carry):
        def store(x, top, end, u, w, r):
            at = (p - 1, x, slice(top, end))
            us[at], ws[at], rs[at] = u, w, r

        near = [plane_of(ks, p + i) for i in (0, -1, 1)]
        first_sweep(tiles, ext, *near, plane_of(fs, p - 1), store)
        return carry

    lax.fori_loop(1, planes - 1, first, 0)


def inner_kernel(sizes, ks, cks, fs, cfs, out_hbm, us, ws, rs, cus, cws, crs, out, sems):
    planes, _, length = sizes
    tiles, ext = ks.shape[1:3]
    inner_level(sizes, ks, fs, us, ws, rs)

    def second(p, carry):
        def store(x, top, end, value):
            out[p - 2, top - SUB : end - SUB, x * LANE : (x + 1) * LANE] = value

        u, w = ([plane_of(held, p - 1 + i) for i in (-1, 0, 1)] for held in (us, ws))
        second_sweep(tiles, ext, plane_of(ks, p), u, w, plane_of(rs, p - 1), store)
        return carry

    lax.fori_loop(2, planes - 2, second, 0)
    copies = send([(out, out_hbm.at[2 : planes - 2])], sems, 0)
    inner_level([n // 2 for n in sizes], cks, cfs, cus, cws, crs)
    for copy in copies:
        copy.wait()


def outer_kernel(sizes, flags, *rest):
    kept, coarse_kept, (k_lo, k_hi, _, out, coarse_out), rest = (
        rest[:5],
        rest[5:10],
        rest[10:15],
        rest[15:],
    )
    scratch = (rest[:6], rest[6:])
    levels = (sizes, tuple(n // 2 for n in sizes))
    waits, start = [], 0
    for halo, *_, sems in scratch:
        at = slice(start, start + halo.shape[1])
        waits.append(load([(k_lo.at[at, :], halo.at[0]), (k_hi.at[at, :], halo.at[1])], sems))
        start += halo.shape[1]
    sent = []
    for size, held, given, copies, target in zip(
        levels, scratch, (kept, coarse_kept), waits, (out, coarse_out)
    ):
        planes = size[0]
        ks, fs, inner_us, inner_ws, inner_rs = given
        halo, us, ws, rs, done, sems = held
        tiles, ext = ks.shape[1:3]
        for copy in copies:
            copy.wait()
        for group, p in enumerate((0, planes - 1)):

            @pl.when(flags[group] == 1)
            def _():
                for x in range(tiles):
                    at = (tiles + x) * ext
                    halo[group, at : at + ext, :] = ks[p, x]

        for flag, to, source in ((2, SUB - 1, SUB), (3, ext - SUB, ext - SUB - 1)):

            @pl.when(flags[flag] == 1)
            def _():
                for group in range(2):
                    for x in range(tiles):
                        at = (tiles + x) * ext
                        halo[group, at + to : at + to + 1, :] = halo[
                            group, at + source : at + source + 1, :
                        ]

        def both_ends(group, carry):
            def halo_plane(slot):
                def get(x, top, end):
                    at = (slot * tiles + x) * ext
                    return halo[group, at + top : at + end, :]

                return get

            inwards = lambda i, count: jnp.where(group == 0, i, count - 1 - i)
            own = [plane_of(ks, inwards(i, planes)) for i in range(2)]
            u, w = (
                [plane_of(new, group, i) for i in range(2)]
                + [plane_of(old, inwards(i, planes - 2)) for i in range(2)]
                for new, old in ((us, inner_us), (ws, inner_ws))
            )
            around = ((halo_plane(1), halo_plane(0), own[0]), (own[0], halo_plane(1), own[1]))
            for i, near in enumerate(around):

                def store(x, top, end, u, w, r):
                    at = (group, i, x, slice(top, end))
                    us[at], ws[at] = u, w
                    if i == 1:
                        rs[group, x, top:end, :] = r

                first_sweep(tiles, ext, *near, plane_of(fs, group, i), store)
            scales = (plane_of(rs, group), plane_of(inner_rs, inwards(0, planes - 2)))
            for i, r in enumerate(scales):

                def store(x, top, end, value):
                    done[group, i, top - SUB : end - SUB, x * LANE : (x + 1) * LANE] = value

                second_sweep(tiles, ext, own[i], u[i : i + 3], w[i : i + 3], r, store)
            return carry

        lax.fori_loop(0, 2, both_ends, 0)
        pairs = [
            (done.at[group, i], target.at[p])
            for group, at in enumerate(((0, 1), (planes - 1, planes - 2)))
            for i, p in enumerate(at)
        ]
        sent += send(pairs, sems, 0)
    for copy in sent:
        copy.wait()


SMEM = pl.BlockSpec(memory_space=pltpu.SMEM)
VMEM = pl.BlockSpec(memory_space=pltpu.VMEM)
AWAY = pl.BlockSpec(memory_space=pltpu.HBM)
ANY = pl.BlockSpec(memory_space=pl.ANY)


def call(kernel, outs, operands, scratch, flops, specs, limit, out_specs=None, aliases=None):
    many = isinstance(outs, (list, tuple))
    written = outs if many else [outs]
    moved = sum(math.prod(x.shape) * x.dtype.itemsize for x in (*operands, *written))
    operands = [
        pltpu.with_memory_space_constraint(x, pltpu.HBM) if spec is AWAY else x
        for x, spec in zip(operands, specs)
    ]
    out_specs = out_specs or [
        VMEM if isinstance(x, jax.ShapeDtypeStruct) else AWAY for x in written
    ]
    return pl.pallas_call(
        kernel,
        out_shape=outs,
        in_specs=specs,
        out_specs=out_specs if many else out_specs[0],
        scratch_shapes=scratch,
        input_output_aliases=aliases or {},
        compiler_params=pltpu.CompilerParams(vmem_limit_bytes=limit * MIB),
        cost_estimate=pl.CostEstimate(flops=flops, bytes_accessed=moved, transcendentals=0),
    )(*operands)


def f32(*shape):
    return jax.ShapeDtypeStruct(shape, jnp.float32)


def room(*arrays):
    return [pltpu.VMEM(x.shape, x.dtype) for x in arrays]


def chain(axis):
    up = [(i, i + 1) for i in range(lax.axis_size(axis) - 1)]
    return up, [(j, i) for i, j in up]


def swap(lo, hi, axis):
    up, down = chain(axis)
    return lax.ppermute(hi, axis, up), lax.ppermute(lo, axis, down)


def held_planes(size, *count):
    planes, cells, length = size
    return f32(*count, length // LANE, cells + 2 * SUB, LANE)


def outer_scratch(size):
    planes, cells, length = size
    return room(
        f32(2, 2 * (length // LANE) * (cells + 2 * SUB), LANE),
        held_planes(size, 2, 2),
        held_planes(size, 2, 2),
        held_planes(size, 2),
        f32(2, 2, cells, length),
    ) + [pltpu.SemaphoreType.DMA((4,))]


def fused_body(noise, source):
    rows, groups = lax.axis_size("row"), lax.axis_size(PLANE)
    devices = rows * groups
    planes, cells, length = noise.shape
    first, second = planes * rows, cells * groups
    bf16 = jnp.bfloat16
    held = length // 2 // devices
    js = list(range(held))
    low = held // 2
    me = lax.axis_index(EVERY)
    row_at, group_at = lax.axis_index("row"), lax.axis_index(PLANE)
    flags = jnp.stack(
        [row_at == 0, row_at == rows - 1, group_at == 0, group_at == groups - 1]
    ).astype(jnp.int32)
    norm = FIELD_SCALE * (float(first) * float(second) * float(length)) ** (-0.5)
    flat = (planes * cells, length)

    pieces = 2
    table = [x.reshape(pieces, -1, length) for x in two_parts(forward_third(length, devices, js))]
    table = np.concatenate(table, axis=1)
    shape = (length * SUB, LANE)
    sent = call(
        functools.partial(forward_kernel, planes),
        pltpu.HBM(shape, jnp.float32),
        (table, noise.reshape(flat)),
        room(table)
        + [
            pltpu.VMEM(flat, bf16),
            pltpu.VMEM(shape, jnp.float32),
            pltpu.SemaphoreType.DMA((2 * pieces + planes // 2,)),
        ],
        4 * length * length * planes * cells,
        [AWAY] * 2,
        12,
    )
    sent, source = lax.optimization_barrier((sent, source))
    sent = sent.reshape(devices, 2 * held, SUB, LANE)
    arrived = lax.all_to_all(sent, EVERY, split_axis=0, concat_axis=0, tiled=True)

    pairs = np.zeros((length, length // 2), np.float32)
    pairs[np.arange(length), np.arange(length) // 2] = 0.125
    level = f32(cells + cells // 4, length)
    side = f32(2 * SUB, length)
    coarse_source, *edges = call(
        functools.partial(source_kernel, planes),
        [f32(planes * cells // 4, length // 2), level, level, side, side],
        (pairs.astype(bf16), source.reshape(flat)),
        [
            pltpu.VMEM((planes * cells, length // 2), jnp.float32),
            pltpu.VMEM((cells, LANE), jnp.float32),
        ],
        planes * cells * length * length,
        [VMEM] * 2,
        12,
    )
    coarse_source = coarse_source.reshape(planes // 2, cells // 2, length // 2)
    edges = (*swap(*edges[:2], "row"), *swap(*edges[2:], PLANE))
    arrived, edges, coarse_source = lax.optimization_barrier((arrived, edges, coarse_source))

    constants = (
        two_parts(second_table(second))
        + two_parts(forward_first(first))
        + two_parts(inverse_first(first))
        + two_parts(inverse_first_coarse(first // 2, rows))
        + two_parts(second_coarse(second // 2, groups))
        + two_parts(second_table(second).transpose(0, 2, 1))
    )
    tiles = 2 * held + low // 2 + 1
    modes = (me + devices * np.array(js)).astype(jnp.float32)
    weight = jnp.where(modes == 0.0, norm, 2.0 * norm).astype(jnp.float32)
    scale = jnp.stack([DECAY * modes * modes, weight], axis=1)
    block = (2, 2 * held * first, second // 2)
    shape = (devices, tiles, SUB, LANE)
    out = call(
        functools.partial(middle_kernel, (first, second, rows, groups, held, low)),
        pltpu.HBM(shape, jnp.float32),
        (scale, arrived, *constants),
        room(*constants)
        + [
            pltpu.VMEM(shape, jnp.float32),
            pltpu.SemaphoreType.DMA((len(constants),)),
            pltpu.VMEM(block, bf16),
            pltpu.VMEM(block, bf16),
            pltpu.VMEM(block, jnp.float32),
            pltpu.VMEM(block, bf16),
            pltpu.VMEM(block, bf16),
            pltpu.VMEM((low // 2 * first, second), bf16),
            pltpu.VMEM((low // 2 * first, second), bf16),
        ],
        6 * 2 * 2 * held * first * second * (second + 2 * first),
        [SMEM, VMEM] + [AWAY] * len(constants),
        22,
    )
    out, source, coarse_source, edges = lax.optimization_barrier(
        (out, source, coarse_source, edges)
    )
    got = lax.all_to_all(out, EVERY, split_axis=0, concat_axis=0, tiled=True)
    size, coarse_size = noise.shape, coarse_source.shape
    sizes = (size, coarse_size)
    sources = (source, coarse_source, *edges)
    laid = call(
        functools.partial(layout_kernel, size),
        [
            held_planes(s, *count)
            for s in sizes
            for count in ((s[0] - 2,), (2, 2))
        ],
        sources,
        room(*sources) + [pltpu.SemaphoreType.DMA((6,))],
        source.size,
        [AWAY] * 6,
        12,
    )
    got, laid = lax.optimization_barrier((got, laid))

    third = inverse_third(length, devices, js)
    constants = (
        two_parts(third)
        + two_parts(third_coarse(length // 2, devices, js[:low]))
        + two_parts(np.repeat(third, HALO, axis=1))
        + two_parts(third_coarse_halo(length // 2, devices, js[:low]))
    )
    ext, coarse_ext = cells + 2 * SUB, cells // 2 + 2 * SUB
    edge = (2 * (length // LANE * ext + length // 2 // LANE * coarse_ext), LANE)
    ks, coarse_ks, lo, hi = call(
        functools.partial(back_kernel, (devices, 2 * held, low, tiles, planes, length)),
        [held_planes(s, s[0]) for s in sizes] + [pltpu.HBM(edge, jnp.float32)] * 2,
        (flags, got.reshape(devices * tiles * SUB, LANE), *constants),
        room(*constants)
        + [pltpu.VMEM((2, planes * cells, devices * held), bf16)] * 2
        + [pltpu.VMEM((planes // 2 * LANE, devices * low), bf16)] * 2
        + [pltpu.SemaphoreType.DMA((8 + 6 * length // LANE,))],
        6 * planes * cells * length * length,
        [SMEM, VMEM] + [AWAY] * 8,
        18,
    )
    k_lo, k_hi = swap(lo, hi, "row")
    inner_f, outer_f, coarse_inner_f, coarse_outer_f = laid
    inner, *kept = call(
        functools.partial(inner_kernel, size),
        [pltpu.HBM(size, jnp.float32)] + [held_planes(s, s[0] - 2) for s in sizes for _ in range(3)],
        (ks, coarse_ks, inner_f, coarse_inner_f),
        room(f32(planes - 4, cells, length)) + [pltpu.SemaphoreType.DMA((1,))],
        30 * source.size,
        [VMEM] * 4,
        18,
    )
    return call(
        functools.partial(outer_kernel, size),
        [pltpu.HBM(s, jnp.float32) for s in sizes],
        (flags, ks, outer_f, *kept[:3], coarse_ks, coarse_outer_f, *kept[3:], k_lo, k_hi, inner),
        outer_scratch(size) + outer_scratch(coarse_size),
        30 * source.size,
        [SMEM] + [VMEM] * 10 + [AWAY] * 3,
        18,
        None,
        {13: 0},
    )


NEIGHBOUR_STEPS = ((1, 0, 0), (-1, 0, 0), (0, 1, 0), (0, -1, 0), (0, 0, 1), (0, 0, -1))


def padded(x, sides, width):
    for axis, dim in sides:
        peers, length = (lax.axis_size(axis), x.shape[dim])
        up = [(i, (i + 1) % peers) for i in range(peers - 1)]
        down = [(j, i) for i, j in up]
        last = lax.slice_in_dim(x, length - width, length, axis=dim)
        leading = lax.slice_in_dim(x, 0, width, axis=dim)
        before = lax.ppermute(last, axis, up)
        after = lax.ppermute(leading, axis, down)
        x = jnp.concatenate([before, x, after], axis=dim)
    return x


def signed_modes(index, length):
    return jnp.where(index < length // 2, index, index - length).astype(jnp.float32)


def amplitude(first_modes, second_modes, third_modes, first_edge, second_edge, third_edge):
    squared = first_modes * first_modes + second_modes * second_modes + third_modes * third_modes
    value = FIELD_SCALE / (1.0 + (2.0 * math.pi * CORRELATION) ** 2 * squared)
    edge = (
        (jnp.abs(first_modes) == first_edge)
        | (jnp.abs(second_modes) == second_edge)
        | (jnp.abs(third_modes) == third_edge)
    )
    return jnp.where(edge, 0.0, value)


def phase_table(count_rows, count_cols, modulus, sign):
    left_index = jnp.arange(count_rows, dtype=jnp.int32)[:, None]
    right_index = jnp.arange(count_cols, dtype=jnp.int32)[None, :]
    angle = 2.0 * math.pi / modulus * (left_index * right_index % modulus).astype(jnp.float32)
    return (jnp.cos(angle), sign * jnp.sin(angle))


def split_length(length):
    outer_len = 2 ** ((length.bit_length() - 1) // 2)
    return (outer_len, length // outer_len)


def real_form(form, left_value, right_value):
    return jnp.einsum(form, left_value, right_value, precision=lax.Precision.HIGHEST)


def complex_form(form, left_real, left_imag, right_real, right_imag):
    real_part = real_form(form, left_real, right_real) - real_form(form, left_imag, right_imag)
    imag_part = real_form(form, left_real, right_imag) + real_form(form, left_imag, right_real)
    return (real_part, imag_part)


def merge_pair(values, out_form, first_letter):
    merge_at = out_form.index(first_letter)
    out_dims = list(values.shape)
    merged = (
        out_dims[:merge_at]
        + [out_dims[merge_at] * out_dims[merge_at + 1]]
        + out_dims[merge_at + 2 :]
    )
    return values.reshape(merged)


def forward_axis(real_part, imag_part, lead_form, out_form, kept_modes):
    length = real_part.shape[-1]
    outer_len, inner_len = split_length(length)
    split_shape = real_part.shape[:-1] + (outer_len, inner_len)
    outer_real, outer_imag = phase_table(outer_len, outer_len, outer_len, -1.0)
    twist_real, twist_imag = phase_table(outer_len, inner_len, length, -1.0)
    inner_real, inner_imag = phase_table(inner_len, kept_modes // outer_len, inner_len, -1.0)
    first_form = lead_form + "ab,ai->" + lead_form + "ib"
    split_real = real_part.reshape(split_shape)
    if imag_part is None:
        section_real = real_form(first_form, split_real, outer_real)
        section_imag = real_form(first_form, split_real, outer_imag)
    else:
        section_real, section_imag = complex_form(
            first_form, split_real, imag_part.reshape(split_shape), outer_real, outer_imag
        )
    turned_real = section_real * twist_real - section_imag * twist_imag
    turned_imag = section_real * twist_imag + section_imag * twist_real
    result_real, result_imag = complex_form(
        lead_form + "ib,bj->" + out_form, turned_real, turned_imag, inner_real, inner_imag
    )
    return (merge_pair(result_real, out_form, "j"), merge_pair(result_imag, out_form, "j"))


def inverse_axis(real_part, imag_part, length, lead_form, out_form, real_only):
    kept_modes = real_part.shape[-1]
    outer_len, inner_len = split_length(length)
    split_shape = real_part.shape[:-1] + (kept_modes // outer_len, outer_len)
    inner_real, inner_imag = phase_table(kept_modes // outer_len, inner_len, inner_len, 1.0)
    twist_real, twist_imag = phase_table(outer_len, inner_len, length, 1.0)
    outer_real, outer_imag = phase_table(outer_len, outer_len, outer_len, 1.0)
    section_real, section_imag = complex_form(
        lead_form + "ji,jb->" + lead_form + "ib",
        real_part.reshape(split_shape),
        imag_part.reshape(split_shape),
        inner_real,
        inner_imag,
    )
    turned_real = section_real * twist_real - section_imag * twist_imag
    turned_imag = section_real * twist_imag + section_imag * twist_real
    second_form = lead_form + "ib,ia->" + out_form
    if real_only:
        result = real_form(second_form, turned_real, outer_real) - real_form(
            second_form, turned_imag, outer_imag
        )
        return merge_pair(result, out_form, "a")
    result_real, result_imag = complex_form(
        second_form, turned_real, turned_imag, outer_real, outer_imag
    )
    return (merge_pair(result_real, out_form, "a"), merge_pair(result_imag, out_form, "a"))


def low_band(values, half_coarse, fine_len):
    return jnp.concatenate(
        [values[:, :, :half_coarse], values[:, :, fine_len - half_coarse :]], axis=2
    )


def window(values, margin, offset):
    return values[
        margin + offset[0] : values.shape[0] - margin + offset[0],
        margin + offset[1] : values.shape[1] - margin + offset[1],
        margin + offset[2] : values.shape[2] - margin + offset[2],
    ]


def face_weight(center, beside):
    return jnp.where(beside > 0.0, 0.5 * (center + beside), center)


def smooth_twice(kappa, source):
    no_shift = (0, 0, 0)
    center = window(kappa, 1, no_shift)
    faces = [face_weight(center, window(kappa, 1, offset)) for offset in NEIGHBOUR_STEPS]
    diagonal = faces[0] + faces[1] + faces[2] + faces[3] + faces[4] + faces[5]
    guarded = jnp.where(center > 0.0, diagonal, 1.0)
    first_sweep = JACOBI_WEIGHT * window(source, 1, no_shift) / guarded
    inner_first = window(first_sweep, 1, no_shift)
    inner_diagonal = window(diagonal, 1, no_shift)
    coupled = jnp.zeros_like(inner_first)
    for face_value, offset in zip(faces, NEIGHBOUR_STEPS):
        coupled = coupled + window(face_value, 1, no_shift) * window(first_sweep, 1, offset)
    residual = window(source, 2, no_shift) - inner_diagonal * inner_first + coupled
    return inner_first + JACOBI_WEIGHT * residual / inner_diagonal


def pad_depth(values):
    return jnp.pad(values, ((0, 0), (0, 0), (2, 2)))


def plain_body(noise, source):
    row_at = lax.axis_index("row")
    group_at = lax.axis_index(("level", "col"))
    fine_field = noise.astype(jnp.float32)
    fine_len = fine_field.shape[-1]
    coarse_len = fine_len // 2
    half_coarse = coarse_len // 2
    kept_modes = fine_len // 2
    real_part, imag_part = forward_axis(fine_field, None, "pq", "pjiq", kept_modes)
    real_part, imag_part = (
        lax.all_to_all(real_part, ("level", "col"), split_axis=1, concat_axis=2, tiled=True),
        lax.all_to_all(imag_part, ("level", "col"), split_axis=1, concat_axis=2, tiled=True),
    )
    real_part, imag_part = forward_axis(real_part, imag_part, "pq", "jiqp", fine_len)
    real_part, imag_part = (
        lax.all_to_all(real_part, "row", split_axis=0, concat_axis=2, tiled=True),
        lax.all_to_all(imag_part, "row", split_axis=0, concat_axis=2, tiled=True),
    )
    slab_len = real_part.shape[-1]
    coarse_slab = slab_len // 2
    half_slab = coarse_slab // 2
    real_part, imag_part = forward_axis(real_part, imag_part, "pq", "pqji", slab_len)
    second_count = real_part.shape[0]
    third_count = real_part.shape[1]
    wave_second = signed_modes(
        row_at * second_count + jnp.arange(second_count, dtype=jnp.int32), fine_len
    )[:, None, None]
    third_index = group_at * third_count + jnp.arange(third_count, dtype=jnp.int32)
    wave_third = signed_modes(third_index, fine_len)[None, :, None]
    spread = 2.0
    mirror_weight = jnp.where(third_index == 0, 1.0, spread).astype(jnp.float32)[None, :, None]
    norm_factor = (float(slab_len) * float(fine_len) * float(fine_len)) ** (-0.5)
    wave_first = signed_modes(jnp.arange(slab_len, dtype=jnp.int32), slab_len)[None, None, :]
    fine_scale = (
        amplitude(
            wave_second, wave_third, wave_first, fine_len / 2.0, fine_len / 2.0, slab_len / 2.0
        )
        * mirror_weight
        * norm_factor
    )
    coarse_first = signed_modes(jnp.arange(coarse_slab, dtype=jnp.int32), coarse_slab)[
        None, None, :
    ]
    coarse_scale = (
        amplitude(
            wave_second,
            wave_third,
            coarse_first,
            coarse_len / 2.0,
            coarse_len / 2.0,
            coarse_slab / 2.0,
        )
        * mirror_weight
        * norm_factor
    )
    coarse_real = low_band(real_part, half_slab, slab_len) * coarse_scale
    coarse_imag = low_band(imag_part, half_slab, slab_len) * coarse_scale
    fine_real, fine_imag = inverse_axis(
        real_part * fine_scale, imag_part * fine_scale, slab_len, "pq", "abqp", False
    )
    coarse_real, coarse_imag = inverse_axis(
        coarse_real, coarse_imag, coarse_slab, "pq", "abqp", False
    )
    fine_real, fine_imag, coarse_real, coarse_imag = (
        lax.all_to_all(fine_real, "row", split_axis=0, concat_axis=2, tiled=True),
        lax.all_to_all(fine_imag, "row", split_axis=0, concat_axis=2, tiled=True),
        lax.all_to_all(coarse_real, "row", split_axis=0, concat_axis=2, tiled=True),
        lax.all_to_all(coarse_imag, "row", split_axis=0, concat_axis=2, tiled=True),
    )
    coarse_real = low_band(coarse_real, half_coarse, fine_len)
    coarse_imag = low_band(coarse_imag, half_coarse, fine_len)
    fine_real, fine_imag = inverse_axis(fine_real, fine_imag, fine_len, "pq", "pabq", False)
    coarse_real, coarse_imag = inverse_axis(
        coarse_real, coarse_imag, coarse_len, "pq", "pabq", False
    )
    fine_real, fine_imag, coarse_real, coarse_imag = (
        lax.all_to_all(fine_real, ("level", "col"), split_axis=1, concat_axis=2, tiled=True),
        lax.all_to_all(fine_imag, ("level", "col"), split_axis=1, concat_axis=2, tiled=True),
        lax.all_to_all(coarse_real, ("level", "col"), split_axis=1, concat_axis=2, tiled=True),
        lax.all_to_all(coarse_imag, ("level", "col"), split_axis=1, concat_axis=2, tiled=True),
    )
    coarse_real = coarse_real[:, :, :half_coarse]
    coarse_imag = coarse_imag[:, :, :half_coarse]
    fine_log = inverse_axis(fine_real, fine_imag, fine_len, "pq", "pqab", True)
    coarse_log = inverse_axis(coarse_real, coarse_imag, coarse_len, "pq", "pqab", True)
    fine_kappa = jnp.exp(fine_log)
    coarse_kappa = jnp.exp(coarse_log)
    fine_source = source.astype(jnp.float32)
    coarse_rows = coarse_log.shape[0]
    coarse_cols = coarse_log.shape[1]
    coarse_source = fine_source.reshape(coarse_rows, 2, coarse_cols, 2, coarse_len, 2).mean(
        axis=(1, 3, 5)
    )
    fine_kappa, fine_source, coarse_kappa, coarse_source = (
        padded(fine_kappa, (("row", 0), (("level", "col"), 1)), 2),
        padded(fine_source, (("row", 0), (("level", "col"), 1)), 2),
        padded(coarse_kappa, (("row", 0), (("level", "col"), 1)), 2),
        padded(coarse_source, (("row", 0), (("level", "col"), 1)), 2),
    )
    fine_pressure = smooth_twice(pad_depth(fine_kappa), pad_depth(fine_source))
    coarse_pressure = smooth_twice(pad_depth(coarse_kappa), pad_depth(coarse_source))
    return (fine_pressure, coarse_pressure)


def body(noise, source):
    planes, cells, length = noise.shape
    devices = lax.axis_size(EVERY)
    held = length // 2 // devices
    if planes == SUB and cells == LANE and held % 4 == 0 and held > 0:
        return fused_body(noise, source)
    return plain_body(noise, source)


def solution(mesh):
    return jax.shard_map(
        body,
        mesh=mesh,
        in_specs=(P("row", ("level", "col"), None), P("row", ("level", "col"), None)),
        out_specs=(P("row", ("level", "col"), None), P("row", ("level", "col"), None)),
        check_vma=False,
    )
```

```python
import functools
import math

import jax
import jax.numpy as jnp
import numpy as np
from jax import lax
from jax.experimental import pallas as pl
from jax.experimental.pallas import tpu as pltpu
from jax.sharding import PartitionSpec as P

JACOBI_WEIGHT = 2.0 / 3.0
CORRELATION = 0.2
FIELD_SCALE = 0.3
DECAY = (2.0 * math.pi * CORRELATION) ** 2
EVERY = ("row", "level", "col")
PLANE = ("level", "col")
MIB = 1 << 20
SUB, LANE = 8, 128
HALO = 4


def two_parts(matrix):
    high = matrix.astype(jnp.bfloat16)
    low = (matrix - high.astype(np.float64)).astype(jnp.bfloat16)
    return high, low


def angles(rows, cols, length):
    return 2.0 * np.pi * (np.outer(rows, cols) % length) / length


def third_modes(devices, js):
    return np.array([[d + devices * j for j in js] for d in range(devices)])


def forward_third(length, devices, js):
    theta = angles(third_modes(devices, js).reshape(-1), np.arange(length), length)
    return np.stack([np.cos(theta), -np.sin(theta)], axis=1).reshape(-1, length)


def inverse_third(length, devices, js):
    modes = third_modes(devices, js).reshape(devices // 2, 2, len(js)).transpose(1, 0, 2)
    theta = 2.0 * np.pi * (modes[..., None] * np.arange(length // 2) % length) / length
    both = np.stack([np.cos(theta), -np.sin(theta)], axis=3)
    return both.reshape(2, -1, length // 2)


def second_modes(length):
    return np.arange(length // 2).reshape(-1, 2).T


def second_table(length):
    theta = second_modes(length)[:, None, :] * np.arange(length // 2)[None, :, None]
    theta = 2.0 * np.pi * (theta % length) / length
    return np.concatenate([np.cos(theta), np.sin(theta)], axis=2)


def forward_first(length):
    theta = angles(np.arange(length), np.arange(length), length)
    cos, sin = np.cos(theta), np.sin(theta)
    return np.block([[cos, sin], [-sin, cos]])


def inverse_first(length):
    theta = angles(np.arange(length), np.arange(length), length)
    cos, sin = np.cos(theta), np.sin(theta)
    cos[:, length // 2] = 0.0
    sin[:, length // 2] = 0.0
    return np.block([[cos, -sin], [sin, cos]])


def inverse_first_coarse(length, rows):
    full = inverse_first(length)
    value = full.reshape(2, rows, length // rows, 2 * length)
    turned = np.concatenate([-full[length:], full[:length]]).reshape(value.shape)
    order = lambda x: x.transpose(1, 0, 2, 3).reshape(2 * length, 2 * length)
    return np.concatenate([order(value), order(turned)])


def second_coarse(length, groups):
    theta = angles(second_modes(length).reshape(-1), np.arange(length), length)
    table = np.concatenate([np.cos(theta), np.sin(theta)])
    span = length // groups
    out = np.zeros((2, length, groups, 2, span))
    for pair in range(2):
        out[pair, :, :, pair, :] = table.reshape(length, groups, span)
    return out.reshape(2 * length, 2 * length)


def third_coarse(length, devices, js):
    modes = third_modes(devices, js).reshape(devices, len(js) // 2, 2)
    theta = 2.0 * np.pi * (modes[..., None] * np.arange(length) % length) / length
    both = np.stack([np.cos(theta), -np.sin(theta)])
    return both.transpose(0, 2, 1, 3, 4).reshape(2 * (len(js) // 2) * devices, 2 * length)


def third_coarse_halo(length, devices, js):
    modes = np.repeat(third_modes(devices, js).reshape(-1), HALO)
    theta = angles(modes, np.arange(length), length)
    return np.concatenate([np.cos(theta), -np.sin(theta)], axis=1)


def split(x):
    high = x.astype(jnp.bfloat16)
    return high, (x - high.astype(jnp.float32)).astype(jnp.bfloat16)


def dot(a, b):
    return lax.dot_general(a, b, (((1,), (0,)), ((), ())), preferred_element_type=jnp.float32)


def dot_t(a, b):
    return lax.dot_general(a, b, (((1,), (1,)), ((), ())), preferred_element_type=jnp.float32)


def stacked(matrix):
    high, low = two_parts(matrix)
    return np.block([[high, high], [low, np.zeros_like(low)]])


def dot_left(stack, x):
    value = dot(stack, jnp.concatenate(split(x), axis=0))
    rows = stack.shape[0] // 2
    return value[:rows] + value[rows:]


def dot3(a, b):
    (ah, al), (bh, bl) = a, b
    return dot(ah, bh) + (dot(ah, bl) + dot(al, bh))


def load(pairs, sems):
    copies = [pltpu.make_async_copy(a, b, sems.at[i]) for i, (a, b) in enumerate(pairs)]
    for copy in copies:
        copy.start()
    return copies


def send(pairs, sems, first):
    copies = [pltpu.make_async_copy(a, b, sems.at[first + i]) for i, (a, b) in enumerate(pairs)]
    for copy in copies:
        copy.start()
    return copies


def forward_kernel(planes, d_hbm, x_hbm, out_hbm, d, x, out, sems):
    pieces, rows = d.shape[0], d.shape[1] // 2
    parts = [slice(p * LANE, (p + 2) * LANE) for p in range(0, planes, 2)]
    pairs = [(x_hbm.at[at, :], x.at[at, :]) for at in parts]
    copies = load([(d_hbm.at[0], d.at[0])] + pairs + [(d_hbm.at[i], d.at[i]) for i in range(1, pieces)], sems)
    sent = []
    copies[0].wait()
    for piece in range(pieces):
        if piece:
            copies[len(parts) + piece].wait()
        for i, at in enumerate(parts):
            if piece == 0:
                copies[i + 1].wait()
            value = dot_t(d[piece], x[at, :])
            value = value[:rows] + value[rows:]
            for h in range(2):
                out[pl.ds(piece * rows * SUB + 2 * i + h, rows, stride=SUB), :] = value[
                    :, h * LANE : (h + 1) * LANE
                ]
        tall = slice(piece * rows * SUB, (piece + 1) * rows * SUB)
        sent += send([(out.at[tall, :], out_hbm.at[tall, :])], sems, len(copies) + piece)
    for copy in sent:
        copy.wait()


def middle_kernel(sizes, scale, b, *rest):
    (first, second, rows, groups, js, low) = sizes
    count = 9
    away, out_hbm, near, rest = (
        rest[:count],
        rest[count],
        rest[count + 1 : 2 * count + 1],
        rest[2 * count + 1 :],
    )
    out, sems, zh, zl, y, oh, ol, qh, ql = rest
    copies = load(list(zip(away, near)), sems)
    csh, csl, forward, inverse, coarse_inverse, cch, ccl, ch, cl = near
    q_count = 2 * js
    half, quarter = second // 2, second // 4
    for q in range(q_count):
        for g in range(groups // 2):
            for r in range(0, rows, 2):
                at = r * groups + g
                near_half = jnp.concatenate([b[at, q], b[at + groups, q]], axis=0)
                at += groups // 2
                far_half = jnp.concatenate([b[at, q], b[at + groups, q]], axis=0)
                at = slice(q * first + r * SUB, q * first + (r + 2) * SUB)
                lanes = slice(g * LANE, (g + 1) * LANE)
                zh[0, at, lanes], zl[0, at, lanes] = split(near_half + far_half)
                zh[1, at, lanes], zl[1, at, lanes] = split(near_half - far_half)
    for copy in copies[:5]:
        copy.wait()
    wide = 8 * first
    for top in range(0, q_count * first, wide):
        at = slice(top, top + wide)
        for parity in range(2):
            y[parity, at, :] = dot3(
                (zh[parity, at, :], zl[parity, at, :]), (csh[parity], csl[parity])
            )
    mode0 = lax.broadcasted_iota(jnp.int32, (first, second), 0)
    mode0 = jnp.where(mode0 < first // 2, mode0, mode0 - first).astype(jnp.float32)
    lane = lax.broadcasted_iota(jnp.int32, (first, second), 1)
    mode1 = jnp.where(lane < half, lane, lane - half)
    mode1 = jnp.where(mode1 < quarter, 2 * mode1, 2 * (mode1 - quarter) + 1).astype(jnp.float32)
    base = 1.0 + DECAY * (mode0 * mode0 + mode1 * mode1)
    for j in range(js):
        top = j * 2 * first
        re, im = slice(top, top + first), slice(top + first, top + 2 * first)
        cos, sin = slice(0, quarter), slice(quarter, half)
        whole = lambda part, lanes: jnp.concatenate(
            [y[0, part, lanes], y[1, part, lanes]], axis=1
        )
        rc, rs, ic, isn = whole(re, cos), whole(re, sin), whole(im, cos), whole(im, sin)
        wave = jnp.concatenate(
            [
                jnp.concatenate([rc + isn, rc - isn], axis=1),
                jnp.concatenate([ic - rs, ic + rs], axis=1),
            ],
            axis=0,
        )
        spectrum = dot_left(forward[...], wave)
        amp = jnp.where(lane == half, 0.0, scale[j, 1] / (base + scale[j, 0]))
        scaled = spectrum * jnp.concatenate([amp, amp], axis=0)
        field = dot_left(inverse[...], scaled)
        plus, minus = field[:, :half], field[:, half:]
        even, odd = plus + minus, plus - minus
        odd = jnp.concatenate([-odd[first:], odd[:first]], axis=0)
        at = slice(top, top + 2 * first)
        for parity, lanes in enumerate((cos, sin)):
            operand = jnp.concatenate([even[:, lanes], odd[:, lanes]], axis=1)
            oh[parity, at, :], ol[parity, at, :] = split(operand)
        if j < low:
            keep = first // 4
            kept = [
                scaled[at : at + keep, :]
                for at in (0, first - keep, first, 2 * first - keep)
            ]
            band = jnp.concatenate(kept, axis=0)
            low_lane = lax.broadcasted_iota(jnp.int32, (first, quarter), 1) < quarter // 2
            pieces = []
            for at in (0, half):
                upper = pltpu.roll(band[:, at + quarter : at + half], quarter // 2, 1)
                pieces.append(jnp.where(low_lane, band[:, at : at + quarter], upper))
            band = jnp.concatenate(pieces, axis=1)
            field = dot_left(coarse_inverse[...], band)
            value, turned = field[:first], field[first:]
            operand = jnp.concatenate(
                [
                    value[:, :quarter] + value[:, quarter:],
                    turned[:, :quarter] - turned[:, quarter:],
                ],
                axis=1,
            )
            at = slice(j // 2 * first, (j // 2 + 1) * first)
            lanes = slice(j % 2 * half, (j % 2 + 1) * half)
            qh[at, lanes], ql[at, lanes] = split(operand)
    for copy in copies[5:]:
        copy.wait()
    copies = []
    wide = 4 * first
    lane = lax.broadcasted_iota(jnp.int32, (SUB, LANE), 1)
    extra = q_count + low // 2

    def leave(start, stop):
        at = slice(start, stop)
        copies.extend(send([(out.at[:, at], out_hbm.at[:, at])], sems, len(copies)))

    def give(value, start):
        tiles = value.shape[0] // first
        for q in range(tiles):
            for r in range(rows):
                for g in range(groups):
                    at = q * first + r * SUB
                    out[r * groups + g, start + q] = value[
                        at : at + SUB, g * LANE : (g + 1) * LANE
                    ]
        leave(start, start + tiles)

    def halo_columns(value, start, held):
        tiles = value.shape[0] // first
        for r in range(rows):
            for g in range(groups):
                total = held[r, g]
                left = max(g - 1, 0) * LANE
                right = min(g + 1, groups - 1) * LANE
                for q in range(tiles):
                    at = slice(q * first + r * SUB, q * first + (r + 1) * SUB)
                    both = jnp.where(
                        lane < LANE // 2,
                        value[at, right : right + LANE],
                        value[at, left : left + LANE],
                    )
                    to = HALO * (start + q)
                    both = pltpu.roll(both, (to + 2) % LANE, 1)
                    total = jnp.where((lane >= to) & (lane < to + HALO), both, total)
                held[r, g] = total

    def coarse_columns(value, held):
        half_lane = LANE // 2
        for j in range(low):
            for r in range(rows):
                at = slice(j // 2 * first + r * SUB, j // 2 * first + (r + 1) * SUB)
                shift = HALO * j + 2 - j % 2 * half_lane
                to = half_lane + HALO * j
                for g in range(groups):
                    left = max(g - 1, 0) * LANE
                    right = min(g + 1, groups - 1) * LANE
                    left = pltpu.roll(value[at, left : left + LANE], shift % LANE, 1)
                    right = pltpu.roll(
                        value[at, right : right + LANE], (shift + half_lane) % LANE, 1
                    )
                    total = jnp.where((lane >= to) & (lane < to + 2), left, held[r, g])
                    held[r, g] = jnp.where(
                        (lane >= to + 2) & (lane < to + HALO), right, total
                    )

    columns = {
        (r, g): jnp.zeros((SUB, LANE), jnp.float32) for r in range(rows) for g in range(groups)
    }
    coarse = dot3((qh[...], ql[...]), (cch[...], ccl[...]))
    give(coarse, q_count)
    coarse_columns(coarse, columns)
    for top in range(0, q_count * first, wide):
        at = slice(top, top + wide)
        even, odd = (
            dot3((oh[parity, at, :], ol[parity, at, :]), (ch[parity], cl[parity]))
            for parity in range(2)
        )
        value = jnp.concatenate([even + odd, even - odd], axis=1)
        give(value, top // first)
        halo_columns(value, top // first, columns)
    for (r, g), total in columns.items():
        out[r * groups + g, extra] = total
    leave(extra, extra + 1)
    for copy in copies:
        copy.wait()


def gather_modes(b, at, sizes, lh, ll):
    devices, q_count, tiles = sizes
    for i, n in enumerate(at):
        for parity in range(2):
            rows = jnp.concatenate(
                [
                    b[pl.ds(s * tiles * SUB + n, q_count, stride=SUB), :]
                    for s in range(parity, devices, 2)
                ],
                axis=0,
            )
            to = slice(i * LANE, (i + 1) * LANE)
            lh[parity, to, :], ll[parity, to, :] = split(jnp.transpose(rows))


def inverse_pair(i, lh, ll, eh, el, ks, to, cells):
    at = slice(i * cells, (i + 2) * cells)
    even, odd = (
        dot3((lh[parity, at, :], ll[parity, at, :]), (eh[parity], el[parity]))
        for parity in range(2)
    )
    value = jnp.exp(jnp.concatenate([even + odd, even - odd], axis=1))
    for n in range(2):
        put_rows(ks, to + n, SUB, value[n * cells : (n + 1) * cells])


def edge_kernel(sizes, flags, b, *rest):
    (devices, q_count, low, tiles, planes, length) = sizes
    away, (ks, cks, cols, lo, hi), rest = rest[:8], rest[8:13], rest[13:]
    near, (lh, ll, mh, ml, sems) = rest[:8], rest[8:]
    copies = load(list(zip(away, near)), sems)
    eh, el, ceh, cel, wh, wl, cwh, cwl = near
    cells, short = LANE, length // 2
    halves, coarse_planes = low // 2, planes // 2
    half = cells // 2
    gather_modes(b, (0, 1, planes - 2, planes - 1), (devices, q_count, tiles), lh, ll)
    for n in range(coarse_planes):
        rows = jnp.concatenate(
            [
                b[pl.ds((q_count + h) * SUB + c * coarse_planes + n, devices, stride=tiles * SUB), :]
                for c in range(2)
                for h in range(halves)
            ],
            axis=0,
        )
        at = slice(n * LANE, (n + 1) * LANE)
        mh[at, :], ml[at, :] = split(jnp.transpose(rows))

    for copy in copies[:4]:
        copy.wait()

    for i in range(0, 4, 2):
        inverse_pair(i, lh, ll, eh, el, ks, i, cells)
    value = dot3((mh[...], ml[...]), (ceh[...], cel[...]))
    for n in range(coarse_planes):
        top = n * cells
        part = value[top : top + half, :short] + value[top + half : top + cells, short:]
        part = jnp.exp(part)
        put_rows(cks, n, SUB, part)

    lane = lax.broadcasted_iota(jnp.int32, (SUB, LANE), 1)
    tile = lambda s: b[(s * tiles + tiles - 1) * SUB : (s + 1) * tiles * SUB, :]

    def spread(parts):
        return jnp.concatenate(
            [
                jnp.concatenate(
                    [jnp.where(lane % HALO == h, part, 0.0) for part in parts], axis=1
                )
                for h in range(HALO)
            ],
            axis=0,
        )

    for copy in copies[4:]:
        copy.wait()
    half_lane = LANE // 2
    results = []
    for parity in range(2):
        parts = [
            jnp.where(lane < half_lane, tile(s), pltpu.roll(tile(s + 2), half_lane, 1))
            for s in range(parity, devices, 4)
        ]
        results.append(dot3(split(spread(parts)), (wh[parity], wl[parity])))
    even, odd = results
    value = jnp.exp(jnp.concatenate([even + odd, even - odd], axis=1))
    cols[...] = value
    for h in range(HALO):
        for i, n in enumerate((0, 1, planes - 2, planes - 1)):
            at = h * planes + n
            put_rows(ks, i, halo_row(h, cells), value[at : at + 1, :])
    width = HALO * low
    fit = LANE // width
    parts = []
    for s in range(0, devices, fit):
        part = jnp.zeros((SUB, LANE), jnp.float32)
        for i in range(fit):
            moved = pltpu.roll(tile(s + i), (i * width - half_lane) % LANE, 1)
            part = jnp.where((lane >= i * width) & (lane < (i + 1) * width), moved, part)
        parts.append(part)
    whole = dot3(split(spread(parts)), (cwh[...], cwl[...]))
    for h in range(HALO):
        top = h * SUB
        part = whole[top : top + coarse_planes, :short] + whole[top + coarse_planes : top + SUB, short:]
        part = jnp.exp(part)
        for n in range(coarse_planes):
            put_rows(cks, n, halo_row(h, half), part[n : n + 1, :])
    for held in (ks, cks):
        repeat_sides(flags, held, [(n,) for n in range(4)])
    sent = []
    for edge, of in ((lo, (1, 0)), (hi, (2, 3))):
        at = 0
        for held in (ks, cks):
            ext = held.shape[2]
            for n in of:
                for x in range(held.shape[1]):
                    sent += send([(held.at[n, x], edge.at[at : at + ext, :])], sems, 8 + len(sent))
                    at += ext
    for copy in sent:
        copy.wait()


def halo_row(h, cells):
    return SUB - 2 + h if h < 2 else SUB + cells + h - 2


def source_kernel(planes, pairs, x, out, lo, hi, left, right, held, summed):
    cells = x.shape[0] // planes
    length = x.shape[1]
    half, fourth = cells // 2, cells // 4
    held[...] = dot(x[...], pairs[...])
    for n in range(planes // 2):
        top = 2 * n * cells
        for at in range(0, out.shape[1], LANE):
            lanes = slice(at, at + LANE)
            summed[...] = held[top : top + cells, lanes] + held[top + cells : top + 2 * cells, lanes]
            out[n * half : (n + 1) * half, lanes] = (
                summed[pl.ds(0, half, stride=2), :] + summed[pl.ds(1, half, stride=2), :]
            )
    for edge, plane in ((lo, 0), (hi, planes - 1)):
        edge[:cells, :] = x[plane * cells : (plane + 1) * cells, :].astype(jnp.float32)
        at = plane // 2 * half
        edge[cells:, : length // 2] = out[at : at + fourth, :]
        edge[cells:, length // 2 :] = out[at + fourth : at + half, :]
    for edge, row in ((left, 0), (right, cells - 1)):
        edge[...] = jnp.zeros_like(edge)
        for n in range(planes):
            at = n * cells + (row // SUB * SUB)
            edge[n : n + 1, :] = x[at : at + SUB, :].astype(jnp.float32)[row % SUB : row % SUB + 1]
        for n in range(planes // 2):
            at = n * half + row // 2
            edge[SUB + n : SUB + n + 1, : length // 2] = out[at : at + 1, :]


def beside(parts, ends):
    lane = lax.broadcasted_iota(jnp.int32, parts[0].shape, 1)
    ahead = [pltpu.roll(x, 1, 1) for x in parts]
    behind = [pltpu.roll(x, LANE - 1, 1) for x in parts]
    sums = []
    for i in range(len(parts)):
        left = jnp.where(lane == 0, ahead[i - 1] if i else ends[0], ahead[i])
        right = jnp.where(
            lane == LANE - 1, behind[i + 1] if i + 1 < len(parts) else ends[1], behind[i]
        )
        sums.append(left + right)
    return sums


def first_sweep(tiles, ext, mid, lower, upper, f, store):
    for top in range(0, ext, SUB):
        end = top + SUB
        parts = [mid(x, top, end) for x in range(tiles)]
        for x, both in enumerate(beside(parts, (parts[0], parts[-1]))):
            k = parts[x]
            above = pltpu.roll(k, 1, 0) if top == 0 else mid(x, top - 1, end - 1)
            below = pltpu.roll(k, SUB - 1, 0) if end == ext else mid(x, top + 1, end + 1)
            total = (lower(x, top, end) + upper(x, top, end)) + (above + below) + both
            scale = JACOBI_WEIGHT / (6.0 * k + total)
            u = f(x, top, end) * (2.0 * scale)
            store(x, top, end, u, k * u, scale)


def second_sweep(tiles, ext, k, u, w, r, store):
    for top in range(SUB, ext - SUB, SUB):
        end = top + SUB
        sums = []
        for lower, mid, upper in (u, w):
            parts = [mid(x, top, end) for x in range(tiles)]
            sums.append(
                [
                    both
                    + (lower(x, top, end) + upper(x, top, end))
                    + (mid(x, top - 1, end - 1) + mid(x, top + 1, end + 1))
                    for x, both in enumerate(beside(parts, (0.0, 0.0)))
                ]
            )
        for x in range(tiles):
            coupled = k(x, top, end) * sums[0][x] + sums[1][x]
            value = (2.0 - JACOBI_WEIGHT) * u[1](x, top, end) + r(x, top, end) * coupled
            store(x, top, end, value)


def plane_of(held, *at):
    return lambda x, top, end: held[(*at, x, slice(top, end), slice(None))]


def put_rows(held, to, at, rows):
    for x in range(held.shape[1]):
        held[to, x, at : at + rows.shape[0], :] = rows[:, x * LANE : (x + 1) * LANE]


def repeat_sides(flags, held, at):
    end = held.shape[-2] - SUB

    @pl.when(flags[2] == 1)
    def _():
        for p in at:
            held[(*p, slice(None), slice(SUB - 1, SUB))] = held[(*p, slice(None), slice(SUB, SUB + 1))]

    @pl.when(flags[3] == 1)
    def _():
        for p in at:
            held[(*p, slice(None), slice(end, end + 1))] = held[
                (*p, slice(None), slice(end - 1, end))
            ]


def put_block(fine, held, to, source, row, cells, length):
    if fine:
        put_rows(held, to, SUB, source[row : row + cells, :])
    else:
        half = cells // 2
        put_rows(held, to, SUB, source[row : row + half, :length])
        put_rows(held, to, SUB + half, source[row : row + half, length:])


def layout_kernel(sizes, *rest):
    away, outs, near, sems = rest[:6], rest[6:10], rest[10:16], rest[16]
    for copy in load(list(zip(away, near)), sems):
        copy.wait()
    source, coarse_source, *edges = near
    sides = edges[2:]
    for fine, inner, outer in ((True, *outs[:2]), (False, *outs[2:])):
        planes, cells, length = sizes if fine else [n // 2 for n in sizes]
        f = source if fine else coarse_source
        source_row = 0 if fine else SUB

        def plane(held, to, p):
            put_rows(held, to, SUB, f[p].astype(jnp.float32))
            for side, row in zip(sides, (SUB - 1, SUB + cells)):
                at = source_row + p
                put_rows(held, to, row, side[at : at + 1, :length])

        for p in range(1, planes - 1):
            plane(inner, p - 1, p)
        for group, p in enumerate((0, planes - 1)):
            row = 0 if fine else 2 * cells
            put_block(fine, outer.at[group], 0, edges[group], row, cells, length)
            plane(outer.at[group], 1, p)


def inner_level(sizes, ks, fs, us, ws, rs):
    planes, _, length = sizes
    tiles, ext = ks.shape[1:3]

    def first(p, carry):
        def store(x, top, end, u, w, r):
            at = (p - 1, x, slice(top, end))
            us[at], ws[at], rs[at] = u, w, r

        near = [plane_of(ks, p + i) for i in (0, -1, 1)]
        first_sweep(tiles, ext, *near, plane_of(fs, p - 1), store)
        return carry

    lax.fori_loop(1, planes - 1, first, 0)


def inner_kernel(sizes, shares, flags, b, eh_hbm, el_hbm, edges, cks, cols, fs, cfs, *rest):
    out_hbm, us, ws, rs, cus, cws, crs, ks, eh, el, lh, ll, out, sems = rest
    planes, cells, length = sizes
    tiles, ext = ks.shape[1:3]
    copies = load([(eh_hbm, eh), (el_hbm, el)], sems)
    middle = range(2, planes - 2)
    gather_modes(b, middle, shares, lh, ll)
    for i, p in enumerate((0, 1, planes - 2, planes - 1)):
        ks[p] = edges[i]
    for h in range(HALO):
        for p in middle:
            at = h * planes + p
            put_rows(ks, p, halo_row(h, cells), cols[at : at + 1, :])
    for copy in copies:
        copy.wait()
    for p in range(2, planes - 2, 2):
        inverse_pair(p - 2, lh, ll, eh, el, ks, p, cells)
    repeat_sides(flags, ks, [(p,) for p in middle])
    inner_level(sizes, ks, fs, us, ws, rs)

    def second(p, carry):
        def store(x, top, end, value):
            out[p - 2, top - SUB : end - SUB, x * LANE : (x + 1) * LANE] = value

        u, w = ([plane_of(held, p - 1 + i) for i in (-1, 0, 1)] for held in (us, ws))
        second_sweep(tiles, ext, plane_of(ks, p), u, w, plane_of(rs, p - 1), store)
        return carry

    lax.fori_loop(2, planes - 2, second, 0)
    copies = send([(out, out_hbm.at[2 : planes - 2])], sems, 0)
    inner_level([n // 2 for n in sizes], cks, cfs, cus, cws, crs)
    for copy in copies:
        copy.wait()


def outer_kernel(sizes, flags, *rest):
    kept, coarse_kept, (k_lo, k_hi, _, out, coarse_out), rest = (
        rest[:5],
        rest[5:10],
        rest[10:15],
        rest[15:],
    )
    scratch = (rest[:6], rest[6:])
    levels = (sizes, tuple(n // 2 for n in sizes))
    start = 0
    sent = []
    for size, held, given, target in zip(
        levels, scratch, (kept, coarse_kept), (out, coarse_out)
    ):
        planes = size[0]
        ks, fs, inner_us, inner_ws, inner_rs = given
        halo, us, ws, rs, done, sems = held
        tiles, ext = ks.shape[1:3]
        at = slice(start, start + halo.shape[1])
        halo[0], halo[1] = k_lo[at, :], k_hi[at, :]
        start += halo.shape[1]
        for group in range(2):

            @pl.when(flags[group] == 1)
            def _():
                for x in range(tiles):
                    at = (tiles + x) * ext
                    halo[group, at : at + ext, :] = ks[3 * group, x]

        for flag, to, source in ((2, SUB - 1, SUB), (3, ext - SUB, ext - SUB - 1)):

            @pl.when(flags[flag] == 1)
            def _():
                for group in range(2):
                    for x in range(tiles):
                        at = (tiles + x) * ext
                        halo[group, at + to : at + to + 1, :] = halo[
                            group, at + source : at + source + 1, :
                        ]

        def both_ends(group, carry):
            def halo_plane(slot):
                def get(x, top, end):
                    at = (slot * tiles + x) * ext
                    return halo[group, at + top : at + end, :]

                return get

            inwards = lambda i, count: jnp.where(group == 0, i, count - 1 - i)
            own = [plane_of(ks, inwards(i, 4)) for i in range(2)]
            u, w = (
                [plane_of(new, group, i) for i in range(2)]
                + [plane_of(old, inwards(i, planes - 2)) for i in range(2)]
                for new, old in ((us, inner_us), (ws, inner_ws))
            )
            around = ((halo_plane(1), halo_plane(0), own[0]), (own[0], halo_plane(1), own[1]))
            for i, near in enumerate(around):

                def store(x, top, end, u, w, r):
                    at = (group, i, x, slice(top, end))
                    us[at], ws[at] = u, w
                    if i == 1:
                        rs[group, x, top:end, :] = r

                first_sweep(tiles, ext, *near, plane_of(fs, group, i), store)
            scales = (plane_of(rs, group), plane_of(inner_rs, inwards(0, planes - 2)))
            for i, r in enumerate(scales):

                def store(x, top, end, value):
                    done[group, i, top - SUB : end - SUB, x * LANE : (x + 1) * LANE] = value

                second_sweep(tiles, ext, own[i], u[i : i + 3], w[i : i + 3], r, store)
            return carry

        lax.fori_loop(0, 2, both_ends, 0)
        pairs = [
            (done.at[group, i], target.at[p])
            for group, at in enumerate(((0, 1), (planes - 1, planes - 2)))
            for i, p in enumerate(at)
        ]
        sent += send(pairs, sems, 0)
    for copy in sent:
        copy.wait()


SMEM = pl.BlockSpec(memory_space=pltpu.SMEM)
VMEM = pl.BlockSpec(memory_space=pltpu.VMEM)
AWAY = pl.BlockSpec(memory_space=pltpu.HBM)
ANY = pl.BlockSpec(memory_space=pl.ANY)


def call(kernel, outs, operands, scratch, flops, specs, limit, out_specs=None, aliases=None):
    many = isinstance(outs, (list, tuple))
    written = outs if many else [outs]
    moved = sum(math.prod(x.shape) * x.dtype.itemsize for x in (*operands, *written))
    operands = [
        pltpu.with_memory_space_constraint(x, pltpu.HBM) if spec is AWAY else x
        for x, spec in zip(operands, specs)
    ]
    out_specs = out_specs or [
        VMEM if isinstance(x, jax.ShapeDtypeStruct) else AWAY for x in written
    ]
    return pl.pallas_call(
        kernel,
        out_shape=outs,
        in_specs=specs,
        out_specs=out_specs if many else out_specs[0],
        scratch_shapes=scratch,
        input_output_aliases=aliases or {},
        compiler_params=pltpu.CompilerParams(vmem_limit_bytes=limit * MIB),
        cost_estimate=pl.CostEstimate(flops=flops, bytes_accessed=moved, transcendentals=0),
    )(*operands)


def f32(*shape):
    return jax.ShapeDtypeStruct(shape, jnp.float32)


def room(*arrays):
    return [pltpu.VMEM(x.shape, x.dtype) for x in arrays]


def chain(axis):
    up = [(i, i + 1) for i in range(lax.axis_size(axis) - 1)]
    return up, [(j, i) for i, j in up]


def swap(lo, hi, axis):
    up, down = chain(axis)
    return lax.ppermute(hi, axis, up), lax.ppermute(lo, axis, down)


def held_planes(size, *count):
    planes, cells, length = size
    return f32(*count, length // LANE, cells + 2 * SUB, LANE)


def outer_scratch(size):
    planes, cells, length = size
    return room(
        f32(2, 2 * (length // LANE) * (cells + 2 * SUB), LANE),
        held_planes(size, 2, 2),
        held_planes(size, 2, 2),
        held_planes(size, 2),
        f32(2, 2, cells, length),
    ) + [pltpu.SemaphoreType.DMA((4,))]


def fused_body(noise, source):
    rows, groups = lax.axis_size("row"), lax.axis_size(PLANE)
    devices = rows * groups
    planes, cells, length = noise.shape
    first, second = planes * rows, cells * groups
    bf16 = jnp.bfloat16
    held = length // 2 // devices
    js = list(range(held))
    low = held // 2
    me = lax.axis_index(EVERY)
    row_at, group_at = lax.axis_index("row"), lax.axis_index(PLANE)
    flags = jnp.stack(
        [row_at == 0, row_at == rows - 1, group_at == 0, group_at == groups - 1]
    ).astype(jnp.int32)
    norm = FIELD_SCALE * (float(first) * float(second) * float(length)) ** (-0.5)
    flat = (planes * cells, length)

    pieces = 4
    table = [x.reshape(pieces, -1, length) for x in two_parts(forward_third(length, devices, js))]
    table = np.concatenate(table, axis=1)
    shape = (length * SUB, LANE)
    sent = call(
        functools.partial(forward_kernel, planes),
        pltpu.HBM(shape, jnp.float32),
        (table, noise.reshape(flat)),
        room(table)
        + [
            pltpu.VMEM(flat, bf16),
            pltpu.VMEM(shape, jnp.float32),
            pltpu.SemaphoreType.DMA((2 * pieces + planes // 2,)),
        ],
        4 * length * length * planes * cells,
        [AWAY] * 2,
        12,
    )
    sent, source = lax.optimization_barrier((sent, source))
    sent = sent.reshape(devices, 2 * held, SUB, LANE)
    arrived = lax.all_to_all(sent, EVERY, split_axis=0, concat_axis=0, tiled=True)

    pairs = np.zeros((length, length // 2), np.float32)
    pairs[np.arange(length), np.arange(length) // 2] = 0.125
    level = f32(cells + cells // 4, length)
    side = f32(2 * SUB, length)
    coarse_source, *edges = call(
        functools.partial(source_kernel, planes),
        [f32(planes * cells // 4, length // 2), level, level, side, side],
        (pairs.astype(bf16), source.reshape(flat)),
        [
            pltpu.VMEM((planes * cells, length // 2), jnp.float32),
            pltpu.VMEM((cells, LANE), jnp.float32),
        ],
        planes * cells * length * length,
        [VMEM] * 2,
        12,
    )
    coarse_source = coarse_source.reshape(planes // 2, cells // 2, length // 2)
    edges = (*swap(*edges[:2], "row"), *swap(*edges[2:], PLANE))
    arrived, edges, coarse_source = lax.optimization_barrier((arrived, edges, coarse_source))

    constants = (
        two_parts(second_table(second))
        + (
            stacked(forward_first(first)),
            stacked(inverse_first(first)),
            stacked(inverse_first_coarse(first // 2, rows)),
        )
        + two_parts(second_coarse(second // 2, groups))
        + two_parts(second_table(second).transpose(0, 2, 1))
    )
    tiles = 2 * held + low // 2 + 1
    modes = (me + devices * np.array(js)).astype(jnp.float32)
    weight = jnp.where(modes == 0.0, norm, 2.0 * norm).astype(jnp.float32)
    scale = jnp.stack([DECAY * modes * modes, weight], axis=1)
    block = (2, 2 * held * first, second // 2)
    shape = (devices, tiles, SUB, LANE)
    out = call(
        functools.partial(middle_kernel, (first, second, rows, groups, held, low)),
        pltpu.HBM(shape, jnp.float32),
        (scale, arrived, *constants),
        room(*constants)
        + [
            pltpu.VMEM(shape, jnp.float32),
            pltpu.SemaphoreType.DMA((len(constants),)),
            pltpu.VMEM(block, bf16),
            pltpu.VMEM(block, bf16),
            pltpu.VMEM(block, jnp.float32),
            pltpu.VMEM(block, bf16),
            pltpu.VMEM(block, bf16),
            pltpu.VMEM((low // 2 * first, second), bf16),
            pltpu.VMEM((low // 2 * first, second), bf16),
        ],
        6 * 2 * 2 * held * first * second * (second + 2 * first),
        [SMEM, VMEM] + [AWAY] * len(constants),
        22,
    )
    out, source, coarse_source, edges = lax.optimization_barrier(
        (out, source, coarse_source, edges)
    )
    got = lax.all_to_all(out, EVERY, split_axis=0, concat_axis=0, tiled=True)
    size, coarse_size = noise.shape, coarse_source.shape
    sizes = (size, coarse_size)
    sources = (source, coarse_source, *edges)
    laid = call(
        functools.partial(layout_kernel, size),
        [
            held_planes(s, *count)
            for s in sizes
            for count in ((s[0] - 2,), (2, 2))
        ],
        sources,
        room(*sources) + [pltpu.SemaphoreType.DMA((6,))],
        source.size,
        [AWAY] * 6,
        12,
    )
    got, laid = lax.optimization_barrier((got, laid))

    third = inverse_third(length, devices, js)
    constants = (
        two_parts(third)
        + two_parts(third_coarse(length // 2, devices, js[:low]))
        + two_parts(np.repeat(third, HALO, axis=1))
        + two_parts(third_coarse_halo(length // 2, devices, js[:low]))
    )
    ext, coarse_ext = cells + 2 * SUB, cells // 2 + 2 * SUB
    edge = (2 * (length // LANE * ext + length // 2 // LANE * coarse_ext), LANE)
    shares = (devices, 2 * held, tiles)
    got = got.reshape(devices * tiles * SUB, LANE)
    ks, coarse_ks, cols, lo, hi = call(
        functools.partial(edge_kernel, (devices, 2 * held, low, tiles, planes, length)),
        [held_planes(s, 4) for s in sizes]
        + [f32(HALO * planes, length)]
        + [pltpu.HBM(edge, jnp.float32)] * 2,
        (flags, got, *constants),
        room(*constants)
        + [pltpu.VMEM((2, 4 * cells, devices * held), bf16)] * 2
        + [pltpu.VMEM((planes // 2 * LANE, devices * low), bf16)] * 2
        + [pltpu.SemaphoreType.DMA((8 + 6 * length // LANE,))],
        3 * planes * cells * length * length,
        [SMEM, VMEM] + [AWAY] * 8,
        18,
    )
    k_lo, k_hi = swap(lo, hi, "row")
    inner_f, outer_f, coarse_inner_f, coarse_outer_f = laid
    inner, *kept = call(
        functools.partial(inner_kernel, size, shares),
        [pltpu.HBM(size, jnp.float32)] + [held_planes(s, s[0] - 2) for s in sizes for _ in range(3)],
        (flags, got, *constants[:2], ks, coarse_ks, cols, inner_f, coarse_inner_f),
        room(held_planes(size, planes), *constants[:2])
        + [pltpu.VMEM((2, (planes - 4) * cells, devices * held), bf16)] * 2
        + room(f32(planes - 4, cells, length))
        + [pltpu.SemaphoreType.DMA((2,))],
        3 * planes * cells * length * length,
        [SMEM, VMEM] + [AWAY] * 2 + [VMEM] * 5,
        18,
    )
    return call(
        functools.partial(outer_kernel, size),
        [pltpu.HBM(s, jnp.float32) for s in sizes],
        (flags, ks, outer_f, *kept[:3], coarse_ks, coarse_outer_f, *kept[3:], k_lo, k_hi, inner),
        outer_scratch(size) + outer_scratch(coarse_size),
        30 * source.size,
        [SMEM] + [VMEM] * 12 + [AWAY],
        18,
        None,
        {13: 0},
    )


NEIGHBOUR_STEPS = ((1, 0, 0), (-1, 0, 0), (0, 1, 0), (0, -1, 0), (0, 0, 1), (0, 0, -1))


def padded(x, sides, width):
    for axis, dim in sides:
        peers, length = (lax.axis_size(axis), x.shape[dim])
        up = [(i, (i + 1) % peers) for i in range(peers - 1)]
        down = [(j, i) for i, j in up]
        last = lax.slice_in_dim(x, length - width, length, axis=dim)
        leading = lax.slice_in_dim(x, 0, width, axis=dim)
        before = lax.ppermute(last, axis, up)
        after = lax.ppermute(leading, axis, down)
        x = jnp.concatenate([before, x, after], axis=dim)
    return x


def signed_modes(index, length):
    return jnp.where(index < length // 2, index, index - length).astype(jnp.float32)


def amplitude(first_modes, second_modes, third_modes, first_edge, second_edge, third_edge):
    squared = first_modes * first_modes + second_modes * second_modes + third_modes * third_modes
    value = FIELD_SCALE / (1.0 + (2.0 * math.pi * CORRELATION) ** 2 * squared)
    edge = (
        (jnp.abs(first_modes) == first_edge)
        | (jnp.abs(second_modes) == second_edge)
        | (jnp.abs(third_modes) == third_edge)
    )
    return jnp.where(edge, 0.0, value)


def phase_table(count_rows, count_cols, modulus, sign):
    left_index = jnp.arange(count_rows, dtype=jnp.int32)[:, None]
    right_index = jnp.arange(count_cols, dtype=jnp.int32)[None, :]
    angle = 2.0 * math.pi / modulus * (left_index * right_index % modulus).astype(jnp.float32)
    return (jnp.cos(angle), sign * jnp.sin(angle))


def split_length(length):
    outer_len = 2 ** ((length.bit_length() - 1) // 2)
    return (outer_len, length // outer_len)


def real_form(form, left_value, right_value):
    return jnp.einsum(form, left_value, right_value, precision=lax.Precision.HIGHEST)


def complex_form(form, left_real, left_imag, right_real, right_imag):
    real_part = real_form(form, left_real, right_real) - real_form(form, left_imag, right_imag)
    imag_part = real_form(form, left_real, right_imag) + real_form(form, left_imag, right_real)
    return (real_part, imag_part)


def merge_pair(values, out_form, first_letter):
    merge_at = out_form.index(first_letter)
    out_dims = list(values.shape)
    merged = (
        out_dims[:merge_at]
        + [out_dims[merge_at] * out_dims[merge_at + 1]]
        + out_dims[merge_at + 2 :]
    )
    return values.reshape(merged)


def forward_axis(real_part, imag_part, lead_form, out_form, kept_modes):
    length = real_part.shape[-1]
    outer_len, inner_len = split_length(length)
    split_shape = real_part.shape[:-1] + (outer_len, inner_len)
    outer_real, outer_imag = phase_table(outer_len, outer_len, outer_len, -1.0)
    twist_real, twist_imag = phase_table(outer_len, inner_len, length, -1.0)
    inner_real, inner_imag = phase_table(inner_len, kept_modes // outer_len, inner_len, -1.0)
    first_form = lead_form + "ab,ai->" + lead_form + "ib"
    split_real = real_part.reshape(split_shape)
    if imag_part is None:
        section_real = real_form(first_form, split_real, outer_real)
        section_imag = real_form(first_form, split_real, outer_imag)
    else:
        section_real, section_imag = complex_form(
            first_form, split_real, imag_part.reshape(split_shape), outer_real, outer_imag
        )
    turned_real = section_real * twist_real - section_imag * twist_imag
    turned_imag = section_real * twist_imag + section_imag * twist_real
    result_real, result_imag = complex_form(
        lead_form + "ib,bj->" + out_form, turned_real, turned_imag, inner_real, inner_imag
    )
    return (merge_pair(result_real, out_form, "j"), merge_pair(result_imag, out_form, "j"))


def inverse_axis(real_part, imag_part, length, lead_form, out_form, real_only):
    kept_modes = real_part.shape[-1]
    outer_len, inner_len = split_length(length)
    split_shape = real_part.shape[:-1] + (kept_modes // outer_len, outer_len)
    inner_real, inner_imag = phase_table(kept_modes // outer_len, inner_len, inner_len, 1.0)
    twist_real, twist_imag = phase_table(outer_len, inner_len, length, 1.0)
    outer_real, outer_imag = phase_table(outer_len, outer_len, outer_len, 1.0)
    section_real, section_imag = complex_form(
        lead_form + "ji,jb->" + lead_form + "ib",
        real_part.reshape(split_shape),
        imag_part.reshape(split_shape),
        inner_real,
        inner_imag,
    )
    turned_real = section_real * twist_real - section_imag * twist_imag
    turned_imag = section_real * twist_imag + section_imag * twist_real
    second_form = lead_form + "ib,ia->" + out_form
    if real_only:
        result = real_form(second_form, turned_real, outer_real) - real_form(
            second_form, turned_imag, outer_imag
        )
        return merge_pair(result, out_form, "a")
    result_real, result_imag = complex_form(
        second_form, turned_real, turned_imag, outer_real, outer_imag
    )
    return (merge_pair(result_real, out_form, "a"), merge_pair(result_imag, out_form, "a"))


def low_band(values, half_coarse, fine_len):
    return jnp.concatenate(
        [values[:, :, :half_coarse], values[:, :, fine_len - half_coarse :]], axis=2
    )


def window(values, margin, offset):
    return values[
        margin + offset[0] : values.shape[0] - margin + offset[0],
        margin + offset[1] : values.shape[1] - margin + offset[1],
        margin + offset[2] : values.shape[2] - margin + offset[2],
    ]


def face_weight(center, beside):
    return jnp.where(beside > 0.0, 0.5 * (center + beside), center)


def smooth_twice(kappa, source):
    no_shift = (0, 0, 0)
    center = window(kappa, 1, no_shift)
    faces = [face_weight(center, window(kappa, 1, offset)) for offset in NEIGHBOUR_STEPS]
    diagonal = faces[0] + faces[1] + faces[2] + faces[3] + faces[4] + faces[5]
    guarded = jnp.where(center > 0.0, diagonal, 1.0)
    first_sweep = JACOBI_WEIGHT * window(source, 1, no_shift) / guarded
    inner_first = window(first_sweep, 1, no_shift)
    inner_diagonal = window(diagonal, 1, no_shift)
    coupled = jnp.zeros_like(inner_first)
    for face_value, offset in zip(faces, NEIGHBOUR_STEPS):
        coupled = coupled + window(face_value, 1, no_shift) * window(first_sweep, 1, offset)
    residual = window(source, 2, no_shift) - inner_diagonal * inner_first + coupled
    return inner_first + JACOBI_WEIGHT * residual / inner_diagonal


def pad_depth(values):
    return jnp.pad(values, ((0, 0), (0, 0), (2, 2)))


def plain_body(noise, source):
    row_at = lax.axis_index("row")
    group_at = lax.axis_index(("level", "col"))
    fine_field = noise.astype(jnp.float32)
    fine_len = fine_field.shape[-1]
    coarse_len = fine_len // 2
    half_coarse = coarse_len // 2
    kept_modes = fine_len // 2
    real_part, imag_part = forward_axis(fine_field, None, "pq", "pjiq", kept_modes)
    real_part, imag_part = (
        lax.all_to_all(real_part, ("level", "col"), split_axis=1, concat_axis=2, tiled=True),
        lax.all_to_all(imag_part, ("level", "col"), split_axis=1, concat_axis=2, tiled=True),
    )
    real_part, imag_part = forward_axis(real_part, imag_part, "pq", "jiqp", fine_len)
    real_part, imag_part = (
        lax.all_to_all(real_part, "row", split_axis=0, concat_axis=2, tiled=True),
        lax.all_to_all(imag_part, "row", split_axis=0, concat_axis=2, tiled=True),
    )
    slab_len = real_part.shape[-1]
    coarse_slab = slab_len // 2
    half_slab = coarse_slab // 2
    real_part, imag_part = forward_axis(real_part, imag_part, "pq", "pqji", slab_len)
    second_count = real_part.shape[0]
    third_count = real_part.shape[1]
    wave_second = signed_modes(
        row_at * second_count + jnp.arange(second_count, dtype=jnp.int32), fine_len
    )[:, None, None]
    third_index = group_at * third_count + jnp.arange(third_count, dtype=jnp.int32)
    wave_third = signed_modes(third_index, fine_len)[None, :, None]
    spread = 2.0
    mirror_weight = jnp.where(third_index == 0, 1.0, spread).astype(jnp.float32)[None, :, None]
    norm_factor = (float(slab_len) * float(fine_len) * float(fine_len)) ** (-0.5)
    wave_first = signed_modes(jnp.arange(slab_len, dtype=jnp.int32), slab_len)[None, None, :]
    fine_scale = (
        amplitude(
            wave_second, wave_third, wave_first, fine_len / 2.0, fine_len / 2.0, slab_len / 2.0
        )
        * mirror_weight
        * norm_factor
    )
    coarse_first = signed_modes(jnp.arange(coarse_slab, dtype=jnp.int32), coarse_slab)[
        None, None, :
    ]
    coarse_scale = (
        amplitude(
            wave_second,
            wave_third,
            coarse_first,
            coarse_len / 2.0,
            coarse_len / 2.0,
            coarse_slab / 2.0,
        )
        * mirror_weight
        * norm_factor
    )
    coarse_real = low_band(real_part, half_slab, slab_len) * coarse_scale
    coarse_imag = low_band(imag_part, half_slab, slab_len) * coarse_scale
    fine_real, fine_imag = inverse_axis(
        real_part * fine_scale, imag_part * fine_scale, slab_len, "pq", "abqp", False
    )
    coarse_real, coarse_imag = inverse_axis(
        coarse_real, coarse_imag, coarse_slab, "pq", "abqp", False
    )
    fine_real, fine_imag, coarse_real, coarse_imag = (
        lax.all_to_all(fine_real, "row", split_axis=0, concat_axis=2, tiled=True),
        lax.all_to_all(fine_imag, "row", split_axis=0, concat_axis=2, tiled=True),
        lax.all_to_all(coarse_real, "row", split_axis=0, concat_axis=2, tiled=True),
        lax.all_to_all(coarse_imag, "row", split_axis=0, concat_axis=2, tiled=True),
    )
    coarse_real = low_band(coarse_real, half_coarse, fine_len)
    coarse_imag = low_band(coarse_imag, half_coarse, fine_len)
    fine_real, fine_imag = inverse_axis(fine_real, fine_imag, fine_len, "pq", "pabq", False)
    coarse_real, coarse_imag = inverse_axis(
        coarse_real, coarse_imag, coarse_len, "pq", "pabq", False
    )
    fine_real, fine_imag, coarse_real, coarse_imag = (
        lax.all_to_all(fine_real, ("level", "col"), split_axis=1, concat_axis=2, tiled=True),
        lax.all_to_all(fine_imag, ("level", "col"), split_axis=1, concat_axis=2, tiled=True),
        lax.all_to_all(coarse_real, ("level", "col"), split_axis=1, concat_axis=2, tiled=True),
        lax.all_to_all(coarse_imag, ("level", "col"), split_axis=1, concat_axis=2, tiled=True),
    )
    coarse_real = coarse_real[:, :, :half_coarse]
    coarse_imag = coarse_imag[:, :, :half_coarse]
    fine_log = inverse_axis(fine_real, fine_imag, fine_len, "pq", "pqab", True)
    coarse_log = inverse_axis(coarse_real, coarse_imag, coarse_len, "pq", "pqab", True)
    fine_kappa = jnp.exp(fine_log)
    coarse_kappa = jnp.exp(coarse_log)
    fine_source = source.astype(jnp.float32)
    coarse_rows = coarse_log.shape[0]
    coarse_cols = coarse_log.shape[1]
    coarse_source = fine_source.reshape(coarse_rows, 2, coarse_cols, 2, coarse_len, 2).mean(
        axis=(1, 3, 5)
    )
    fine_kappa, fine_source, coarse_kappa, coarse_source = (
        padded(fine_kappa, (("row", 0), (("level", "col"), 1)), 2),
        padded(fine_source, (("row", 0), (("level", "col"), 1)), 2),
        padded(coarse_kappa, (("row", 0), (("level", "col"), 1)), 2),
        padded(coarse_source, (("row", 0), (("level", "col"), 1)), 2),
    )
    fine_pressure = smooth_twice(pad_depth(fine_kappa), pad_depth(fine_source))
    coarse_pressure = smooth_twice(pad_depth(coarse_kappa), pad_depth(coarse_source))
    return (fine_pressure, coarse_pressure)


def body(noise, source):
    planes, cells, length = noise.shape
    devices = lax.axis_size(EVERY)
    held = length // 2 // devices
    if planes == SUB and cells == LANE and held % 4 == 0 and held > 0:
        return fused_body(noise, source)
    return plain_body(noise, source)


def solution(mesh):
    return jax.shard_map(
        body,
        mesh=mesh,
        in_specs=(P("row", ("level", "col"), None), P("row", ("level", "col"), None)),
        out_specs=(P("row", ("level", "col"), None), P("row", ("level", "col"), None)),
        check_vma=False,
    )
```

```python
import functools
import math

import jax
import jax.numpy as jnp
import numpy as np
from jax import lax
from jax.experimental import pallas as pl
from jax.experimental.pallas import tpu as pltpu
from jax.sharding import PartitionSpec as P

JACOBI_WEIGHT = 2.0 / 3.0
CORRELATION = 0.2
FIELD_SCALE = 0.3
DECAY = (2.0 * math.pi * CORRELATION) ** 2
EVERY = ("row", "level", "col")
PLANE = ("level", "col")
MIB = 1 << 20
SUB, LANE = 8, 128
HALO = 4


def two_parts(matrix):
    high = matrix.astype(jnp.bfloat16)
    low = (matrix - high.astype(np.float64)).astype(jnp.bfloat16)
    return high, low


def angles(rows, cols, length):
    return 2.0 * np.pi * (np.outer(rows, cols) % length) / length


def third_modes(devices, js):
    return np.array([[d + devices * j for j in js] for d in range(devices)])


def forward_third(length, devices, js):
    theta = angles(third_modes(devices, js).reshape(-1), np.arange(length), length)
    return np.stack([np.cos(theta), -np.sin(theta)], axis=1).reshape(-1, length)


def inverse_third(length, devices, js):
    modes = third_modes(devices, js).reshape(devices // 2, 2, len(js)).transpose(1, 0, 2)
    theta = 2.0 * np.pi * (modes[..., None] * np.arange(length // 2) % length) / length
    both = np.stack([np.cos(theta), -np.sin(theta)], axis=3)
    return both.reshape(2, -1, length // 2)


def second_modes(length):
    return np.arange(length // 2).reshape(-1, 2).T


def second_table(length):
    theta = second_modes(length)[:, None, :] * np.arange(length // 2)[None, :, None]
    theta = 2.0 * np.pi * (theta % length) / length
    return np.concatenate([np.cos(theta), np.sin(theta)], axis=2)


def forward_first(length):
    theta = angles(np.arange(length), np.arange(length), length)
    cos, sin = np.cos(theta), np.sin(theta)
    return np.block([[cos, sin], [-sin, cos]])


def inverse_first(length):
    theta = angles(np.arange(length), np.arange(length), length)
    cos, sin = np.cos(theta), np.sin(theta)
    cos[:, length // 2] = 0.0
    sin[:, length // 2] = 0.0
    return np.block([[cos, -sin], [sin, cos]])


def inverse_first_coarse(length, rows):
    full = inverse_first(length)
    value = full.reshape(2, rows, length // rows, 2 * length)
    turned = np.concatenate([-full[length:], full[:length]]).reshape(value.shape)
    order = lambda x: x.transpose(1, 0, 2, 3).reshape(2 * length, 2 * length)
    return np.concatenate([order(value), order(turned)])


def second_coarse(length, groups):
    theta = angles(second_modes(length).reshape(-1), np.arange(length), length)
    table = np.concatenate([np.cos(theta), np.sin(theta)])
    span = length // groups
    out = np.zeros((2, length, groups, 2, span))
    for pair in range(2):
        out[pair, :, :, pair, :] = table.reshape(length, groups, span)
    return out.reshape(2 * length, 2 * length)


def third_coarse(length, devices, js):
    modes = third_modes(devices, js).reshape(devices, len(js) // 2, 2)
    theta = 2.0 * np.pi * (modes[..., None] * np.arange(length) % length) / length
    both = np.stack([np.cos(theta), -np.sin(theta)])
    return both.transpose(0, 2, 1, 3, 4).reshape(2 * (len(js) // 2) * devices, 2 * length)


def third_coarse_halo(length, devices, js):
    theta = angles(third_modes(devices, js).reshape(-1), np.arange(length), length)
    return np.concatenate([np.cos(theta), -np.sin(theta)], axis=1)


def lane_order(parts, coarse_parts):
    out = np.zeros((LANE, LANE))
    for h in range(HALO):
        for q in range(parts):
            out[HALO * q + h, parts * h + q] = 1.0
        for j in range(coarse_parts):
            out[LANE // 2 + HALO * j + h, LANE // 2 + coarse_parts * h + j] = 1.0
    return out


def split(x):
    high = x.astype(jnp.bfloat16)
    return high, (x - high.astype(jnp.float32)).astype(jnp.bfloat16)


def dot(a, b):
    return lax.dot_general(a, b, (((1,), (0,)), ((), ())), preferred_element_type=jnp.float32)


def dot_t(a, b):
    return lax.dot_general(a, b, (((1,), (1,)), ((), ())), preferred_element_type=jnp.float32)


def stacked(matrix):
    high, low = two_parts(matrix)
    return np.block([[high, high], [low, np.zeros_like(low)]])


def dot_left(stack, x):
    value = dot(stack, jnp.concatenate(split(x), axis=0))
    rows = stack.shape[0] // 2
    return value[:rows] + value[rows:]


def dot3(a, b):
    (ah, al), (bh, bl) = a, b
    return dot(ah, bh) + (dot(ah, bl) + dot(al, bh))


def load(pairs, sems):
    copies = [pltpu.make_async_copy(a, b, sems.at[i]) for i, (a, b) in enumerate(pairs)]
    for copy in copies:
        copy.start()
    return copies


def send(pairs, sems, first):
    copies = [pltpu.make_async_copy(a, b, sems.at[first + i]) for i, (a, b) in enumerate(pairs)]
    for copy in copies:
        copy.start()
    return copies


def forward_kernel(planes, d_hbm, x_hbm, out_hbm, d, x, out, sems):
    pieces, rows = d.shape[0], d.shape[1] // 2
    parts = [slice(p * LANE, (p + 2) * LANE) for p in range(0, planes, 2)]
    pairs = [(x_hbm.at[at, :], x.at[at, :]) for at in parts]
    copies = load([(d_hbm.at[0], d.at[0])] + pairs + [(d_hbm.at[i], d.at[i]) for i in range(1, pieces)], sems)
    sent = []
    copies[0].wait()
    for piece in range(pieces):
        if piece:
            copies[len(parts) + piece].wait()
        for i, at in enumerate(parts):
            if piece == 0:
                copies[i + 1].wait()
            value = dot_t(d[piece], x[at, :])
            value = value[:rows] + value[rows:]
            for h in range(2):
                out[pl.ds(piece * rows * SUB + 2 * i + h, rows, stride=SUB), :] = value[
                    :, h * LANE : (h + 1) * LANE
                ]
        tall = slice(piece * rows * SUB, (piece + 1) * rows * SUB)
        sent += send([(out.at[tall, :], out_hbm.at[tall, :])], sems, len(copies) + piece)
    for copy in sent:
        copy.wait()


def middle_kernel(sizes, scale, b, *rest):
    (first, second, rows, groups, js, low) = sizes
    count = 9
    away, out_hbm, near, rest = (
        rest[:count],
        rest[count],
        rest[count + 1 : 2 * count + 1],
        rest[2 * count + 1 :],
    )
    out, sems, zh, zl, y, oh, ol, qh, ql = rest
    copies = load(list(zip(away, near)), sems)
    csh, csl, forward, inverse, coarse_inverse, cch, ccl, ch, cl = near
    q_count = 2 * js
    half, quarter = second // 2, second // 4
    for q in range(q_count):
        for g in range(groups // 2):
            for r in range(0, rows, 2):
                at = r * groups + g
                near_half = jnp.concatenate([b[at, q], b[at + groups, q]], axis=0)
                at += groups // 2
                far_half = jnp.concatenate([b[at, q], b[at + groups, q]], axis=0)
                at = slice(q * first + r * SUB, q * first + (r + 2) * SUB)
                lanes = slice(g * LANE, (g + 1) * LANE)
                zh[0, at, lanes], zl[0, at, lanes] = split(near_half + far_half)
                zh[1, at, lanes], zl[1, at, lanes] = split(near_half - far_half)
    for copy in copies[:5]:
        copy.wait()
    wide = 8 * first
    for top in range(0, q_count * first, wide):
        at = slice(top, top + wide)
        for parity in range(2):
            y[parity, at, :] = dot3(
                (zh[parity, at, :], zl[parity, at, :]), (csh[parity], csl[parity])
            )
    mode0 = lax.broadcasted_iota(jnp.int32, (first, second), 0)
    mode0 = jnp.where(mode0 < first // 2, mode0, mode0 - first).astype(jnp.float32)
    lane = lax.broadcasted_iota(jnp.int32, (first, second), 1)
    mode1 = jnp.where(lane < half, lane, lane - half)
    mode1 = jnp.where(mode1 < quarter, 2 * mode1, 2 * (mode1 - quarter) + 1).astype(jnp.float32)
    base = 1.0 + DECAY * (mode0 * mode0 + mode1 * mode1)
    for j in range(js):
        top = j * 2 * first
        re, im = slice(top, top + first), slice(top + first, top + 2 * first)
        cos, sin = slice(0, quarter), slice(quarter, half)
        whole = lambda part, lanes: jnp.concatenate(
            [y[0, part, lanes], y[1, part, lanes]], axis=1
        )
        rc, rs, ic, isn = whole(re, cos), whole(re, sin), whole(im, cos), whole(im, sin)
        wave = jnp.concatenate(
            [
                jnp.concatenate([rc + isn, rc - isn], axis=1),
                jnp.concatenate([ic - rs, ic + rs], axis=1),
            ],
            axis=0,
        )
        spectrum = dot_left(forward[...], wave)
        amp = jnp.where(lane == half, 0.0, scale[j, 1] / (base + scale[j, 0]))
        scaled = spectrum * jnp.concatenate([amp, amp], axis=0)
        field = dot_left(inverse[...], scaled)
        plus, minus = field[:, :half], field[:, half:]
        even, odd = plus + minus, plus - minus
        odd = jnp.concatenate([-odd[first:], odd[:first]], axis=0)
        at = slice(top, top + 2 * first)
        for parity, lanes in enumerate((cos, sin)):
            operand = jnp.concatenate([even[:, lanes], odd[:, lanes]], axis=1)
            oh[parity, at, :], ol[parity, at, :] = split(operand)
        if j < low:
            keep = first // 4
            kept = [
                scaled[at : at + keep, :]
                for at in (0, first - keep, first, 2 * first - keep)
            ]
            band = jnp.concatenate(kept, axis=0)
            low_lane = lax.broadcasted_iota(jnp.int32, (first, quarter), 1) < quarter // 2
            pieces = []
            for at in (0, half):
                upper = pltpu.roll(band[:, at + quarter : at + half], quarter // 2, 1)
                pieces.append(jnp.where(low_lane, band[:, at : at + quarter], upper))
            band = jnp.concatenate(pieces, axis=1)
            field = dot_left(coarse_inverse[...], band)
            value, turned = field[:first], field[first:]
            operand = jnp.concatenate(
                [
                    value[:, :quarter] + value[:, quarter:],
                    turned[:, :quarter] - turned[:, quarter:],
                ],
                axis=1,
            )
            at = slice(j // 2 * first, (j // 2 + 1) * first)
            lanes = slice(j % 2 * half, (j % 2 + 1) * half)
            qh[at, lanes], ql[at, lanes] = split(operand)
    for copy in copies[5:]:
        copy.wait()
    copies = []
    wide = 4 * first
    lane = lax.broadcasted_iota(jnp.int32, (SUB, LANE), 1)
    extra = q_count + low // 2

    def leave(start, stop):
        at = slice(start, stop)
        copies.extend(send([(out.at[:, at], out_hbm.at[:, at])], sems, len(copies)))

    def give(value, start):
        tiles = value.shape[0] // first
        for q in range(tiles):
            for r in range(rows):
                for g in range(groups):
                    at = q * first + r * SUB
                    out[r * groups + g, start + q] = value[
                        at : at + SUB, g * LANE : (g + 1) * LANE
                    ]
        leave(start, start + tiles)

    def halo_columns(value, start, held):
        tiles = value.shape[0] // first
        for r in range(rows):
            for g in range(groups):
                total = held[r, g]
                left = max(g - 1, 0) * LANE
                right = min(g + 1, groups - 1) * LANE
                for q in range(tiles):
                    at = slice(q * first + r * SUB, q * first + (r + 1) * SUB)
                    both = jnp.where(
                        lane < LANE // 2,
                        value[at, right : right + LANE],
                        value[at, left : left + LANE],
                    )
                    to = HALO * (start + q)
                    both = pltpu.roll(both, (to + 2) % LANE, 1)
                    total = jnp.where((lane >= to) & (lane < to + HALO), both, total)
                held[r, g] = total

    def coarse_columns(value, held):
        half_lane = LANE // 2
        for j in range(low):
            for r in range(rows):
                at = slice(j // 2 * first + r * SUB, j // 2 * first + (r + 1) * SUB)
                shift = HALO * j + 2 - j % 2 * half_lane
                to = half_lane + HALO * j
                for g in range(groups):
                    left = max(g - 1, 0) * LANE
                    right = min(g + 1, groups - 1) * LANE
                    left = pltpu.roll(value[at, left : left + LANE], shift % LANE, 1)
                    right = pltpu.roll(
                        value[at, right : right + LANE], (shift + half_lane) % LANE, 1
                    )
                    total = jnp.where((lane >= to) & (lane < to + 2), left, held[r, g])
                    held[r, g] = jnp.where(
                        (lane >= to + 2) & (lane < to + HALO), right, total
                    )

    columns = {
        (r, g): jnp.zeros((SUB, LANE), jnp.float32) for r in range(rows) for g in range(groups)
    }
    coarse = dot3((qh[...], ql[...]), (cch[...], ccl[...]))
    give(coarse, q_count)
    coarse_columns(coarse, columns)
    for top in range(0, q_count * first, wide):
        at = slice(top, top + wide)
        even, odd = (
            dot3((oh[parity, at, :], ol[parity, at, :]), (ch[parity], cl[parity]))
            for parity in range(2)
        )
        value = jnp.concatenate([even + odd, even - odd], axis=1)
        give(value, top // first)
        halo_columns(value, top // first, columns)
    for (r, g), total in columns.items():
        out[r * groups + g, extra] = total
    leave(extra, extra + 1)
    for copy in copies:
        copy.wait()


def gather_modes(b, at, sizes, lh, ll):
    devices, q_count, tiles = sizes
    for i, n in enumerate(at):
        for parity in range(2):
            rows = jnp.concatenate(
                [
                    b[pl.ds(s * tiles * SUB + n, q_count, stride=SUB), :]
                    for s in range(parity, devices, 2)
                ],
                axis=0,
            )
            to = slice(i * LANE, (i + 1) * LANE)
            lh[parity, to, :], ll[parity, to, :] = split(jnp.transpose(rows))


def inverse_pair(i, lh, ll, eh, el, ks, to, cells):
    at = slice(i * cells, (i + 2) * cells)
    even, odd = (
        dot3((lh[parity, at, :], ll[parity, at, :]), (eh[parity], el[parity]))
        for parity in range(2)
    )
    value = jnp.exp(jnp.concatenate([even + odd, even - odd], axis=1))
    for n in range(2):
        put_rows(ks, to + n, SUB, value[n * cells : (n + 1) * cells])


def edge_kernel(sizes, flags, b, *rest):
    (devices, q_count, low, tiles, planes, length) = sizes
    away, (ks, cks, cols, lo, hi), rest = rest[:7], rest[7:12], rest[12:]
    near, (lh, ll, mh, ml, sems) = rest[:7], rest[7:]
    copies = load(list(zip(away, near)), sems)
    eh, el, ceh, cel, order, cwh, cwl = near
    cells, short = LANE, length // 2
    halves, coarse_planes = low // 2, planes // 2
    half = cells // 2
    gather_modes(b, (0, 1, planes - 2, planes - 1), (devices, q_count, tiles), lh, ll)
    for n in range(coarse_planes):
        rows = jnp.concatenate(
            [
                b[pl.ds((q_count + h) * SUB + c * coarse_planes + n, devices, stride=tiles * SUB), :]
                for c in range(2)
                for h in range(halves)
            ],
            axis=0,
        )
        at = slice(n * LANE, (n + 1) * LANE)
        mh[at, :], ml[at, :] = split(jnp.transpose(rows))

    for copy in copies[:4]:
        copy.wait()

    for i in range(0, 4, 2):
        inverse_pair(i, lh, ll, eh, el, ks, i, cells)
    value = dot3((mh[...], ml[...]), (ceh[...], cel[...]))
    for n in range(coarse_planes):
        top = n * cells
        part = value[top : top + half, :short] + value[top + half : top + cells, short:]
        part = jnp.exp(part)
        put_rows(cks, n, SUB, part)

    for copy in copies[4:]:
        copy.wait()
    lane = lax.broadcasted_iota(jnp.int32, (SUB, LANE), 1)
    tile_rows = [b[(s * tiles + tiles - 1) * SUB : (s + 1) * tiles * SUB, :] for s in range(devices)]
    high, rest_part = split(jnp.concatenate(tile_rows, axis=0))
    ordered = dot(high, order[...]) + dot(rest_part, order[...])

    def joined(of, width, start):
        fit = LANE // width
        cells_of = []
        for h in range(HALO):
            parts = []
            for i, s in enumerate(of):
                moved = ordered[s * SUB : (s + 1) * SUB]
                shift = (i % fit * width - start - h * width) % LANE
                moved = pltpu.roll(moved, shift, 1) if shift else moved
                if i % fit == 0:
                    parts.append(moved)
                else:
                    parts[-1] = jnp.where(lane >= i % fit * width, moved, parts[-1])
            cells_of.append(jnp.concatenate(parts, axis=1))
        return split(jnp.concatenate(cells_of, axis=0))

    even, odd = (
        dot3(joined(range(parity, devices, 2), q_count, 0), (eh[parity], el[parity]))
        for parity in range(2)
    )
    value = jnp.exp(jnp.concatenate([even + odd, even - odd], axis=1))
    cols[...] = value
    for h in range(HALO):
        for i, n in enumerate((0, 1, planes - 2, planes - 1)):
            at = h * planes + n
            put_rows(ks, i, halo_row(h, cells), value[at : at + 1, :])
    whole = dot3(joined(range(devices), low, LANE // 2), (cwh[...], cwl[...]))
    for h in range(HALO):
        top = h * SUB
        part = whole[top : top + coarse_planes, :short] + whole[top + coarse_planes : top + SUB, short:]
        part = jnp.exp(part)
        for n in range(coarse_planes):
            put_rows(cks, n, halo_row(h, half), part[n : n + 1, :])
    for held in (ks, cks):
        repeat_sides(flags, held, [(n,) for n in range(4)])
    for edge, of in ((lo, (1, 0)), (hi, (2, 3))):
        at = 0
        for held in (ks, cks):
            count, end = held.shape[1], held.shape[2] - SUB
            for n in of:
                for x in range(count):
                    edge[at : at + end - SUB, :] = held[n, x, SUB:end, :]
                    at += end - SUB
            for x in range(count):
                edge[at + x : at + x + 1, :] = held[of[1], x, SUB - 1 : SUB, :]
                edge[at + count + x : at + count + x + 1, :] = held[of[1], x, end : end + 1, :]
            at += SUB


def halo_row(h, cells):
    return SUB - 2 + h if h < 2 else SUB + cells + h - 2


def source_kernel(planes, pairs, x, out, lo, hi, left, right, held, summed):
    cells = x.shape[0] // planes
    length = x.shape[1]
    half, fourth = cells // 2, cells // 4
    held[...] = dot(x[...], pairs[...])
    for n in range(planes // 2):
        top = 2 * n * cells
        for at in range(0, out.shape[1], LANE):
            lanes = slice(at, at + LANE)
            summed[...] = held[top : top + cells, lanes] + held[top + cells : top + 2 * cells, lanes]
            out[n * half : (n + 1) * half, lanes] = (
                summed[pl.ds(0, half, stride=2), :] + summed[pl.ds(1, half, stride=2), :]
            )
    for edge, plane in ((lo, 0), (hi, planes - 1)):
        edge[:cells, :] = x[plane * cells : (plane + 1) * cells, :].astype(jnp.float32)
        at = plane // 2 * half
        edge[cells:, : length // 2] = out[at : at + fourth, :]
        edge[cells:, length // 2 :] = out[at + fourth : at + half, :]
    for edge, row in ((left, 0), (right, cells - 1)):
        edge[...] = jnp.zeros_like(edge)
        for n in range(planes):
            at = n * cells + (row // SUB * SUB)
            edge[n : n + 1, :] = x[at : at + SUB, :].astype(jnp.float32)[row % SUB : row % SUB + 1]
        for n in range(planes // 2):
            at = n * half + row // 2
            edge[SUB + n : SUB + n + 1, : length // 2] = out[at : at + 1, :]


def beside(parts, ends):
    lane = lax.broadcasted_iota(jnp.int32, parts[0].shape, 1)
    ahead = [pltpu.roll(x, 1, 1) for x in parts]
    behind = [pltpu.roll(x, LANE - 1, 1) for x in parts]
    sums = []
    for i in range(len(parts)):
        left = jnp.where(lane == 0, ahead[i - 1] if i else ends[0], ahead[i])
        right = jnp.where(
            lane == LANE - 1, behind[i + 1] if i + 1 < len(parts) else ends[1], behind[i]
        )
        sums.append(left + right)
    return sums


def first_sweep(tiles, ext, mid, lower, upper, f, store):
    for top in range(0, ext, SUB):
        end = top + SUB
        parts = [mid(x, top, end) for x in range(tiles)]
        for x, both in enumerate(beside(parts, (parts[0], parts[-1]))):
            k = parts[x]
            above = pltpu.roll(k, 1, 0) if top == 0 else mid(x, top - 1, end - 1)
            below = pltpu.roll(k, SUB - 1, 0) if end == ext else mid(x, top + 1, end + 1)
            total = (lower(x, top, end) + upper(x, top, end)) + (above + below) + both
            scale = JACOBI_WEIGHT / (6.0 * k + total)
            u = f(x, top, end) * (2.0 * scale)
            store(x, top, end, u, k * u, scale)


def second_sweep(tiles, ext, k, u, w, r, store):
    for top in range(SUB, ext - SUB, SUB):
        end = top + SUB
        sums = []
        for lower, mid, upper in (u, w):
            parts = [mid(x, top, end) for x in range(tiles)]
            sums.append(
                [
                    both
                    + (lower(x, top, end) + upper(x, top, end))
                    + (mid(x, top - 1, end - 1) + mid(x, top + 1, end + 1))
                    for x, both in enumerate(beside(parts, (0.0, 0.0)))
                ]
            )
        for x in range(tiles):
            coupled = k(x, top, end) * sums[0][x] + sums[1][x]
            value = (2.0 - JACOBI_WEIGHT) * u[1](x, top, end) + r(x, top, end) * coupled
            store(x, top, end, value)


def plane_of(held, *at):
    return lambda x, top, end: held[(*at, x, slice(top, end), slice(None))]


def put_rows(held, to, at, rows):
    for x in range(held.shape[1]):
        held[to, x, at : at + rows.shape[0], :] = rows[:, x * LANE : (x + 1) * LANE]


def repeat_sides(flags, held, at):
    end = held.shape[-2] - SUB

    @pl.when(flags[2] == 1)
    def _():
        for p in at:
            held[(*p, slice(None), slice(SUB - 1, SUB))] = held[(*p, slice(None), slice(SUB, SUB + 1))]

    @pl.when(flags[3] == 1)
    def _():
        for p in at:
            held[(*p, slice(None), slice(end, end + 1))] = held[
                (*p, slice(None), slice(end - 1, end))
            ]


def put_block(fine, held, to, source, row, cells, length):
    if fine:
        put_rows(held, to, SUB, source[row : row + cells, :])
    else:
        half = cells // 2
        put_rows(held, to, SUB, source[row : row + half, :length])
        put_rows(held, to, SUB + half, source[row : row + half, length:])


def layout_kernel(sizes, *rest):
    away, outs, near, sems = rest[:6], rest[6:10], rest[10:16], rest[16]
    for copy in load(list(zip(away, near)), sems):
        copy.wait()
    source, coarse_source, *edges = near
    sides = edges[2:]
    for fine, inner, outer in ((True, *outs[:2]), (False, *outs[2:])):
        planes, cells, length = sizes if fine else [n // 2 for n in sizes]
        f = source if fine else coarse_source
        source_row = 0 if fine else SUB

        def plane(held, to, p):
            put_rows(held, to, SUB, f[p].astype(jnp.float32))
            for side, row in zip(sides, (SUB - 1, SUB + cells)):
                at = source_row + p
                put_rows(held, to, row, side[at : at + 1, :length])

        for p in range(1, planes - 1):
            plane(inner, p - 1, p)
        for group, p in enumerate((0, planes - 1)):
            row = 0 if fine else 2 * cells
            put_block(fine, outer.at[group], 0, edges[group], row, cells, length)
            plane(outer.at[group], 1, p)


def inner_level(sizes, ks, fs, us, ws, rs):
    planes, _, length = sizes
    tiles, ext = ks.shape[1:3]

    def first(p, carry):
        def store(x, top, end, u, w, r):
            at = (p - 1, x, slice(top, end))
            us[at], ws[at], rs[at] = u, w, r

        near = [plane_of(ks, p + i) for i in (0, -1, 1)]
        first_sweep(tiles, ext, *near, plane_of(fs, p - 1), store)
        return carry

    lax.fori_loop(1, planes - 1, first, 0)


def inner_kernel(sizes, shares, flags, b, eh_hbm, el_hbm, edges, cks, cols, fs, cfs, *rest):
    out_hbm, us, ws, rs, cus, cws, crs, ks, eh, el, lh, ll, out, sems = rest
    planes, cells, length = sizes
    tiles, ext = ks.shape[1:3]
    copies = load([(eh_hbm, eh), (el_hbm, el)], sems)
    middle = range(2, planes - 2)
    gather_modes(b, middle, shares, lh, ll)
    for i, p in enumerate((0, 1, planes - 2, planes - 1)):
        ks[p] = edges[i]
    for h in range(HALO):
        for p in middle:
            at = h * planes + p
            put_rows(ks, p, halo_row(h, cells), cols[at : at + 1, :])
    for copy in copies:
        copy.wait()
    for p in range(2, planes - 2, 2):
        inverse_pair(p - 2, lh, ll, eh, el, ks, p, cells)
    repeat_sides(flags, ks, [(p,) for p in middle])
    inner_level(sizes, ks, fs, us, ws, rs)

    def second(p, carry):
        def store(x, top, end, value):
            out[p - 2, top - SUB : end - SUB, x * LANE : (x + 1) * LANE] = value

        u, w = ([plane_of(held, p - 1 + i) for i in (-1, 0, 1)] for held in (us, ws))
        second_sweep(tiles, ext, plane_of(ks, p), u, w, plane_of(rs, p - 1), store)
        return carry

    lax.fori_loop(2, planes - 2, second, 0)
    copies = send([(out, out_hbm.at[2 : planes - 2])], sems, 0)
    inner_level([n // 2 for n in sizes], cks, cfs, cus, cws, crs)
    for copy in copies:
        copy.wait()


def outer_kernel(sizes, flags, *rest):
    kept, coarse_kept, (k_lo, k_hi, _, out, coarse_out), rest = (
        rest[:5],
        rest[5:10],
        rest[10:15],
        rest[15:],
    )
    scratch = (rest[:6], rest[6:])
    levels = (sizes, tuple(n // 2 for n in sizes))
    start = 0
    sent = []
    for size, held, given, target in zip(
        levels, scratch, (kept, coarse_kept), (out, coarse_out)
    ):
        planes = size[0]
        ks, fs, inner_us, inner_ws, inner_rs = given
        halo, us, ws, rs, done, sems = held
        tiles, ext = ks.shape[1:3]
        rows = size[1]
        for group, edge in enumerate((k_lo, k_hi)):
            at = start
            for place in range(2 * tiles):
                to = place * ext + SUB
                halo[group, to : to + rows, :] = edge[at : at + rows, :]
                at += rows
            for x in range(tiles):
                to = (tiles + x) * ext
                halo[group, to + SUB - 1 : to + SUB, :] = edge[at + x : at + x + 1, :]
                to += SUB + rows
                halo[group, to : to + 1, :] = edge[at + tiles + x : at + tiles + x + 1, :]
        start = at + SUB
        for group in range(2):

            @pl.when(flags[group] == 1)
            def _():
                for x in range(tiles):
                    at = (tiles + x) * ext
                    halo[group, at : at + ext, :] = ks[3 * group, x]

        def both_ends(group, carry):
            def halo_plane(slot):
                def get(x, top, end):
                    at = (slot * tiles + x) * ext
                    return halo[group, at + top : at + end, :]

                return get

            inwards = lambda i, count: jnp.where(group == 0, i, count - 1 - i)
            own = [plane_of(ks, inwards(i, 4)) for i in range(2)]
            u, w = (
                [plane_of(new, group, i) for i in range(2)]
                + [plane_of(old, inwards(i, planes - 2)) for i in range(2)]
                for new, old in ((us, inner_us), (ws, inner_ws))
            )
            around = ((halo_plane(1), halo_plane(0), own[0]), (own[0], halo_plane(1), own[1]))
            for i, near in enumerate(around):

                def store(x, top, end, u, w, r):
                    at = (group, i, x, slice(top, end))
                    us[at], ws[at] = u, w
                    if i == 1:
                        rs[group, x, top:end, :] = r

                first_sweep(tiles, ext, *near, plane_of(fs, group, i), store)
            scales = (plane_of(rs, group), plane_of(inner_rs, inwards(0, planes - 2)))
            for i, r in enumerate(scales):

                def store(x, top, end, value):
                    done[group, i, top - SUB : end - SUB, x * LANE : (x + 1) * LANE] = value

                second_sweep(tiles, ext, own[i], u[i : i + 3], w[i : i + 3], r, store)
            return carry

        lax.fori_loop(0, 2, both_ends, 0)
        pairs = [
            (done.at[group, i], target.at[p])
            for group, at in enumerate(((0, 1), (planes - 1, planes - 2)))
            for i, p in enumerate(at)
        ]
        sent += send(pairs, sems, 0)
    for copy in sent:
        copy.wait()


SMEM = pl.BlockSpec(memory_space=pltpu.SMEM)
VMEM = pl.BlockSpec(memory_space=pltpu.VMEM)
AWAY = pl.BlockSpec(memory_space=pltpu.HBM)
ANY = pl.BlockSpec(memory_space=pl.ANY)


def call(kernel, outs, operands, scratch, flops, specs, limit, out_specs=None, aliases=None):
    many = isinstance(outs, (list, tuple))
    written = outs if many else [outs]
    moved = sum(math.prod(x.shape) * x.dtype.itemsize for x in (*operands, *written))
    operands = [
        pltpu.with_memory_space_constraint(x, pltpu.HBM) if spec is AWAY else x
        for x, spec in zip(operands, specs)
    ]
    out_specs = out_specs or [
        VMEM if isinstance(x, jax.ShapeDtypeStruct) else AWAY for x in written
    ]
    return pl.pallas_call(
        kernel,
        out_shape=outs,
        in_specs=specs,
        out_specs=out_specs if many else out_specs[0],
        scratch_shapes=scratch,
        input_output_aliases=aliases or {},
        compiler_params=pltpu.CompilerParams(vmem_limit_bytes=limit * MIB),
        cost_estimate=pl.CostEstimate(flops=flops, bytes_accessed=moved, transcendentals=0),
    )(*operands)


def f32(*shape):
    return jax.ShapeDtypeStruct(shape, jnp.float32)


def room(*arrays):
    return [pltpu.VMEM(x.shape, x.dtype) for x in arrays]


def chain(axis):
    up = [(i, i + 1) for i in range(lax.axis_size(axis) - 1)]
    return up, [(j, i) for i, j in up]


def swap(lo, hi, axis):
    up, down = chain(axis)
    return lax.ppermute(hi, axis, up), lax.ppermute(lo, axis, down)


def held_planes(size, *count):
    planes, cells, length = size
    return f32(*count, length // LANE, cells + 2 * SUB, LANE)


def outer_scratch(size):
    planes, cells, length = size
    return room(
        f32(2, 2 * (length // LANE) * (cells + 2 * SUB), LANE),
        held_planes(size, 2, 2),
        held_planes(size, 2, 2),
        held_planes(size, 2),
        f32(2, 2, cells, length),
    ) + [pltpu.SemaphoreType.DMA((4,))]


def fused_body(noise, source):
    rows, groups = lax.axis_size("row"), lax.axis_size(PLANE)
    devices = rows * groups
    planes, cells, length = noise.shape
    first, second = planes * rows, cells * groups
    bf16 = jnp.bfloat16
    held = length // 2 // devices
    js = list(range(held))
    low = held // 2
    me = lax.axis_index(EVERY)
    row_at, group_at = lax.axis_index("row"), lax.axis_index(PLANE)
    flags = jnp.stack(
        [row_at == 0, row_at == rows - 1, group_at == 0, group_at == groups - 1]
    ).astype(jnp.int32)
    norm = FIELD_SCALE * (float(first) * float(second) * float(length)) ** (-0.5)
    flat = (planes * cells, length)

    pieces = 4
    table = [x.reshape(pieces, -1, length) for x in two_parts(forward_third(length, devices, js))]
    table = np.concatenate(table, axis=1)
    shape = (length * SUB, LANE)
    sent = call(
        functools.partial(forward_kernel, planes),
        pltpu.HBM(shape, jnp.float32),
        (table, noise.reshape(flat)),
        room(table)
        + [
            pltpu.VMEM(flat, bf16),
            pltpu.VMEM(shape, jnp.float32),
            pltpu.SemaphoreType.DMA((2 * pieces + planes // 2,)),
        ],
        4 * length * length * planes * cells,
        [AWAY] * 2,
        12,
    )
    sent, source = lax.optimization_barrier((sent, source))
    sent = sent.reshape(devices, 2 * held, SUB, LANE)
    arrived = lax.all_to_all(sent, EVERY, split_axis=0, concat_axis=0, tiled=True)

    pairs = np.zeros((length, length // 2), np.float32)
    pairs[np.arange(length), np.arange(length) // 2] = 0.125
    level = f32(cells + cells // 4, length)
    side = f32(2 * SUB, length)
    coarse_source, *edges = call(
        functools.partial(source_kernel, planes),
        [f32(planes * cells // 4, length // 2), level, level, side, side],
        (pairs.astype(bf16), source.reshape(flat)),
        [
            pltpu.VMEM((planes * cells, length // 2), jnp.float32),
            pltpu.VMEM((cells, LANE), jnp.float32),
        ],
        planes * cells * length * length,
        [VMEM] * 2,
        12,
    )
    coarse_source = coarse_source.reshape(planes // 2, cells // 2, length // 2)
    edges = (*swap(*edges[:2], "row"), *swap(*edges[2:], PLANE))
    arrived, edges, coarse_source = lax.optimization_barrier((arrived, edges, coarse_source))

    constants = (
        two_parts(second_table(second))
        + (
            stacked(forward_first(first)),
            stacked(inverse_first(first)),
            stacked(inverse_first_coarse(first // 2, rows)),
        )
        + two_parts(second_coarse(second // 2, groups))
        + two_parts(second_table(second).transpose(0, 2, 1))
    )
    tiles = 2 * held + low // 2 + 1
    modes = (me + devices * np.array(js)).astype(jnp.float32)
    weight = jnp.where(modes == 0.0, norm, 2.0 * norm).astype(jnp.float32)
    scale = jnp.stack([DECAY * modes * modes, weight], axis=1)
    block = (2, 2 * held * first, second // 2)
    shape = (devices, tiles, SUB, LANE)
    out = call(
        functools.partial(middle_kernel, (first, second, rows, groups, held, low)),
        pltpu.HBM(shape, jnp.float32),
        (scale, arrived, *constants),
        room(*constants)
        + [
            pltpu.VMEM(shape, jnp.float32),
            pltpu.SemaphoreType.DMA((len(constants),)),
            pltpu.VMEM(block, bf16),
            pltpu.VMEM(block, bf16),
            pltpu.VMEM(block, jnp.float32),
            pltpu.VMEM(block, bf16),
            pltpu.VMEM(block, bf16),
            pltpu.VMEM((low // 2 * first, second), bf16),
            pltpu.VMEM((low // 2 * first, second), bf16),
        ],
        6 * 2 * 2 * held * first * second * (second + 2 * first),
        [SMEM, VMEM] + [AWAY] * len(constants),
        22,
    )
    out, source, coarse_source, edges = lax.optimization_barrier(
        (out, source, coarse_source, edges)
    )
    got = lax.all_to_all(out, EVERY, split_axis=0, concat_axis=0, tiled=True)
    size, coarse_size = noise.shape, coarse_source.shape
    sizes = (size, coarse_size)
    sources = (source, coarse_source, *edges)
    laid = call(
        functools.partial(layout_kernel, size),
        [
            held_planes(s, *count)
            for s in sizes
            for count in ((s[0] - 2,), (2, 2))
        ],
        sources,
        room(*sources) + [pltpu.SemaphoreType.DMA((6,))],
        source.size,
        [AWAY] * 6,
        12,
    )
    got, laid = lax.optimization_barrier((got, laid))

    third = inverse_third(length, devices, js)
    constants = (
        two_parts(third)
        + two_parts(third_coarse(length // 2, devices, js[:low]))
        + (lane_order(2 * held, low).astype(bf16),)
        + two_parts(third_coarse_halo(length // 2, devices, js[:low]))
    )
    edge = f32(sum(2 * (s[2] // LANE) * s[1] + SUB for s in sizes), LANE)
    shares = (devices, 2 * held, tiles)
    got = got.reshape(devices * tiles * SUB, LANE)
    ks, coarse_ks, cols, lo, hi = call(
        functools.partial(edge_kernel, (devices, 2 * held, low, tiles, planes, length)),
        [held_planes(s, 4) for s in sizes] + [f32(HALO * planes, length), edge, edge],
        (flags, got, *constants),
        room(*constants)
        + [pltpu.VMEM((2, 4 * cells, devices * held), bf16)] * 2
        + [pltpu.VMEM((planes // 2 * LANE, devices * low), bf16)] * 2
        + [pltpu.SemaphoreType.DMA((7,))],
        3 * planes * cells * length * length,
        [SMEM, VMEM] + [AWAY] * 7,
        16,
    )
    k_lo, k_hi = swap(lo, hi, "row")
    inner_f, outer_f, coarse_inner_f, coarse_outer_f = laid
    inner, *kept = call(
        functools.partial(inner_kernel, size, shares),
        [pltpu.HBM(size, jnp.float32)] + [held_planes(s, s[0] - 2) for s in sizes for _ in range(3)],
        (flags, got, *constants[:2], ks, coarse_ks, cols, inner_f, coarse_inner_f),
        room(held_planes(size, planes), *constants[:2])
        + [pltpu.VMEM((2, (planes - 4) * cells, devices * held), bf16)] * 2
        + room(f32(planes - 4, cells, length))
        + [pltpu.SemaphoreType.DMA((2,))],
        3 * planes * cells * length * length,
        [SMEM, VMEM] + [AWAY] * 2 + [VMEM] * 5,
        18,
    )
    return call(
        functools.partial(outer_kernel, size),
        [pltpu.HBM(s, jnp.float32) for s in sizes],
        (flags, ks, outer_f, *kept[:3], coarse_ks, coarse_outer_f, *kept[3:], k_lo, k_hi, inner),
        outer_scratch(size) + outer_scratch(coarse_size),
        30 * source.size,
        [SMEM] + [VMEM] * 12 + [AWAY],
        18,
        None,
        {13: 0},
    )


NEIGHBOUR_STEPS = ((1, 0, 0), (-1, 0, 0), (0, 1, 0), (0, -1, 0), (0, 0, 1), (0, 0, -1))


def padded(x, sides, width):
    for axis, dim in sides:
        peers, length = (lax.axis_size(axis), x.shape[dim])
        up = [(i, (i + 1) % peers) for i in range(peers - 1)]
        down = [(j, i) for i, j in up]
        last = lax.slice_in_dim(x, length - width, length, axis=dim)
        leading = lax.slice_in_dim(x, 0, width, axis=dim)
        before = lax.ppermute(last, axis, up)
        after = lax.ppermute(leading, axis, down)
        x = jnp.concatenate([before, x, after], axis=dim)
    return x


def signed_modes(index, length):
    return jnp.where(index < length // 2, index, index - length).astype(jnp.float32)


def amplitude(first_modes, second_modes, third_modes, first_edge, second_edge, third_edge):
    squared = first_modes * first_modes + second_modes * second_modes + third_modes * third_modes
    value = FIELD_SCALE / (1.0 + (2.0 * math.pi * CORRELATION) ** 2 * squared)
    edge = (
        (jnp.abs(first_modes) == first_edge)
        | (jnp.abs(second_modes) == second_edge)
        | (jnp.abs(third_modes) == third_edge)
    )
    return jnp.where(edge, 0.0, value)


def phase_table(count_rows, count_cols, modulus, sign):
    left_index = jnp.arange(count_rows, dtype=jnp.int32)[:, None]
    right_index = jnp.arange(count_cols, dtype=jnp.int32)[None, :]
    angle = 2.0 * math.pi / modulus * (left_index * right_index % modulus).astype(jnp.float32)
    return (jnp.cos(angle), sign * jnp.sin(angle))


def split_length(length):
    outer_len = 2 ** ((length.bit_length() - 1) // 2)
    return (outer_len, length // outer_len)


def real_form(form, left_value, right_value):
    return jnp.einsum(form, left_value, right_value, precision=lax.Precision.HIGHEST)


def complex_form(form, left_real, left_imag, right_real, right_imag):
    real_part = real_form(form, left_real, right_real) - real_form(form, left_imag, right_imag)
    imag_part = real_form(form, left_real, right_imag) + real_form(form, left_imag, right_real)
    return (real_part, imag_part)


def merge_pair(values, out_form, first_letter):
    merge_at = out_form.index(first_letter)
    out_dims = list(values.shape)
    merged = (
        out_dims[:merge_at]
        + [out_dims[merge_at] * out_dims[merge_at + 1]]
        + out_dims[merge_at + 2 :]
    )
    return values.reshape(merged)


def forward_axis(real_part, imag_part, lead_form, out_form, kept_modes):
    length = real_part.shape[-1]
    outer_len, inner_len = split_length(length)
    split_shape = real_part.shape[:-1] + (outer_len, inner_len)
    outer_real, outer_imag = phase_table(outer_len, outer_len, outer_len, -1.0)
    twist_real, twist_imag = phase_table(outer_len, inner_len, length, -1.0)
    inner_real, inner_imag = phase_table(inner_len, kept_modes // outer_len, inner_len, -1.0)
    first_form = lead_form + "ab,ai->" + lead_form + "ib"
    split_real = real_part.reshape(split_shape)
    if imag_part is None:
        section_real = real_form(first_form, split_real, outer_real)
        section_imag = real_form(first_form, split_real, outer_imag)
    else:
        section_real, section_imag = complex_form(
            first_form, split_real, imag_part.reshape(split_shape), outer_real, outer_imag
        )
    turned_real = section_real * twist_real - section_imag * twist_imag
    turned_imag = section_real * twist_imag + section_imag * twist_real
    result_real, result_imag = complex_form(
        lead_form + "ib,bj->" + out_form, turned_real, turned_imag, inner_real, inner_imag
    )
    return (merge_pair(result_real, out_form, "j"), merge_pair(result_imag, out_form, "j"))


def inverse_axis(real_part, imag_part, length, lead_form, out_form, real_only):
    kept_modes = real_part.shape[-1]
    outer_len, inner_len = split_length(length)
    split_shape = real_part.shape[:-1] + (kept_modes // outer_len, outer_len)
    inner_real, inner_imag = phase_table(kept_modes // outer_len, inner_len, inner_len, 1.0)
    twist_real, twist_imag = phase_table(outer_len, inner_len, length, 1.0)
    outer_real, outer_imag = phase_table(outer_len, outer_len, outer_len, 1.0)
    section_real, section_imag = complex_form(
        lead_form + "ji,jb->" + lead_form + "ib",
        real_part.reshape(split_shape),
        imag_part.reshape(split_shape),
        inner_real,
        inner_imag,
    )
    turned_real = section_real * twist_real - section_imag * twist_imag
    turned_imag = section_real * twist_imag + section_imag * twist_real
    second_form = lead_form + "ib,ia->" + out_form
    if real_only:
        result = real_form(second_form, turned_real, outer_real) - real_form(
            second_form, turned_imag, outer_imag
        )
        return merge_pair(result, out_form, "a")
    result_real, result_imag = complex_form(
        second_form, turned_real, turned_imag, outer_real, outer_imag
    )
    return (merge_pair(result_real, out_form, "a"), merge_pair(result_imag, out_form, "a"))


def low_band(values, half_coarse, fine_len):
    return jnp.concatenate(
        [values[:, :, :half_coarse], values[:, :, fine_len - half_coarse :]], axis=2
    )


def window(values, margin, offset):
    return values[
        margin + offset[0] : values.shape[0] - margin + offset[0],
        margin + offset[1] : values.shape[1] - margin + offset[1],
        margin + offset[2] : values.shape[2] - margin + offset[2],
    ]


def face_weight(center, beside):
    return jnp.where(beside > 0.0, 0.5 * (center + beside), center)


def smooth_twice(kappa, source):
    no_shift = (0, 0, 0)
    center = window(kappa, 1, no_shift)
    faces = [face_weight(center, window(kappa, 1, offset)) for offset in NEIGHBOUR_STEPS]
    diagonal = faces[0] + faces[1] + faces[2] + faces[3] + faces[4] + faces[5]
    guarded = jnp.where(center > 0.0, diagonal, 1.0)
    first_sweep = JACOBI_WEIGHT * window(source, 1, no_shift) / guarded
    inner_first = window(first_sweep, 1, no_shift)
    inner_diagonal = window(diagonal, 1, no_shift)
    coupled = jnp.zeros_like(inner_first)
    for face_value, offset in zip(faces, NEIGHBOUR_STEPS):
        coupled = coupled + window(face_value, 1, no_shift) * window(first_sweep, 1, offset)
    residual = window(source, 2, no_shift) - inner_diagonal * inner_first + coupled
    return inner_first + JACOBI_WEIGHT * residual / inner_diagonal


def pad_depth(values):
    return jnp.pad(values, ((0, 0), (0, 0), (2, 2)))


def plain_body(noise, source):
    row_at = lax.axis_index("row")
    group_at = lax.axis_index(("level", "col"))
    fine_field = noise.astype(jnp.float32)
    fine_len = fine_field.shape[-1]
    coarse_len = fine_len // 2
    half_coarse = coarse_len // 2
    kept_modes = fine_len // 2
    real_part, imag_part = forward_axis(fine_field, None, "pq", "pjiq", kept_modes)
    real_part, imag_part = (
        lax.all_to_all(real_part, ("level", "col"), split_axis=1, concat_axis=2, tiled=True),
        lax.all_to_all(imag_part, ("level", "col"), split_axis=1, concat_axis=2, tiled=True),
    )
    real_part, imag_part = forward_axis(real_part, imag_part, "pq", "jiqp", fine_len)
    real_part, imag_part = (
        lax.all_to_all(real_part, "row", split_axis=0, concat_axis=2, tiled=True),
        lax.all_to_all(imag_part, "row", split_axis=0, concat_axis=2, tiled=True),
    )
    slab_len = real_part.shape[-1]
    coarse_slab = slab_len // 2
    half_slab = coarse_slab // 2
    real_part, imag_part = forward_axis(real_part, imag_part, "pq", "pqji", slab_len)
    second_count = real_part.shape[0]
    third_count = real_part.shape[1]
    wave_second = signed_modes(
        row_at * second_count + jnp.arange(second_count, dtype=jnp.int32), fine_len
    )[:, None, None]
    third_index = group_at * third_count + jnp.arange(third_count, dtype=jnp.int32)
    wave_third = signed_modes(third_index, fine_len)[None, :, None]
    spread = 2.0
    mirror_weight = jnp.where(third_index == 0, 1.0, spread).astype(jnp.float32)[None, :, None]
    norm_factor = (float(slab_len) * float(fine_len) * float(fine_len)) ** (-0.5)
    wave_first = signed_modes(jnp.arange(slab_len, dtype=jnp.int32), slab_len)[None, None, :]
    fine_scale = (
        amplitude(
            wave_second, wave_third, wave_first, fine_len / 2.0, fine_len / 2.0, slab_len / 2.0
        )
        * mirror_weight
        * norm_factor
    )
    coarse_first = signed_modes(jnp.arange(coarse_slab, dtype=jnp.int32), coarse_slab)[
        None, None, :
    ]
    coarse_scale = (
        amplitude(
            wave_second,
            wave_third,
            coarse_first,
            coarse_len / 2.0,
            coarse_len / 2.0,
            coarse_slab / 2.0,
        )
        * mirror_weight
        * norm_factor
    )
    coarse_real = low_band(real_part, half_slab, slab_len) * coarse_scale
    coarse_imag = low_band(imag_part, half_slab, slab_len) * coarse_scale
    fine_real, fine_imag = inverse_axis(
        real_part * fine_scale, imag_part * fine_scale, slab_len, "pq", "abqp", False
    )
    coarse_real, coarse_imag = inverse_axis(
        coarse_real, coarse_imag, coarse_slab, "pq", "abqp", False
    )
    fine_real, fine_imag, coarse_real, coarse_imag = (
        lax.all_to_all(fine_real, "row", split_axis=0, concat_axis=2, tiled=True),
        lax.all_to_all(fine_imag, "row", split_axis=0, concat_axis=2, tiled=True),
        lax.all_to_all(coarse_real, "row", split_axis=0, concat_axis=2, tiled=True),
        lax.all_to_all(coarse_imag, "row", split_axis=0, concat_axis=2, tiled=True),
    )
    coarse_real = low_band(coarse_real, half_coarse, fine_len)
    coarse_imag = low_band(coarse_imag, half_coarse, fine_len)
    fine_real, fine_imag = inverse_axis(fine_real, fine_imag, fine_len, "pq", "pabq", False)
    coarse_real, coarse_imag = inverse_axis(
        coarse_real, coarse_imag, coarse_len, "pq", "pabq", False
    )
    fine_real, fine_imag, coarse_real, coarse_imag = (
        lax.all_to_all(fine_real, ("level", "col"), split_axis=1, concat_axis=2, tiled=True),
        lax.all_to_all(fine_imag, ("level", "col"), split_axis=1, concat_axis=2, tiled=True),
        lax.all_to_all(coarse_real, ("level", "col"), split_axis=1, concat_axis=2, tiled=True),
        lax.all_to_all(coarse_imag, ("level", "col"), split_axis=1, concat_axis=2, tiled=True),
    )
    coarse_real = coarse_real[:, :, :half_coarse]
    coarse_imag = coarse_imag[:, :, :half_coarse]
    fine_log = inverse_axis(fine_real, fine_imag, fine_len, "pq", "pqab", True)
    coarse_log = inverse_axis(coarse_real, coarse_imag, coarse_len, "pq", "pqab", True)
    fine_kappa = jnp.exp(fine_log)
    coarse_kappa = jnp.exp(coarse_log)
    fine_source = source.astype(jnp.float32)
    coarse_rows = coarse_log.shape[0]
    coarse_cols = coarse_log.shape[1]
    coarse_source = fine_source.reshape(coarse_rows, 2, coarse_cols, 2, coarse_len, 2).mean(
        axis=(1, 3, 5)
    )
    fine_kappa, fine_source, coarse_kappa, coarse_source = (
        padded(fine_kappa, (("row", 0), (("level", "col"), 1)), 2),
        padded(fine_source, (("row", 0), (("level", "col"), 1)), 2),
        padded(coarse_kappa, (("row", 0), (("level", "col"), 1)), 2),
        padded(coarse_source, (("row", 0), (("level", "col"), 1)), 2),
    )
    fine_pressure = smooth_twice(pad_depth(fine_kappa), pad_depth(fine_source))
    coarse_pressure = smooth_twice(pad_depth(coarse_kappa), pad_depth(coarse_source))
    return (fine_pressure, coarse_pressure)


def body(noise, source):
    planes, cells, length = noise.shape
    rows, groups = lax.axis_size("row"), lax.axis_size(PLANE)
    modes = length // 2 // (rows * groups)
    fills = planes == SUB and cells == LANE and 2 * HALO * modes == LANE // 2
    if fills and length % (4 * LANE) == 0 and rows % 2 == 0 and groups % 4 == 0:
        return fused_body(noise, source)
    return plain_body(noise, source)


def solution(mesh):
    return jax.shard_map(
        body,
        mesh=mesh,
        in_specs=(P("row", ("level", "col"), None), P("row", ("level", "col"), None)),
        out_specs=(P("row", ("level", "col"), None), P("row", ("level", "col"), None)),
        check_vma=False,
    )
```

```python
import functools
import math

import jax
import jax.numpy as jnp
import numpy as np
from jax import lax
from jax.experimental import pallas as pl
from jax.experimental.pallas import tpu as pltpu
from jax.sharding import PartitionSpec as P

JACOBI_WEIGHT = 2.0 / 3.0
CORRELATION = 0.2
FIELD_SCALE = 0.3
DECAY = (2.0 * math.pi * CORRELATION) ** 2
EVERY = ("row", "level", "col")
PLANE = ("level", "col")
MIB = 1 << 20
SUB, LANE = 8, 128
HALO = 4


def two_parts(matrix):
    high = matrix.astype(jnp.bfloat16)
    low = (matrix - high.astype(np.float64)).astype(jnp.bfloat16)
    return high, low


def angles(rows, cols, length):
    return 2.0 * np.pi * (np.outer(rows, cols) % length) / length


def third_modes(devices, js):
    return np.array([[d + devices * j for j in js] for d in range(devices)])


def forward_third(length, devices, js):
    theta = angles(third_modes(devices, js).reshape(-1), np.arange(length), length)
    return np.stack([np.cos(theta), -np.sin(theta)], axis=1).reshape(-1, length)


def inverse_third(length, devices, js):
    modes = third_modes(devices, js).reshape(devices // 2, 2, len(js)).transpose(1, 0, 2)
    theta = 2.0 * np.pi * (modes[..., None] * np.arange(length // 2) % length) / length
    both = np.stack([np.cos(theta), -np.sin(theta)], axis=3)
    return both.reshape(2, -1, length // 2)


def second_modes(length):
    return np.arange(length // 2).reshape(-1, 2).T


def second_table(length):
    theta = second_modes(length)[:, None, :] * np.arange(length // 2)[None, :, None]
    theta = 2.0 * np.pi * (theta % length) / length
    return np.concatenate([np.cos(theta), np.sin(theta)], axis=2)


def forward_first(length):
    theta = angles(np.arange(length), np.arange(length), length)
    cos, sin = np.cos(theta), np.sin(theta)
    return np.block([[cos, sin], [-sin, cos]])


def inverse_first(length):
    theta = angles(np.arange(length), np.arange(length), length)
    cos, sin = np.cos(theta), np.sin(theta)
    cos[:, length // 2] = 0.0
    sin[:, length // 2] = 0.0
    return np.block([[cos, -sin], [sin, cos]])


def inverse_first_coarse(length, rows):
    full = inverse_first(length)
    value = full.reshape(2, rows, length // rows, 2 * length)
    turned = np.concatenate([-full[length:], full[:length]]).reshape(value.shape)
    order = lambda x: x.transpose(1, 0, 2, 3).reshape(2 * length, 2 * length)
    return np.concatenate([order(value), order(turned)])


def second_coarse(length, groups):
    theta = angles(second_modes(length).reshape(-1), np.arange(length), length)
    table = np.concatenate([np.cos(theta), np.sin(theta)])
    span = length // groups
    out = np.zeros((2, length, groups, 2, span))
    for pair in range(2):
        out[pair, :, :, pair, :] = table.reshape(length, groups, span)
    return out.reshape(2 * length, 2 * length)


def third_coarse(length, devices, js):
    modes = third_modes(devices, js).reshape(devices, len(js) // 2, 2)
    theta = 2.0 * np.pi * (modes[..., None] * np.arange(length) % length) / length
    both = np.stack([np.cos(theta), -np.sin(theta)])
    return both.transpose(0, 2, 1, 3, 4).reshape(2 * (len(js) // 2) * devices, 2 * length)


def third_coarse_halo(length, devices, js):
    theta = angles(third_modes(devices, js).reshape(-1), np.arange(length), length)
    return np.concatenate([np.cos(theta), -np.sin(theta)], axis=1)


def lane_order(parts, coarse_parts):
    out = np.zeros((LANE, LANE))
    for h in range(HALO):
        for q in range(parts):
            out[HALO * q + h, parts * h + q] = 1.0
        for j in range(coarse_parts):
            out[LANE // 2 + HALO * j + h, LANE // 2 + coarse_parts * h + j] = 1.0
    return out


def split(x):
    high = x.astype(jnp.bfloat16)
    return high, (x - high.astype(jnp.float32)).astype(jnp.bfloat16)


def dot(a, b):
    return lax.dot_general(a, b, (((1,), (0,)), ((), ())), preferred_element_type=jnp.float32)


def dot_t(a, b):
    return lax.dot_general(a, b, (((1,), (1,)), ((), ())), preferred_element_type=jnp.float32)


def stacked(matrix):
    high, low = two_parts(matrix)
    return np.block([[high, high], [low, np.zeros_like(low)]])


def dot_left(stack, x):
    value = dot(stack, jnp.concatenate(split(x), axis=0))
    rows = stack.shape[0] // 2
    return value[:rows] + value[rows:]


def dot3(a, b):
    (ah, al), (bh, bl) = a, b
    return dot(ah, bh) + (dot(ah, bl) + dot(al, bh))


def load(pairs, sems):
    copies = [pltpu.make_async_copy(a, b, sems.at[i]) for i, (a, b) in enumerate(pairs)]
    for copy in copies:
        copy.start()
    return copies


def send(pairs, sems, first):
    copies = [pltpu.make_async_copy(a, b, sems.at[first + i]) for i, (a, b) in enumerate(pairs)]
    for copy in copies:
        copy.start()
    return copies


def forward_kernel(planes, d_hbm, x_hbm, out_hbm, d, x, out, sems):
    pieces, rows = d.shape[0], d.shape[1] // 2
    parts = [slice(p * LANE, (p + 2) * LANE) for p in range(0, planes, 2)]
    pairs = [(x_hbm.at[at, :], x.at[at, :]) for at in parts]
    copies = load([(d_hbm.at[0], d.at[0])] + pairs + [(d_hbm.at[i], d.at[i]) for i in range(1, pieces)], sems)
    sent = []
    copies[0].wait()
    for piece in range(pieces):
        if piece:
            copies[len(parts) + piece].wait()
        for i, at in enumerate(parts):
            if piece == 0:
                copies[i + 1].wait()
            value = dot_t(d[piece], x[at, :])
            value = value[:rows] + value[rows:]
            for h in range(2):
                out[pl.ds(piece * rows * SUB + 2 * i + h, rows, stride=SUB), :] = value[
                    :, h * LANE : (h + 1) * LANE
                ]
        tall = slice(piece * rows * SUB, (piece + 1) * rows * SUB)
        sent += send([(out.at[tall, :], out_hbm.at[tall, :])], sems, len(copies) + piece)
    for copy in sent:
        copy.wait()


def middle_kernel(sizes, scale, b, *rest):
    (first, second, rows, groups, js, low) = sizes
    count = 9
    away, out_hbm, near, rest = (
        rest[:count],
        rest[count],
        rest[count + 1 : 2 * count + 1],
        rest[2 * count + 1 :],
    )
    out, sems, zh, zl, y, oh, ol, qh, ql = rest
    copies = load(list(zip(away, near)), sems)
    csh, csl, forward, inverse, coarse_inverse, cch, ccl, ch, cl = near
    q_count = 2 * js
    half, quarter = second // 2, second // 4
    for q in range(q_count):
        for g in range(groups // 2):
            for r in range(0, rows, 2):
                at = r * groups + g
                near_half = jnp.concatenate([b[at, q], b[at + groups, q]], axis=0)
                at += groups // 2
                far_half = jnp.concatenate([b[at, q], b[at + groups, q]], axis=0)
                at = slice(q * first + r * SUB, q * first + (r + 2) * SUB)
                lanes = slice(g * LANE, (g + 1) * LANE)
                zh[0, at, lanes], zl[0, at, lanes] = split(near_half + far_half)
                zh[1, at, lanes], zl[1, at, lanes] = split(near_half - far_half)
    for copy in copies[:5]:
        copy.wait()
    wide = 8 * first
    for top in range(0, q_count * first, wide):
        at = slice(top, top + wide)
        for parity in range(2):
            y[parity, at, :] = dot3(
                (zh[parity, at, :], zl[parity, at, :]), (csh[parity], csl[parity])
            )
    mode0 = lax.broadcasted_iota(jnp.int32, (first, second), 0)
    mode0 = jnp.where(mode0 < first // 2, mode0, mode0 - first).astype(jnp.float32)
    lane = lax.broadcasted_iota(jnp.int32, (first, second), 1)
    mode1 = jnp.where(lane < half, lane, lane - half)
    mode1 = jnp.where(mode1 < quarter, 2 * mode1, 2 * (mode1 - quarter) + 1).astype(jnp.float32)
    base = 1.0 + DECAY * (mode0 * mode0 + mode1 * mode1)
    for j in range(js):
        top = j * 2 * first
        re, im = slice(top, top + first), slice(top + first, top + 2 * first)
        cos, sin = slice(0, quarter), slice(quarter, half)
        whole = lambda part, lanes: jnp.concatenate(
            [y[0, part, lanes], y[1, part, lanes]], axis=1
        )
        rc, rs, ic, isn = whole(re, cos), whole(re, sin), whole(im, cos), whole(im, sin)
        wave = jnp.concatenate(
            [
                jnp.concatenate([rc + isn, rc - isn], axis=1),
                jnp.concatenate([ic - rs, ic + rs], axis=1),
            ],
            axis=0,
        )
        spectrum = dot_left(forward[...], wave)
        amp = jnp.where(lane == half, 0.0, scale[j, 1] / (base + scale[j, 0]))
        scaled = spectrum * jnp.concatenate([amp, amp], axis=0)
        field = dot_left(inverse[...], scaled)
        plus, minus = field[:, :half], field[:, half:]
        even, odd = plus + minus, plus - minus
        odd = jnp.concatenate([-odd[first:], odd[:first]], axis=0)
        at = slice(top, top + 2 * first)
        for parity, lanes in enumerate((cos, sin)):
            operand = jnp.concatenate([even[:, lanes], odd[:, lanes]], axis=1)
            oh[parity, at, :], ol[parity, at, :] = split(operand)
        if j < low:
            keep = first // 4
            kept = [
                scaled[at : at + keep, :]
                for at in (0, first - keep, first, 2 * first - keep)
            ]
            band = jnp.concatenate(kept, axis=0)
            low_lane = lax.broadcasted_iota(jnp.int32, (first, quarter), 1) < quarter // 2
            pieces = []
            for at in (0, half):
                upper = pltpu.roll(band[:, at + quarter : at + half], quarter // 2, 1)
                pieces.append(jnp.where(low_lane, band[:, at : at + quarter], upper))
            band = jnp.concatenate(pieces, axis=1)
            field = dot_left(coarse_inverse[...], band)
            value, turned = field[:first], field[first:]
            operand = jnp.concatenate(
                [
                    value[:, :quarter] + value[:, quarter:],
                    turned[:, :quarter] - turned[:, quarter:],
                ],
                axis=1,
            )
            at = slice(j // 2 * first, (j // 2 + 1) * first)
            lanes = slice(j % 2 * half, (j % 2 + 1) * half)
            qh[at, lanes], ql[at, lanes] = split(operand)
    for copy in copies[5:]:
        copy.wait()
    copies = []
    wide = 4 * first
    lane = lax.broadcasted_iota(jnp.int32, (SUB, LANE), 1)
    extra = q_count + low // 2

    def leave(start, stop):
        at = slice(start, stop)
        copies.extend(send([(out.at[:, at], out_hbm.at[:, at])], sems, len(copies)))

    def give(value, start):
        tiles = value.shape[0] // first
        for q in range(tiles):
            for r in range(rows):
                for g in range(groups):
                    at = q * first + r * SUB
                    out[r * groups + g, start + q] = value[
                        at : at + SUB, g * LANE : (g + 1) * LANE
                    ]
        leave(start, start + tiles)

    def halo_columns(value, start, held):
        tiles = value.shape[0] // first
        for r in range(rows):
            for g in range(groups):
                total = held[r, g]
                left = max(g - 1, 0) * LANE
                right = min(g + 1, groups - 1) * LANE
                for q in range(tiles):
                    at = slice(q * first + r * SUB, q * first + (r + 1) * SUB)
                    both = jnp.where(
                        lane < LANE // 2,
                        value[at, right : right + LANE],
                        value[at, left : left + LANE],
                    )
                    to = HALO * (start + q)
                    both = pltpu.roll(both, (to + 2) % LANE, 1)
                    total = jnp.where((lane >= to) & (lane < to + HALO), both, total)
                held[r, g] = total

    def coarse_columns(value, held):
        half_lane = LANE // 2
        for j in range(low):
            for r in range(rows):
                at = slice(j // 2 * first + r * SUB, j // 2 * first + (r + 1) * SUB)
                shift = HALO * j + 2 - j % 2 * half_lane
                to = half_lane + HALO * j
                for g in range(groups):
                    left = max(g - 1, 0) * LANE
                    right = min(g + 1, groups - 1) * LANE
                    left = pltpu.roll(value[at, left : left + LANE], shift % LANE, 1)
                    right = pltpu.roll(
                        value[at, right : right + LANE], (shift + half_lane) % LANE, 1
                    )
                    total = jnp.where((lane >= to) & (lane < to + 2), left, held[r, g])
                    held[r, g] = jnp.where(
                        (lane >= to + 2) & (lane < to + HALO), right, total
                    )

    columns = {
        (r, g): jnp.zeros((SUB, LANE), jnp.float32) for r in range(rows) for g in range(groups)
    }
    coarse = dot3((qh[...], ql[...]), (cch[...], ccl[...]))
    give(coarse, q_count)
    coarse_columns(coarse, columns)
    for top in range(0, q_count * first, wide):
        at = slice(top, top + wide)
        even, odd = (
            dot3((oh[parity, at, :], ol[parity, at, :]), (ch[parity], cl[parity]))
            for parity in range(2)
        )
        value = jnp.concatenate([even + odd, even - odd], axis=1)
        give(value, top // first)
        halo_columns(value, top // first, columns)
    for (r, g), total in columns.items():
        out[r * groups + g, extra] = total
    leave(extra, extra + 1)
    for copy in copies:
        copy.wait()


def gather_modes(b, at, sizes, lh, ll):
    devices, q_count, tiles = sizes
    for i, n in enumerate(at):
        for parity in range(2):
            rows = jnp.concatenate(
                [
                    b[pl.ds(s * tiles * SUB + n, q_count, stride=SUB), :]
                    for s in range(parity, devices, 2)
                ],
                axis=0,
            )
            to = slice(i * LANE, (i + 1) * LANE)
            lh[parity, to, :], ll[parity, to, :] = split(jnp.transpose(rows))


def inverse_pair(i, lh, ll, eh, el, ks, to, cells):
    at = slice(i * cells, (i + 2) * cells)
    even, odd = (
        dot3((lh[parity, at, :], ll[parity, at, :]), (eh[parity], el[parity]))
        for parity in range(2)
    )
    value = jnp.exp(jnp.concatenate([even + odd, even - odd], axis=1))
    for n in range(2):
        put_rows(ks, to + n, SUB, value[n * cells : (n + 1) * cells])


def edge_kernel(sizes, flags, b, *rest):
    (devices, q_count, low, tiles, planes, length) = sizes
    away, (ks, cks, cols, far, near_edge), rest = rest[:7], rest[7:12], rest[12:]
    near, (lh, ll, mh, ml, sems) = rest[:7], rest[7:]
    copies = load(list(zip(away, near)), sems)
    eh, el, ceh, cel, order, cwh, cwl = near
    cells, short = LANE, length // 2
    halves, coarse_planes = low // 2, planes // 2
    half = cells // 2
    gather_modes(b, (0, 1, planes - 2, planes - 1), (devices, q_count, tiles), lh, ll)
    for n in range(coarse_planes):
        rows = jnp.concatenate(
            [
                b[pl.ds((q_count + h) * SUB + c * coarse_planes + n, devices, stride=tiles * SUB), :]
                for c in range(2)
                for h in range(halves)
            ],
            axis=0,
        )
        at = slice(n * LANE, (n + 1) * LANE)
        mh[at, :], ml[at, :] = split(jnp.transpose(rows))

    for copy in copies[:4]:
        copy.wait()

    for i in range(0, 4, 2):
        inverse_pair(i, lh, ll, eh, el, ks, i, cells)
    value = dot3((mh[...], ml[...]), (ceh[...], cel[...]))
    for n in range(coarse_planes):
        top = n * cells
        part = value[top : top + half, :short] + value[top + half : top + cells, short:]
        part = jnp.exp(part)
        put_rows(cks, n, SUB, part)

    for copy in copies[4:]:
        copy.wait()
    lane = lax.broadcasted_iota(jnp.int32, (SUB, LANE), 1)
    tile_rows = [b[(s * tiles + tiles - 1) * SUB : (s + 1) * tiles * SUB, :] for s in range(devices)]
    high, rest_part = split(jnp.concatenate(tile_rows, axis=0))
    ordered = dot(high, order[...]) + dot(rest_part, order[...])

    def joined(of, width, start):
        fit = LANE // width
        cells_of = []
        for h in range(HALO):
            parts = []
            for i, s in enumerate(of):
                moved = ordered[s * SUB : (s + 1) * SUB]
                shift = (i % fit * width - start - h * width) % LANE
                moved = pltpu.roll(moved, shift, 1) if shift else moved
                if i % fit == 0:
                    parts.append(moved)
                else:
                    parts[-1] = jnp.where(lane >= i % fit * width, moved, parts[-1])
            cells_of.append(jnp.concatenate(parts, axis=1))
        return split(jnp.concatenate(cells_of, axis=0))

    even, odd = (
        dot3(joined(range(parity, devices, 2), q_count, 0), (eh[parity], el[parity]))
        for parity in range(2)
    )
    value = jnp.exp(jnp.concatenate([even + odd, even - odd], axis=1))
    cols[...] = value
    for h in range(HALO):
        for i, n in enumerate((0, 1, planes - 2, planes - 1)):
            at = h * planes + n
            put_rows(ks, i, halo_row(h, cells), value[at : at + 1, :])
    whole = dot3(joined(range(devices), low, LANE // 2), (cwh[...], cwl[...]))
    for h in range(HALO):
        top = h * SUB
        part = whole[top : top + coarse_planes, :short] + whole[top + coarse_planes : top + SUB, short:]
        part = jnp.exp(part)
        for n in range(coarse_planes):
            put_rows(cks, n, halo_row(h, half), part[n : n + 1, :])
    for held in (ks, cks):
        repeat_sides(flags, held, [(n,) for n in range(4)])
    odd_row = flags[4] == 1
    low_end = (jnp.where(odd_row, 2, 1), jnp.where(odd_row, 3, 0))
    high_end = (jnp.where(odd_row, 1, 2), jnp.where(odd_row, 0, 3))
    for edge, of in ((far, low_end), (near_edge, high_end)):
        at = 0
        for held in (ks, cks):
            count, end = held.shape[1], held.shape[2] - SUB
            for n in of:
                for x in range(count):
                    edge[at : at + end - SUB, :] = held[n, x, SUB:end, :]
                    at += end - SUB
            for x in range(count):
                edge[at + x : at + x + 1, :] = held[of[1], x, SUB - 1 : SUB, :]
                edge[at + count + x : at + count + x + 1, :] = held[of[1], x, end : end + 1, :]
            at += SUB


def halo_row(h, cells):
    return SUB - 2 + h if h < 2 else SUB + cells + h - 2


def source_kernel(planes, pairs, x, out, lo, hi, left, right, held, summed):
    cells = x.shape[0] // planes
    length = x.shape[1]
    half, fourth = cells // 2, cells // 4
    held[...] = dot(x[...], pairs[...])
    for n in range(planes // 2):
        top = 2 * n * cells
        for at in range(0, out.shape[1], LANE):
            lanes = slice(at, at + LANE)
            summed[...] = held[top : top + cells, lanes] + held[top + cells : top + 2 * cells, lanes]
            out[n * half : (n + 1) * half, lanes] = (
                summed[pl.ds(0, half, stride=2), :] + summed[pl.ds(1, half, stride=2), :]
            )
    for edge, plane in ((lo, 0), (hi, planes - 1)):
        edge[:cells, :] = x[plane * cells : (plane + 1) * cells, :].astype(jnp.float32)
        at = plane // 2 * half
        edge[cells:, : length // 2] = out[at : at + fourth, :]
        edge[cells:, length // 2 :] = out[at + fourth : at + half, :]
    for edge, row in ((left, 0), (right, cells - 1)):
        edge[...] = jnp.zeros_like(edge)
        for n in range(planes):
            at = n * cells + (row // SUB * SUB)
            edge[n : n + 1, :] = x[at : at + SUB, :].astype(jnp.float32)[row % SUB : row % SUB + 1]
        for n in range(planes // 2):
            at = n * half + row // 2
            edge[SUB + n : SUB + n + 1, : length // 2] = out[at : at + 1, :]


def beside(parts, ends):
    lane = lax.broadcasted_iota(jnp.int32, parts[0].shape, 1)
    ahead = [pltpu.roll(x, 1, 1) for x in parts]
    behind = [pltpu.roll(x, LANE - 1, 1) for x in parts]
    sums = []
    for i in range(len(parts)):
        left = jnp.where(lane == 0, ahead[i - 1] if i else ends[0], ahead[i])
        right = jnp.where(
            lane == LANE - 1, behind[i + 1] if i + 1 < len(parts) else ends[1], behind[i]
        )
        sums.append(left + right)
    return sums


def first_sweep(tiles, ext, mid, lower, upper, f, store):
    for top in range(0, ext, SUB):
        end = top + SUB
        parts = [mid(x, top, end) for x in range(tiles)]
        for x, both in enumerate(beside(parts, (parts[0], parts[-1]))):
            k = parts[x]
            above = pltpu.roll(k, 1, 0) if top == 0 else mid(x, top - 1, end - 1)
            below = pltpu.roll(k, SUB - 1, 0) if end == ext else mid(x, top + 1, end + 1)
            total = (lower(x, top, end) + upper(x, top, end)) + (above + below) + both
            scale = JACOBI_WEIGHT / (6.0 * k + total)
            u = f(x, top, end) * (2.0 * scale)
            store(x, top, end, u, k * u, scale)


def second_sweep(tiles, ext, k, u, w, r, store):
    for top in range(SUB, ext - SUB, SUB):
        end = top + SUB
        sums = []
        for lower, mid, upper in (u, w):
            parts = [mid(x, top, end) for x in range(tiles)]
            sums.append(
                [
                    both
                    + (lower(x, top, end) + upper(x, top, end))
                    + (mid(x, top - 1, end - 1) + mid(x, top + 1, end + 1))
                    for x, both in enumerate(beside(parts, (0.0, 0.0)))
                ]
            )
        for x in range(tiles):
            coupled = k(x, top, end) * sums[0][x] + sums[1][x]
            value = (2.0 - JACOBI_WEIGHT) * u[1](x, top, end) + r(x, top, end) * coupled
            store(x, top, end, value)


def plane_of(held, *at):
    return lambda x, top, end: held[(*at, x, slice(top, end), slice(None))]


def put_rows(held, to, at, rows):
    for x in range(held.shape[1]):
        held[to, x, at : at + rows.shape[0], :] = rows[:, x * LANE : (x + 1) * LANE]


def repeat_sides(flags, held, at):
    end = held.shape[-2] - SUB

    @pl.when(flags[2] == 1)
    def _():
        for p in at:
            held[(*p, slice(None), slice(SUB - 1, SUB))] = held[(*p, slice(None), slice(SUB, SUB + 1))]

    @pl.when(flags[3] == 1)
    def _():
        for p in at:
            held[(*p, slice(None), slice(end, end + 1))] = held[
                (*p, slice(None), slice(end - 1, end))
            ]


def put_block(fine, held, to, source, row, cells, length):
    if fine:
        put_rows(held, to, SUB, source[row : row + cells, :])
    else:
        half = cells // 2
        put_rows(held, to, SUB, source[row : row + half, :length])
        put_rows(held, to, SUB + half, source[row : row + half, length:])


def layout_kernel(sizes, *rest):
    away, outs, near, sems = rest[:6], rest[6:10], rest[10:16], rest[16]
    for copy in load(list(zip(away, near)), sems):
        copy.wait()
    source, coarse_source, *edges = near
    sides = edges[2:]
    for fine, inner, outer in ((True, *outs[:2]), (False, *outs[2:])):
        planes, cells, length = sizes if fine else [n // 2 for n in sizes]
        f = source if fine else coarse_source
        source_row = 0 if fine else SUB

        def plane(held, to, p):
            put_rows(held, to, SUB, f[p].astype(jnp.float32))
            for side, row in zip(sides, (SUB - 1, SUB + cells)):
                at = source_row + p
                put_rows(held, to, row, side[at : at + 1, :length])

        for p in range(1, planes - 1):
            plane(inner, p - 1, p)
        for group, p in enumerate((0, planes - 1)):
            row = 0 if fine else 2 * cells
            put_block(fine, outer.at[group], 0, edges[group], row, cells, length)
            plane(outer.at[group], 1, p)


def inner_level(sizes, ks, fs, us, ws, rs):
    planes, _, length = sizes
    tiles, ext = ks.shape[1:3]

    def first(p, carry):
        def store(x, top, end, u, w, r):
            at = (p - 1, x, slice(top, end))
            us[at], ws[at], rs[at] = u, w, r

        near = [plane_of(ks, p + i) for i in (0, -1, 1)]
        first_sweep(tiles, ext, *near, plane_of(fs, p - 1), store)
        return carry

    lax.fori_loop(1, planes - 1, first, 0)


def inner_kernel(sizes, shares, flags, b, eh_hbm, el_hbm, edges, cks, cols, fs, cfs, *rest):
    out_hbm, us, ws, rs, cus, cws, crs, ks, eh, el, lh, ll, out, sems = rest
    planes, cells, length = sizes
    tiles, ext = ks.shape[1:3]
    copies = load([(eh_hbm, eh), (el_hbm, el)], sems)
    middle = range(2, planes - 2)
    gather_modes(b, middle, shares, lh, ll)
    for i, p in enumerate((0, 1, planes - 2, planes - 1)):
        ks[p] = edges[i]
    for h in range(HALO):
        for p in middle:
            at = h * planes + p
            put_rows(ks, p, halo_row(h, cells), cols[at : at + 1, :])
    for copy in copies:
        copy.wait()
    for p in range(2, planes - 2, 2):
        inverse_pair(p - 2, lh, ll, eh, el, ks, p, cells)
    repeat_sides(flags, ks, [(p,) for p in middle])
    inner_level(sizes, ks, fs, us, ws, rs)

    def second(p, carry):
        def store(x, top, end, value):
            out[p - 2, top - SUB : end - SUB, x * LANE : (x + 1) * LANE] = value

        u, w = ([plane_of(held, p - 1 + i) for i in (-1, 0, 1)] for held in (us, ws))
        second_sweep(tiles, ext, plane_of(ks, p), u, w, plane_of(rs, p - 1), store)
        return carry

    lax.fori_loop(2, planes - 2, second, 0)
    copies = send([(out, out_hbm.at[2 : planes - 2])], sems, 0)
    inner_level([n // 2 for n in sizes], cks, cfs, cus, cws, crs)
    for copy in copies:
        copy.wait()


def outer_kernel(sizes, flags, *rest):
    kept, coarse_kept, (k_far, k_near, _, out, coarse_out), rest = (
        rest[:5],
        rest[5:10],
        rest[10:15],
        rest[15:],
    )
    scratch = (rest[:6], rest[6:])
    levels = (sizes, tuple(n // 2 for n in sizes))
    start = 0
    sent = []
    for size, held, given, target in zip(
        levels, scratch, (kept, coarse_kept), (out, coarse_out)
    ):
        planes = size[0]
        ks, fs, inner_us, inner_ws, inner_rs = given
        halo, us, ws, rs, done, sems = held
        tiles, ext = ks.shape[1:3]
        rows = size[1]
        for group, edge in ((flags[4], k_far), (1 - flags[4], k_near)):
            at = start
            for place in range(2 * tiles):
                to = place * ext + SUB
                halo[group, to : to + rows, :] = edge[at : at + rows, :]
                at += rows
            for x in range(tiles):
                to = (tiles + x) * ext
                halo[group, to + SUB - 1 : to + SUB, :] = edge[at + x : at + x + 1, :]
                to += SUB + rows
                halo[group, to : to + 1, :] = edge[at + tiles + x : at + tiles + x + 1, :]
        start = at + SUB
        for group in range(2):

            @pl.when(flags[group] == 1)
            def _():
                for x in range(tiles):
                    at = (tiles + x) * ext
                    halo[group, at : at + ext, :] = ks[3 * group, x]

        def both_ends(group, carry):
            def halo_plane(slot):
                def get(x, top, end):
                    at = (slot * tiles + x) * ext
                    return halo[group, at + top : at + end, :]

                return get

            inwards = lambda i, count: jnp.where(group == 0, i, count - 1 - i)
            own = [plane_of(ks, inwards(i, 4)) for i in range(2)]
            u, w = (
                [plane_of(new, group, i) for i in range(2)]
                + [plane_of(old, inwards(i, planes - 2)) for i in range(2)]
                for new, old in ((us, inner_us), (ws, inner_ws))
            )
            around = ((halo_plane(1), halo_plane(0), own[0]), (own[0], halo_plane(1), own[1]))
            for i, near in enumerate(around):

                def store(x, top, end, u, w, r):
                    at = (group, i, x, slice(top, end))
                    us[at], ws[at] = u, w
                    if i == 1:
                        rs[group, x, top:end, :] = r

                first_sweep(tiles, ext, *near, plane_of(fs, group, i), store)
            scales = (plane_of(rs, group), plane_of(inner_rs, inwards(0, planes - 2)))
            for i, r in enumerate(scales):

                def store(x, top, end, value):
                    done[group, i, top - SUB : end - SUB, x * LANE : (x + 1) * LANE] = value

                second_sweep(tiles, ext, own[i], u[i : i + 3], w[i : i + 3], r, store)
                pltpu.make_async_copy(
                    done.at[group, i], target.at[inwards(i, planes)], sems.at[2 * group + i]
                ).start()
            return carry

        lax.fori_loop(0, 2, both_ends, 0)
        for group, at in enumerate(((0, 1), (planes - 1, planes - 2))):
            for i, p in enumerate(at):
                sent.append(
                    pltpu.make_async_copy(
                        done.at[group, i], target.at[p], sems.at[2 * group + i]
                    )
                )
    for copy in sent:
        copy.wait()


SMEM = pl.BlockSpec(memory_space=pltpu.SMEM)
VMEM = pl.BlockSpec(memory_space=pltpu.VMEM)
AWAY = pl.BlockSpec(memory_space=pltpu.HBM)
ANY = pl.BlockSpec(memory_space=pl.ANY)


def call(kernel, outs, operands, scratch, flops, specs, limit, out_specs=None, aliases=None):
    many = isinstance(outs, (list, tuple))
    written = outs if many else [outs]
    moved = sum(math.prod(x.shape) * x.dtype.itemsize for x in (*operands, *written))
    operands = [
        pltpu.with_memory_space_constraint(x, pltpu.HBM) if spec is AWAY else x
        for x, spec in zip(operands, specs)
    ]
    out_specs = out_specs or [
        VMEM if isinstance(x, jax.ShapeDtypeStruct) else AWAY for x in written
    ]
    return pl.pallas_call(
        kernel,
        out_shape=outs,
        in_specs=specs,
        out_specs=out_specs if many else out_specs[0],
        scratch_shapes=scratch,
        input_output_aliases=aliases or {},
        compiler_params=pltpu.CompilerParams(vmem_limit_bytes=limit * MIB),
        cost_estimate=pl.CostEstimate(flops=flops, bytes_accessed=moved, transcendentals=0),
    )(*operands)


def f32(*shape):
    return jax.ShapeDtypeStruct(shape, jnp.float32)


def room(*arrays):
    return [pltpu.VMEM(x.shape, x.dtype) for x in arrays]


def chain(axis):
    up = [(i, i + 1) for i in range(lax.axis_size(axis) - 1)]
    return up, [(j, i) for i, j in up]


def swap(lo, hi, axis):
    up, down = chain(axis)
    return lax.ppermute(hi, axis, up), lax.ppermute(lo, axis, down)


def held_planes(size, *count):
    planes, cells, length = size
    return f32(*count, length // LANE, cells + 2 * SUB, LANE)


def outer_scratch(size):
    planes, cells, length = size
    return room(
        f32(2, 2 * (length // LANE) * (cells + 2 * SUB), LANE),
        held_planes(size, 2, 2),
        held_planes(size, 2, 2),
        held_planes(size, 2),
        f32(2, 2, cells, length),
    ) + [pltpu.SemaphoreType.DMA((4,))]


def fused_body(noise, source):
    rows, groups = lax.axis_size("row"), lax.axis_size(PLANE)
    devices = rows * groups
    planes, cells, length = noise.shape
    first, second = planes * rows, cells * groups
    bf16 = jnp.bfloat16
    held = length // 2 // devices
    js = list(range(held))
    low = held // 2
    me = lax.axis_index(EVERY)
    row_at, group_at = lax.axis_index("row"), lax.axis_index(PLANE)
    flags = jnp.stack(
        [
            row_at == 0,
            row_at == rows - 1,
            group_at == 0,
            group_at == groups - 1,
            row_at % 2 == 1,
        ]
    ).astype(jnp.int32)
    norm = FIELD_SCALE * (float(first) * float(second) * float(length)) ** (-0.5)
    flat = (planes * cells, length)

    pieces = 4
    table = [x.reshape(pieces, -1, length) for x in two_parts(forward_third(length, devices, js))]
    table = np.concatenate(table, axis=1)
    shape = (length * SUB, LANE)
    sent = call(
        functools.partial(forward_kernel, planes),
        pltpu.HBM(shape, jnp.float32),
        (table, noise.reshape(flat)),
        room(table)
        + [
            pltpu.VMEM(flat, bf16),
            pltpu.VMEM(shape, jnp.float32),
            pltpu.SemaphoreType.DMA((2 * pieces + planes // 2,)),
        ],
        4 * length * length * planes * cells,
        [AWAY] * 2,
        12,
    )
    sent, source = lax.optimization_barrier((sent, source))
    sent = sent.reshape(devices, 2 * held, SUB, LANE)
    arrived = lax.all_to_all(sent, EVERY, split_axis=0, concat_axis=0, tiled=True)

    pairs = np.zeros((length, length // 2), np.float32)
    pairs[np.arange(length), np.arange(length) // 2] = 0.125
    level = f32(cells + cells // 4, length)
    side = f32(2 * SUB, length)
    coarse_source, *edges = call(
        functools.partial(source_kernel, planes),
        [f32(planes * cells // 4, length // 2), level, level, side, side],
        (pairs.astype(bf16), source.reshape(flat)),
        [
            pltpu.VMEM((planes * cells, length // 2), jnp.float32),
            pltpu.VMEM((cells, LANE), jnp.float32),
        ],
        planes * cells * length * length,
        [VMEM] * 2,
        12,
    )
    coarse_source = coarse_source.reshape(planes // 2, cells // 2, length // 2)
    edges = (*swap(*edges[:2], "row"), *swap(*edges[2:], PLANE))
    arrived, edges, coarse_source = lax.optimization_barrier((arrived, edges, coarse_source))

    constants = (
        two_parts(second_table(second))
        + (
            stacked(forward_first(first)),
            stacked(inverse_first(first)),
            stacked(inverse_first_coarse(first // 2, rows)),
        )
        + two_parts(second_coarse(second // 2, groups))
        + two_parts(second_table(second).transpose(0, 2, 1))
    )
    tiles = 2 * held + low // 2 + 1
    modes = (me + devices * np.array(js)).astype(jnp.float32)
    weight = jnp.where(modes == 0.0, norm, 2.0 * norm).astype(jnp.float32)
    scale = jnp.stack([DECAY * modes * modes, weight], axis=1)
    block = (2, 2 * held * first, second // 2)
    shape = (devices, tiles, SUB, LANE)
    out = call(
        functools.partial(middle_kernel, (first, second, rows, groups, held, low)),
        pltpu.HBM(shape, jnp.float32),
        (scale, arrived, *constants),
        room(*constants)
        + [
            pltpu.VMEM(shape, jnp.float32),
            pltpu.SemaphoreType.DMA((len(constants),)),
            pltpu.VMEM(block, bf16),
            pltpu.VMEM(block, bf16),
            pltpu.VMEM(block, jnp.float32),
            pltpu.VMEM(block, bf16),
            pltpu.VMEM(block, bf16),
            pltpu.VMEM((low // 2 * first, second), bf16),
            pltpu.VMEM((low // 2 * first, second), bf16),
        ],
        6 * 2 * 2 * held * first * second * (second + 2 * first),
        [SMEM, VMEM] + [AWAY] * len(constants),
        22,
    )
    out, source, coarse_source, edges = lax.optimization_barrier(
        (out, source, coarse_source, edges)
    )
    got = lax.all_to_all(out, EVERY, split_axis=0, concat_axis=0, tiled=True)
    size, coarse_size = noise.shape, coarse_source.shape
    sizes = (size, coarse_size)
    sources = (source, coarse_source, *edges)
    laid = call(
        functools.partial(layout_kernel, size),
        [
            held_planes(s, *count)
            for s in sizes
            for count in ((s[0] - 2,), (2, 2))
        ],
        sources,
        room(*sources) + [pltpu.SemaphoreType.DMA((6,))],
        source.size,
        [AWAY] * 6,
        12,
    )
    got, laid = lax.optimization_barrier((got, laid))

    third = inverse_third(length, devices, js)
    constants = (
        two_parts(third)
        + two_parts(third_coarse(length // 2, devices, js[:low]))
        + (lane_order(2 * held, low).astype(bf16),)
        + two_parts(third_coarse_halo(length // 2, devices, js[:low]))
    )
    edge = f32(sum(2 * (s[2] // LANE) * s[1] + SUB for s in sizes), LANE)
    shares = (devices, 2 * held, tiles)
    got = got.reshape(devices * tiles * SUB, LANE)
    ks, coarse_ks, cols, far, near = call(
        functools.partial(edge_kernel, (devices, 2 * held, low, tiles, planes, length)),
        [held_planes(s, 4) for s in sizes] + [f32(HALO * planes, length), edge, edge],
        (flags, got, *constants),
        room(*constants)
        + [pltpu.VMEM((2, 4 * cells, devices * held), bf16)] * 2
        + [pltpu.VMEM((planes // 2 * LANE, devices * low), bf16)] * 2
        + [pltpu.SemaphoreType.DMA((7,))],
        3 * planes * cells * length * length,
        [SMEM, VMEM] + [AWAY] * 7,
        16,
    )
    k_far, k_near = (
        lax.ppermute(
            x, "row", [p for i in range(at, rows - 1, 2) for p in ((i, i + 1), (i + 1, i))]
        )
        for x, at in ((far, 1), (near, 0))
    )
    inner_f, outer_f, coarse_inner_f, coarse_outer_f = laid
    inner, *kept = call(
        functools.partial(inner_kernel, size, shares),
        [pltpu.HBM(size, jnp.float32)] + [held_planes(s, s[0] - 2) for s in sizes for _ in range(3)],
        (flags, got, *constants[:2], ks, coarse_ks, cols, inner_f, coarse_inner_f),
        room(held_planes(size, planes), *constants[:2])
        + [pltpu.VMEM((2, (planes - 4) * cells, devices * held), bf16)] * 2
        + room(f32(planes - 4, cells, length))
        + [pltpu.SemaphoreType.DMA((2,))],
        3 * planes * cells * length * length,
        [SMEM, VMEM] + [AWAY] * 2 + [VMEM] * 5,
        18,
    )
    return call(
        functools.partial(outer_kernel, size),
        [pltpu.HBM(s, jnp.float32) for s in sizes],
        (flags, ks, outer_f, *kept[:3], coarse_ks, coarse_outer_f, *kept[3:], k_far, k_near, inner),
        outer_scratch(size) + outer_scratch(coarse_size),
        30 * source.size,
        [SMEM] + [VMEM] * 12 + [AWAY],
        18,
        None,
        {13: 0},
    )


NEIGHBOUR_STEPS = ((1, 0, 0), (-1, 0, 0), (0, 1, 0), (0, -1, 0), (0, 0, 1), (0, 0, -1))


def padded(x, sides, width):
    for axis, dim in sides:
        peers, length = (lax.axis_size(axis), x.shape[dim])
        up = [(i, (i + 1) % peers) for i in range(peers - 1)]
        down = [(j, i) for i, j in up]
        last = lax.slice_in_dim(x, length - width, length, axis=dim)
        leading = lax.slice_in_dim(x, 0, width, axis=dim)
        before = lax.ppermute(last, axis, up)
        after = lax.ppermute(leading, axis, down)
        x = jnp.concatenate([before, x, after], axis=dim)
    return x


def signed_modes(index, length):
    return jnp.where(index < length // 2, index, index - length).astype(jnp.float32)


def amplitude(first_modes, second_modes, third_modes, first_edge, second_edge, third_edge):
    squared = first_modes * first_modes + second_modes * second_modes + third_modes * third_modes
    value = FIELD_SCALE / (1.0 + (2.0 * math.pi * CORRELATION) ** 2 * squared)
    edge = (
        (jnp.abs(first_modes) == first_edge)
        | (jnp.abs(second_modes) == second_edge)
        | (jnp.abs(third_modes) == third_edge)
    )
    return jnp.where(edge, 0.0, value)


def phase_table(count_rows, count_cols, modulus, sign):
    left_index = jnp.arange(count_rows, dtype=jnp.int32)[:, None]
    right_index = jnp.arange(count_cols, dtype=jnp.int32)[None, :]
    angle = 2.0 * math.pi / modulus * (left_index * right_index % modulus).astype(jnp.float32)
    return (jnp.cos(angle), sign * jnp.sin(angle))


def split_length(length):
    outer_len = 2 ** ((length.bit_length() - 1) // 2)
    return (outer_len, length // outer_len)


def real_form(form, left_value, right_value):
    return jnp.einsum(form, left_value, right_value, precision=lax.Precision.HIGHEST)


def complex_form(form, left_real, left_imag, right_real, right_imag):
    real_part = real_form(form, left_real, right_real) - real_form(form, left_imag, right_imag)
    imag_part = real_form(form, left_real, right_imag) + real_form(form, left_imag, right_real)
    return (real_part, imag_part)


def merge_pair(values, out_form, first_letter):
    merge_at = out_form.index(first_letter)
    out_dims = list(values.shape)
    merged = (
        out_dims[:merge_at]
        + [out_dims[merge_at] * out_dims[merge_at + 1]]
        + out_dims[merge_at + 2 :]
    )
    return values.reshape(merged)


def forward_axis(real_part, imag_part, lead_form, out_form, kept_modes):
    length = real_part.shape[-1]
    outer_len, inner_len = split_length(length)
    split_shape = real_part.shape[:-1] + (outer_len, inner_len)
    outer_real, outer_imag = phase_table(outer_len, outer_len, outer_len, -1.0)
    twist_real, twist_imag = phase_table(outer_len, inner_len, length, -1.0)
    inner_real, inner_imag = phase_table(inner_len, kept_modes // outer_len, inner_len, -1.0)
    first_form = lead_form + "ab,ai->" + lead_form + "ib"
    split_real = real_part.reshape(split_shape)
    if imag_part is None:
        section_real = real_form(first_form, split_real, outer_real)
        section_imag = real_form(first_form, split_real, outer_imag)
    else:
        section_real, section_imag = complex_form(
            first_form, split_real, imag_part.reshape(split_shape), outer_real, outer_imag
        )
    turned_real = section_real * twist_real - section_imag * twist_imag
    turned_imag = section_real * twist_imag + section_imag * twist_real
    result_real, result_imag = complex_form(
        lead_form + "ib,bj->" + out_form, turned_real, turned_imag, inner_real, inner_imag
    )
    return (merge_pair(result_real, out_form, "j"), merge_pair(result_imag, out_form, "j"))


def inverse_axis(real_part, imag_part, length, lead_form, out_form, real_only):
    kept_modes = real_part.shape[-1]
    outer_len, inner_len = split_length(length)
    split_shape = real_part.shape[:-1] + (kept_modes // outer_len, outer_len)
    inner_real, inner_imag = phase_table(kept_modes // outer_len, inner_len, inner_len, 1.0)
    twist_real, twist_imag = phase_table(outer_len, inner_len, length, 1.0)
    outer_real, outer_imag = phase_table(outer_len, outer_len, outer_len, 1.0)
    section_real, section_imag = complex_form(
        lead_form + "ji,jb->" + lead_form + "ib",
        real_part.reshape(split_shape),
        imag_part.reshape(split_shape),
        inner_real,
        inner_imag,
    )
    turned_real = section_real * twist_real - section_imag * twist_imag
    turned_imag = section_real * twist_imag + section_imag * twist_real
    second_form = lead_form + "ib,ia->" + out_form
    if real_only:
        result = real_form(second_form, turned_real, outer_real) - real_form(
            second_form, turned_imag, outer_imag
        )
        return merge_pair(result, out_form, "a")
    result_real, result_imag = complex_form(
        second_form, turned_real, turned_imag, outer_real, outer_imag
    )
    return (merge_pair(result_real, out_form, "a"), merge_pair(result_imag, out_form, "a"))


def low_band(values, half_coarse, fine_len):
    return jnp.concatenate(
        [values[:, :, :half_coarse], values[:, :, fine_len - half_coarse :]], axis=2
    )


def window(values, margin, offset):
    return values[
        margin + offset[0] : values.shape[0] - margin + offset[0],
        margin + offset[1] : values.shape[1] - margin + offset[1],
        margin + offset[2] : values.shape[2] - margin + offset[2],
    ]


def face_weight(center, beside):
    return jnp.where(beside > 0.0, 0.5 * (center + beside), center)


def smooth_twice(kappa, source):
    no_shift = (0, 0, 0)
    center = window(kappa, 1, no_shift)
    faces = [face_weight(center, window(kappa, 1, offset)) for offset in NEIGHBOUR_STEPS]
    diagonal = faces[0] + faces[1] + faces[2] + faces[3] + faces[4] + faces[5]
    guarded = jnp.where(center > 0.0, diagonal, 1.0)
    first_sweep = JACOBI_WEIGHT * window(source, 1, no_shift) / guarded
    inner_first = window(first_sweep, 1, no_shift)
    inner_diagonal = window(diagonal, 1, no_shift)
    coupled = jnp.zeros_like(inner_first)
    for face_value, offset in zip(faces, NEIGHBOUR_STEPS):
        coupled = coupled + window(face_value, 1, no_shift) * window(first_sweep, 1, offset)
    residual = window(source, 2, no_shift) - inner_diagonal * inner_first + coupled
    return inner_first + JACOBI_WEIGHT * residual / inner_diagonal


def pad_depth(values):
    return jnp.pad(values, ((0, 0), (0, 0), (2, 2)))


def plain_body(noise, source):
    row_at = lax.axis_index("row")
    group_at = lax.axis_index(("level", "col"))
    fine_field = noise.astype(jnp.float32)
    fine_len = fine_field.shape[-1]
    coarse_len = fine_len // 2
    half_coarse = coarse_len // 2
    kept_modes = fine_len // 2
    real_part, imag_part = forward_axis(fine_field, None, "pq", "pjiq", kept_modes)
    real_part, imag_part = (
        lax.all_to_all(real_part, ("level", "col"), split_axis=1, concat_axis=2, tiled=True),
        lax.all_to_all(imag_part, ("level", "col"), split_axis=1, concat_axis=2, tiled=True),
    )
    real_part, imag_part = forward_axis(real_part, imag_part, "pq", "jiqp", fine_len)
    real_part, imag_part = (
        lax.all_to_all(real_part, "row", split_axis=0, concat_axis=2, tiled=True),
        lax.all_to_all(imag_part, "row", split_axis=0, concat_axis=2, tiled=True),
    )
    slab_len = real_part.shape[-1]
    coarse_slab = slab_len // 2
    half_slab = coarse_slab // 2
    real_part, imag_part = forward_axis(real_part, imag_part, "pq", "pqji", slab_len)
    second_count = real_part.shape[0]
    third_count = real_part.shape[1]
    wave_second = signed_modes(
        row_at * second_count + jnp.arange(second_count, dtype=jnp.int32), fine_len
    )[:, None, None]
    third_index = group_at * third_count + jnp.arange(third_count, dtype=jnp.int32)
    wave_third = signed_modes(third_index, fine_len)[None, :, None]
    spread = 2.0
    mirror_weight = jnp.where(third_index == 0, 1.0, spread).astype(jnp.float32)[None, :, None]
    norm_factor = (float(slab_len) * float(fine_len) * float(fine_len)) ** (-0.5)
    wave_first = signed_modes(jnp.arange(slab_len, dtype=jnp.int32), slab_len)[None, None, :]
    fine_scale = (
        amplitude(
            wave_second, wave_third, wave_first, fine_len / 2.0, fine_len / 2.0, slab_len / 2.0
        )
        * mirror_weight
        * norm_factor
    )
    coarse_first = signed_modes(jnp.arange(coarse_slab, dtype=jnp.int32), coarse_slab)[
        None, None, :
    ]
    coarse_scale = (
        amplitude(
            wave_second,
            wave_third,
            coarse_first,
            coarse_len / 2.0,
            coarse_len / 2.0,
            coarse_slab / 2.0,
        )
        * mirror_weight
        * norm_factor
    )
    coarse_real = low_band(real_part, half_slab, slab_len) * coarse_scale
    coarse_imag = low_band(imag_part, half_slab, slab_len) * coarse_scale
    fine_real, fine_imag = inverse_axis(
        real_part * fine_scale, imag_part * fine_scale, slab_len, "pq", "abqp", False
    )
    coarse_real, coarse_imag = inverse_axis(
        coarse_real, coarse_imag, coarse_slab, "pq", "abqp", False
    )
    fine_real, fine_imag, coarse_real, coarse_imag = (
        lax.all_to_all(fine_real, "row", split_axis=0, concat_axis=2, tiled=True),
        lax.all_to_all(fine_imag, "row", split_axis=0, concat_axis=2, tiled=True),
        lax.all_to_all(coarse_real, "row", split_axis=0, concat_axis=2, tiled=True),
        lax.all_to_all(coarse_imag, "row", split_axis=0, concat_axis=2, tiled=True),
    )
    coarse_real = low_band(coarse_real, half_coarse, fine_len)
    coarse_imag = low_band(coarse_imag, half_coarse, fine_len)
    fine_real, fine_imag = inverse_axis(fine_real, fine_imag, fine_len, "pq", "pabq", False)
    coarse_real, coarse_imag = inverse_axis(
        coarse_real, coarse_imag, coarse_len, "pq", "pabq", False
    )
    fine_real, fine_imag, coarse_real, coarse_imag = (
        lax.all_to_all(fine_real, ("level", "col"), split_axis=1, concat_axis=2, tiled=True),
        lax.all_to_all(fine_imag, ("level", "col"), split_axis=1, concat_axis=2, tiled=True),
        lax.all_to_all(coarse_real, ("level", "col"), split_axis=1, concat_axis=2, tiled=True),
        lax.all_to_all(coarse_imag, ("level", "col"), split_axis=1, concat_axis=2, tiled=True),
    )
    coarse_real = coarse_real[:, :, :half_coarse]
    coarse_imag = coarse_imag[:, :, :half_coarse]
    fine_log = inverse_axis(fine_real, fine_imag, fine_len, "pq", "pqab", True)
    coarse_log = inverse_axis(coarse_real, coarse_imag, coarse_len, "pq", "pqab", True)
    fine_kappa = jnp.exp(fine_log)
    coarse_kappa = jnp.exp(coarse_log)
    fine_source = source.astype(jnp.float32)
    coarse_rows = coarse_log.shape[0]
    coarse_cols = coarse_log.shape[1]
    coarse_source = fine_source.reshape(coarse_rows, 2, coarse_cols, 2, coarse_len, 2).mean(
        axis=(1, 3, 5)
    )
    fine_kappa, fine_source, coarse_kappa, coarse_source = (
        padded(fine_kappa, (("row", 0), (("level", "col"), 1)), 2),
        padded(fine_source, (("row", 0), (("level", "col"), 1)), 2),
        padded(coarse_kappa, (("row", 0), (("level", "col"), 1)), 2),
        padded(coarse_source, (("row", 0), (("level", "col"), 1)), 2),
    )
    fine_pressure = smooth_twice(pad_depth(fine_kappa), pad_depth(fine_source))
    coarse_pressure = smooth_twice(pad_depth(coarse_kappa), pad_depth(coarse_source))
    return (fine_pressure, coarse_pressure)


def body(noise, source):
    planes, cells, length = noise.shape
    rows, groups = lax.axis_size("row"), lax.axis_size(PLANE)
    modes = length // 2 // (rows * groups)
    fills = planes == SUB and cells == LANE and 2 * HALO * modes == LANE // 2
    if fills and length % (4 * LANE) == 0 and rows % 2 == 0 and groups % 4 == 0:
        return fused_body(noise, source)
    return plain_body(noise, source)


def solution(mesh):
    return jax.shard_map(
        body,
        mesh=mesh,
        in_specs=(P("row", ("level", "col"), None), P("row", ("level", "col"), None)),
        out_specs=(P("row", ("level", "col"), None), P("row", ("level", "col"), None)),
        check_vma=False,
    )
```

```python
import functools
import math

import jax
import jax.numpy as jnp
import numpy as np
from jax import lax
from jax.experimental import pallas as pl
from jax.experimental.pallas import tpu as pltpu
from jax.sharding import PartitionSpec as P

JACOBI_WEIGHT = 2.0 / 3.0
CORRELATION = 0.2
FIELD_SCALE = 0.3
DECAY = (2.0 * math.pi * CORRELATION) ** 2
EVERY = ("row", "level", "col")
PLANE = ("level", "col")
MIB = 1 << 20
SUB, LANE = 8, 128
HALO = 4


def two_parts(matrix):
    high = matrix.astype(jnp.bfloat16)
    low = (matrix - high.astype(np.float64)).astype(jnp.bfloat16)
    return high, low


def angles(rows, cols, length):
    return 2.0 * np.pi * (np.outer(rows, cols) % length) / length


def third_modes(devices, js):
    return np.array([[d + devices * j for j in js] for d in range(devices)])


def forward_third(length, devices, js):
    theta = angles(third_modes(devices, js).reshape(-1), np.arange(length), length)
    return np.stack([np.cos(theta), -np.sin(theta)], axis=1).reshape(-1, length)


def inverse_third(length, devices, js):
    modes = third_modes(devices, js).reshape(devices // 2, 2, len(js)).transpose(1, 0, 2)
    theta = 2.0 * np.pi * (modes[..., None] * np.arange(length // 2) % length) / length
    both = np.stack([np.cos(theta), -np.sin(theta)], axis=3)
    return both.reshape(2, -1, length // 2)


def second_modes(length):
    return np.arange(length // 2).reshape(-1, 2).T


def second_table(length):
    theta = second_modes(length)[:, None, :] * np.arange(length // 2)[None, :, None]
    theta = 2.0 * np.pi * (theta % length) / length
    return np.concatenate([np.cos(theta), np.sin(theta)], axis=2)


def forward_first(length):
    theta = angles(np.arange(length), np.arange(length), length)
    cos, sin = np.cos(theta), np.sin(theta)
    return np.block([[cos, sin], [-sin, cos]])


def inverse_first(length):
    theta = angles(np.arange(length), np.arange(length), length)
    cos, sin = np.cos(theta), np.sin(theta)
    cos[:, length // 2] = 0.0
    sin[:, length // 2] = 0.0
    return np.block([[cos, -sin], [sin, cos]])


def inverse_first_coarse(length, rows):
    full = inverse_first(length)
    value = full.reshape(2, rows, length // rows, 2 * length)
    turned = np.concatenate([-full[length:], full[:length]]).reshape(value.shape)
    order = lambda x: x.transpose(1, 0, 2, 3).reshape(2 * length, 2 * length)
    return np.concatenate([order(value), order(turned)])


def second_coarse(length, groups):
    theta = angles(second_modes(length).reshape(-1), np.arange(length), length)
    table = np.concatenate([np.cos(theta), np.sin(theta)])
    span = length // groups
    out = np.zeros((2, length, groups, 2, span))
    for pair in range(2):
        out[pair, :, :, pair, :] = table.reshape(length, groups, span)
    return out.reshape(2 * length, 2 * length)


def third_coarse(length, devices, js):
    modes = third_modes(devices, js).reshape(devices, len(js) // 2, 2)
    theta = 2.0 * np.pi * (modes[..., None] * np.arange(length) % length) / length
    both = np.stack([np.cos(theta), -np.sin(theta)])
    return both.transpose(0, 2, 1, 3, 4).reshape(2 * (len(js) // 2) * devices, 2 * length)


def third_coarse_halo(length, devices, js):
    theta = angles(third_modes(devices, js).reshape(-1), np.arange(length), length)
    return np.concatenate([np.cos(theta), -np.sin(theta)], axis=1)


def lane_order(parts, coarse_parts):
    out = np.zeros((LANE, LANE))
    for h in range(HALO):
        for q in range(parts):
            out[HALO * q + h, parts * h + q] = 1.0
        for j in range(coarse_parts):
            out[LANE // 2 + HALO * j + h, LANE // 2 + coarse_parts * h + j] = 1.0
    return out


def split(x):
    high = x.astype(jnp.bfloat16)
    return high, (x - high.astype(jnp.float32)).astype(jnp.bfloat16)


def dot(a, b):
    return lax.dot_general(a, b, (((1,), (0,)), ((), ())), preferred_element_type=jnp.float32)


def dot_t(a, b):
    return lax.dot_general(a, b, (((1,), (1,)), ((), ())), preferred_element_type=jnp.float32)


def stacked(matrix):
    high, low = two_parts(matrix)
    return np.block([[high, high], [low, np.zeros_like(low)]])


def dot_left(stack, x):
    value = dot(stack, jnp.concatenate(split(x), axis=0))
    rows = stack.shape[0] // 2
    return value[:rows] + value[rows:]


def dot3(a, b):
    (ah, al), (bh, bl) = a, b
    return dot(ah, bh) + (dot(ah, bl) + dot(al, bh))


def load(pairs, sems):
    copies = [pltpu.make_async_copy(a, b, sems.at[i]) for i, (a, b) in enumerate(pairs)]
    for copy in copies:
        copy.start()
    return copies


def send(pairs, sems, first):
    copies = [pltpu.make_async_copy(a, b, sems.at[first + i]) for i, (a, b) in enumerate(pairs)]
    for copy in copies:
        copy.start()
    return copies


def forward_kernel(planes, d_hbm, x_hbm, out_hbm, d, x, out, sems):
    pieces, rows = d.shape[0], d.shape[1] // 2
    parts = [slice(p * LANE, (p + 2) * LANE) for p in range(0, planes, 2)]
    pairs = [(x_hbm.at[at, :], x.at[at, :]) for at in parts]
    copies = load([(d_hbm.at[0], d.at[0])] + pairs + [(d_hbm.at[i], d.at[i]) for i in range(1, pieces)], sems)
    sent = []
    copies[0].wait()
    for piece in range(pieces):
        if piece:
            copies[len(parts) + piece].wait()
        for i, at in enumerate(parts):
            if piece == 0:
                copies[i + 1].wait()
            value = dot_t(d[piece], x[at, :])
            value = value[:rows] + value[rows:]
            for h in range(2):
                out[pl.ds(piece * rows * SUB + 2 * i + h, rows, stride=SUB), :] = value[
                    :, h * LANE : (h + 1) * LANE
                ]
        tall = slice(piece * rows * SUB, (piece + 1) * rows * SUB)
        sent += send([(out.at[tall, :], out_hbm.at[tall, :])], sems, len(copies) + piece)
    for copy in sent:
        copy.wait()


def middle_kernel(sizes, scale, b, *rest):
    (first, second, rows, groups, js, low) = sizes
    count = 9
    away, out_hbm, near, rest = (
        rest[:count],
        rest[count],
        rest[count + 1 : 2 * count + 1],
        rest[2 * count + 1 :],
    )
    out, sems, zh, zl, y, oh, ol, qh, ql = rest
    copies = load(list(zip(away, near)), sems)
    csh, csl, forward, inverse, coarse_inverse, cch, ccl, ch, cl = near
    q_count = 2 * js
    half, quarter = second // 2, second // 4
    for q in range(q_count):
        for g in range(groups // 2):
            for r in range(0, rows, 2):
                at = r * groups + g
                near_half = jnp.concatenate([b[at, q], b[at + groups, q]], axis=0)
                at += groups // 2
                far_half = jnp.concatenate([b[at, q], b[at + groups, q]], axis=0)
                at = slice(q * first + r * SUB, q * first + (r + 2) * SUB)
                lanes = slice(g * LANE, (g + 1) * LANE)
                zh[0, at, lanes], zl[0, at, lanes] = split(near_half + far_half)
                zh[1, at, lanes], zl[1, at, lanes] = split(near_half - far_half)
    for copy in copies[:5]:
        copy.wait()
    wide = 8 * first
    for top in range(0, q_count * first, wide):
        at = slice(top, top + wide)
        for parity in range(2):
            y[parity, at, :] = dot3(
                (zh[parity, at, :], zl[parity, at, :]), (csh[parity], csl[parity])
            )
    mode0 = lax.broadcasted_iota(jnp.int32, (first, second), 0)
    mode0 = jnp.where(mode0 < first // 2, mode0, mode0 - first).astype(jnp.float32)
    lane = lax.broadcasted_iota(jnp.int32, (first, second), 1)
    mode1 = jnp.where(lane < half, lane, lane - half)
    mode1 = jnp.where(mode1 < quarter, 2 * mode1, 2 * (mode1 - quarter) + 1).astype(jnp.float32)
    base = 1.0 + DECAY * (mode0 * mode0 + mode1 * mode1)
    for j in range(js):
        top = j * 2 * first
        re, im = slice(top, top + first), slice(top + first, top + 2 * first)
        cos, sin = slice(0, quarter), slice(quarter, half)
        whole = lambda part, lanes: jnp.concatenate(
            [y[0, part, lanes], y[1, part, lanes]], axis=1
        )
        rc, rs, ic, isn = whole(re, cos), whole(re, sin), whole(im, cos), whole(im, sin)
        wave = jnp.concatenate(
            [
                jnp.concatenate([rc + isn, rc - isn], axis=1),
                jnp.concatenate([ic - rs, ic + rs], axis=1),
            ],
            axis=0,
        )
        spectrum = dot_left(forward[...], wave)
        amp = jnp.where(lane == half, 0.0, scale[j, 1] / (base + scale[j, 0]))
        scaled = spectrum * jnp.concatenate([amp, amp], axis=0)
        field = dot_left(inverse[...], scaled)
        plus, minus = field[:, :half], field[:, half:]
        even, odd = plus + minus, plus - minus
        odd = jnp.concatenate([-odd[first:], odd[:first]], axis=0)
        at = slice(top, top + 2 * first)
        for parity, lanes in enumerate((cos, sin)):
            operand = jnp.concatenate([even[:, lanes], odd[:, lanes]], axis=1)
            oh[parity, at, :], ol[parity, at, :] = split(operand)
        if j < low:
            keep = first // 4
            kept = [
                scaled[at : at + keep, :]
                for at in (0, first - keep, first, 2 * first - keep)
            ]
            band = jnp.concatenate(kept, axis=0)
            low_lane = lax.broadcasted_iota(jnp.int32, (first, quarter), 1) < quarter // 2
            pieces = []
            for at in (0, half):
                upper = pltpu.roll(band[:, at + quarter : at + half], quarter // 2, 1)
                pieces.append(jnp.where(low_lane, band[:, at : at + quarter], upper))
            band = jnp.concatenate(pieces, axis=1)
            field = dot_left(coarse_inverse[...], band)
            value, turned = field[:first], field[first:]
            operand = jnp.concatenate(
                [
                    value[:, :quarter] + value[:, quarter:],
                    turned[:, :quarter] - turned[:, quarter:],
                ],
                axis=1,
            )
            at = slice(j // 2 * first, (j // 2 + 1) * first)
            lanes = slice(j % 2 * half, (j % 2 + 1) * half)
            qh[at, lanes], ql[at, lanes] = split(operand)
    for copy in copies[5:]:
        copy.wait()
    copies = []
    wide = 4 * first
    lane = lax.broadcasted_iota(jnp.int32, (SUB, LANE), 1)
    extra = q_count + low // 2

    def leave(start, stop):
        at = slice(start, stop)
        copies.extend(send([(out.at[:, at], out_hbm.at[:, at])], sems, len(copies)))

    def give(value, start):
        tiles = value.shape[0] // first
        for q in range(tiles):
            for r in range(rows):
                for g in range(groups):
                    at = q * first + r * SUB
                    out[r * groups + g, start + q] = value[
                        at : at + SUB, g * LANE : (g + 1) * LANE
                    ]
        leave(start, start + tiles)

    def halo_columns(value, start, held):
        tiles = value.shape[0] // first
        for r in range(rows):
            for g in range(groups):
                total = held[r, g]
                left = max(g - 1, 0) * LANE
                right = min(g + 1, groups - 1) * LANE
                for q in range(tiles):
                    at = slice(q * first + r * SUB, q * first + (r + 1) * SUB)
                    both = jnp.where(
                        lane < LANE // 2,
                        value[at, right : right + LANE],
                        value[at, left : left + LANE],
                    )
                    to = HALO * (start + q)
                    both = pltpu.roll(both, (to + 2) % LANE, 1)
                    total = jnp.where((lane >= to) & (lane < to + HALO), both, total)
                held[r, g] = total

    def coarse_columns(value, held):
        half_lane = LANE // 2
        for j in range(low):
            for r in range(rows):
                at = slice(j // 2 * first + r * SUB, j // 2 * first + (r + 1) * SUB)
                shift = HALO * j + 2 - j % 2 * half_lane
                to = half_lane + HALO * j
                for g in range(groups):
                    left = max(g - 1, 0) * LANE
                    right = min(g + 1, groups - 1) * LANE
                    left = pltpu.roll(value[at, left : left + LANE], shift % LANE, 1)
                    right = pltpu.roll(
                        value[at, right : right + LANE], (shift + half_lane) % LANE, 1
                    )
                    total = jnp.where((lane >= to) & (lane < to + 2), left, held[r, g])
                    held[r, g] = jnp.where(
                        (lane >= to + 2) & (lane < to + HALO), right, total
                    )

    columns = {
        (r, g): jnp.zeros((SUB, LANE), jnp.float32) for r in range(rows) for g in range(groups)
    }
    coarse = dot3((qh[...], ql[...]), (cch[...], ccl[...]))
    give(coarse, q_count)
    coarse_columns(coarse, columns)
    for top in range(0, q_count * first, wide):
        at = slice(top, top + wide)
        even, odd = (
            dot3((oh[parity, at, :], ol[parity, at, :]), (ch[parity], cl[parity]))
            for parity in range(2)
        )
        value = jnp.concatenate([even + odd, even - odd], axis=1)
        give(value, top // first)
        halo_columns(value, top // first, columns)
    for (r, g), total in columns.items():
        out[r * groups + g, extra] = total
    leave(extra, extra + 1)
    for copy in copies:
        copy.wait()


def gather_modes(b, at, sizes, lh, ll):
    devices, q_count, tiles = sizes
    for i, n in enumerate(at):
        for parity in range(2):
            rows = jnp.concatenate(
                [
                    b[pl.ds(s * tiles * SUB + n, q_count, stride=SUB), :]
                    for s in range(parity, devices, 2)
                ],
                axis=0,
            )
            to = slice(i * LANE, (i + 1) * LANE)
            lh[parity, to, :], ll[parity, to, :] = split(jnp.transpose(rows))


def inverse_pair(i, lh, ll, eh, el, ks, to, cells):
    at = slice(i * cells, (i + 2) * cells)
    even, odd = (
        dot3((lh[parity, at, :], ll[parity, at, :]), (eh[parity], el[parity]))
        for parity in range(2)
    )
    value = jnp.exp(jnp.concatenate([even + odd, even - odd], axis=1))
    for n in range(2):
        put_rows(ks, to + n, SUB, value[n * cells : (n + 1) * cells])


def edge_kernel(sizes, flags, b, *rest):
    (devices, q_count, low, tiles, planes, length) = sizes
    away, (ks, cks, cols, far, near_edge), rest = rest[:7], rest[7:12], rest[12:]
    near, (lh, ll, mh, ml, sems) = rest[:7], rest[7:]
    copies = load(list(zip(away, near)), sems)
    eh, el, ceh, cel, order, cwh, cwl = near
    cells, short = LANE, length // 2
    halves, coarse_planes = low // 2, planes // 2
    half = cells // 2
    gather_modes(b, (0, 1, planes - 2, planes - 1), (devices, q_count, tiles), lh, ll)
    for n in range(coarse_planes):
        rows = jnp.concatenate(
            [
                b[pl.ds((q_count + h) * SUB + c * coarse_planes + n, devices, stride=tiles * SUB), :]
                for c in range(2)
                for h in range(halves)
            ],
            axis=0,
        )
        at = slice(n * LANE, (n + 1) * LANE)
        mh[at, :], ml[at, :] = split(jnp.transpose(rows))

    for copy in copies[:4]:
        copy.wait()

    for i in range(0, 4, 2):
        inverse_pair(i, lh, ll, eh, el, ks, i, cells)
    value = dot3((mh[...], ml[...]), (ceh[...], cel[...]))
    for n in range(coarse_planes):
        top = n * cells
        part = value[top : top + half, :short] + value[top + half : top + cells, short:]
        part = jnp.exp(part)
        put_rows(cks, n, SUB, part)

    for copy in copies[4:]:
        copy.wait()
    lane = lax.broadcasted_iota(jnp.int32, (SUB, LANE), 1)
    tile_rows = [b[(s * tiles + tiles - 1) * SUB : (s + 1) * tiles * SUB, :] for s in range(devices)]
    high, rest_part = split(jnp.concatenate(tile_rows, axis=0))
    ordered = dot(high, order[...]) + dot(rest_part, order[...])

    def joined(of, width, start):
        fit = LANE // width
        cells_of = []
        for h in range(HALO):
            parts = []
            for i, s in enumerate(of):
                moved = ordered[s * SUB : (s + 1) * SUB]
                shift = (i % fit * width - start - h * width) % LANE
                moved = pltpu.roll(moved, shift, 1) if shift else moved
                if i % fit == 0:
                    parts.append(moved)
                else:
                    parts[-1] = jnp.where(lane >= i % fit * width, moved, parts[-1])
            cells_of.append(jnp.concatenate(parts, axis=1))
        return split(jnp.concatenate(cells_of, axis=0))

    even, odd = (
        dot3(joined(range(parity, devices, 2), q_count, 0), (eh[parity], el[parity]))
        for parity in range(2)
    )
    value = jnp.exp(jnp.concatenate([even + odd, even - odd], axis=1))
    cols[...] = value
    for h in range(HALO):
        for i, n in enumerate((0, 1, planes - 2, planes - 1)):
            at = h * planes + n
            put_rows(ks, i, halo_row(h, cells), value[at : at + 1, :])
    whole = dot3(joined(range(devices), low, LANE // 2), (cwh[...], cwl[...]))
    for h in range(HALO):
        top = h * SUB
        part = whole[top : top + coarse_planes, :short] + whole[top + coarse_planes : top + SUB, short:]
        part = jnp.exp(part)
        for n in range(coarse_planes):
            put_rows(cks, n, halo_row(h, half), part[n : n + 1, :])
    for held in (ks, cks):
        repeat_sides(flags, held, [(n,) for n in range(4)])
    odd_row = flags[4] == 1
    low_end = (jnp.where(odd_row, 2, 1), jnp.where(odd_row, 3, 0))
    high_end = (jnp.where(odd_row, 1, 2), jnp.where(odd_row, 0, 3))
    for edge, of in ((far, low_end), (near_edge, high_end)):
        at = 0
        for held in (ks, cks):
            count, end = held.shape[1], held.shape[2] - SUB
            for n in of:
                for x in range(count):
                    edge[at : at + end - SUB, :] = held[n, x, SUB:end, :]
                    at += end - SUB
            for x in range(count):
                edge[at + x : at + x + 1, :] = held[of[1], x, SUB - 1 : SUB, :]
                edge[at + count + x : at + count + x + 1, :] = held[of[1], x, end : end + 1, :]
            at += SUB


def halo_row(h, cells):
    return SUB - 2 + h if h < 2 else SUB + cells + h - 2


def source_kernel(planes, flags, pairs, x, out, far, near, left, right, held, summed):
    cells = x.shape[0] // planes
    length = x.shape[1]
    half, fourth = cells // 2, cells // 4
    held[...] = dot(x[...], pairs[...])
    for n in range(planes // 2):
        top = 2 * n * cells
        for at in range(0, out.shape[1], LANE):
            lanes = slice(at, at + LANE)
            summed[...] = held[top : top + cells, lanes] + held[top + cells : top + 2 * cells, lanes]
            out[n * half : (n + 1) * half, lanes] = (
                summed[pl.ds(0, half, stride=2), :] + summed[pl.ds(1, half, stride=2), :]
            )
    odd_row = flags[4] == 1
    ends = (0, planes - 1)
    for edge, plane in (
        (far, jnp.where(odd_row, ends[1], ends[0])),
        (near, jnp.where(odd_row, ends[0], ends[1])),
    ):
        at = pl.multiple_of(plane * cells, cells)
        edge[:cells, :] = x[pl.ds(at, cells), :].astype(jnp.float32)
        at = pl.multiple_of(lax.div(plane, 2) * half, half)
        edge[cells:, : length // 2] = out[pl.ds(at, fourth), :]
        edge[cells:, length // 2 :] = out[pl.ds(at + fourth, fourth), :]
    for edge, row in ((left, 0), (right, cells - 1)):
        edge[...] = jnp.zeros_like(edge)
        for n in range(planes):
            at = n * cells + (row // SUB * SUB)
            edge[n : n + 1, :] = x[at : at + SUB, :].astype(jnp.float32)[row % SUB : row % SUB + 1]
        for n in range(planes // 2):
            at = n * half + row // 2
            edge[SUB + n : SUB + n + 1, : length // 2] = out[at : at + 1, :]


def beside(parts, ends):
    lane = lax.broadcasted_iota(jnp.int32, parts[0].shape, 1)
    ahead = [pltpu.roll(x, 1, 1) for x in parts]
    behind = [pltpu.roll(x, LANE - 1, 1) for x in parts]
    sums = []
    for i in range(len(parts)):
        left = jnp.where(lane == 0, ahead[i - 1] if i else ends[0], ahead[i])
        right = jnp.where(
            lane == LANE - 1, behind[i + 1] if i + 1 < len(parts) else ends[1], behind[i]
        )
        sums.append(left + right)
    return sums


def first_sweep(tiles, ext, mid, lower, upper, f, store):
    for top in range(0, ext, SUB):
        end = top + SUB
        parts = [mid(x, top, end) for x in range(tiles)]
        for x, both in enumerate(beside(parts, (parts[0], parts[-1]))):
            k = parts[x]
            above = pltpu.roll(k, 1, 0) if top == 0 else mid(x, top - 1, end - 1)
            below = pltpu.roll(k, SUB - 1, 0) if end == ext else mid(x, top + 1, end + 1)
            total = (lower(x, top, end) + upper(x, top, end)) + (above + below) + both
            scale = JACOBI_WEIGHT / (6.0 * k + total)
            u = f(x, top, end) * (2.0 * scale)
            store(x, top, end, u, k * u, scale)


def second_sweep(tiles, ext, k, u, w, r, store):
    for top in range(SUB, ext - SUB, SUB):
        end = top + SUB
        sums = []
        for lower, mid, upper in (u, w):
            parts = [mid(x, top, end) for x in range(tiles)]
            sums.append(
                [
                    both
                    + (lower(x, top, end) + upper(x, top, end))
                    + (mid(x, top - 1, end - 1) + mid(x, top + 1, end + 1))
                    for x, both in enumerate(beside(parts, (0.0, 0.0)))
                ]
            )
        for x in range(tiles):
            coupled = k(x, top, end) * sums[0][x] + sums[1][x]
            value = (2.0 - JACOBI_WEIGHT) * u[1](x, top, end) + r(x, top, end) * coupled
            store(x, top, end, value)


def plane_of(held, *at):
    return lambda x, top, end: held[(*at, x, slice(top, end), slice(None))]


def put_rows(held, to, at, rows):
    for x in range(held.shape[1]):
        held[to, x, at : at + rows.shape[0], :] = rows[:, x * LANE : (x + 1) * LANE]


def repeat_sides(flags, held, at):
    end = held.shape[-2] - SUB

    @pl.when(flags[2] == 1)
    def _():
        for p in at:
            held[(*p, slice(None), slice(SUB - 1, SUB))] = held[(*p, slice(None), slice(SUB, SUB + 1))]

    @pl.when(flags[3] == 1)
    def _():
        for p in at:
            held[(*p, slice(None), slice(end, end + 1))] = held[
                (*p, slice(None), slice(end - 1, end))
            ]


def put_block(fine, held, to, source, row, cells, length):
    if fine:
        put_rows(held, to, SUB, source[row : row + cells, :])
    else:
        half = cells // 2
        put_rows(held, to, SUB, source[row : row + half, :length])
        put_rows(held, to, SUB + half, source[row : row + half, length:])


def layout_kernel(sizes, flags, *rest):
    away, outs, near, sems = rest[:6], rest[6:10], rest[10:16], rest[16]
    for copy in load(list(zip(away, near)), sems):
        copy.wait()
    source, coarse_source, *edges = near
    sides = edges[2:]
    for fine, inner, outer in ((True, *outs[:2]), (False, *outs[2:])):
        planes, cells, length = sizes if fine else [n // 2 for n in sizes]
        f = source if fine else coarse_source
        source_row = 0 if fine else SUB

        def plane(held, to, p):
            put_rows(held, to, SUB, f[p].astype(jnp.float32))
            for side, row in zip(sides, (SUB - 1, SUB + cells)):
                at = source_row + p
                put_rows(held, to, row, side[at : at + 1, :length])

        for p in range(1, planes - 1):
            plane(inner, p - 1, p)
        row = 0 if fine else 2 * cells
        for group, edge in ((flags[4], edges[0]), (1 - flags[4], edges[1])):
            put_block(fine, outer.at[group], 0, edge, row, cells, length)
        for group, p in enumerate((0, planes - 1)):
            plane(outer.at[group], 1, p)


def inner_level(sizes, ks, fs, us, ws, rs):
    planes, _, length = sizes
    tiles, ext = ks.shape[1:3]

    def first(p, carry):
        def store(x, top, end, u, w, r):
            at = (p - 1, x, slice(top, end))
            us[at], ws[at], rs[at] = u, w, r

        near = [plane_of(ks, p + i) for i in (0, -1, 1)]
        first_sweep(tiles, ext, *near, plane_of(fs, p - 1), store)
        return carry

    lax.fori_loop(1, planes - 1, first, 0)


def inner_kernel(sizes, shares, flags, b, eh_hbm, el_hbm, edges, cks, cols, fs, cfs, *rest):
    out_hbm, us, ws, rs, cus, cws, crs, ks, eh, el, lh, ll, out, sems = rest
    planes, cells, length = sizes
    tiles, ext = ks.shape[1:3]
    copies = load([(eh_hbm, eh), (el_hbm, el)], sems)
    middle = range(2, planes - 2)
    gather_modes(b, middle, shares, lh, ll)
    for i, p in enumerate((0, 1, planes - 2, planes - 1)):
        ks[p] = edges[i]
    for h in range(HALO):
        for p in middle:
            at = h * planes + p
            put_rows(ks, p, halo_row(h, cells), cols[at : at + 1, :])
    for copy in copies:
        copy.wait()
    for p in range(2, planes - 2, 2):
        inverse_pair(p - 2, lh, ll, eh, el, ks, p, cells)
    repeat_sides(flags, ks, [(p,) for p in middle])
    inner_level(sizes, ks, fs, us, ws, rs)

    def second(p, carry):
        def store(x, top, end, value):
            out[p - 2, top - SUB : end - SUB, x * LANE : (x + 1) * LANE] = value

        u, w = ([plane_of(held, p - 1 + i) for i in (-1, 0, 1)] for held in (us, ws))
        second_sweep(tiles, ext, plane_of(ks, p), u, w, plane_of(rs, p - 1), store)
        return carry

    lax.fori_loop(2, planes - 2, second, 0)
    copies = send([(out, out_hbm.at[2 : planes - 2])], sems, 0)
    inner_level([n // 2 for n in sizes], cks, cfs, cus, cws, crs)
    for copy in copies:
        copy.wait()


def outer_kernel(sizes, flags, *rest):
    kept, coarse_kept, (k_far, k_near, _, out, coarse_out), rest = (
        rest[:5],
        rest[5:10],
        rest[10:15],
        rest[15:],
    )
    scratch = (rest[:6], rest[6:])
    levels = (sizes, tuple(n // 2 for n in sizes))
    start = 0
    sent = []
    for size, held, given, target in zip(
        levels, scratch, (kept, coarse_kept), (out, coarse_out)
    ):
        planes = size[0]
        ks, fs, inner_us, inner_ws, inner_rs = given
        halo, us, ws, rs, done, sems = held
        tiles, ext = ks.shape[1:3]
        rows = size[1]
        for group, edge in ((flags[4], k_far), (1 - flags[4], k_near)):
            at = start
            for place in range(2 * tiles):
                to = place * ext + SUB
                halo[group, to : to + rows, :] = edge[at : at + rows, :]
                at += rows
            for x in range(tiles):
                to = (tiles + x) * ext
                halo[group, to + SUB - 1 : to + SUB, :] = edge[at + x : at + x + 1, :]
                to += SUB + rows
                halo[group, to : to + 1, :] = edge[at + tiles + x : at + tiles + x + 1, :]
        start = at + SUB
        for group in range(2):

            @pl.when(flags[group] == 1)
            def _():
                for x in range(tiles):
                    at = (tiles + x) * ext
                    halo[group, at : at + ext, :] = ks[3 * group, x]

        def both_ends(group, carry):
            def halo_plane(slot):
                def get(x, top, end):
                    at = (slot * tiles + x) * ext
                    return halo[group, at + top : at + end, :]

                return get

            inwards = lambda i, count: jnp.where(group == 0, i, count - 1 - i)
            own = [plane_of(ks, inwards(i, 4)) for i in range(2)]
            u, w = (
                [plane_of(new, group, i) for i in range(2)]
                + [plane_of(old, inwards(i, planes - 2)) for i in range(2)]
                for new, old in ((us, inner_us), (ws, inner_ws))
            )
            around = ((halo_plane(1), halo_plane(0), own[0]), (own[0], halo_plane(1), own[1]))
            for i, near in enumerate(around):

                def store(x, top, end, u, w, r):
                    at = (group, i, x, slice(top, end))
                    us[at], ws[at] = u, w
                    if i == 1:
                        rs[group, x, top:end, :] = r

                first_sweep(tiles, ext, *near, plane_of(fs, group, i), store)
            scales = (plane_of(rs, group), plane_of(inner_rs, inwards(0, planes - 2)))
            for i, r in enumerate(scales):

                def store(x, top, end, value):
                    done[group, i, top - SUB : end - SUB, x * LANE : (x + 1) * LANE] = value

                second_sweep(tiles, ext, own[i], u[i : i + 3], w[i : i + 3], r, store)
                pltpu.make_async_copy(
                    done.at[group, i], target.at[inwards(i, planes)], sems.at[2 * group + i]
                ).start()
            return carry

        lax.fori_loop(0, 2, both_ends, 0)
        for group, at in enumerate(((0, 1), (planes - 1, planes - 2))):
            for i, p in enumerate(at):
                sent.append(
                    pltpu.make_async_copy(
                        done.at[group, i], target.at[p], sems.at[2 * group + i]
                    )
                )
    for copy in sent:
        copy.wait()


SMEM = pl.BlockSpec(memory_space=pltpu.SMEM)
VMEM = pl.BlockSpec(memory_space=pltpu.VMEM)
AWAY = pl.BlockSpec(memory_space=pltpu.HBM)
ANY = pl.BlockSpec(memory_space=pl.ANY)


def call(kernel, outs, operands, scratch, flops, specs, limit, out_specs=None, aliases=None):
    many = isinstance(outs, (list, tuple))
    written = outs if many else [outs]
    moved = sum(math.prod(x.shape) * x.dtype.itemsize for x in (*operands, *written))
    operands = [
        pltpu.with_memory_space_constraint(x, pltpu.HBM) if spec is AWAY else x
        for x, spec in zip(operands, specs)
    ]
    out_specs = out_specs or [
        VMEM if isinstance(x, jax.ShapeDtypeStruct) else AWAY for x in written
    ]
    return pl.pallas_call(
        kernel,
        out_shape=outs,
        in_specs=specs,
        out_specs=out_specs if many else out_specs[0],
        scratch_shapes=scratch,
        input_output_aliases=aliases or {},
        compiler_params=pltpu.CompilerParams(vmem_limit_bytes=limit * MIB),
        cost_estimate=pl.CostEstimate(flops=flops, bytes_accessed=moved, transcendentals=0),
    )(*operands)


def f32(*shape):
    return jax.ShapeDtypeStruct(shape, jnp.float32)


def room(*arrays):
    return [pltpu.VMEM(x.shape, x.dtype) for x in arrays]


def chain(axis):
    up = [(i, i + 1) for i in range(lax.axis_size(axis) - 1)]
    return up, [(j, i) for i, j in up]


def swap(lo, hi, axis):
    up, down = chain(axis)
    return lax.ppermute(hi, axis, up), lax.ppermute(lo, axis, down)


def trade(x, start):
    rows = lax.axis_size("row")
    pairs = [p for i in range(start, rows - 1, 2) for p in ((i, i + 1), (i + 1, i))]
    return lax.ppermute(x, "row", pairs)


def held_planes(size, *count):
    planes, cells, length = size
    return f32(*count, length // LANE, cells + 2 * SUB, LANE)


def outer_scratch(size):
    planes, cells, length = size
    return room(
        f32(2, 2 * (length // LANE) * (cells + 2 * SUB), LANE),
        held_planes(size, 2, 2),
        held_planes(size, 2, 2),
        held_planes(size, 2),
        f32(2, 2, cells, length),
    ) + [pltpu.SemaphoreType.DMA((4,))]


def fused_body(noise, source):
    rows, groups = lax.axis_size("row"), lax.axis_size(PLANE)
    devices = rows * groups
    planes, cells, length = noise.shape
    first, second = planes * rows, cells * groups
    bf16 = jnp.bfloat16
    held = length // 2 // devices
    js = list(range(held))
    low = held // 2
    me = lax.axis_index(EVERY)
    row_at, group_at = lax.axis_index("row"), lax.axis_index(PLANE)
    flags = jnp.stack(
        [
            row_at == 0,
            row_at == rows - 1,
            group_at == 0,
            group_at == groups - 1,
            row_at % 2 == 1,
        ]
    ).astype(jnp.int32)
    norm = FIELD_SCALE * (float(first) * float(second) * float(length)) ** (-0.5)
    flat = (planes * cells, length)

    pieces = 4
    table = [x.reshape(pieces, -1, length) for x in two_parts(forward_third(length, devices, js))]
    table = np.concatenate(table, axis=1)
    shape = (length * SUB, LANE)
    sent = call(
        functools.partial(forward_kernel, planes),
        pltpu.HBM(shape, jnp.float32),
        (table, noise.reshape(flat)),
        room(table)
        + [
            pltpu.VMEM(flat, bf16),
            pltpu.VMEM(shape, jnp.float32),
            pltpu.SemaphoreType.DMA((2 * pieces + planes // 2,)),
        ],
        4 * length * length * planes * cells,
        [AWAY] * 2,
        12,
    )
    sent, source = lax.optimization_barrier((sent, source))
    sent = sent.reshape(devices, 2 * held, SUB, LANE)
    arrived = lax.all_to_all(sent, EVERY, split_axis=0, concat_axis=0, tiled=True)

    pairs = np.zeros((length, length // 2), np.float32)
    pairs[np.arange(length), np.arange(length) // 2] = 0.125
    level = f32(cells + cells // 4, length)
    side = f32(2 * SUB, length)
    coarse_source, *edges = call(
        functools.partial(source_kernel, planes),
        [f32(planes * cells // 4, length // 2), level, level, side, side],
        (flags, pairs.astype(bf16), source.reshape(flat)),
        [
            pltpu.VMEM((planes * cells, length // 2), jnp.float32),
            pltpu.VMEM((cells, LANE), jnp.float32),
        ],
        planes * cells * length * length,
        [SMEM] + [VMEM] * 2,
        12,
    )
    coarse_source = coarse_source.reshape(planes // 2, cells // 2, length // 2)
    far, near, *sides = edges
    near, sides = trade(near, 0), swap(*sides, PLANE)
    arrived, far, near, sides, coarse_source = lax.optimization_barrier(
        (arrived, far, near, sides, coarse_source)
    )
    edges = (trade(far, 1), near, *sides)

    constants = (
        two_parts(second_table(second))
        + (
            stacked(forward_first(first)),
            stacked(inverse_first(first)),
            stacked(inverse_first_coarse(first // 2, rows)),
        )
        + two_parts(second_coarse(second // 2, groups))
        + two_parts(second_table(second).transpose(0, 2, 1))
    )
    tiles = 2 * held + low // 2 + 1
    modes = (me + devices * np.array(js)).astype(jnp.float32)
    weight = jnp.where(modes == 0.0, norm, 2.0 * norm).astype(jnp.float32)
    scale = jnp.stack([DECAY * modes * modes, weight], axis=1)
    block = (2, 2 * held * first, second // 2)
    shape = (devices, tiles, SUB, LANE)
    out = call(
        functools.partial(middle_kernel, (first, second, rows, groups, held, low)),
        pltpu.HBM(shape, jnp.float32),
        (scale, arrived, *constants),
        room(*constants)
        + [
            pltpu.VMEM(shape, jnp.float32),
            pltpu.SemaphoreType.DMA((len(constants),)),
            pltpu.VMEM(block, bf16),
            pltpu.VMEM(block, bf16),
            pltpu.VMEM(block, jnp.float32),
            pltpu.VMEM(block, bf16),
            pltpu.VMEM(block, bf16),
            pltpu.VMEM((low // 2 * first, second), bf16),
            pltpu.VMEM((low // 2 * first, second), bf16),
        ],
        6 * 2 * 2 * held * first * second * (second + 2 * first),
        [SMEM, VMEM] + [AWAY] * len(constants),
        22,
    )
    out, source, coarse_source, edges = lax.optimization_barrier(
        (out, source, coarse_source, edges)
    )
    got = lax.all_to_all(out, EVERY, split_axis=0, concat_axis=0, tiled=True)
    size, coarse_size = noise.shape, coarse_source.shape
    sizes = (size, coarse_size)
    sources = (source, coarse_source, *edges)
    laid = call(
        functools.partial(layout_kernel, size),
        [
            held_planes(s, *count)
            for s in sizes
            for count in ((s[0] - 2,), (2, 2))
        ],
        (flags, *sources),
        room(*sources) + [pltpu.SemaphoreType.DMA((6,))],
        source.size,
        [SMEM] + [AWAY] * 6,
        12,
    )
    got, laid = lax.optimization_barrier((got, laid))

    third = inverse_third(length, devices, js)
    constants = (
        two_parts(third)
        + two_parts(third_coarse(length // 2, devices, js[:low]))
        + (lane_order(2 * held, low).astype(bf16),)
        + two_parts(third_coarse_halo(length // 2, devices, js[:low]))
    )
    edge = f32(sum(2 * (s[2] // LANE) * s[1] + SUB for s in sizes), LANE)
    shares = (devices, 2 * held, tiles)
    got = got.reshape(devices * tiles * SUB, LANE)
    ks, coarse_ks, cols, far, near = call(
        functools.partial(edge_kernel, (devices, 2 * held, low, tiles, planes, length)),
        [held_planes(s, 4) for s in sizes] + [f32(HALO * planes, length), edge, edge],
        (flags, got, *constants),
        room(*constants)
        + [pltpu.VMEM((2, 4 * cells, devices * held), bf16)] * 2
        + [pltpu.VMEM((planes // 2 * LANE, devices * low), bf16)] * 2
        + [pltpu.SemaphoreType.DMA((7,))],
        3 * planes * cells * length * length,
        [SMEM, VMEM] + [AWAY] * 7,
        16,
    )
    k_far, k_near = trade(far, 1), trade(near, 0)
    inner_f, outer_f, coarse_inner_f, coarse_outer_f = laid
    inner, *kept = call(
        functools.partial(inner_kernel, size, shares),
        [pltpu.HBM(size, jnp.float32)] + [held_planes(s, s[0] - 2) for s in sizes for _ in range(3)],
        (flags, got, *constants[:2], ks, coarse_ks, cols, inner_f, coarse_inner_f),
        room(held_planes(size, planes), *constants[:2])
        + [pltpu.VMEM((2, (planes - 4) * cells, devices * held), bf16)] * 2
        + room(f32(planes - 4, cells, length))
        + [pltpu.SemaphoreType.DMA((2,))],
        3 * planes * cells * length * length,
        [SMEM, VMEM] + [AWAY] * 2 + [VMEM] * 5,
        18,
    )
    return call(
        functools.partial(outer_kernel, size),
        [pltpu.HBM(s, jnp.float32) for s in sizes],
        (flags, ks, outer_f, *kept[:3], coarse_ks, coarse_outer_f, *kept[3:], k_far, k_near, inner),
        outer_scratch(size) + outer_scratch(coarse_size),
        30 * source.size,
        [SMEM] + [VMEM] * 12 + [AWAY],
        18,
        None,
        {13: 0},
    )


NEIGHBOUR_STEPS = ((1, 0, 0), (-1, 0, 0), (0, 1, 0), (0, -1, 0), (0, 0, 1), (0, 0, -1))


def padded(x, sides, width):
    for axis, dim in sides:
        peers, length = (lax.axis_size(axis), x.shape[dim])
        up = [(i, (i + 1) % peers) for i in range(peers - 1)]
        down = [(j, i) for i, j in up]
        last = lax.slice_in_dim(x, length - width, length, axis=dim)
        leading = lax.slice_in_dim(x, 0, width, axis=dim)
        before = lax.ppermute(last, axis, up)
        after = lax.ppermute(leading, axis, down)
        x = jnp.concatenate([before, x, after], axis=dim)
    return x


def signed_modes(index, length):
    return jnp.where(index < length // 2, index, index - length).astype(jnp.float32)


def amplitude(first_modes, second_modes, third_modes, first_edge, second_edge, third_edge):
    squared = first_modes * first_modes + second_modes * second_modes + third_modes * third_modes
    value = FIELD_SCALE / (1.0 + (2.0 * math.pi * CORRELATION) ** 2 * squared)
    edge = (
        (jnp.abs(first_modes) == first_edge)
        | (jnp.abs(second_modes) == second_edge)
        | (jnp.abs(third_modes) == third_edge)
    )
    return jnp.where(edge, 0.0, value)


def phase_table(count_rows, count_cols, modulus, sign):
    left_index = jnp.arange(count_rows, dtype=jnp.int32)[:, None]
    right_index = jnp.arange(count_cols, dtype=jnp.int32)[None, :]
    angle = 2.0 * math.pi / modulus * (left_index * right_index % modulus).astype(jnp.float32)
    return (jnp.cos(angle), sign * jnp.sin(angle))


def split_length(length):
    outer_len = 2 ** ((length.bit_length() - 1) // 2)
    return (outer_len, length // outer_len)


def real_form(form, left_value, right_value):
    return jnp.einsum(form, left_value, right_value, precision=lax.Precision.HIGHEST)


def complex_form(form, left_real, left_imag, right_real, right_imag):
    real_part = real_form(form, left_real, right_real) - real_form(form, left_imag, right_imag)
    imag_part = real_form(form, left_real, right_imag) + real_form(form, left_imag, right_real)
    return (real_part, imag_part)


def merge_pair(values, out_form, first_letter):
    merge_at = out_form.index(first_letter)
    out_dims = list(values.shape)
    merged = (
        out_dims[:merge_at]
        + [out_dims[merge_at] * out_dims[merge_at + 1]]
        + out_dims[merge_at + 2 :]
    )
    return values.reshape(merged)


def forward_axis(real_part, imag_part, lead_form, out_form, kept_modes):
    length = real_part.shape[-1]
    outer_len, inner_len = split_length(length)
    split_shape = real_part.shape[:-1] + (outer_len, inner_len)
    outer_real, outer_imag = phase_table(outer_len, outer_len, outer_len, -1.0)
    twist_real, twist_imag = phase_table(outer_len, inner_len, length, -1.0)
    inner_real, inner_imag = phase_table(inner_len, kept_modes // outer_len, inner_len, -1.0)
    first_form = lead_form + "ab,ai->" + lead_form + "ib"
    split_real = real_part.reshape(split_shape)
    if imag_part is None:
        section_real = real_form(first_form, split_real, outer_real)
        section_imag = real_form(first_form, split_real, outer_imag)
    else:
        section_real, section_imag = complex_form(
            first_form, split_real, imag_part.reshape(split_shape), outer_real, outer_imag
        )
    turned_real = section_real * twist_real - section_imag * twist_imag
    turned_imag = section_real * twist_imag + section_imag * twist_real
    result_real, result_imag = complex_form(
        lead_form + "ib,bj->" + out_form, turned_real, turned_imag, inner_real, inner_imag
    )
    return (merge_pair(result_real, out_form, "j"), merge_pair(result_imag, out_form, "j"))


def inverse_axis(real_part, imag_part, length, lead_form, out_form, real_only):
    kept_modes = real_part.shape[-1]
    outer_len, inner_len = split_length(length)
    split_shape = real_part.shape[:-1] + (kept_modes // outer_len, outer_len)
    inner_real, inner_imag = phase_table(kept_modes // outer_len, inner_len, inner_len, 1.0)
    twist_real, twist_imag = phase_table(outer_len, inner_len, length, 1.0)
    outer_real, outer_imag = phase_table(outer_len, outer_len, outer_len, 1.0)
    section_real, section_imag = complex_form(
        lead_form + "ji,jb->" + lead_form + "ib",
        real_part.reshape(split_shape),
        imag_part.reshape(split_shape),
        inner_real,
        inner_imag,
    )
    turned_real = section_real * twist_real - section_imag * twist_imag
    turned_imag = section_real * twist_imag + section_imag * twist_real
    second_form = lead_form + "ib,ia->" + out_form
    if real_only:
        result = real_form(second_form, turned_real, outer_real) - real_form(
            second_form, turned_imag, outer_imag
        )
        return merge_pair(result, out_form, "a")
    result_real, result_imag = complex_form(
        second_form, turned_real, turned_imag, outer_real, outer_imag
    )
    return (merge_pair(result_real, out_form, "a"), merge_pair(result_imag, out_form, "a"))


def low_band(values, half_coarse, fine_len):
    return jnp.concatenate(
        [values[:, :, :half_coarse], values[:, :, fine_len - half_coarse :]], axis=2
    )


def window(values, margin, offset):
    return values[
        margin + offset[0] : values.shape[0] - margin + offset[0],
        margin + offset[1] : values.shape[1] - margin + offset[1],
        margin + offset[2] : values.shape[2] - margin + offset[2],
    ]


def face_weight(center, beside):
    return jnp.where(beside > 0.0, 0.5 * (center + beside), center)


def smooth_twice(kappa, source):
    no_shift = (0, 0, 0)
    center = window(kappa, 1, no_shift)
    faces = [face_weight(center, window(kappa, 1, offset)) for offset in NEIGHBOUR_STEPS]
    diagonal = faces[0] + faces[1] + faces[2] + faces[3] + faces[4] + faces[5]
    guarded = jnp.where(center > 0.0, diagonal, 1.0)
    first_sweep = JACOBI_WEIGHT * window(source, 1, no_shift) / guarded
    inner_first = window(first_sweep, 1, no_shift)
    inner_diagonal = window(diagonal, 1, no_shift)
    coupled = jnp.zeros_like(inner_first)
    for face_value, offset in zip(faces, NEIGHBOUR_STEPS):
        coupled = coupled + window(face_value, 1, no_shift) * window(first_sweep, 1, offset)
    residual = window(source, 2, no_shift) - inner_diagonal * inner_first + coupled
    return inner_first + JACOBI_WEIGHT * residual / inner_diagonal


def pad_depth(values):
    return jnp.pad(values, ((0, 0), (0, 0), (2, 2)))


def plain_body(noise, source):
    row_at = lax.axis_index("row")
    group_at = lax.axis_index(("level", "col"))
    fine_field = noise.astype(jnp.float32)
    fine_len = fine_field.shape[-1]
    coarse_len = fine_len // 2
    half_coarse = coarse_len // 2
    kept_modes = fine_len // 2
    real_part, imag_part = forward_axis(fine_field, None, "pq", "pjiq", kept_modes)
    real_part, imag_part = (
        lax.all_to_all(real_part, ("level", "col"), split_axis=1, concat_axis=2, tiled=True),
        lax.all_to_all(imag_part, ("level", "col"), split_axis=1, concat_axis=2, tiled=True),
    )
    real_part, imag_part = forward_axis(real_part, imag_part, "pq", "jiqp", fine_len)
    real_part, imag_part = (
        lax.all_to_all(real_part, "row", split_axis=0, concat_axis=2, tiled=True),
        lax.all_to_all(imag_part, "row", split_axis=0, concat_axis=2, tiled=True),
    )
    slab_len = real_part.shape[-1]
    coarse_slab = slab_len // 2
    half_slab = coarse_slab // 2
    real_part, imag_part = forward_axis(real_part, imag_part, "pq", "pqji", slab_len)
    second_count = real_part.shape[0]
    third_count = real_part.shape[1]
    wave_second = signed_modes(
        row_at * second_count + jnp.arange(second_count, dtype=jnp.int32), fine_len
    )[:, None, None]
    third_index = group_at * third_count + jnp.arange(third_count, dtype=jnp.int32)
    wave_third = signed_modes(third_index, fine_len)[None, :, None]
    spread = 2.0
    mirror_weight = jnp.where(third_index == 0, 1.0, spread).astype(jnp.float32)[None, :, None]
    norm_factor = (float(slab_len) * float(fine_len) * float(fine_len)) ** (-0.5)
    wave_first = signed_modes(jnp.arange(slab_len, dtype=jnp.int32), slab_len)[None, None, :]
    fine_scale = (
        amplitude(
            wave_second, wave_third, wave_first, fine_len / 2.0, fine_len / 2.0, slab_len / 2.0
        )
        * mirror_weight
        * norm_factor
    )
    coarse_first = signed_modes(jnp.arange(coarse_slab, dtype=jnp.int32), coarse_slab)[
        None, None, :
    ]
    coarse_scale = (
        amplitude(
            wave_second,
            wave_third,
            coarse_first,
            coarse_len / 2.0,
            coarse_len / 2.0,
            coarse_slab / 2.0,
        )
        * mirror_weight
        * norm_factor
    )
    coarse_real = low_band(real_part, half_slab, slab_len) * coarse_scale
    coarse_imag = low_band(imag_part, half_slab, slab_len) * coarse_scale
    fine_real, fine_imag = inverse_axis(
        real_part * fine_scale, imag_part * fine_scale, slab_len, "pq", "abqp", False
    )
    coarse_real, coarse_imag = inverse_axis(
        coarse_real, coarse_imag, coarse_slab, "pq", "abqp", False
    )
    fine_real, fine_imag, coarse_real, coarse_imag = (
        lax.all_to_all(fine_real, "row", split_axis=0, concat_axis=2, tiled=True),
        lax.all_to_all(fine_imag, "row", split_axis=0, concat_axis=2, tiled=True),
        lax.all_to_all(coarse_real, "row", split_axis=0, concat_axis=2, tiled=True),
        lax.all_to_all(coarse_imag, "row", split_axis=0, concat_axis=2, tiled=True),
    )
    coarse_real = low_band(coarse_real, half_coarse, fine_len)
    coarse_imag = low_band(coarse_imag, half_coarse, fine_len)
    fine_real, fine_imag = inverse_axis(fine_real, fine_imag, fine_len, "pq", "pabq", False)
    coarse_real, coarse_imag = inverse_axis(
        coarse_real, coarse_imag, coarse_len, "pq", "pabq", False
    )
    fine_real, fine_imag, coarse_real, coarse_imag = (
        lax.all_to_all(fine_real, ("level", "col"), split_axis=1, concat_axis=2, tiled=True),
        lax.all_to_all(fine_imag, ("level", "col"), split_axis=1, concat_axis=2, tiled=True),
        lax.all_to_all(coarse_real, ("level", "col"), split_axis=1, concat_axis=2, tiled=True),
        lax.all_to_all(coarse_imag, ("level", "col"), split_axis=1, concat_axis=2, tiled=True),
    )
    coarse_real = coarse_real[:, :, :half_coarse]
    coarse_imag = coarse_imag[:, :, :half_coarse]
    fine_log = inverse_axis(fine_real, fine_imag, fine_len, "pq", "pqab", True)
    coarse_log = inverse_axis(coarse_real, coarse_imag, coarse_len, "pq", "pqab", True)
    fine_kappa = jnp.exp(fine_log)
    coarse_kappa = jnp.exp(coarse_log)
    fine_source = source.astype(jnp.float32)
    coarse_rows = coarse_log.shape[0]
    coarse_cols = coarse_log.shape[1]
    coarse_source = fine_source.reshape(coarse_rows, 2, coarse_cols, 2, coarse_len, 2).mean(
        axis=(1, 3, 5)
    )
    fine_kappa, fine_source, coarse_kappa, coarse_source = (
        padded(fine_kappa, (("row", 0), (("level", "col"), 1)), 2),
        padded(fine_source, (("row", 0), (("level", "col"), 1)), 2),
        padded(coarse_kappa, (("row", 0), (("level", "col"), 1)), 2),
        padded(coarse_source, (("row", 0), (("level", "col"), 1)), 2),
    )
    fine_pressure = smooth_twice(pad_depth(fine_kappa), pad_depth(fine_source))
    coarse_pressure = smooth_twice(pad_depth(coarse_kappa), pad_depth(coarse_source))
    return (fine_pressure, coarse_pressure)


def body(noise, source):
    planes, cells, length = noise.shape
    rows, groups = lax.axis_size("row"), lax.axis_size(PLANE)
    modes = length // 2 // (rows * groups)
    fills = planes == SUB and cells == LANE and 2 * HALO * modes == LANE // 2
    if fills and length % (4 * LANE) == 0 and rows % 2 == 0 and groups % 4 == 0:
        return fused_body(noise, source)
    return plain_body(noise, source)


def solution(mesh):
    return jax.shard_map(
        body,
        mesh=mesh,
        in_specs=(P("row", ("level", "col"), None), P("row", ("level", "col"), None)),
        out_specs=(P("row", ("level", "col"), None), P("row", ("level", "col"), None)),
        check_vma=False,
    )
```

```python
import functools
import math

import jax
import jax.numpy as jnp
import numpy as np
from jax import lax
from jax.experimental import pallas as pl
from jax.experimental.pallas import tpu as pltpu
from jax.sharding import PartitionSpec as P

JACOBI_WEIGHT = 2.0 / 3.0
CORRELATION = 0.2
FIELD_SCALE = 0.3
DECAY = (2.0 * math.pi * CORRELATION) ** 2
EVERY = ("row", "level", "col")
PLANE = ("level", "col")
MIB = 1 << 20
SUB, LANE = 8, 128
HALO = 4


def two_parts(matrix):
    high = matrix.astype(jnp.bfloat16)
    low = (matrix - high.astype(np.float64)).astype(jnp.bfloat16)
    return high, low


def angles(rows, cols, length):
    return 2.0 * np.pi * (np.outer(rows, cols) % length) / length


def third_modes(devices, js):
    return np.array([[d + devices * j for j in js] for d in range(devices)])


def forward_third(length, devices, js):
    theta = angles(third_modes(devices, js).reshape(-1), np.arange(length), length)
    return np.stack([np.cos(theta), -np.sin(theta)], axis=1).reshape(-1, length)


def inverse_third(length, devices, js):
    modes = third_modes(devices, js).reshape(devices // 2, 2, len(js)).transpose(1, 0, 2)
    theta = 2.0 * np.pi * (modes[..., None] * np.arange(length // 2) % length) / length
    both = np.stack([np.cos(theta), -np.sin(theta)], axis=3)
    return both.reshape(2, -1, length // 2)


def second_modes(length):
    return np.arange(length // 2).reshape(-1, 2).T


def second_table(length):
    theta = second_modes(length)[:, None, :] * np.arange(length // 2)[None, :, None]
    theta = 2.0 * np.pi * (theta % length) / length
    return np.concatenate([np.cos(theta), np.sin(theta)], axis=2)


def forward_first(length):
    theta = angles(np.arange(length), np.arange(length), length)
    cos, sin = np.cos(theta), np.sin(theta)
    return np.block([[cos, sin], [-sin, cos]])


def inverse_first(length):
    theta = angles(np.arange(length), np.arange(length), length)
    cos, sin = np.cos(theta), np.sin(theta)
    cos[:, length // 2] = 0.0
    sin[:, length // 2] = 0.0
    return np.block([[cos, -sin], [sin, cos]])


def inverse_first_coarse(length, rows):
    full = inverse_first(length)
    value = full.reshape(2, rows, length // rows, 2 * length)
    turned = np.concatenate([-full[length:], full[:length]]).reshape(value.shape)
    order = lambda x: x.transpose(1, 0, 2, 3).reshape(2 * length, 2 * length)
    return np.concatenate([order(value), order(turned)])


def second_coarse(length, groups):
    theta = angles(second_modes(length).reshape(-1), np.arange(length), length)
    table = np.concatenate([np.cos(theta), np.sin(theta)])
    span = length // groups
    out = np.zeros((2, length, groups, 2, span))
    for pair in range(2):
        out[pair, :, :, pair, :] = table.reshape(length, groups, span)
    return out.reshape(2 * length, 2 * length)


def third_coarse(length, devices, js):
    modes = third_modes(devices, js).reshape(devices, len(js) // 2, 2)
    theta = 2.0 * np.pi * (modes[..., None] * np.arange(length) % length) / length
    both = np.stack([np.cos(theta), -np.sin(theta)])
    return both.transpose(0, 2, 1, 3, 4).reshape(2 * (len(js) // 2) * devices, 2 * length)


def third_coarse_halo(length, devices, js):
    theta = angles(third_modes(devices, js).reshape(-1), np.arange(length), length)
    return np.concatenate([np.cos(theta), -np.sin(theta)], axis=1)


def lane_order(parts, coarse_parts):
    out = np.zeros((LANE, LANE))
    for h in range(HALO):
        for q in range(parts):
            out[HALO * q + h, parts * h + q] = 1.0
        for j in range(coarse_parts):
            out[LANE // 2 + HALO * j + h, LANE // 2 + coarse_parts * h + j] = 1.0
    return out


def split(x):
    high = x.astype(jnp.bfloat16)
    return high, (x - high.astype(jnp.float32)).astype(jnp.bfloat16)


def dot(a, b):
    return lax.dot_general(a, b, (((1,), (0,)), ((), ())), preferred_element_type=jnp.float32)


def dot_t(a, b):
    return lax.dot_general(a, b, (((1,), (1,)), ((), ())), preferred_element_type=jnp.float32)


def stacked(matrix):
    high, low = two_parts(matrix)
    return np.block([[high, high], [low, np.zeros_like(low)]])


def dot_left(stack, x):
    value = dot(stack, jnp.concatenate(split(x), axis=0))
    rows = stack.shape[0] // 2
    return value[:rows] + value[rows:]


def dot3(a, b):
    (ah, al), (bh, bl) = a, b
    return dot(ah, bh) + (dot(ah, bl) + dot(al, bh))


def load(pairs, sems):
    copies = [pltpu.make_async_copy(a, b, sems.at[i]) for i, (a, b) in enumerate(pairs)]
    for copy in copies:
        copy.start()
    return copies


def send(pairs, sems, first):
    copies = [pltpu.make_async_copy(a, b, sems.at[first + i]) for i, (a, b) in enumerate(pairs)]
    for copy in copies:
        copy.start()
    return copies


def forward_kernel(planes, d_hbm, x_hbm, out_hbm, d, x, out, sems):
    pieces, rows = d.shape[0], d.shape[1] // 2
    parts = [slice(p * LANE, (p + 2) * LANE) for p in range(0, planes, 2)]
    pairs = [(x_hbm.at[at, :], x.at[at, :]) for at in parts]
    copies = load([(d_hbm.at[0], d.at[0])] + pairs + [(d_hbm.at[i], d.at[i]) for i in range(1, pieces)], sems)
    sent = []
    copies[0].wait()
    for piece in range(pieces):
        if piece:
            copies[len(parts) + piece].wait()
        for i, at in enumerate(parts):
            if piece == 0:
                copies[i + 1].wait()
            value = dot_t(d[piece], x[at, :])
            value = value[:rows] + value[rows:]
            for h in range(2):
                out[pl.ds(piece * rows * SUB + 2 * i + h, rows, stride=SUB), :] = value[
                    :, h * LANE : (h + 1) * LANE
                ]
        tall = slice(piece * rows * SUB, (piece + 1) * rows * SUB)
        sent += send([(out.at[tall, :], out_hbm.at[tall, :])], sems, len(copies) + piece)
    for copy in sent:
        copy.wait()


def middle_kernel(sizes, scale, b, *rest):
    (first, second, rows, groups, js, low) = sizes
    count = 9
    away, out_hbm, near, rest = (
        rest[:count],
        rest[count],
        rest[count + 1 : 2 * count + 1],
        rest[2 * count + 1 :],
    )
    out, sems, zh, zl, y, oh, ol, qh, ql = rest
    copies = load(list(zip(away, near)), sems)
    csh, csl, forward, inverse, coarse_inverse, cch, ccl, ch, cl = near
    q_count = 2 * js
    half, quarter = second // 2, second // 4
    for q in range(q_count):
        for g in range(groups // 2):
            for r in range(0, rows, 2):
                at = r * groups + g
                near_half = jnp.concatenate([b[at, q], b[at + groups, q]], axis=0)
                at += groups // 2
                far_half = jnp.concatenate([b[at, q], b[at + groups, q]], axis=0)
                at = slice(q * first + r * SUB, q * first + (r + 2) * SUB)
                lanes = slice(g * LANE, (g + 1) * LANE)
                zh[0, at, lanes], zl[0, at, lanes] = split(near_half + far_half)
                zh[1, at, lanes], zl[1, at, lanes] = split(near_half - far_half)
    for copy in copies[:5]:
        copy.wait()
    wide = 8 * first
    for top in range(0, q_count * first, wide):
        at = slice(top, top + wide)
        for parity in range(2):
            y[parity, at, :] = dot3(
                (zh[parity, at, :], zl[parity, at, :]), (csh[parity], csl[parity])
            )
    mode0 = lax.broadcasted_iota(jnp.int32, (first, second), 0)
    mode0 = jnp.where(mode0 < first // 2, mode0, mode0 - first).astype(jnp.float32)
    lane = lax.broadcasted_iota(jnp.int32, (first, second), 1)
    mode1 = jnp.where(lane < half, lane, lane - half)
    mode1 = jnp.where(mode1 < quarter, 2 * mode1, 2 * (mode1 - quarter) + 1).astype(jnp.float32)
    base = 1.0 + DECAY * (mode0 * mode0 + mode1 * mode1)
    for j in range(js):
        top = j * 2 * first
        re, im = slice(top, top + first), slice(top + first, top + 2 * first)
        cos, sin = slice(0, quarter), slice(quarter, half)
        whole = lambda part, lanes: jnp.concatenate(
            [y[0, part, lanes], y[1, part, lanes]], axis=1
        )
        rc, rs, ic, isn = whole(re, cos), whole(re, sin), whole(im, cos), whole(im, sin)
        wave = jnp.concatenate(
            [
                jnp.concatenate([rc + isn, rc - isn], axis=1),
                jnp.concatenate([ic - rs, ic + rs], axis=1),
            ],
            axis=0,
        )
        spectrum = dot_left(forward[...], wave)
        amp = jnp.where(lane == half, 0.0, scale[j, 1] / (base + scale[j, 0]))
        scaled = spectrum * jnp.concatenate([amp, amp], axis=0)
        field = dot_left(inverse[...], scaled)
        plus, minus = field[:, :half], field[:, half:]
        even, odd = plus + minus, plus - minus
        odd = jnp.concatenate([-odd[first:], odd[:first]], axis=0)
        at = slice(top, top + 2 * first)
        for parity, lanes in enumerate((cos, sin)):
            operand = jnp.concatenate([even[:, lanes], odd[:, lanes]], axis=1)
            oh[parity, at, :], ol[parity, at, :] = split(operand)
        if j < low:
            keep = first // 4
            kept = [
                scaled[at : at + keep, :]
                for at in (0, first - keep, first, 2 * first - keep)
            ]
            band = jnp.concatenate(kept, axis=0)
            low_lane = lax.broadcasted_iota(jnp.int32, (first, quarter), 1) < quarter // 2
            pieces = []
            for at in (0, half):
                upper = pltpu.roll(band[:, at + quarter : at + half], quarter // 2, 1)
                pieces.append(jnp.where(low_lane, band[:, at : at + quarter], upper))
            band = jnp.concatenate(pieces, axis=1)
            field = dot_left(coarse_inverse[...], band)
            value, turned = field[:first], field[first:]
            operand = jnp.concatenate(
                [
                    value[:, :quarter] + value[:, quarter:],
                    turned[:, :quarter] - turned[:, quarter:],
                ],
                axis=1,
            )
            at = slice(j // 2 * first, (j // 2 + 1) * first)
            lanes = slice(j % 2 * half, (j % 2 + 1) * half)
            qh[at, lanes], ql[at, lanes] = split(operand)
    for copy in copies[5:]:
        copy.wait()
    copies = []
    wide = 4 * first
    lane = lax.broadcasted_iota(jnp.int32, (SUB, LANE), 1)
    extra = q_count + low // 2

    def leave(start, stop):
        at = slice(start, stop)
        copies.extend(send([(out.at[:, at], out_hbm.at[:, at])], sems, len(copies)))

    def give(value, start):
        tiles = value.shape[0] // first
        for q in range(tiles):
            for r in range(rows):
                for g in range(groups):
                    at = q * first + r * SUB
                    out[r * groups + g, start + q] = value[
                        at : at + SUB, g * LANE : (g + 1) * LANE
                    ]
        leave(start, start + tiles)

    def halo_columns(value, start, held):
        tiles = value.shape[0] // first
        for r in range(rows):
            for g in range(groups):
                total = held[r, g]
                left = max(g - 1, 0) * LANE
                right = min(g + 1, groups - 1) * LANE
                for q in range(tiles):
                    at = slice(q * first + r * SUB, q * first + (r + 1) * SUB)
                    both = jnp.where(
                        lane < LANE // 2,
                        value[at, right : right + LANE],
                        value[at, left : left + LANE],
                    )
                    to = HALO * (start + q)
                    both = pltpu.roll(both, (to + 2) % LANE, 1)
                    total = jnp.where((lane >= to) & (lane < to + HALO), both, total)
                held[r, g] = total

    def coarse_columns(value, held):
        half_lane = LANE // 2
        for j in range(low):
            for r in range(rows):
                at = slice(j // 2 * first + r * SUB, j // 2 * first + (r + 1) * SUB)
                shift = HALO * j + 2 - j % 2 * half_lane
                to = half_lane + HALO * j
                for g in range(groups):
                    left = max(g - 1, 0) * LANE
                    right = min(g + 1, groups - 1) * LANE
                    left = pltpu.roll(value[at, left : left + LANE], shift % LANE, 1)
                    right = pltpu.roll(
                        value[at, right : right + LANE], (shift + half_lane) % LANE, 1
                    )
                    total = jnp.where((lane >= to) & (lane < to + 2), left, held[r, g])
                    held[r, g] = jnp.where(
                        (lane >= to + 2) & (lane < to + HALO), right, total
                    )

    columns = {
        (r, g): jnp.zeros((SUB, LANE), jnp.float32) for r in range(rows) for g in range(groups)
    }
    coarse = dot3((qh[...], ql[...]), (cch[...], ccl[...]))
    give(coarse, q_count)
    coarse_columns(coarse, columns)
    for top in range(0, q_count * first, wide):
        at = slice(top, top + wide)
        even, odd = (
            dot3((oh[parity, at, :], ol[parity, at, :]), (ch[parity], cl[parity]))
            for parity in range(2)
        )
        value = jnp.concatenate([even + odd, even - odd], axis=1)
        give(value, top // first)
        halo_columns(value, top // first, columns)
    for (r, g), total in columns.items():
        out[r * groups + g, extra] = total
    leave(extra, extra + 1)
    for copy in copies:
        copy.wait()


def gather_modes(b, at, sizes, lh, ll):
    devices, q_count, tiles = sizes
    for i, n in enumerate(at):
        for parity in range(2):
            rows = jnp.concatenate(
                [
                    b[pl.ds(s * tiles * SUB + n, q_count, stride=SUB), :]
                    for s in range(parity, devices, 2)
                ],
                axis=0,
            )
            to = slice(i * LANE, (i + 1) * LANE)
            lh[parity, to, :], ll[parity, to, :] = split(jnp.transpose(rows))


def inverse_pair(i, lh, ll, eh, el, ks, to, cells):
    at = slice(i * cells, (i + 2) * cells)
    even, odd = (
        dot3((lh[parity, at, :], ll[parity, at, :]), (eh[parity], el[parity]))
        for parity in range(2)
    )
    value = jnp.exp(jnp.concatenate([even + odd, even - odd], axis=1))
    for n in range(2):
        put_rows(ks, to + n, SUB, value[n * cells : (n + 1) * cells])


def edge_kernel(sizes, flags, b, f, cf, *rest):
    (devices, q_count, low, tiles, planes, length) = sizes
    away, (ks, cks, cols, far, near_edge), rest = rest[:7], rest[7:12], rest[12:]
    near, (lh, ll, mh, ml, sems) = rest[:7], rest[7:]
    copies = load(list(zip(away, near)), sems)
    eh, el, ceh, cel, order, cwh, cwl = near
    cells, short = LANE, length // 2
    halves, coarse_planes = low // 2, planes // 2
    half = cells // 2
    gather_modes(b, (0, 1, planes - 2, planes - 1), (devices, q_count, tiles), lh, ll)
    for n in range(coarse_planes):
        rows = jnp.concatenate(
            [
                b[pl.ds((q_count + h) * SUB + c * coarse_planes + n, devices, stride=tiles * SUB), :]
                for c in range(2)
                for h in range(halves)
            ],
            axis=0,
        )
        at = slice(n * LANE, (n + 1) * LANE)
        mh[at, :], ml[at, :] = split(jnp.transpose(rows))

    for copy in copies[:4]:
        copy.wait()

    for i in range(0, 4, 2):
        inverse_pair(i, lh, ll, eh, el, ks, i, cells)
    value = dot3((mh[...], ml[...]), (ceh[...], cel[...]))
    for n in range(coarse_planes):
        top = n * cells
        part = value[top : top + half, :short] + value[top + half : top + cells, short:]
        part = jnp.exp(part)
        put_rows(cks, n, SUB, part)

    for copy in copies[4:]:
        copy.wait()
    lane = lax.broadcasted_iota(jnp.int32, (SUB, LANE), 1)
    tile_rows = [b[(s * tiles + tiles - 1) * SUB : (s + 1) * tiles * SUB, :] for s in range(devices)]
    high, rest_part = split(jnp.concatenate(tile_rows, axis=0))
    ordered = dot(high, order[...]) + dot(rest_part, order[...])

    def joined(of, width, start):
        fit = LANE // width
        cells_of = []
        for h in range(HALO):
            parts = []
            for i, s in enumerate(of):
                moved = ordered[s * SUB : (s + 1) * SUB]
                shift = (i % fit * width - start - h * width) % LANE
                moved = pltpu.roll(moved, shift, 1) if shift else moved
                if i % fit == 0:
                    parts.append(moved)
                else:
                    parts[-1] = jnp.where(lane >= i % fit * width, moved, parts[-1])
            cells_of.append(jnp.concatenate(parts, axis=1))
        return split(jnp.concatenate(cells_of, axis=0))

    even, odd = (
        dot3(joined(range(parity, devices, 2), q_count, 0), (eh[parity], el[parity]))
        for parity in range(2)
    )
    value = jnp.exp(jnp.concatenate([even + odd, even - odd], axis=1))
    cols[...] = value
    for h in range(HALO):
        for i, n in enumerate((0, 1, planes - 2, planes - 1)):
            at = h * planes + n
            put_rows(ks, i, halo_row(h, cells), value[at : at + 1, :])
    whole = dot3(joined(range(devices), low, LANE // 2), (cwh[...], cwl[...]))
    for h in range(HALO):
        top = h * SUB
        part = whole[top : top + coarse_planes, :short] + whole[top + coarse_planes : top + SUB, short:]
        part = jnp.exp(part)
        for n in range(coarse_planes):
            put_rows(cks, n, halo_row(h, half), part[n : n + 1, :])
    for held in (ks, cks):
        repeat_sides(flags, held, [(n,) for n in range(4)])
    odd_row = flags[4] == 1
    low_end = (jnp.where(odd_row, 2, 1), jnp.where(odd_row, 3, 0))
    high_end = (jnp.where(odd_row, 1, 2), jnp.where(odd_row, 0, 3))
    for edge, of, group in ((far, low_end, flags[4]), (near_edge, high_end, 1 - flags[4])):
        at = 0
        for held, source in ((ks, f), (cks, cf)):
            count, end = held.shape[1], held.shape[2] - SUB
            for n in of:
                for x in range(count):
                    edge[at : at + end - SUB, :] = held[n, x, SUB:end, :]
                    at += end - SUB
            for x in range(count):
                edge[at + x : at + x + 1, :] = held[of[1], x, SUB - 1 : SUB, :]
                edge[at + count + x : at + count + x + 1, :] = held[of[1], x, end : end + 1, :]
            at += SUB
            for x in range(count):
                edge[at : at + end - SUB, :] = source[group, x, SUB:end, :]
                at += end - SUB


def halo_row(h, cells):
    return SUB - 2 + h if h < 2 else SUB + cells + h - 2


def source_kernel(planes, pairs, x, out, left, right, held, summed):
    cells = x.shape[0] // planes
    length = x.shape[1]
    half = cells // 2
    held[...] = dot(x[...], pairs[...])
    for n in range(planes // 2):
        top = 2 * n * cells
        for at in range(0, out.shape[1], LANE):
            lanes = slice(at, at + LANE)
            summed[...] = held[top : top + cells, lanes] + held[top + cells : top + 2 * cells, lanes]
            out[n * half : (n + 1) * half, lanes] = (
                summed[pl.ds(0, half, stride=2), :] + summed[pl.ds(1, half, stride=2), :]
            )
    for edge, row in ((left, 0), (right, cells - 1)):
        edge[...] = jnp.zeros_like(edge)
        for n in range(planes):
            at = n * cells + (row // SUB * SUB)
            edge[n : n + 1, :] = x[at : at + SUB, :].astype(jnp.float32)[row % SUB : row % SUB + 1]
        for n in range(planes // 2):
            at = n * half + row // 2
            edge[SUB + n : SUB + n + 1, : length // 2] = out[at : at + 1, :]


def beside(parts, ends):
    lane = lax.broadcasted_iota(jnp.int32, parts[0].shape, 1)
    ahead = [pltpu.roll(x, 1, 1) for x in parts]
    behind = [pltpu.roll(x, LANE - 1, 1) for x in parts]
    sums = []
    for i in range(len(parts)):
        left = jnp.where(lane == 0, ahead[i - 1] if i else ends[0], ahead[i])
        right = jnp.where(
            lane == LANE - 1, behind[i + 1] if i + 1 < len(parts) else ends[1], behind[i]
        )
        sums.append(left + right)
    return sums


def first_sweep(tiles, ext, mid, lower, upper, f, store):
    for top in range(0, ext, SUB):
        end = top + SUB
        parts = [mid(x, top, end) for x in range(tiles)]
        for x, both in enumerate(beside(parts, (parts[0], parts[-1]))):
            k = parts[x]
            above = pltpu.roll(k, 1, 0) if top == 0 else mid(x, top - 1, end - 1)
            below = pltpu.roll(k, SUB - 1, 0) if end == ext else mid(x, top + 1, end + 1)
            total = (lower(x, top, end) + upper(x, top, end)) + (above + below) + both
            scale = JACOBI_WEIGHT / (6.0 * k + total)
            u = f(x, top, end) * (2.0 * scale)
            store(x, top, end, u, k * u, scale)


def second_sweep(tiles, ext, k, u, w, r, store):
    for top in range(SUB, ext - SUB, SUB):
        end = top + SUB
        sums = []
        for lower, mid, upper in (u, w):
            parts = [mid(x, top, end) for x in range(tiles)]
            sums.append(
                [
                    both
                    + (lower(x, top, end) + upper(x, top, end))
                    + (mid(x, top - 1, end - 1) + mid(x, top + 1, end + 1))
                    for x, both in enumerate(beside(parts, (0.0, 0.0)))
                ]
            )
        for x in range(tiles):
            coupled = k(x, top, end) * sums[0][x] + sums[1][x]
            value = (2.0 - JACOBI_WEIGHT) * u[1](x, top, end) + r(x, top, end) * coupled
            store(x, top, end, value)


def plane_of(held, *at):
    return lambda x, top, end: held[(*at, x, slice(top, end), slice(None))]


def put_rows(held, to, at, rows):
    for x in range(held.shape[1]):
        held[to, x, at : at + rows.shape[0], :] = rows[:, x * LANE : (x + 1) * LANE]


def repeat_sides(flags, held, at):
    end = held.shape[-2] - SUB

    @pl.when(flags[2] == 1)
    def _():
        for p in at:
            held[(*p, slice(None), slice(SUB - 1, SUB))] = held[(*p, slice(None), slice(SUB, SUB + 1))]

    @pl.when(flags[3] == 1)
    def _():
        for p in at:
            held[(*p, slice(None), slice(end, end + 1))] = held[
                (*p, slice(None), slice(end - 1, end))
            ]


def layout_kernel(sizes, *rest):
    away, outs, near, sems = rest[:4], rest[4:8], rest[8:12], rest[12]
    for copy in load(list(zip(away, near)), sems):
        copy.wait()
    source, coarse_source, *sides = near
    for fine, inner, outer in ((True, *outs[:2]), (False, *outs[2:])):
        planes, cells, length = sizes if fine else [n // 2 for n in sizes]
        f = source if fine else coarse_source
        source_row = 0 if fine else SUB

        def plane(held, to, p):
            put_rows(held, to, SUB, f[p].astype(jnp.float32))
            for side, row in zip(sides, (SUB - 1, SUB + cells)):
                at = source_row + p
                put_rows(held, to, row, side[at : at + 1, :length])

        for p in range(1, planes - 1):
            plane(inner, p - 1, p)
        for group, p in enumerate((0, planes - 1)):
            plane(outer, group, p)


def inner_level(sizes, ks, fs, us, ws, rs):
    planes, _, length = sizes
    tiles, ext = ks.shape[1:3]

    def first(p, carry):
        def store(x, top, end, u, w, r):
            at = (p - 1, x, slice(top, end))
            us[at], ws[at], rs[at] = u, w, r

        near = [plane_of(ks, p + i) for i in (0, -1, 1)]
        first_sweep(tiles, ext, *near, plane_of(fs, p - 1), store)
        return carry

    lax.fori_loop(1, planes - 1, first, 0)


def inner_kernel(sizes, shares, flags, b, eh_hbm, el_hbm, edges, cks, cols, fs, cfs, *rest):
    out_hbm, us, ws, rs, cus, cws, crs, ks, eh, el, lh, ll, out, sems = rest
    planes, cells, length = sizes
    tiles, ext = ks.shape[1:3]
    copies = load([(eh_hbm, eh), (el_hbm, el)], sems)
    middle = range(2, planes - 2)
    gather_modes(b, middle, shares, lh, ll)
    for i, p in enumerate((0, 1, planes - 2, planes - 1)):
        ks[p] = edges[i]
    for h in range(HALO):
        for p in middle:
            at = h * planes + p
            put_rows(ks, p, halo_row(h, cells), cols[at : at + 1, :])
    for copy in copies:
        copy.wait()
    for p in range(2, planes - 2, 2):
        inverse_pair(p - 2, lh, ll, eh, el, ks, p, cells)
    repeat_sides(flags, ks, [(p,) for p in middle])
    inner_level(sizes, ks, fs, us, ws, rs)

    def second(p, carry):
        def store(x, top, end, value):
            out[p - 2, top - SUB : end - SUB, x * LANE : (x + 1) * LANE] = value

        u, w = ([plane_of(held, p - 1 + i) for i in (-1, 0, 1)] for held in (us, ws))
        second_sweep(tiles, ext, plane_of(ks, p), u, w, plane_of(rs, p - 1), store)
        return carry

    lax.fori_loop(2, planes - 2, second, 0)
    copies = send([(out, out_hbm.at[2 : planes - 2])], sems, 0)
    inner_level([n // 2 for n in sizes], cks, cfs, cus, cws, crs)
    for copy in copies:
        copy.wait()


def outer_kernel(sizes, near, flags, *rest):
    aliased = 1 if near else 2
    kept, coarse_kept, edge = rest[:5], rest[5:10], rest[10]
    (out, coarse_out), scratch = rest[11 + aliased : 13 + aliased], rest[13 + aliased :]
    half = len(scratch) // 2
    group = 1 - flags[4] if near else flags[4]
    inwards = lambda i, count: jnp.where(group == 0, i, count - 1 - i)
    start, sent = 0, []
    for size, held, given, target in (
        (sizes, scratch[:half], kept, out),
        ([n // 2 for n in sizes], scratch[half:], coarse_kept, coarse_out),
    ):
        planes, rows, _ = size
        ks, fs, inner_us, inner_ws, inner_rs = given
        halo, halo_f, us, ws, rs, done, sems = held
        tiles, ext = ks.shape[1:3]
        at = start
        for place in range(2 * tiles):
            to = place * ext + SUB
            halo[to : to + rows, :] = edge[at : at + rows, :]
            at += rows
        for x in range(tiles):
            to = (tiles + x) * ext
            halo[to + SUB - 1 : to + SUB, :] = edge[at + x : at + x + 1, :]
            to += SUB + rows
            halo[to : to + 1, :] = edge[at + tiles + x : at + tiles + x + 1, :]
        at += SUB
        for x in range(tiles):
            halo_f[0, x, SUB : SUB + rows, :] = edge[at : at + rows, :]
            at += rows
        start = at

        @pl.when(flags[group] == 1)
        def _():
            for x in range(tiles):
                at = (tiles + x) * ext
                halo[at : at + ext, :] = ks[3 * group, x]

        def halo_plane(slot):
            def get(x, top, end):
                at = (slot * tiles + x) * ext
                return halo[at + top : at + end, :]

            return get

        own = [plane_of(ks, inwards(i, 4)) for i in range(2)]
        u, w = (
            [plane_of(new, i) for i in range(2)]
            + [plane_of(old, inwards(i, planes - 2)) for i in range(2)]
            for new, old in ((us, inner_us), (ws, inner_ws))
        )
        around = ((halo_plane(1), halo_plane(0), own[0]), (own[0], halo_plane(1), own[1]))
        sources = (plane_of(halo_f, 0), plane_of(fs, group))
        for i in range(2):

            def store(x, top, end, u, w, r):
                at = (i, x, slice(top, end))
                us[at], ws[at] = u, w
                if i == 1:
                    rs[0, x, top:end, :] = r

            first_sweep(tiles, ext, *around[i], sources[i], store)
        scales = (plane_of(rs, 0), plane_of(inner_rs, inwards(0, planes - 2)))
        for i, r in enumerate(scales):

            def store(x, top, end, value):
                done[i, top - SUB : end - SUB, x * LANE : (x + 1) * LANE] = value

            second_sweep(tiles, ext, own[i], u[i : i + 3], w[i : i + 3], r, store)
            sent += send([(done.at[i], target.at[inwards(i, planes)])], sems, i)
    for copy in sent:
        copy.wait()


SMEM = pl.BlockSpec(memory_space=pltpu.SMEM)
VMEM = pl.BlockSpec(memory_space=pltpu.VMEM)
AWAY = pl.BlockSpec(memory_space=pltpu.HBM)
ANY = pl.BlockSpec(memory_space=pl.ANY)


def call(kernel, outs, operands, scratch, flops, specs, limit, out_specs=None, aliases=None):
    many = isinstance(outs, (list, tuple))
    written = outs if many else [outs]
    moved = sum(math.prod(x.shape) * x.dtype.itemsize for x in (*operands, *written))
    operands = [
        pltpu.with_memory_space_constraint(x, pltpu.HBM) if spec is AWAY else x
        for x, spec in zip(operands, specs)
    ]
    out_specs = out_specs or [
        VMEM if isinstance(x, jax.ShapeDtypeStruct) else AWAY for x in written
    ]
    return pl.pallas_call(
        kernel,
        out_shape=outs,
        in_specs=specs,
        out_specs=out_specs if many else out_specs[0],
        scratch_shapes=scratch,
        input_output_aliases=aliases or {},
        compiler_params=pltpu.CompilerParams(vmem_limit_bytes=limit * MIB),
        cost_estimate=pl.CostEstimate(flops=flops, bytes_accessed=moved, transcendentals=0),
    )(*operands)


def f32(*shape):
    return jax.ShapeDtypeStruct(shape, jnp.float32)


def room(*arrays):
    return [pltpu.VMEM(x.shape, x.dtype) for x in arrays]


def chain(axis):
    up = [(i, i + 1) for i in range(lax.axis_size(axis) - 1)]
    return up, [(j, i) for i, j in up]


def swap(lo, hi, axis):
    up, down = chain(axis)
    return lax.ppermute(hi, axis, up), lax.ppermute(lo, axis, down)


def held_planes(size, *count):
    planes, cells, length = size
    return f32(*count, length // LANE, cells + 2 * SUB, LANE)


def outer_scratch(size):
    planes, cells, length = size
    return room(
        f32(2 * (length // LANE) * (cells + 2 * SUB), LANE),
        held_planes(size, 1),
        held_planes(size, 2),
        held_planes(size, 2),
        held_planes(size, 1),
        f32(2, cells, length),
    ) + [pltpu.SemaphoreType.DMA((2,))]


def fused_body(noise, source):
    rows, groups = lax.axis_size("row"), lax.axis_size(PLANE)
    devices = rows * groups
    planes, cells, length = noise.shape
    first, second = planes * rows, cells * groups
    bf16 = jnp.bfloat16
    held = length // 2 // devices
    js = list(range(held))
    low = held // 2
    me = lax.axis_index(EVERY)
    row_at, group_at = lax.axis_index("row"), lax.axis_index(PLANE)
    flags = jnp.stack(
        [
            row_at == 0,
            row_at == rows - 1,
            group_at == 0,
            group_at == groups - 1,
            row_at % 2 == 1,
        ]
    ).astype(jnp.int32)
    norm = FIELD_SCALE * (float(first) * float(second) * float(length)) ** (-0.5)
    flat = (planes * cells, length)

    pieces = 4
    table = [x.reshape(pieces, -1, length) for x in two_parts(forward_third(length, devices, js))]
    table = np.concatenate(table, axis=1)
    shape = (length * SUB, LANE)
    sent = call(
        functools.partial(forward_kernel, planes),
        pltpu.HBM(shape, jnp.float32),
        (table, noise.reshape(flat)),
        room(table)
        + [
            pltpu.VMEM(flat, bf16),
            pltpu.VMEM(shape, jnp.float32),
            pltpu.SemaphoreType.DMA((2 * pieces + planes // 2,)),
        ],
        4 * length * length * planes * cells,
        [AWAY] * 2,
        12,
    )
    sent, source = lax.optimization_barrier((sent, source))
    sent = sent.reshape(devices, 2 * held, SUB, LANE)
    arrived = lax.all_to_all(sent, EVERY, split_axis=0, concat_axis=0, tiled=True)

    pairs = np.zeros((length, length // 2), np.float32)
    pairs[np.arange(length), np.arange(length) // 2] = 0.125
    side = f32(2 * SUB, length)
    coarse_source, *sides = call(
        functools.partial(source_kernel, planes),
        [f32(planes * cells // 4, length // 2), side, side],
        (pairs.astype(bf16), source.reshape(flat)),
        [
            pltpu.VMEM((planes * cells, length // 2), jnp.float32),
            pltpu.VMEM((cells, LANE), jnp.float32),
        ],
        planes * cells * length * length,
        [VMEM] * 2,
        12,
    )
    coarse_source = coarse_source.reshape(planes // 2, cells // 2, length // 2)
    sides = swap(*sides, PLANE)
    arrived, sides, coarse_source = lax.optimization_barrier((arrived, sides, coarse_source))

    constants = (
        two_parts(second_table(second))
        + (
            stacked(forward_first(first)),
            stacked(inverse_first(first)),
            stacked(inverse_first_coarse(first // 2, rows)),
        )
        + two_parts(second_coarse(second // 2, groups))
        + two_parts(second_table(second).transpose(0, 2, 1))
    )
    tiles = 2 * held + low // 2 + 1
    modes = (me + devices * np.array(js)).astype(jnp.float32)
    weight = jnp.where(modes == 0.0, norm, 2.0 * norm).astype(jnp.float32)
    scale = jnp.stack([DECAY * modes * modes, weight], axis=1)
    block = (2, 2 * held * first, second // 2)
    shape = (devices, tiles, SUB, LANE)
    out = call(
        functools.partial(middle_kernel, (first, second, rows, groups, held, low)),
        pltpu.HBM(shape, jnp.float32),
        (scale, arrived, *constants),
        room(*constants)
        + [
            pltpu.VMEM(shape, jnp.float32),
            pltpu.SemaphoreType.DMA((len(constants),)),
            pltpu.VMEM(block, bf16),
            pltpu.VMEM(block, bf16),
            pltpu.VMEM(block, jnp.float32),
            pltpu.VMEM(block, bf16),
            pltpu.VMEM(block, bf16),
            pltpu.VMEM((low // 2 * first, second), bf16),
            pltpu.VMEM((low // 2 * first, second), bf16),
        ],
        6 * 2 * 2 * held * first * second * (second + 2 * first),
        [SMEM, VMEM] + [AWAY] * len(constants),
        22,
    )
    out, source, coarse_source, sides = lax.optimization_barrier(
        (out, source, coarse_source, sides)
    )
    got = lax.all_to_all(out, EVERY, split_axis=0, concat_axis=0, tiled=True)
    size, coarse_size = noise.shape, coarse_source.shape
    sizes = (size, coarse_size)
    sources = (source, coarse_source, *sides)
    laid = call(
        functools.partial(layout_kernel, size),
        [
            held_planes(s, count)
            for s in sizes
            for count in (s[0] - 2, 2)
        ],
        sources,
        room(*sources) + [pltpu.SemaphoreType.DMA((4,))],
        source.size,
        [AWAY] * 4,
        12,
    )
    got, laid = lax.optimization_barrier((got, laid))

    third = inverse_third(length, devices, js)
    constants = (
        two_parts(third)
        + two_parts(third_coarse(length // 2, devices, js[:low]))
        + (lane_order(2 * held, low).astype(bf16),)
        + two_parts(third_coarse_halo(length // 2, devices, js[:low]))
    )
    edge = f32(sum(3 * (s[2] // LANE) * s[1] + SUB for s in sizes), LANE)
    shares = (devices, 2 * held, tiles)
    inner_f, outer_f, coarse_inner_f, coarse_outer_f = laid
    got = got.reshape(devices * tiles * SUB, LANE)
    ks, coarse_ks, cols, far, near = call(
        functools.partial(edge_kernel, (devices, 2 * held, low, tiles, planes, length)),
        [held_planes(s, 4) for s in sizes] + [f32(HALO * planes, length), edge, edge],
        (flags, got, outer_f, coarse_outer_f, *constants),
        room(*constants)
        + [pltpu.VMEM((2, 4 * cells, devices * held), bf16)] * 2
        + [pltpu.VMEM((planes // 2 * LANE, devices * low), bf16)] * 2
        + [pltpu.SemaphoreType.DMA((7,))],
        3 * planes * cells * length * length,
        [SMEM] + [VMEM] * 3 + [AWAY] * 7,
        16,
    )
    k_far, k_near = (
        lax.ppermute(
            x, "row", [p for i in range(at, rows - 1, 2) for p in ((i, i + 1), (i + 1, i))]
        )
        for x, at in ((far, 1), (near, 0))
    )
    inner, *kept = call(
        functools.partial(inner_kernel, size, shares),
        [pltpu.HBM(size, jnp.float32)] + [held_planes(s, s[0] - 2) for s in sizes for _ in range(3)],
        (flags, got, *constants[:2], ks, coarse_ks, cols, inner_f, coarse_inner_f),
        room(held_planes(size, planes), *constants[:2])
        + [pltpu.VMEM((2, (planes - 4) * cells, devices * held), bf16)] * 2
        + room(f32(planes - 4, cells, length))
        + [pltpu.SemaphoreType.DMA((2,))],
        3 * planes * cells * length * length,
        [SMEM, VMEM] + [AWAY] * 2 + [VMEM] * 5,
        18,
    )
    own = (flags, ks, outer_f, *kept[:3], coarse_ks, coarse_outer_f, *kept[3:])
    done = (inner,)
    for near, edge in ((True, k_near), (False, k_far)):
        done = call(
            functools.partial(outer_kernel, size, near),
            [pltpu.HBM(s, jnp.float32) for s in sizes],
            (*own, edge, *done),
            outer_scratch(size) + outer_scratch(coarse_size),
            15 * source.size,
            [SMEM] + [VMEM] * 11 + [AWAY] * len(done),
            14,
            None,
            {12 + i: i for i in range(len(done))},
        )
    return tuple(done)


NEIGHBOUR_STEPS = ((1, 0, 0), (-1, 0, 0), (0, 1, 0), (0, -1, 0), (0, 0, 1), (0, 0, -1))


def padded(x, sides, width):
    for axis, dim in sides:
        peers, length = (lax.axis_size(axis), x.shape[dim])
        up = [(i, (i + 1) % peers) for i in range(peers - 1)]
        down = [(j, i) for i, j in up]
        last = lax.slice_in_dim(x, length - width, length, axis=dim)
        leading = lax.slice_in_dim(x, 0, width, axis=dim)
        before = lax.ppermute(last, axis, up)
        after = lax.ppermute(leading, axis, down)
        x = jnp.concatenate([before, x, after], axis=dim)
    return x


def signed_modes(index, length):
    return jnp.where(index < length // 2, index, index - length).astype(jnp.float32)


def amplitude(first_modes, second_modes, third_modes, first_edge, second_edge, third_edge):
    squared = first_modes * first_modes + second_modes * second_modes + third_modes * third_modes
    value = FIELD_SCALE / (1.0 + (2.0 * math.pi * CORRELATION) ** 2 * squared)
    edge = (
        (jnp.abs(first_modes) == first_edge)
        | (jnp.abs(second_modes) == second_edge)
        | (jnp.abs(third_modes) == third_edge)
    )
    return jnp.where(edge, 0.0, value)


def phase_table(count_rows, count_cols, modulus, sign):
    left_index = jnp.arange(count_rows, dtype=jnp.int32)[:, None]
    right_index = jnp.arange(count_cols, dtype=jnp.int32)[None, :]
    angle = 2.0 * math.pi / modulus * (left_index * right_index % modulus).astype(jnp.float32)
    return (jnp.cos(angle), sign * jnp.sin(angle))


def split_length(length):
    outer_len = 2 ** ((length.bit_length() - 1) // 2)
    return (outer_len, length // outer_len)


def real_form(form, left_value, right_value):
    return jnp.einsum(form, left_value, right_value, precision=lax.Precision.HIGHEST)


def complex_form(form, left_real, left_imag, right_real, right_imag):
    real_part = real_form(form, left_real, right_real) - real_form(form, left_imag, right_imag)
    imag_part = real_form(form, left_real, right_imag) + real_form(form, left_imag, right_real)
    return (real_part, imag_part)


def merge_pair(values, out_form, first_letter):
    merge_at = out_form.index(first_letter)
    out_dims = list(values.shape)
    merged = (
        out_dims[:merge_at]
        + [out_dims[merge_at] * out_dims[merge_at + 1]]
        + out_dims[merge_at + 2 :]
    )
    return values.reshape(merged)


def forward_axis(real_part, imag_part, lead_form, out_form, kept_modes):
    length = real_part.shape[-1]
    outer_len, inner_len = split_length(length)
    split_shape = real_part.shape[:-1] + (outer_len, inner_len)
    outer_real, outer_imag = phase_table(outer_len, outer_len, outer_len, -1.0)
    twist_real, twist_imag = phase_table(outer_len, inner_len, length, -1.0)
    inner_real, inner_imag = phase_table(inner_len, kept_modes // outer_len, inner_len, -1.0)
    first_form = lead_form + "ab,ai->" + lead_form + "ib"
    split_real = real_part.reshape(split_shape)
    if imag_part is None:
        section_real = real_form(first_form, split_real, outer_real)
        section_imag = real_form(first_form, split_real, outer_imag)
    else:
        section_real, section_imag = complex_form(
            first_form, split_real, imag_part.reshape(split_shape), outer_real, outer_imag
        )
    turned_real = section_real * twist_real - section_imag * twist_imag
    turned_imag = section_real * twist_imag + section_imag * twist_real
    result_real, result_imag = complex_form(
        lead_form + "ib,bj->" + out_form, turned_real, turned_imag, inner_real, inner_imag
    )
    return (merge_pair(result_real, out_form, "j"), merge_pair(result_imag, out_form, "j"))


def inverse_axis(real_part, imag_part, length, lead_form, out_form, real_only):
    kept_modes = real_part.shape[-1]
    outer_len, inner_len = split_length(length)
    split_shape = real_part.shape[:-1] + (kept_modes // outer_len, outer_len)
    inner_real, inner_imag = phase_table(kept_modes // outer_len, inner_len, inner_len, 1.0)
    twist_real, twist_imag = phase_table(outer_len, inner_len, length, 1.0)
    outer_real, outer_imag = phase_table(outer_len, outer_len, outer_len, 1.0)
    section_real, section_imag = complex_form(
        lead_form + "ji,jb->" + lead_form + "ib",
        real_part.reshape(split_shape),
        imag_part.reshape(split_shape),
        inner_real,
        inner_imag,
    )
    turned_real = section_real * twist_real - section_imag * twist_imag
    turned_imag = section_real * twist_imag + section_imag * twist_real
    second_form = lead_form + "ib,ia->" + out_form
    if real_only:
        result = real_form(second_form, turned_real, outer_real) - real_form(
            second_form, turned_imag, outer_imag
        )
        return merge_pair(result, out_form, "a")
    result_real, result_imag = complex_form(
        second_form, turned_real, turned_imag, outer_real, outer_imag
    )
    return (merge_pair(result_real, out_form, "a"), merge_pair(result_imag, out_form, "a"))


def low_band(values, half_coarse, fine_len):
    return jnp.concatenate(
        [values[:, :, :half_coarse], values[:, :, fine_len - half_coarse :]], axis=2
    )


def window(values, margin, offset):
    return values[
        margin + offset[0] : values.shape[0] - margin + offset[0],
        margin + offset[1] : values.shape[1] - margin + offset[1],
        margin + offset[2] : values.shape[2] - margin + offset[2],
    ]


def face_weight(center, beside):
    return jnp.where(beside > 0.0, 0.5 * (center + beside), center)


def smooth_twice(kappa, source):
    no_shift = (0, 0, 0)
    center = window(kappa, 1, no_shift)
    faces = [face_weight(center, window(kappa, 1, offset)) for offset in NEIGHBOUR_STEPS]
    diagonal = faces[0] + faces[1] + faces[2] + faces[3] + faces[4] + faces[5]
    guarded = jnp.where(center > 0.0, diagonal, 1.0)
    first_sweep = JACOBI_WEIGHT * window(source, 1, no_shift) / guarded
    inner_first = window(first_sweep, 1, no_shift)
    inner_diagonal = window(diagonal, 1, no_shift)
    coupled = jnp.zeros_like(inner_first)
    for face_value, offset in zip(faces, NEIGHBOUR_STEPS):
        coupled = coupled + window(face_value, 1, no_shift) * window(first_sweep, 1, offset)
    residual = window(source, 2, no_shift) - inner_diagonal * inner_first + coupled
    return inner_first + JACOBI_WEIGHT * residual / inner_diagonal


def pad_depth(values):
    return jnp.pad(values, ((0, 0), (0, 0), (2, 2)))


def plain_body(noise, source):
    row_at = lax.axis_index("row")
    group_at = lax.axis_index(("level", "col"))
    fine_field = noise.astype(jnp.float32)
    fine_len = fine_field.shape[-1]
    coarse_len = fine_len // 2
    half_coarse = coarse_len // 2
    kept_modes = fine_len // 2
    real_part, imag_part = forward_axis(fine_field, None, "pq", "pjiq", kept_modes)
    real_part, imag_part = (
        lax.all_to_all(real_part, ("level", "col"), split_axis=1, concat_axis=2, tiled=True),
        lax.all_to_all(imag_part, ("level", "col"), split_axis=1, concat_axis=2, tiled=True),
    )
    real_part, imag_part = forward_axis(real_part, imag_part, "pq", "jiqp", fine_len)
    real_part, imag_part = (
        lax.all_to_all(real_part, "row", split_axis=0, concat_axis=2, tiled=True),
        lax.all_to_all(imag_part, "row", split_axis=0, concat_axis=2, tiled=True),
    )
    slab_len = real_part.shape[-1]
    coarse_slab = slab_len // 2
    half_slab = coarse_slab // 2
    real_part, imag_part = forward_axis(real_part, imag_part, "pq", "pqji", slab_len)
    second_count = real_part.shape[0]
    third_count = real_part.shape[1]
    wave_second = signed_modes(
        row_at * second_count + jnp.arange(second_count, dtype=jnp.int32), fine_len
    )[:, None, None]
    third_index = group_at * third_count + jnp.arange(third_count, dtype=jnp.int32)
    wave_third = signed_modes(third_index, fine_len)[None, :, None]
    spread = 2.0
    mirror_weight = jnp.where(third_index == 0, 1.0, spread).astype(jnp.float32)[None, :, None]
    norm_factor = (float(slab_len) * float(fine_len) * float(fine_len)) ** (-0.5)
    wave_first = signed_modes(jnp.arange(slab_len, dtype=jnp.int32), slab_len)[None, None, :]
    fine_scale = (
        amplitude(
            wave_second, wave_third, wave_first, fine_len / 2.0, fine_len / 2.0, slab_len / 2.0
        )
        * mirror_weight
        * norm_factor
    )
    coarse_first = signed_modes(jnp.arange(coarse_slab, dtype=jnp.int32), coarse_slab)[
        None, None, :
    ]
    coarse_scale = (
        amplitude(
            wave_second,
            wave_third,
            coarse_first,
            coarse_len / 2.0,
            coarse_len / 2.0,
            coarse_slab / 2.0,
        )
        * mirror_weight
        * norm_factor
    )
    coarse_real = low_band(real_part, half_slab, slab_len) * coarse_scale
    coarse_imag = low_band(imag_part, half_slab, slab_len) * coarse_scale
    fine_real, fine_imag = inverse_axis(
        real_part * fine_scale, imag_part * fine_scale, slab_len, "pq", "abqp", False
    )
    coarse_real, coarse_imag = inverse_axis(
        coarse_real, coarse_imag, coarse_slab, "pq", "abqp", False
    )
    fine_real, fine_imag, coarse_real, coarse_imag = (
        lax.all_to_all(fine_real, "row", split_axis=0, concat_axis=2, tiled=True),
        lax.all_to_all(fine_imag, "row", split_axis=0, concat_axis=2, tiled=True),
        lax.all_to_all(coarse_real, "row", split_axis=0, concat_axis=2, tiled=True),
        lax.all_to_all(coarse_imag, "row", split_axis=0, concat_axis=2, tiled=True),
    )
    coarse_real = low_band(coarse_real, half_coarse, fine_len)
    coarse_imag = low_band(coarse_imag, half_coarse, fine_len)
    fine_real, fine_imag = inverse_axis(fine_real, fine_imag, fine_len, "pq", "pabq", False)
    coarse_real, coarse_imag = inverse_axis(
        coarse_real, coarse_imag, coarse_len, "pq", "pabq", False
    )
    fine_real, fine_imag, coarse_real, coarse_imag = (
        lax.all_to_all(fine_real, ("level", "col"), split_axis=1, concat_axis=2, tiled=True),
        lax.all_to_all(fine_imag, ("level", "col"), split_axis=1, concat_axis=2, tiled=True),
        lax.all_to_all(coarse_real, ("level", "col"), split_axis=1, concat_axis=2, tiled=True),
        lax.all_to_all(coarse_imag, ("level", "col"), split_axis=1, concat_axis=2, tiled=True),
    )
    coarse_real = coarse_real[:, :, :half_coarse]
    coarse_imag = coarse_imag[:, :, :half_coarse]
    fine_log = inverse_axis(fine_real, fine_imag, fine_len, "pq", "pqab", True)
    coarse_log = inverse_axis(coarse_real, coarse_imag, coarse_len, "pq", "pqab", True)
    fine_kappa = jnp.exp(fine_log)
    coarse_kappa = jnp.exp(coarse_log)
    fine_source = source.astype(jnp.float32)
    coarse_rows = coarse_log.shape[0]
    coarse_cols = coarse_log.shape[1]
    coarse_source = fine_source.reshape(coarse_rows, 2, coarse_cols, 2, coarse_len, 2).mean(
        axis=(1, 3, 5)
    )
    fine_kappa, fine_source, coarse_kappa, coarse_source = (
        padded(fine_kappa, (("row", 0), (("level", "col"), 1)), 2),
        padded(fine_source, (("row", 0), (("level", "col"), 1)), 2),
        padded(coarse_kappa, (("row", 0), (("level", "col"), 1)), 2),
        padded(coarse_source, (("row", 0), (("level", "col"), 1)), 2),
    )
    fine_pressure = smooth_twice(pad_depth(fine_kappa), pad_depth(fine_source))
    coarse_pressure = smooth_twice(pad_depth(coarse_kappa), pad_depth(coarse_source))
    return (fine_pressure, coarse_pressure)


def body(noise, source):
    planes, cells, length = noise.shape
    rows, groups = lax.axis_size("row"), lax.axis_size(PLANE)
    modes = length // 2 // (rows * groups)
    fills = planes == SUB and cells == LANE and 2 * HALO * modes == LANE // 2
    if fills and length % (4 * LANE) == 0 and rows % 2 == 0 and groups % 4 == 0:
        return fused_body(noise, source)
    return plain_body(noise, source)


def solution(mesh):
    return jax.shard_map(
        body,
        mesh=mesh,
        in_specs=(P("row", ("level", "col"), None), P("row", ("level", "col"), None)),
        out_specs=(P("row", ("level", "col"), None), P("row", ("level", "col"), None)),
        check_vma=False,
    )
```

```python
import functools
import math

import jax
import jax.numpy as jnp
import numpy as np
from jax import lax
from jax.experimental import pallas as pl
from jax.experimental.pallas import tpu as pltpu
from jax.sharding import PartitionSpec as P

JACOBI_WEIGHT = 2.0 / 3.0
CORRELATION = 0.2
FIELD_SCALE = 0.3
DECAY = (2.0 * math.pi * CORRELATION) ** 2
EVERY = ("row", "level", "col")
PLANE = ("level", "col")
MIB = 1 << 20
SUB, LANE = 8, 128
HALO = 4


def two_parts(matrix):
    high = matrix.astype(jnp.bfloat16)
    low = (matrix - high.astype(np.float64)).astype(jnp.bfloat16)
    return high, low


def angles(rows, cols, length):
    return 2.0 * np.pi * (np.outer(rows, cols) % length) / length


def third_modes(devices, js):
    return np.array([[d + devices * j for j in js] for d in range(devices)])


def forward_third(length, devices, js):
    theta = angles(third_modes(devices, js).reshape(-1), np.arange(length), length)
    return np.stack([np.cos(theta), -np.sin(theta)], axis=1).reshape(-1, length)


def inverse_third(length, devices, js):
    modes = third_modes(devices, js).reshape(devices // 2, 2, len(js)).transpose(1, 0, 2)
    theta = 2.0 * np.pi * (modes[..., None] * np.arange(length // 2) % length) / length
    both = np.stack([np.cos(theta), -np.sin(theta)], axis=3)
    return both.reshape(2, -1, length // 2)


def second_modes(length):
    return np.arange(length // 2).reshape(-1, 2).T


def second_table(length):
    theta = second_modes(length)[:, None, :] * np.arange(length // 2)[None, :, None]
    theta = 2.0 * np.pi * (theta % length) / length
    return np.concatenate([np.cos(theta), np.sin(theta)], axis=2)


def forward_first(length):
    theta = angles(np.arange(length), np.arange(length), length)
    cos, sin = np.cos(theta), np.sin(theta)
    return np.block([[cos, sin], [-sin, cos]])


def inverse_first(length):
    theta = angles(np.arange(length), np.arange(length), length)
    cos, sin = np.cos(theta), np.sin(theta)
    cos[:, length // 2] = 0.0
    sin[:, length // 2] = 0.0
    return np.block([[cos, -sin], [sin, cos]])


def inverse_first_coarse(length, rows):
    full = inverse_first(length)
    value = full.reshape(2, rows, length // rows, 2 * length)
    turned = np.concatenate([-full[length:], full[:length]]).reshape(value.shape)
    order = lambda x: x.transpose(1, 0, 2, 3).reshape(2 * length, 2 * length)
    return np.concatenate([order(value), order(turned)])


def second_coarse(length, groups):
    theta = angles(second_modes(length).reshape(-1), np.arange(length), length)
    table = np.concatenate([np.cos(theta), np.sin(theta)])
    span = length // groups
    out = np.zeros((2, length, groups, 2, span))
    for pair in range(2):
        out[pair, :, :, pair, :] = table.reshape(length, groups, span)
    return out.reshape(2 * length, 2 * length)


def third_coarse(length, devices, js):
    modes = third_modes(devices, js).reshape(devices, len(js) // 2, 2)
    theta = 2.0 * np.pi * (modes[..., None] * np.arange(length) % length) / length
    both = np.stack([np.cos(theta), -np.sin(theta)])
    return both.transpose(0, 2, 1, 3, 4).reshape(2 * (len(js) // 2) * devices, 2 * length)


def third_coarse_halo(length, devices, js):
    theta = angles(third_modes(devices, js).reshape(-1), np.arange(length), length)
    return np.concatenate([np.cos(theta), -np.sin(theta)], axis=1)


def lane_order(parts, coarse_parts):
    out = np.zeros((LANE, LANE))
    for h in range(HALO):
        for q in range(parts):
            out[HALO * q + h, parts * h + q] = 1.0
        for j in range(coarse_parts):
            out[LANE // 2 + HALO * j + h, LANE // 2 + coarse_parts * h + j] = 1.0
    return out


def split(x):
    high = x.astype(jnp.bfloat16)
    return high, (x - high.astype(jnp.float32)).astype(jnp.bfloat16)


def dot(a, b):
    return lax.dot_general(a, b, (((1,), (0,)), ((), ())), preferred_element_type=jnp.float32)


def dot_t(a, b):
    return lax.dot_general(a, b, (((1,), (1,)), ((), ())), preferred_element_type=jnp.float32)


def stacked(matrix):
    high, low = two_parts(matrix)
    return np.block([[high, high], [low, np.zeros_like(low)]])


def dot_left(stack, x):
    value = dot(stack, jnp.concatenate(split(x), axis=0))
    rows = stack.shape[0] // 2
    return value[:rows] + value[rows:]


def dot3(a, b):
    (ah, al), (bh, bl) = a, b
    return dot(ah, bh) + (dot(ah, bl) + dot(al, bh))


def load(pairs, sems):
    copies = [pltpu.make_async_copy(a, b, sems.at[i]) for i, (a, b) in enumerate(pairs)]
    for copy in copies:
        copy.start()
    return copies


def send(pairs, sems, first):
    copies = [pltpu.make_async_copy(a, b, sems.at[first + i]) for i, (a, b) in enumerate(pairs)]
    for copy in copies:
        copy.start()
    return copies


def forward_kernel(planes, d_hbm, x_hbm, out_hbm, d, x, out, sems):
    pieces, rows = d.shape[0], d.shape[1] // 2
    parts = [slice(p * LANE, (p + 2) * LANE) for p in range(0, planes, 2)]
    pairs = [(x_hbm.at[at, :], x.at[at, :]) for at in parts]
    copies = load([(d_hbm.at[0], d.at[0])] + pairs + [(d_hbm.at[i], d.at[i]) for i in range(1, pieces)], sems)
    sent = []
    copies[0].wait()
    for piece in range(pieces):
        if piece:
            copies[len(parts) + piece].wait()
        for i, at in enumerate(parts):
            if piece == 0:
                copies[i + 1].wait()
            value = dot_t(d[piece], x[at, :])
            value = value[:rows] + value[rows:]
            for h in range(2):
                out[pl.ds(piece * rows * SUB + 2 * i + h, rows, stride=SUB), :] = value[
                    :, h * LANE : (h + 1) * LANE
                ]
        tall = slice(piece * rows * SUB, (piece + 1) * rows * SUB)
        sent += send([(out.at[tall, :], out_hbm.at[tall, :])], sems, len(copies) + piece)
    for copy in sent:
        copy.wait()


def middle_kernel(sizes, scale, b, *rest):
    (first, second, rows, groups, js, low) = sizes
    count = 9
    away, out_hbm, near, rest = (
        rest[:count],
        rest[count],
        rest[count + 1 : 2 * count + 1],
        rest[2 * count + 1 :],
    )
    out, sems, zh, zl, y, oh, ol, qh, ql = rest
    copies = load(list(zip(away, near)), sems)
    csh, csl, forward, inverse, coarse_inverse, cch, ccl, ch, cl = near
    q_count = 2 * js
    half, quarter = second // 2, second // 4
    for q in range(q_count):
        for g in range(groups // 2):
            for r in range(0, rows, 2):
                at = r * groups + g
                near_half = jnp.concatenate([b[at, q], b[at + groups, q]], axis=0)
                at += groups // 2
                far_half = jnp.concatenate([b[at, q], b[at + groups, q]], axis=0)
                at = slice(q * first + r * SUB, q * first + (r + 2) * SUB)
                lanes = slice(g * LANE, (g + 1) * LANE)
                zh[0, at, lanes], zl[0, at, lanes] = split(near_half + far_half)
                zh[1, at, lanes], zl[1, at, lanes] = split(near_half - far_half)
    for copy in copies[:5]:
        copy.wait()
    wide = 8 * first
    for top in range(0, q_count * first, wide):
        at = slice(top, top + wide)
        for parity in range(2):
            y[parity, at, :] = dot3(
                (zh[parity, at, :], zl[parity, at, :]), (csh[parity], csl[parity])
            )
    mode0 = lax.broadcasted_iota(jnp.int32, (first, second), 0)
    mode0 = jnp.where(mode0 < first // 2, mode0, mode0 - first).astype(jnp.float32)
    lane = lax.broadcasted_iota(jnp.int32, (first, second), 1)
    mode1 = jnp.where(lane < half, lane, lane - half)
    mode1 = jnp.where(mode1 < quarter, 2 * mode1, 2 * (mode1 - quarter) + 1).astype(jnp.float32)
    base = 1.0 + DECAY * (mode0 * mode0 + mode1 * mode1)
    for j in range(js):
        top = j * 2 * first
        re, im = slice(top, top + first), slice(top + first, top + 2 * first)
        cos, sin = slice(0, quarter), slice(quarter, half)
        whole = lambda part, lanes: jnp.concatenate(
            [y[0, part, lanes], y[1, part, lanes]], axis=1
        )
        rc, rs, ic, isn = whole(re, cos), whole(re, sin), whole(im, cos), whole(im, sin)
        wave = jnp.concatenate(
            [
                jnp.concatenate([rc + isn, rc - isn], axis=1),
                jnp.concatenate([ic - rs, ic + rs], axis=1),
            ],
            axis=0,
        )
        spectrum = dot_left(forward[...], wave)
        amp = jnp.where(lane == half, 0.0, scale[j, 1] / (base + scale[j, 0]))
        scaled = spectrum * jnp.concatenate([amp, amp], axis=0)
        field = dot_left(inverse[...], scaled)
        plus, minus = field[:, :half], field[:, half:]
        even, odd = plus + minus, plus - minus
        odd = jnp.concatenate([-odd[first:], odd[:first]], axis=0)
        at = slice(top, top + 2 * first)
        for parity, lanes in enumerate((cos, sin)):
            operand = jnp.concatenate([even[:, lanes], odd[:, lanes]], axis=1)
            oh[parity, at, :], ol[parity, at, :] = split(operand)
        if j < low:
            keep = first // 4
            kept = [
                scaled[at : at + keep, :]
                for at in (0, first - keep, first, 2 * first - keep)
            ]
            band = jnp.concatenate(kept, axis=0)
            low_lane = lax.broadcasted_iota(jnp.int32, (first, quarter), 1) < quarter // 2
            pieces = []
            for at in (0, half):
                upper = pltpu.roll(band[:, at + quarter : at + half], quarter // 2, 1)
                pieces.append(jnp.where(low_lane, band[:, at : at + quarter], upper))
            band = jnp.concatenate(pieces, axis=1)
            field = dot_left(coarse_inverse[...], band)
            value, turned = field[:first], field[first:]
            operand = jnp.concatenate(
                [
                    value[:, :quarter] + value[:, quarter:],
                    turned[:, :quarter] - turned[:, quarter:],
                ],
                axis=1,
            )
            at = slice(j // 2 * first, (j // 2 + 1) * first)
            lanes = slice(j % 2 * half, (j % 2 + 1) * half)
            qh[at, lanes], ql[at, lanes] = split(operand)
    for copy in copies[5:]:
        copy.wait()
    copies = []
    wide = 4 * first
    lane = lax.broadcasted_iota(jnp.int32, (SUB, LANE), 1)
    extra = q_count + low // 2

    def leave(start, stop):
        at = slice(start, stop)
        copies.extend(send([(out.at[:, at], out_hbm.at[:, at])], sems, len(copies)))

    def give(value, start):
        tiles = value.shape[0] // first
        for q in range(tiles):
            for r in range(rows):
                for g in range(groups):
                    at = q * first + r * SUB
                    out[r * groups + g, start + q] = value[
                        at : at + SUB, g * LANE : (g + 1) * LANE
                    ]
        leave(start, start + tiles)

    def halo_columns(value, start, held):
        tiles = value.shape[0] // first
        for r in range(rows):
            for g in range(groups):
                total = held[r, g]
                left = max(g - 1, 0) * LANE
                right = min(g + 1, groups - 1) * LANE
                for q in range(tiles):
                    at = slice(q * first + r * SUB, q * first + (r + 1) * SUB)
                    both = jnp.where(
                        lane < LANE // 2,
                        value[at, right : right + LANE],
                        value[at, left : left + LANE],
                    )
                    to = HALO * (start + q)
                    both = pltpu.roll(both, (to + 2) % LANE, 1)
                    total = jnp.where((lane >= to) & (lane < to + HALO), both, total)
                held[r, g] = total

    def coarse_columns(value, held):
        half_lane = LANE // 2
        for j in range(low):
            for r in range(rows):
                at = slice(j // 2 * first + r * SUB, j // 2 * first + (r + 1) * SUB)
                shift = HALO * j + 2 - j % 2 * half_lane
                to = half_lane + HALO * j
                for g in range(groups):
                    left = max(g - 1, 0) * LANE
                    right = min(g + 1, groups - 1) * LANE
                    left = pltpu.roll(value[at, left : left + LANE], shift % LANE, 1)
                    right = pltpu.roll(
                        value[at, right : right + LANE], (shift + half_lane) % LANE, 1
                    )
                    total = jnp.where((lane >= to) & (lane < to + 2), left, held[r, g])
                    held[r, g] = jnp.where(
                        (lane >= to + 2) & (lane < to + HALO), right, total
                    )

    columns = {
        (r, g): jnp.zeros((SUB, LANE), jnp.float32) for r in range(rows) for g in range(groups)
    }
    coarse = dot3((qh[...], ql[...]), (cch[...], ccl[...]))
    give(coarse, q_count)
    coarse_columns(coarse, columns)
    for top in range(0, q_count * first, wide):
        at = slice(top, top + wide)
        even, odd = (
            dot3((oh[parity, at, :], ol[parity, at, :]), (ch[parity], cl[parity]))
            for parity in range(2)
        )
        value = jnp.concatenate([even + odd, even - odd], axis=1)
        give(value, top // first)
        halo_columns(value, top // first, columns)
    for (r, g), total in columns.items():
        out[r * groups + g, extra] = total
    leave(extra, extra + 1)
    for copy in copies:
        copy.wait()


def gather_modes(b, at, sizes, lh, ll):
    devices, q_count, tiles = sizes
    for i, n in enumerate(at):
        for parity in range(2):
            rows = jnp.concatenate(
                [
                    b[pl.ds(s * tiles * SUB + n, q_count, stride=SUB), :]
                    for s in range(parity, devices, 2)
                ],
                axis=0,
            )
            to = slice(i * LANE, (i + 1) * LANE)
            lh[parity, to, :], ll[parity, to, :] = split(jnp.transpose(rows))


def inverse_pair(i, lh, ll, eh, el, ks, to, cells):
    at = slice(i * cells, (i + 2) * cells)
    even, odd = (
        dot3((lh[parity, at, :], ll[parity, at, :]), (eh[parity], el[parity]))
        for parity in range(2)
    )
    value = jnp.exp(jnp.concatenate([even + odd, even - odd], axis=1))
    for n in range(2):
        put_rows(ks, to + n, SUB, value[n * cells : (n + 1) * cells])


def edge_kernel(sizes, flags, b, *rest):
    (devices, q_count, low, tiles, planes, length) = sizes
    away, (ks, cks, cols, far, near_edge), rest = rest[:7], rest[7:12], rest[12:]
    near, (lh, ll, mh, ml, sems) = rest[:7], rest[7:]
    copies = load(list(zip(away, near)), sems)
    eh, el, ceh, cel, order, cwh, cwl = near
    cells, short = LANE, length // 2
    halves, coarse_planes = low // 2, planes // 2
    half = cells // 2
    gather_modes(b, (0, 1, planes - 2, planes - 1), (devices, q_count, tiles), lh, ll)
    for n in range(coarse_planes):
        rows = jnp.concatenate(
            [
                b[pl.ds((q_count + h) * SUB + c * coarse_planes + n, devices, stride=tiles * SUB), :]
                for c in range(2)
                for h in range(halves)
            ],
            axis=0,
        )
        at = slice(n * LANE, (n + 1) * LANE)
        mh[at, :], ml[at, :] = split(jnp.transpose(rows))

    for copy in copies[:4]:
        copy.wait()

    for i in range(0, 4, 2):
        inverse_pair(i, lh, ll, eh, el, ks, i, cells)
    value = dot3((mh[...], ml[...]), (ceh[...], cel[...]))
    for n in range(coarse_planes):
        top = n * cells
        part = value[top : top + half, :short] + value[top + half : top + cells, short:]
        part = jnp.exp(part)
        put_rows(cks, n, SUB, part)

    for copy in copies[4:]:
        copy.wait()
    lane = lax.broadcasted_iota(jnp.int32, (SUB, LANE), 1)
    tile_rows = [b[(s * tiles + tiles - 1) * SUB : (s + 1) * tiles * SUB, :] for s in range(devices)]
    high, rest_part = split(jnp.concatenate(tile_rows, axis=0))
    ordered = dot(high, order[...]) + dot(rest_part, order[...])

    def joined(of, width, start):
        fit = LANE // width
        cells_of = []
        for h in range(HALO):
            parts = []
            for i, s in enumerate(of):
                moved = ordered[s * SUB : (s + 1) * SUB]
                shift = (i % fit * width - start - h * width) % LANE
                moved = pltpu.roll(moved, shift, 1) if shift else moved
                if i % fit == 0:
                    parts.append(moved)
                else:
                    parts[-1] = jnp.where(lane >= i % fit * width, moved, parts[-1])
            cells_of.append(jnp.concatenate(parts, axis=1))
        return split(jnp.concatenate(cells_of, axis=0))

    even, odd = (
        dot3(joined(range(parity, devices, 2), q_count, 0), (eh[parity], el[parity]))
        for parity in range(2)
    )
    value = jnp.exp(jnp.concatenate([even + odd, even - odd], axis=1))
    cols[...] = value
    for h in range(HALO):
        for i, n in enumerate((0, 1, planes - 2, planes - 1)):
            at = h * planes + n
            put_rows(ks, i, halo_row(h, cells), value[at : at + 1, :])
    whole = dot3(joined(range(devices), low, LANE // 2), (cwh[...], cwl[...]))
    for h in range(HALO):
        top = h * SUB
        part = whole[top : top + coarse_planes, :short] + whole[top + coarse_planes : top + SUB, short:]
        part = jnp.exp(part)
        for n in range(coarse_planes):
            put_rows(cks, n, halo_row(h, half), part[n : n + 1, :])
    for held in (ks, cks):
        repeat_sides(flags, held, [(n,) for n in range(4)])
    odd_row = flags[4] == 1
    low_end = (jnp.where(odd_row, 2, 1), jnp.where(odd_row, 3, 0))
    high_end = (jnp.where(odd_row, 1, 2), jnp.where(odd_row, 0, 3))
    for edge, of in ((far, low_end), (near_edge, high_end)):
        at = 0
        for held in (ks, cks):
            count, end = held.shape[1], held.shape[2] - SUB
            for n in of:
                for x in range(count):
                    edge[at : at + end - SUB, :] = held[n, x, SUB:end, :]
                    at += end - SUB
            for x in range(count):
                edge[at + x : at + x + 1, :] = held[of[1], x, SUB - 1 : SUB, :]
                edge[at + count + x : at + count + x + 1, :] = held[of[1], x, end : end + 1, :]
            at += SUB


def halo_row(h, cells):
    return SUB - 2 + h if h < 2 else SUB + cells + h - 2


def source_kernel(planes, pairs, x, out, lo, hi, left, right, held, summed):
    cells = x.shape[0] // planes
    length = x.shape[1]
    half, fourth = cells // 2, cells // 4
    held[...] = dot(x[...], pairs[...])
    for n in range(planes // 2):
        top = 2 * n * cells
        for at in range(0, out.shape[1], LANE):
            lanes = slice(at, at + LANE)
            summed[...] = held[top : top + cells, lanes] + held[top + cells : top + 2 * cells, lanes]
            out[n * half : (n + 1) * half, lanes] = (
                summed[pl.ds(0, half, stride=2), :] + summed[pl.ds(1, half, stride=2), :]
            )
    for edge, plane in ((lo, 0), (hi, planes - 1)):
        edge[:cells, :] = x[plane * cells : (plane + 1) * cells, :].astype(jnp.float32)
        at = plane // 2 * half
        edge[cells:, : length // 2] = out[at : at + fourth, :]
        edge[cells:, length // 2 :] = out[at + fourth : at + half, :]
    for edge, row in ((left, 0), (right, cells - 1)):
        edge[...] = jnp.zeros_like(edge)
        for n in range(planes):
            at = n * cells + (row // SUB * SUB)
            edge[n : n + 1, :] = x[at : at + SUB, :].astype(jnp.float32)[row % SUB : row % SUB + 1]
        for n in range(planes // 2):
            at = n * half + row // 2
            edge[SUB + n : SUB + n + 1, : length // 2] = out[at : at + 1, :]


def beside(parts, ends):
    lane = lax.broadcasted_iota(jnp.int32, parts[0].shape, 1)
    ahead = [pltpu.roll(x, 1, 1) for x in parts]
    behind = [pltpu.roll(x, LANE - 1, 1) for x in parts]
    sums = []
    for i in range(len(parts)):
        left = jnp.where(lane == 0, ahead[i - 1] if i else ends[0], ahead[i])
        right = jnp.where(
            lane == LANE - 1, behind[i + 1] if i + 1 < len(parts) else ends[1], behind[i]
        )
        sums.append(left + right)
    return sums


def first_sweep(tiles, ext, mid, lower, upper, f, store):
    for top in range(0, ext, SUB):
        end = top + SUB
        parts = [mid(x, top, end) for x in range(tiles)]
        for x, both in enumerate(beside(parts, (parts[0], parts[-1]))):
            k = parts[x]
            above = pltpu.roll(k, 1, 0) if top == 0 else mid(x, top - 1, end - 1)
            below = pltpu.roll(k, SUB - 1, 0) if end == ext else mid(x, top + 1, end + 1)
            total = (lower(x, top, end) + upper(x, top, end)) + (above + below) + both
            scale = JACOBI_WEIGHT / (6.0 * k + total)
            u = f(x, top, end) * (2.0 * scale)
            store(x, top, end, u, k * u, scale)


def second_sweep(tiles, ext, k, u, w, r, store):
    for top in range(SUB, ext - SUB, SUB):
        end = top + SUB
        sums = []
        for lower, mid, upper in (u, w):
            parts = [mid(x, top, end) for x in range(tiles)]
            sums.append(
                [
                    both
                    + (lower(x, top, end) + upper(x, top, end))
                    + (mid(x, top - 1, end - 1) + mid(x, top + 1, end + 1))
                    for x, both in enumerate(beside(parts, (0.0, 0.0)))
                ]
            )
        for x in range(tiles):
            coupled = k(x, top, end) * sums[0][x] + sums[1][x]
            value = (2.0 - JACOBI_WEIGHT) * u[1](x, top, end) + r(x, top, end) * coupled
            store(x, top, end, value)


def around(tiles, ext, mid, beyond, store):
    for top in range(0, ext, SUB):
        end = top + SUB
        parts = [mid(x, top, end) for x in range(tiles)]
        for x, both in enumerate(beside(parts, (parts[0], parts[-1]))):
            k = parts[x]
            above = pltpu.roll(k, 1, 0) if top == 0 else mid(x, top - 1, end - 1)
            below = pltpu.roll(k, SUB - 1, 0) if end == ext else mid(x, top + 1, end + 1)
            store(x, top, end, (6.0 * k + beyond(x, top, end)) + (above + below) + both)


def plane_of(held, *at):
    return lambda x, top, end: held[(*at, x, slice(top, end), slice(None))]


def put_rows(held, to, at, rows):
    for x in range(held.shape[1]):
        held[to, x, at : at + rows.shape[0], :] = rows[:, x * LANE : (x + 1) * LANE]


def repeat_sides(flags, held, at):
    end = held.shape[-2] - SUB

    @pl.when(flags[2] == 1)
    def _():
        for p in at:
            held[(*p, slice(None), slice(SUB - 1, SUB))] = held[(*p, slice(None), slice(SUB, SUB + 1))]

    @pl.when(flags[3] == 1)
    def _():
        for p in at:
            held[(*p, slice(None), slice(end, end + 1))] = held[
                (*p, slice(None), slice(end - 1, end))
            ]


def put_block(fine, held, to, source, row, cells, length):
    if fine:
        put_rows(held, to, SUB, source[row : row + cells, :])
    else:
        half = cells // 2
        put_rows(held, to, SUB, source[row : row + half, :length])
        put_rows(held, to, SUB + half, source[row : row + half, length:])


def layout_kernel(sizes, *rest):
    away, outs, near, sems = rest[:6], rest[6:10], rest[10:16], rest[16]
    for copy in load(list(zip(away, near)), sems):
        copy.wait()
    source, coarse_source, *edges = near
    sides = edges[2:]
    for fine, inner, outer in ((True, *outs[:2]), (False, *outs[2:])):
        planes, cells, length = sizes if fine else [n // 2 for n in sizes]
        f = source if fine else coarse_source
        source_row = 0 if fine else SUB

        def plane(held, to, p):
            put_rows(held, to, SUB, f[p].astype(jnp.float32))
            for side, row in zip(sides, (SUB - 1, SUB + cells)):
                at = source_row + p
                put_rows(held, to, row, side[at : at + 1, :length])

        for p in range(1, planes - 1):
            plane(inner, p - 1, p)
        for group, p in enumerate((0, planes - 1)):
            row = 0 if fine else 2 * cells
            put_block(fine, outer.at[group], 0, edges[group], row, cells, length)
            plane(outer.at[group], 1, p)


def inner_level(sizes, ks, fs, us, ws, rs):
    planes, _, length = sizes
    tiles, ext = ks.shape[1:3]

    def first(p, carry):
        def store(x, top, end, u, w, r):
            at = (p - 1, x, slice(top, end))
            us[at], ws[at], rs[at] = u, w, r

        near = [plane_of(ks, p + i) for i in (0, -1, 1)]
        first_sweep(tiles, ext, *near, plane_of(fs, p - 1), store)
        return carry

    lax.fori_loop(1, planes - 1, first, 0)


def prepare(ks, us, ws, rs, sums, ready):
    planes, tiles, ext, _ = ks.shape

    def end_of(group, carry):
        inwards = lambda i, count: jnp.where(group == 0, i, count - 1 - i)

        def store_sum(x, top, end, value):
            sums[group, x, top:end, :] = value

        own = [plane_of(ks, inwards(i, planes)) for i in range(2)]
        around(tiles, ext, *own, store_sum)

        def store(x, top, end, value):
            ready[group, x, top:end, :] = value

        nothing = lambda x, top, end: 0.0
        u, w = (
            [nothing] + [plane_of(held, inwards(i, planes - 2)) for i in range(2)]
            for held in (us, ws)
        )
        scale = plane_of(rs, inwards(0, planes - 2))
        second_sweep(tiles, ext, own[1], u, w, scale, store)
        return carry

    lax.fori_loop(0, 2, end_of, 0)


def inner_kernel(sizes, shares, flags, b, eh_hbm, el_hbm, edges, cks, cols, fs, cfs, *rest):
    out_hbm, us, ws, rs, cus, cws, crs, sums, ready, csums, cready, *rest = rest
    ks, eh, el, lh, ll, out, sems = rest
    planes, cells, length = sizes
    tiles, ext = ks.shape[1:3]
    copies = load([(eh_hbm, eh), (el_hbm, el)], sems)
    middle = range(2, planes - 2)
    gather_modes(b, middle, shares, lh, ll)
    for i, p in enumerate((0, 1, planes - 2, planes - 1)):
        ks[p] = edges[i]
    for h in range(HALO):
        for p in middle:
            at = h * planes + p
            put_rows(ks, p, halo_row(h, cells), cols[at : at + 1, :])
    for copy in copies:
        copy.wait()
    for p in range(2, planes - 2, 2):
        inverse_pair(p - 2, lh, ll, eh, el, ks, p, cells)
    repeat_sides(flags, ks, [(p,) for p in middle])
    inner_level(sizes, ks, fs, us, ws, rs)

    def second(p, carry):
        def store(x, top, end, value):
            out[p - 2, top - SUB : end - SUB, x * LANE : (x + 1) * LANE] = value

        u, w = ([plane_of(held, p - 1 + i) for i in (-1, 0, 1)] for held in (us, ws))
        second_sweep(tiles, ext, plane_of(ks, p), u, w, plane_of(rs, p - 1), store)
        return carry

    lax.fori_loop(2, planes - 2, second, 0)
    copies = send([(out, out_hbm.at[2 : planes - 2])], sems, 0)
    prepare(ks, us, ws, rs, sums, ready)
    inner_level([n // 2 for n in sizes], cks, cfs, cus, cws, crs)
    prepare(cks, cus, cws, crs, csums, cready)
    for copy in copies:
        copy.wait()


def outer_kernel(sizes, flags, *rest):
    kept, coarse_kept, (k_far, k_near, _, out, coarse_out), rest = (
        rest[:7],
        rest[7:14],
        rest[14:19],
        rest[19:],
    )
    scratch = (rest[:6], rest[6:])
    levels = (sizes, tuple(n // 2 for n in sizes))
    start = 0
    sent = []
    for size, held, given, target in zip(
        levels, scratch, (kept, coarse_kept), (out, coarse_out)
    ):
        planes = size[0]
        ks, fs, inner_us, inner_ws, inner_rs, sums, ready = given
        halo, us, ws, rs, done, sems = held
        tiles, ext = ks.shape[1:3]
        rows = size[1]
        for group, edge in ((flags[4], k_far), (1 - flags[4], k_near)):
            at = start
            for place in range(2 * tiles):
                to = place * ext + SUB
                halo[group, to : to + rows, :] = edge[at : at + rows, :]
                at += rows
            for x in range(tiles):
                to = (tiles + x) * ext
                halo[group, to + SUB - 1 : to + SUB, :] = edge[at + x : at + x + 1, :]
                to += SUB + rows
                halo[group, to : to + 1, :] = edge[at + tiles + x : at + tiles + x + 1, :]
        start = at + SUB
        for group in range(2):

            @pl.when(flags[group] == 1)
            def _():
                for x in range(tiles):
                    at = (tiles + x) * ext
                    halo[group, at : at + ext, :] = ks[3 * group, x]

        def both_ends(group, carry):
            def halo_plane(slot):
                def get(x, top, end):
                    at = (slot * tiles + x) * ext
                    return halo[group, at + top : at + end, :]

                return get

            inwards = lambda i, count: jnp.where(group == 0, i, count - 1 - i)
            own = [plane_of(ks, inwards(i, 4)) for i in range(2)]
            def store_outer(x, top, end, u, w, r):
                at = (group, 0, x, slice(top, end))
                us[at], ws[at] = u, w

            beyond = halo_plane(1)
            first_sweep(
                tiles, ext, beyond, halo_plane(0), own[0], plane_of(fs, group, 0), store_outer
            )
            for top in range(0, ext, SUB):
                for x in range(tiles):
                    at = (x, slice(top, top + SUB))
                    near_sum = sums[(group, *at)] + beyond(x, top, top + SUB)
                    scale = JACOBI_WEIGHT / near_sum
                    u = fs[(group, 1, *at)] * (2.0 * scale)
                    us[(group, 1, *at)] = u
                    ws[(group, 1, *at)] = own[0](x, top, top + SUB) * u
                    rs[(group, *at)] = scale
            u, w = (
                [plane_of(new, group, i) for i in range(2)]
                + [plane_of(old, inwards(0, planes - 2))]
                for new, old in ((us, inner_us), (ws, inner_ws))
            )

            def store(x, top, end, value):
                done[group, 0, top - SUB : end - SUB, x * LANE : (x + 1) * LANE] = value

            second_sweep(tiles, ext, own[0], u, w, plane_of(rs, group), store)
            scale = plane_of(inner_rs, inwards(0, planes - 2))
            for top in range(SUB, ext - SUB, SUB):
                for x in range(tiles):
                    at = (x, top, top + SUB)
                    coupled = own[1](*at) * u[1](*at) + w[1](*at)
                    value = ready[group, x, top : top + SUB, :] + scale(*at) * coupled
                    done[group, 1, top - SUB : top, x * LANE : (x + 1) * LANE] = value
            for i in range(2):
                pltpu.make_async_copy(
                    done.at[group, i], target.at[inwards(i, planes)], sems.at[2 * group + i]
                ).start()
            return carry

        lax.fori_loop(0, 2, both_ends, 0)
        for group, at in enumerate(((0, 1), (planes - 1, planes - 2))):
            for i, p in enumerate(at):
                sent.append(
                    pltpu.make_async_copy(
                        done.at[group, i], target.at[p], sems.at[2 * group + i]
                    )
                )
    for copy in sent:
        copy.wait()


SMEM = pl.BlockSpec(memory_space=pltpu.SMEM)
VMEM = pl.BlockSpec(memory_space=pltpu.VMEM)
AWAY = pl.BlockSpec(memory_space=pltpu.HBM)
ANY = pl.BlockSpec(memory_space=pl.ANY)


def call(kernel, outs, operands, scratch, flops, specs, limit, out_specs=None, aliases=None):
    many = isinstance(outs, (list, tuple))
    written = outs if many else [outs]
    moved = sum(math.prod(x.shape) * x.dtype.itemsize for x in (*operands, *written))
    operands = [
        pltpu.with_memory_space_constraint(x, pltpu.HBM) if spec is AWAY else x
        for x, spec in zip(operands, specs)
    ]
    out_specs = out_specs or [
        VMEM if isinstance(x, jax.ShapeDtypeStruct) else AWAY for x in written
    ]
    return pl.pallas_call(
        kernel,
        out_shape=outs,
        in_specs=specs,
        out_specs=out_specs if many else out_specs[0],
        scratch_shapes=scratch,
        input_output_aliases=aliases or {},
        compiler_params=pltpu.CompilerParams(vmem_limit_bytes=limit * MIB),
        cost_estimate=pl.CostEstimate(flops=flops, bytes_accessed=moved, transcendentals=0),
    )(*operands)


def f32(*shape):
    return jax.ShapeDtypeStruct(shape, jnp.float32)


def room(*arrays):
    return [pltpu.VMEM(x.shape, x.dtype) for x in arrays]


def chain(axis):
    up = [(i, i + 1) for i in range(lax.axis_size(axis) - 1)]
    return up, [(j, i) for i, j in up]


def swap(lo, hi, axis):
    up, down = chain(axis)
    return lax.ppermute(hi, axis, up), lax.ppermute(lo, axis, down)


def held_planes(size, *count):
    planes, cells, length = size
    return f32(*count, length // LANE, cells + 2 * SUB, LANE)


def outer_scratch(size):
    planes, cells, length = size
    return room(
        f32(2, 2 * (length // LANE) * (cells + 2 * SUB), LANE),
        held_planes(size, 2, 2),
        held_planes(size, 2, 2),
        held_planes(size, 2),
        f32(2, 2, cells, length),
    ) + [pltpu.SemaphoreType.DMA((4,))]


def fused_body(noise, source):
    rows, groups = lax.axis_size("row"), lax.axis_size(PLANE)
    devices = rows * groups
    planes, cells, length = noise.shape
    first, second = planes * rows, cells * groups
    bf16 = jnp.bfloat16
    held = length // 2 // devices
    js = list(range(held))
    low = held // 2
    me = lax.axis_index(EVERY)
    row_at, group_at = lax.axis_index("row"), lax.axis_index(PLANE)
    flags = jnp.stack(
        [
            row_at == 0,
            row_at == rows - 1,
            group_at == 0,
            group_at == groups - 1,
            row_at % 2 == 1,
        ]
    ).astype(jnp.int32)
    norm = FIELD_SCALE * (float(first) * float(second) * float(length)) ** (-0.5)
    flat = (planes * cells, length)

    pieces = 4
    table = [x.reshape(pieces, -1, length) for x in two_parts(forward_third(length, devices, js))]
    table = np.concatenate(table, axis=1)
    shape = (length * SUB, LANE)
    sent = call(
        functools.partial(forward_kernel, planes),
        pltpu.HBM(shape, jnp.float32),
        (table, noise.reshape(flat)),
        room(table)
        + [
            pltpu.VMEM(flat, bf16),
            pltpu.VMEM(shape, jnp.float32),
            pltpu.SemaphoreType.DMA((2 * pieces + planes // 2,)),
        ],
        4 * length * length * planes * cells,
        [AWAY] * 2,
        12,
    )
    sent, source = lax.optimization_barrier((sent, source))
    sent = sent.reshape(devices, 2 * held, SUB, LANE)
    arrived = lax.all_to_all(sent, EVERY, split_axis=0, concat_axis=0, tiled=True)

    pairs = np.zeros((length, length // 2), np.float32)
    pairs[np.arange(length), np.arange(length) // 2] = 0.125
    level = f32(cells + cells // 4, length)
    side = f32(2 * SUB, length)
    coarse_source, *edges = call(
        functools.partial(source_kernel, planes),
        [f32(planes * cells // 4, length // 2), level, level, side, side],
        (pairs.astype(bf16), source.reshape(flat)),
        [
            pltpu.VMEM((planes * cells, length // 2), jnp.float32),
            pltpu.VMEM((cells, LANE), jnp.float32),
        ],
        planes * cells * length * length,
        [VMEM] * 2,
        12,
    )
    coarse_source = coarse_source.reshape(planes // 2, cells // 2, length // 2)
    edges = (*swap(*edges[:2], "row"), *swap(*edges[2:], PLANE))
    arrived, edges, coarse_source = lax.optimization_barrier((arrived, edges, coarse_source))

    constants = (
        two_parts(second_table(second))
        + (
            stacked(forward_first(first)),
            stacked(inverse_first(first)),
            stacked(inverse_first_coarse(first // 2, rows)),
        )
        + two_parts(second_coarse(second // 2, groups))
        + two_parts(second_table(second).transpose(0, 2, 1))
    )
    tiles = 2 * held + low // 2 + 1
    modes = (me + devices * np.array(js)).astype(jnp.float32)
    weight = jnp.where(modes == 0.0, norm, 2.0 * norm).astype(jnp.float32)
    scale = jnp.stack([DECAY * modes * modes, weight], axis=1)
    block = (2, 2 * held * first, second // 2)
    shape = (devices, tiles, SUB, LANE)
    out = call(
        functools.partial(middle_kernel, (first, second, rows, groups, held, low)),
        pltpu.HBM(shape, jnp.float32),
        (scale, arrived, *constants),
        room(*constants)
        + [
            pltpu.VMEM(shape, jnp.float32),
            pltpu.SemaphoreType.DMA((len(constants),)),
            pltpu.VMEM(block, bf16),
            pltpu.VMEM(block, bf16),
            pltpu.VMEM(block, jnp.float32),
            pltpu.VMEM(block, bf16),
            pltpu.VMEM(block, bf16),
            pltpu.VMEM((low // 2 * first, second), bf16),
            pltpu.VMEM((low // 2 * first, second), bf16),
        ],
        6 * 2 * 2 * held * first * second * (second + 2 * first),
        [SMEM, VMEM] + [AWAY] * len(constants),
        22,
    )
    out, source, coarse_source, edges = lax.optimization_barrier(
        (out, source, coarse_source, edges)
    )
    got = lax.all_to_all(out, EVERY, split_axis=0, concat_axis=0, tiled=True)
    size, coarse_size = noise.shape, coarse_source.shape
    sizes = (size, coarse_size)
    sources = (source, coarse_source, *edges)
    laid = call(
        functools.partial(layout_kernel, size),
        [
            held_planes(s, *count)
            for s in sizes
            for count in ((s[0] - 2,), (2, 2))
        ],
        sources,
        room(*sources) + [pltpu.SemaphoreType.DMA((6,))],
        source.size,
        [AWAY] * 6,
        12,
    )
    got, laid = lax.optimization_barrier((got, laid))

    third = inverse_third(length, devices, js)
    constants = (
        two_parts(third)
        + two_parts(third_coarse(length // 2, devices, js[:low]))
        + (lane_order(2 * held, low).astype(bf16),)
        + two_parts(third_coarse_halo(length // 2, devices, js[:low]))
    )
    edge = f32(sum(2 * (s[2] // LANE) * s[1] + SUB for s in sizes), LANE)
    shares = (devices, 2 * held, tiles)
    got = got.reshape(devices * tiles * SUB, LANE)
    ks, coarse_ks, cols, far, near = call(
        functools.partial(edge_kernel, (devices, 2 * held, low, tiles, planes, length)),
        [held_planes(s, 4) for s in sizes] + [f32(HALO * planes, length), edge, edge],
        (flags, got, *constants),
        room(*constants)
        + [pltpu.VMEM((2, 4 * cells, devices * held), bf16)] * 2
        + [pltpu.VMEM((planes // 2 * LANE, devices * low), bf16)] * 2
        + [pltpu.SemaphoreType.DMA((7,))],
        3 * planes * cells * length * length,
        [SMEM, VMEM] + [AWAY] * 7,
        16,
    )
    k_far, k_near = (
        lax.ppermute(
            x, "row", [p for i in range(at, rows - 1, 2) for p in ((i, i + 1), (i + 1, i))]
        )
        for x, at in ((far, 1), (near, 0))
    )
    inner_f, outer_f, coarse_inner_f, coarse_outer_f = laid
    inner, *kept = call(
        functools.partial(inner_kernel, size, shares),
        [pltpu.HBM(size, jnp.float32)]
        + [held_planes(s, s[0] - 2) for s in sizes for _ in range(3)]
        + [held_planes(s, 2) for s in sizes for _ in range(2)],
        (flags, got, *constants[:2], ks, coarse_ks, cols, inner_f, coarse_inner_f),
        room(held_planes(size, planes), *constants[:2])
        + [pltpu.VMEM((2, (planes - 4) * cells, devices * held), bf16)] * 2
        + room(f32(planes - 4, cells, length))
        + [pltpu.SemaphoreType.DMA((2,))],
        3 * planes * cells * length * length,
        [SMEM, VMEM] + [AWAY] * 2 + [VMEM] * 5,
        18,
    )
    return call(
        functools.partial(outer_kernel, size),
        [pltpu.HBM(s, jnp.float32) for s in sizes],
        (
            flags,
            *(ks, outer_f, *kept[:3], *kept[6:8]),
            *(coarse_ks, coarse_outer_f, *kept[3:6], *kept[8:]),
            *(k_far, k_near, inner),
        ),
        outer_scratch(size) + outer_scratch(coarse_size),
        30 * source.size,
        [SMEM] + [VMEM] * 16 + [AWAY],
        18,
        None,
        {17: 0},
    )


NEIGHBOUR_STEPS = ((1, 0, 0), (-1, 0, 0), (0, 1, 0), (0, -1, 0), (0, 0, 1), (0, 0, -1))


def padded(x, sides, width):
    for axis, dim in sides:
        peers, length = (lax.axis_size(axis), x.shape[dim])
        up = [(i, (i + 1) % peers) for i in range(peers - 1)]
        down = [(j, i) for i, j in up]
        last = lax.slice_in_dim(x, length - width, length, axis=dim)
        leading = lax.slice_in_dim(x, 0, width, axis=dim)
        before = lax.ppermute(last, axis, up)
        after = lax.ppermute(leading, axis, down)
        x = jnp.concatenate([before, x, after], axis=dim)
    return x


def signed_modes(index, length):
    return jnp.where(index < length // 2, index, index - length).astype(jnp.float32)


def amplitude(first_modes, second_modes, third_modes, first_edge, second_edge, third_edge):
    squared = first_modes * first_modes + second_modes * second_modes + third_modes * third_modes
    value = FIELD_SCALE / (1.0 + (2.0 * math.pi * CORRELATION) ** 2 * squared)
    edge = (
        (jnp.abs(first_modes) == first_edge)
        | (jnp.abs(second_modes) == second_edge)
        | (jnp.abs(third_modes) == third_edge)
    )
    return jnp.where(edge, 0.0, value)


def phase_table(count_rows, count_cols, modulus, sign):
    left_index = jnp.arange(count_rows, dtype=jnp.int32)[:, None]
    right_index = jnp.arange(count_cols, dtype=jnp.int32)[None, :]
    angle = 2.0 * math.pi / modulus * (left_index * right_index % modulus).astype(jnp.float32)
    return (jnp.cos(angle), sign * jnp.sin(angle))


def split_length(length):
    outer_len = 2 ** ((length.bit_length() - 1) // 2)
    return (outer_len, length // outer_len)


def real_form(form, left_value, right_value):
    return jnp.einsum(form, left_value, right_value, precision=lax.Precision.HIGHEST)


def complex_form(form, left_real, left_imag, right_real, right_imag):
    real_part = real_form(form, left_real, right_real) - real_form(form, left_imag, right_imag)
    imag_part = real_form(form, left_real, right_imag) + real_form(form, left_imag, right_real)
    return (real_part, imag_part)


def merge_pair(values, out_form, first_letter):
    merge_at = out_form.index(first_letter)
    out_dims = list(values.shape)
    merged = (
        out_dims[:merge_at]
        + [out_dims[merge_at] * out_dims[merge_at + 1]]
        + out_dims[merge_at + 2 :]
    )
    return values.reshape(merged)


def forward_axis(real_part, imag_part, lead_form, out_form, kept_modes):
    length = real_part.shape[-1]
    outer_len, inner_len = split_length(length)
    split_shape = real_part.shape[:-1] + (outer_len, inner_len)
    outer_real, outer_imag = phase_table(outer_len, outer_len, outer_len, -1.0)
    twist_real, twist_imag = phase_table(outer_len, inner_len, length, -1.0)
    inner_real, inner_imag = phase_table(inner_len, kept_modes // outer_len, inner_len, -1.0)
    first_form = lead_form + "ab,ai->" + lead_form + "ib"
    split_real = real_part.reshape(split_shape)
    if imag_part is None:
        section_real = real_form(first_form, split_real, outer_real)
        section_imag = real_form(first_form, split_real, outer_imag)
    else:
        section_real, section_imag = complex_form(
            first_form, split_real, imag_part.reshape(split_shape), outer_real, outer_imag
        )
    turned_real = section_real * twist_real - section_imag * twist_imag
    turned_imag = section_real * twist_imag + section_imag * twist_real
    result_real, result_imag = complex_form(
        lead_form + "ib,bj->" + out_form, turned_real, turned_imag, inner_real, inner_imag
    )
    return (merge_pair(result_real, out_form, "j"), merge_pair(result_imag, out_form, "j"))


def inverse_axis(real_part, imag_part, length, lead_form, out_form, real_only):
    kept_modes = real_part.shape[-1]
    outer_len, inner_len = split_length(length)
    split_shape = real_part.shape[:-1] + (kept_modes // outer_len, outer_len)
    inner_real, inner_imag = phase_table(kept_modes // outer_len, inner_len, inner_len, 1.0)
    twist_real, twist_imag = phase_table(outer_len, inner_len, length, 1.0)
    outer_real, outer_imag = phase_table(outer_len, outer_len, outer_len, 1.0)
    section_real, section_imag = complex_form(
        lead_form + "ji,jb->" + lead_form + "ib",
        real_part.reshape(split_shape),
        imag_part.reshape(split_shape),
        inner_real,
        inner_imag,
    )
    turned_real = section_real * twist_real - section_imag * twist_imag
    turned_imag = section_real * twist_imag + section_imag * twist_real
    second_form = lead_form + "ib,ia->" + out_form
    if real_only:
        result = real_form(second_form, turned_real, outer_real) - real_form(
            second_form, turned_imag, outer_imag
        )
        return merge_pair(result, out_form, "a")
    result_real, result_imag = complex_form(
        second_form, turned_real, turned_imag, outer_real, outer_imag
    )
    return (merge_pair(result_real, out_form, "a"), merge_pair(result_imag, out_form, "a"))


def low_band(values, half_coarse, fine_len):
    return jnp.concatenate(
        [values[:, :, :half_coarse], values[:, :, fine_len - half_coarse :]], axis=2
    )


def window(values, margin, offset):
    return values[
        margin + offset[0] : values.shape[0] - margin + offset[0],
        margin + offset[1] : values.shape[1] - margin + offset[1],
        margin + offset[2] : values.shape[2] - margin + offset[2],
    ]


def face_weight(center, beside):
    return jnp.where(beside > 0.0, 0.5 * (center + beside), center)


def smooth_twice(kappa, source):
    no_shift = (0, 0, 0)
    center = window(kappa, 1, no_shift)
    faces = [face_weight(center, window(kappa, 1, offset)) for offset in NEIGHBOUR_STEPS]
    diagonal = faces[0] + faces[1] + faces[2] + faces[3] + faces[4] + faces[5]
    guarded = jnp.where(center > 0.0, diagonal, 1.0)
    first_sweep = JACOBI_WEIGHT * window(source, 1, no_shift) / guarded
    inner_first = window(first_sweep, 1, no_shift)
    inner_diagonal = window(diagonal, 1, no_shift)
    coupled = jnp.zeros_like(inner_first)
    for face_value, offset in zip(faces, NEIGHBOUR_STEPS):
        coupled = coupled + window(face_value, 1, no_shift) * window(first_sweep, 1, offset)
    residual = window(source, 2, no_shift) - inner_diagonal * inner_first + coupled
    return inner_first + JACOBI_WEIGHT * residual / inner_diagonal


def pad_depth(values):
    return jnp.pad(values, ((0, 0), (0, 0), (2, 2)))


def plain_body(noise, source):
    row_at = lax.axis_index("row")
    group_at = lax.axis_index(("level", "col"))
    fine_field = noise.astype(jnp.float32)
    fine_len = fine_field.shape[-1]
    coarse_len = fine_len // 2
    half_coarse = coarse_len // 2
    kept_modes = fine_len // 2
    real_part, imag_part = forward_axis(fine_field, None, "pq", "pjiq", kept_modes)
    real_part, imag_part = (
        lax.all_to_all(real_part, ("level", "col"), split_axis=1, concat_axis=2, tiled=True),
        lax.all_to_all(imag_part, ("level", "col"), split_axis=1, concat_axis=2, tiled=True),
    )
    real_part, imag_part = forward_axis(real_part, imag_part, "pq", "jiqp", fine_len)
    real_part, imag_part = (
        lax.all_to_all(real_part, "row", split_axis=0, concat_axis=2, tiled=True),
        lax.all_to_all(imag_part, "row", split_axis=0, concat_axis=2, tiled=True),
    )
    slab_len = real_part.shape[-1]
    coarse_slab = slab_len // 2
    half_slab = coarse_slab // 2
    real_part, imag_part = forward_axis(real_part, imag_part, "pq", "pqji", slab_len)
    second_count = real_part.shape[0]
    third_count = real_part.shape[1]
    wave_second = signed_modes(
        row_at * second_count + jnp.arange(second_count, dtype=jnp.int32), fine_len
    )[:, None, None]
    third_index = group_at * third_count + jnp.arange(third_count, dtype=jnp.int32)
    wave_third = signed_modes(third_index, fine_len)[None, :, None]
    spread = 2.0
    mirror_weight = jnp.where(third_index == 0, 1.0, spread).astype(jnp.float32)[None, :, None]
    norm_factor = (float(slab_len) * float(fine_len) * float(fine_len)) ** (-0.5)
    wave_first = signed_modes(jnp.arange(slab_len, dtype=jnp.int32), slab_len)[None, None, :]
    fine_scale = (
        amplitude(
            wave_second, wave_third, wave_first, fine_len / 2.0, fine_len / 2.0, slab_len / 2.0
        )
        * mirror_weight
        * norm_factor
    )
    coarse_first = signed_modes(jnp.arange(coarse_slab, dtype=jnp.int32), coarse_slab)[
        None, None, :
    ]
    coarse_scale = (
        amplitude(
            wave_second,
            wave_third,
            coarse_first,
            coarse_len / 2.0,
            coarse_len / 2.0,
            coarse_slab / 2.0,
        )
        * mirror_weight
        * norm_factor
    )
    coarse_real = low_band(real_part, half_slab, slab_len) * coarse_scale
    coarse_imag = low_band(imag_part, half_slab, slab_len) * coarse_scale
    fine_real, fine_imag = inverse_axis(
        real_part * fine_scale, imag_part * fine_scale, slab_len, "pq", "abqp", False
    )
    coarse_real, coarse_imag = inverse_axis(
        coarse_real, coarse_imag, coarse_slab, "pq", "abqp", False
    )
    fine_real, fine_imag, coarse_real, coarse_imag = (
        lax.all_to_all(fine_real, "row", split_axis=0, concat_axis=2, tiled=True),
        lax.all_to_all(fine_imag, "row", split_axis=0, concat_axis=2, tiled=True),
        lax.all_to_all(coarse_real, "row", split_axis=0, concat_axis=2, tiled=True),
        lax.all_to_all(coarse_imag, "row", split_axis=0, concat_axis=2, tiled=True),
    )
    coarse_real = low_band(coarse_real, half_coarse, fine_len)
    coarse_imag = low_band(coarse_imag, half_coarse, fine_len)
    fine_real, fine_imag = inverse_axis(fine_real, fine_imag, fine_len, "pq", "pabq", False)
    coarse_real, coarse_imag = inverse_axis(
        coarse_real, coarse_imag, coarse_len, "pq", "pabq", False
    )
    fine_real, fine_imag, coarse_real, coarse_imag = (
        lax.all_to_all(fine_real, ("level", "col"), split_axis=1, concat_axis=2, tiled=True),
        lax.all_to_all(fine_imag, ("level", "col"), split_axis=1, concat_axis=2, tiled=True),
        lax.all_to_all(coarse_real, ("level", "col"), split_axis=1, concat_axis=2, tiled=True),
        lax.all_to_all(coarse_imag, ("level", "col"), split_axis=1, concat_axis=2, tiled=True),
    )
    coarse_real = coarse_real[:, :, :half_coarse]
    coarse_imag = coarse_imag[:, :, :half_coarse]
    fine_log = inverse_axis(fine_real, fine_imag, fine_len, "pq", "pqab", True)
    coarse_log = inverse_axis(coarse_real, coarse_imag, coarse_len, "pq", "pqab", True)
    fine_kappa = jnp.exp(fine_log)
    coarse_kappa = jnp.exp(coarse_log)
    fine_source = source.astype(jnp.float32)
    coarse_rows = coarse_log.shape[0]
    coarse_cols = coarse_log.shape[1]
    coarse_source = fine_source.reshape(coarse_rows, 2, coarse_cols, 2, coarse_len, 2).mean(
        axis=(1, 3, 5)
    )
    fine_kappa, fine_source, coarse_kappa, coarse_source = (
        padded(fine_kappa, (("row", 0), (("level", "col"), 1)), 2),
        padded(fine_source, (("row", 0), (("level", "col"), 1)), 2),
        padded(coarse_kappa, (("row", 0), (("level", "col"), 1)), 2),
        padded(coarse_source, (("row", 0), (("level", "col"), 1)), 2),
    )
    fine_pressure = smooth_twice(pad_depth(fine_kappa), pad_depth(fine_source))
    coarse_pressure = smooth_twice(pad_depth(coarse_kappa), pad_depth(coarse_source))
    return (fine_pressure, coarse_pressure)


def body(noise, source):
    planes, cells, length = noise.shape
    rows, groups = lax.axis_size("row"), lax.axis_size(PLANE)
    modes = length // 2 // (rows * groups)
    fills = planes == SUB and cells == LANE and 2 * HALO * modes == LANE // 2
    if fills and length % (4 * LANE) == 0 and rows % 2 == 0 and groups % 4 == 0:
        return fused_body(noise, source)
    return plain_body(noise, source)


def solution(mesh):
    return jax.shard_map(
        body,
        mesh=mesh,
        in_specs=(P("row", ("level", "col"), None), P("row", ("level", "col"), None)),
        out_specs=(P("row", ("level", "col"), None), P("row", ("level", "col"), None)),
        check_vma=False,
    )
```

```python
import functools
import math

import jax
import jax.numpy as jnp
import numpy as np
from jax import lax
from jax.experimental import pallas as pl
from jax.experimental.pallas import tpu as pltpu
from jax.sharding import PartitionSpec as P

JACOBI_WEIGHT = 2.0 / 3.0
CORRELATION = 0.2
FIELD_SCALE = 0.3
DECAY = (2.0 * math.pi * CORRELATION) ** 2
EVERY = ("row", "level", "col")
PLANE = ("level", "col")
MIB = 1 << 20
SUB, LANE = 8, 128
HALO = 4


def two_parts(matrix):
    high = matrix.astype(jnp.bfloat16)
    low = (matrix - high.astype(np.float64)).astype(jnp.bfloat16)
    return high, low


def angles(rows, cols, length):
    return 2.0 * np.pi * (np.outer(rows, cols) % length) / length


def third_modes(devices, js):
    return np.array([[d + devices * j for j in js] for d in range(devices)])


def forward_third(length, devices, js):
    theta = angles(third_modes(devices, js).reshape(-1), np.arange(length), length)
    return np.stack([np.cos(theta), -np.sin(theta)], axis=1).reshape(-1, length)


def inverse_third(length, devices, js):
    modes = third_modes(devices, js).reshape(devices // 2, 2, len(js)).transpose(1, 0, 2)
    theta = 2.0 * np.pi * (modes[..., None] * np.arange(length // 2) % length) / length
    both = np.stack([np.cos(theta), -np.sin(theta)], axis=3)
    return both.reshape(2, -1, length // 2)


def second_modes(length):
    return np.arange(length // 2).reshape(-1, 2).T


def second_table(length):
    theta = second_modes(length)[:, None, :] * np.arange(length // 2)[None, :, None]
    theta = 2.0 * np.pi * (theta % length) / length
    return np.concatenate([np.cos(theta), np.sin(theta)], axis=2)


def forward_first(length):
    theta = angles(np.arange(length), np.arange(length), length)
    cos, sin = np.cos(theta), np.sin(theta)
    return np.block([[cos, sin], [-sin, cos]])


def inverse_first(length):
    theta = angles(np.arange(length), np.arange(length), length)
    cos, sin = np.cos(theta), np.sin(theta)
    cos[:, length // 2] = 0.0
    sin[:, length // 2] = 0.0
    return np.block([[cos, -sin], [sin, cos]])


def inverse_first_coarse(length, rows):
    full = inverse_first(length)
    value = full.reshape(2, rows, length // rows, 2 * length)
    turned = np.concatenate([-full[length:], full[:length]]).reshape(value.shape)
    order = lambda x: x.transpose(1, 0, 2, 3).reshape(2 * length, 2 * length)
    return np.concatenate([order(value), order(turned)])


def second_coarse(length, groups):
    theta = angles(second_modes(length).reshape(-1), np.arange(length), length)
    table = np.concatenate([np.cos(theta), np.sin(theta)])
    span = length // groups
    out = np.zeros((2, length, groups, 2, span))
    for pair in range(2):
        out[pair, :, :, pair, :] = table.reshape(length, groups, span)
    return out.reshape(2 * length, 2 * length)


def third_coarse(length, devices, js):
    modes = third_modes(devices, js).reshape(devices, len(js) // 2, 2)
    theta = 2.0 * np.pi * (modes[..., None] * np.arange(length) % length) / length
    both = np.stack([np.cos(theta), -np.sin(theta)])
    return both.transpose(0, 2, 1, 3, 4).reshape(2 * (len(js) // 2) * devices, 2 * length)


def third_coarse_halo(length, devices, js):
    theta = angles(third_modes(devices, js).reshape(-1), np.arange(length), length)
    return np.concatenate([np.cos(theta), -np.sin(theta)], axis=1)


def lane_order(parts, coarse_parts):
    out = np.zeros((LANE, LANE))
    for h in range(HALO):
        for q in range(parts):
            out[HALO * q + h, parts * h + q] = 1.0
        for j in range(coarse_parts):
            out[LANE // 2 + HALO * j + h, LANE // 2 + coarse_parts * h + j] = 1.0
    return out


def split(x):
    high = x.astype(jnp.bfloat16)
    return high, (x - high.astype(jnp.float32)).astype(jnp.bfloat16)


def dot(a, b):
    return lax.dot_general(a, b, (((1,), (0,)), ((), ())), preferred_element_type=jnp.float32)


def dot_t(a, b):
    return lax.dot_general(a, b, (((1,), (1,)), ((), ())), preferred_element_type=jnp.float32)


def stacked(matrix):
    high, low = two_parts(matrix)
    return np.block([[high, high], [low, np.zeros_like(low)]])


def dot_left(stack, x):
    value = dot(stack, jnp.concatenate(split(x), axis=0))
    rows = stack.shape[0] // 2
    return value[:rows] + value[rows:]


def dot3(a, b):
    (ah, al), (bh, bl) = a, b
    return dot(ah, bh) + (dot(ah, bl) + dot(al, bh))


def load(pairs, sems):
    copies = [pltpu.make_async_copy(a, b, sems.at[i]) for i, (a, b) in enumerate(pairs)]
    for copy in copies:
        copy.start()
    return copies


def send(pairs, sems, first):
    copies = [pltpu.make_async_copy(a, b, sems.at[first + i]) for i, (a, b) in enumerate(pairs)]
    for copy in copies:
        copy.start()
    return copies


def forward_kernel(planes, d_hbm, x_hbm, out_hbm, d, x, out, sems):
    pieces, rows = d.shape[0], d.shape[1] // 2
    parts = [slice(p * LANE, (p + 2) * LANE) for p in range(0, planes, 2)]
    pairs = [(x_hbm.at[at, :], x.at[at, :]) for at in parts]
    copies = load([(d_hbm.at[0], d.at[0])] + pairs, sems)
    later = [(d_hbm.at[i], d.at[i]) for i in range(1, pieces)]
    sent = []
    copies[0].wait()
    for piece in range(pieces):
        if piece:
            copies[len(parts) + piece].wait()
        for i, at in enumerate(parts):
            if piece == 0:
                copies[i + 1].wait()
            if piece == 0 and at is parts[-1]:
                copies += send(later, sems, len(copies))
            value = dot_t(d[piece], x[at, :])
            value = value[:rows] + value[rows:]
            for h in range(2):
                out[pl.ds(piece * rows * SUB + 2 * i + h, rows, stride=SUB), :] = value[
                    :, h * LANE : (h + 1) * LANE
                ]
        tall = slice(piece * rows * SUB, (piece + 1) * rows * SUB)
        sent += send([(out.at[tall, :], out_hbm.at[tall, :])], sems, len(copies) + piece)
    for copy in sent:
        copy.wait()


def middle_kernel(sizes, scale, b, *rest):
    (first, second, rows, groups, js, low) = sizes
    count = 9
    away, out_hbm, near, rest = (
        rest[:count],
        rest[count],
        rest[count + 1 : 2 * count + 1],
        rest[2 * count + 1 :],
    )
    out, sems, zh, zl, y, oh, ol, qh, ql = rest
    copies = load(list(zip(away, near))[:5], sems)
    csh, csl, forward, inverse, coarse_inverse, cch, ccl, ch, cl = near
    q_count = 2 * js
    half, quarter = second // 2, second // 4
    for q in range(q_count):
        for g in range(groups // 2):
            for r in range(0, rows, 2):
                at = r * groups + g
                near_half = jnp.concatenate([b[at, q], b[at + groups, q]], axis=0)
                at += groups // 2
                far_half = jnp.concatenate([b[at, q], b[at + groups, q]], axis=0)
                at = slice(q * first + r * SUB, q * first + (r + 2) * SUB)
                lanes = slice(g * LANE, (g + 1) * LANE)
                zh[0, at, lanes], zl[0, at, lanes] = split(near_half + far_half)
                zh[1, at, lanes], zl[1, at, lanes] = split(near_half - far_half)
    for copy in copies:
        copy.wait()
    copies = send(list(zip(away, near))[5:], sems, 5)
    wide = 16 * first
    for top in range(0, q_count * first, wide):
        at = slice(top, top + wide)
        for parity in range(2):
            y[parity, at, :] = dot3(
                (zh[parity, at, :], zl[parity, at, :]), (csh[parity], csl[parity])
            )
    mode0 = lax.broadcasted_iota(jnp.int32, (first, second), 0)
    mode0 = jnp.where(mode0 < first // 2, mode0, mode0 - first).astype(jnp.float32)
    lane = lax.broadcasted_iota(jnp.int32, (first, second), 1)
    mode1 = jnp.where(lane < half, lane, lane - half)
    mode1 = jnp.where(mode1 < quarter, 2 * mode1, 2 * (mode1 - quarter) + 1).astype(jnp.float32)
    base = 1.0 + DECAY * (mode0 * mode0 + mode1 * mode1)
    for j in range(js):
        top = j * 2 * first
        re, im = slice(top, top + first), slice(top + first, top + 2 * first)
        cos, sin = slice(0, quarter), slice(quarter, half)
        whole = lambda part, lanes: jnp.concatenate(
            [y[0, part, lanes], y[1, part, lanes]], axis=1
        )
        rc, rs, ic, isn = whole(re, cos), whole(re, sin), whole(im, cos), whole(im, sin)
        wave = jnp.concatenate(
            [
                jnp.concatenate([rc + isn, rc - isn], axis=1),
                jnp.concatenate([ic - rs, ic + rs], axis=1),
            ],
            axis=0,
        )
        spectrum = dot_left(forward[...], wave)
        amp = jnp.where(lane == half, 0.0, scale[j, 1] / (base + scale[j, 0]))
        scaled = spectrum * jnp.concatenate([amp, amp], axis=0)
        field = dot_left(inverse[...], scaled)
        plus, minus = field[:, :half], field[:, half:]
        even, odd = plus + minus, plus - minus
        odd = jnp.concatenate([-odd[first:], odd[:first]], axis=0)
        at = slice(top, top + 2 * first)
        for parity, lanes in enumerate((cos, sin)):
            operand = jnp.concatenate([even[:, lanes], odd[:, lanes]], axis=1)
            oh[parity, at, :], ol[parity, at, :] = split(operand)
        if j < low:
            keep = first // 4
            kept = [
                scaled[at : at + keep, :]
                for at in (0, first - keep, first, 2 * first - keep)
            ]
            band = jnp.concatenate(kept, axis=0)
            low_lane = lax.broadcasted_iota(jnp.int32, (first, quarter), 1) < quarter // 2
            pieces = []
            for at in (0, half):
                upper = pltpu.roll(band[:, at + quarter : at + half], quarter // 2, 1)
                pieces.append(jnp.where(low_lane, band[:, at : at + quarter], upper))
            band = jnp.concatenate(pieces, axis=1)
            field = dot_left(coarse_inverse[...], band)
            value, turned = field[:first], field[first:]
            operand = jnp.concatenate(
                [
                    value[:, :quarter] + value[:, quarter:],
                    turned[:, :quarter] - turned[:, quarter:],
                ],
                axis=1,
            )
            at = slice(j // 2 * first, (j // 2 + 1) * first)
            lanes = slice(j % 2 * half, (j % 2 + 1) * half)
            qh[at, lanes], ql[at, lanes] = split(operand)
    for copy in copies:
        copy.wait()
    copies = []
    wide = 4 * first
    lane = lax.broadcasted_iota(jnp.int32, (SUB, LANE), 1)
    extra = q_count + low // 2

    def leave(start, stop):
        at = slice(start, stop)
        copies.extend(send([(out.at[:, at], out_hbm.at[:, at])], sems, len(copies)))

    def give(value, start):
        tiles = value.shape[0] // first
        for q in range(tiles):
            for r in range(rows):
                for g in range(groups):
                    at = q * first + r * SUB
                    out[r * groups + g, start + q] = value[
                        at : at + SUB, g * LANE : (g + 1) * LANE
                    ]
        leave(start, start + tiles)

    def halo_columns(value, start, held):
        tiles = value.shape[0] // first
        for r in range(rows):
            for g in range(groups):
                total = held[r, g]
                left = max(g - 1, 0) * LANE
                right = min(g + 1, groups - 1) * LANE
                for q in range(tiles):
                    at = slice(q * first + r * SUB, q * first + (r + 1) * SUB)
                    both = jnp.where(
                        lane < LANE // 2,
                        value[at, right : right + LANE],
                        value[at, left : left + LANE],
                    )
                    to = HALO * (start + q)
                    both = pltpu.roll(both, (to + 2) % LANE, 1)
                    total = jnp.where((lane >= to) & (lane < to + HALO), both, total)
                held[r, g] = total

    def coarse_columns(value, held):
        half_lane = LANE // 2
        for j in range(low):
            for r in range(rows):
                at = slice(j // 2 * first + r * SUB, j // 2 * first + (r + 1) * SUB)
                shift = HALO * j + 2 - j % 2 * half_lane
                to = half_lane + HALO * j
                for g in range(groups):
                    left = max(g - 1, 0) * LANE
                    right = min(g + 1, groups - 1) * LANE
                    left = pltpu.roll(value[at, left : left + LANE], shift % LANE, 1)
                    right = pltpu.roll(
                        value[at, right : right + LANE], (shift + half_lane) % LANE, 1
                    )
                    total = jnp.where((lane >= to) & (lane < to + 2), left, held[r, g])
                    held[r, g] = jnp.where(
                        (lane >= to + 2) & (lane < to + HALO), right, total
                    )

    columns = {
        (r, g): jnp.zeros((SUB, LANE), jnp.float32) for r in range(rows) for g in range(groups)
    }
    coarse = dot3((qh[...], ql[...]), (cch[...], ccl[...]))
    give(coarse, q_count)
    coarse_columns(coarse, columns)
    for top in range(0, q_count * first, wide):
        at = slice(top, top + wide)
        even, odd = (
            dot3((oh[parity, at, :], ol[parity, at, :]), (ch[parity], cl[parity]))
            for parity in range(2)
        )
        value = jnp.concatenate([even + odd, even - odd], axis=1)
        give(value, top // first)
        halo_columns(value, top // first, columns)
    for (r, g), total in columns.items():
        out[r * groups + g, extra] = total
    leave(extra, extra + 1)
    for copy in copies:
        copy.wait()


def gather_modes(b, at, sizes, lh, ll):
    devices, q_count, tiles = sizes
    for i, n in enumerate(at):
        for parity in range(2):
            rows = jnp.concatenate(
                [
                    b[pl.ds(s * tiles * SUB + n, q_count, stride=SUB), :]
                    for s in range(parity, devices, 2)
                ],
                axis=0,
            )
            to = slice(i * LANE, (i + 1) * LANE)
            lh[parity, to, :], ll[parity, to, :] = split(jnp.transpose(rows))


def inverse_pair(i, lh, ll, eh, el, ks, to, cells):
    at = slice(i * cells, (i + 2) * cells)
    even, odd = (
        dot3((lh[parity, at, :], ll[parity, at, :]), (eh[parity], el[parity]))
        for parity in range(2)
    )
    value = jnp.exp(jnp.concatenate([even + odd, even - odd], axis=1))
    for n in range(2):
        put_rows(ks, to + n, SUB, value[n * cells : (n + 1) * cells])


def edge_kernel(sizes, flags, b, *rest):
    (devices, q_count, low, tiles, planes, length) = sizes
    away, (ks, cks, cols, far, near_edge), rest = rest[:7], rest[7:12], rest[12:]
    near, (lh, ll, mh, ml, sems) = rest[:7], rest[7:]
    copies = load(list(zip(away, near))[:4], sems)
    eh, el, ceh, cel, order, cwh, cwl = near
    cells, short = LANE, length // 2
    halves, coarse_planes = low // 2, planes // 2
    half = cells // 2
    gather_modes(b, (0, 1, planes - 2, planes - 1), (devices, q_count, tiles), lh, ll)
    for n in range(coarse_planes):
        rows = jnp.concatenate(
            [
                b[pl.ds((q_count + h) * SUB + c * coarse_planes + n, devices, stride=tiles * SUB), :]
                for c in range(2)
                for h in range(halves)
            ],
            axis=0,
        )
        at = slice(n * LANE, (n + 1) * LANE)
        mh[at, :], ml[at, :] = split(jnp.transpose(rows))

    for copy in copies:
        copy.wait()
    copies = send(list(zip(away, near))[4:], sems, 4)

    for i in range(0, 4, 2):
        inverse_pair(i, lh, ll, eh, el, ks, i, cells)
    value = dot3((mh[...], ml[...]), (ceh[...], cel[...]))
    for n in range(coarse_planes):
        top = n * cells
        part = value[top : top + half, :short] + value[top + half : top + cells, short:]
        part = jnp.exp(part)
        put_rows(cks, n, SUB, part)

    for copy in copies:
        copy.wait()
    lane = lax.broadcasted_iota(jnp.int32, (SUB, LANE), 1)
    tile_rows = [b[(s * tiles + tiles - 1) * SUB : (s + 1) * tiles * SUB, :] for s in range(devices)]
    high, rest_part = split(jnp.concatenate(tile_rows, axis=0))
    ordered = dot(high, order[...]) + dot(rest_part, order[...])

    def joined(of, width, start):
        fit = LANE // width
        cells_of = []
        for h in range(HALO):
            parts = []
            for i, s in enumerate(of):
                moved = ordered[s * SUB : (s + 1) * SUB]
                shift = (i % fit * width - start - h * width) % LANE
                moved = pltpu.roll(moved, shift, 1) if shift else moved
                if i % fit == 0:
                    parts.append(moved)
                else:
                    parts[-1] = jnp.where(lane >= i % fit * width, moved, parts[-1])
            cells_of.append(jnp.concatenate(parts, axis=1))
        return split(jnp.concatenate(cells_of, axis=0))

    even, odd = (
        dot3(joined(range(parity, devices, 2), q_count, 0), (eh[parity], el[parity]))
        for parity in range(2)
    )
    value = jnp.exp(jnp.concatenate([even + odd, even - odd], axis=1))
    cols[...] = value
    for h in range(HALO):
        for i, n in enumerate((0, 1, planes - 2, planes - 1)):
            at = h * planes + n
            put_rows(ks, i, halo_row(h, cells), value[at : at + 1, :])
    whole = dot3(joined(range(devices), low, LANE // 2), (cwh[...], cwl[...]))
    for h in range(HALO):
        top = h * SUB
        part = whole[top : top + coarse_planes, :short] + whole[top + coarse_planes : top + SUB, short:]
        part = jnp.exp(part)
        for n in range(coarse_planes):
            put_rows(cks, n, halo_row(h, half), part[n : n + 1, :])
    for held in (ks, cks):
        repeat_sides(flags, held, [(n,) for n in range(4)])
    odd_row = flags[4] == 1
    low_end = (jnp.where(odd_row, 2, 1), jnp.where(odd_row, 3, 0))
    high_end = (jnp.where(odd_row, 1, 2), jnp.where(odd_row, 0, 3))
    for edge, of in ((far, low_end), (near_edge, high_end)):
        at = 0
        for held in (ks, cks):
            count, end = held.shape[1], held.shape[2] - SUB
            for n in of:
                for x in range(count):
                    edge[at : at + end - SUB, :] = held[n, x, SUB:end, :]
                    at += end - SUB
            for x in range(count):
                edge[at + x : at + x + 1, :] = held[of[1], x, SUB - 1 : SUB, :]
                edge[at + count + x : at + count + x + 1, :] = held[of[1], x, end : end + 1, :]
            at += SUB


def halo_row(h, cells):
    return SUB - 2 + h if h < 2 else SUB + cells + h - 2


def source_kernel(planes, pairs, x, out, lo, hi, left, right, held, summed):
    cells = x.shape[0] // planes
    length = x.shape[1]
    half, fourth = cells // 2, cells // 4
    held[...] = dot(x[...], pairs[...])
    for n in range(planes // 2):
        top = 2 * n * cells
        for at in range(0, out.shape[1], LANE):
            lanes = slice(at, at + LANE)
            summed[...] = held[top : top + cells, lanes] + held[top + cells : top + 2 * cells, lanes]
            out[n * half : (n + 1) * half, lanes] = (
                summed[pl.ds(0, half, stride=2), :] + summed[pl.ds(1, half, stride=2), :]
            )
    for edge, plane in ((lo, 0), (hi, planes - 1)):
        edge[:cells, :] = x[plane * cells : (plane + 1) * cells, :].astype(jnp.float32)
        at = plane // 2 * half
        edge[cells:, : length // 2] = out[at : at + fourth, :]
        edge[cells:, length // 2 :] = out[at + fourth : at + half, :]
    for edge, row in ((left, 0), (right, cells - 1)):
        edge[...] = jnp.zeros_like(edge)
        for n in range(planes):
            at = n * cells + (row // SUB * SUB)
            edge[n : n + 1, :] = x[at : at + SUB, :].astype(jnp.float32)[row % SUB : row % SUB + 1]
        for n in range(planes // 2):
            at = n * half + row // 2
            edge[SUB + n : SUB + n + 1, : length // 2] = out[at : at + 1, :]


def beside(parts, ends):
    lane = lax.broadcasted_iota(jnp.int32, parts[0].shape, 1)
    ahead = [pltpu.roll(x, 1, 1) for x in parts]
    behind = [pltpu.roll(x, LANE - 1, 1) for x in parts]
    sums = []
    for i in range(len(parts)):
        left = jnp.where(lane == 0, ahead[i - 1] if i else ends[0], ahead[i])
        right = jnp.where(
            lane == LANE - 1, behind[i + 1] if i + 1 < len(parts) else ends[1], behind[i]
        )
        sums.append(left + right)
    return sums


def first_sweep(tiles, ext, mid, lower, upper, f, store):
    for top in range(0, ext, SUB):
        end = top + SUB
        parts = [mid(x, top, end) for x in range(tiles)]
        for x, both in enumerate(beside(parts, (parts[0], parts[-1]))):
            k = parts[x]
            above = pltpu.roll(k, 1, 0) if top == 0 else mid(x, top - 1, end - 1)
            below = pltpu.roll(k, SUB - 1, 0) if end == ext else mid(x, top + 1, end + 1)
            total = (lower(x, top, end) + upper(x, top, end)) + (above + below) + both
            scale = JACOBI_WEIGHT / (6.0 * k + total)
            u = f(x, top, end) * (2.0 * scale)
            store(x, top, end, u, k * u, scale)


def second_sweep(tiles, ext, k, u, w, r, store):
    for top in range(SUB, ext - SUB, SUB):
        end = top + SUB
        sums = []
        for lower, mid, upper in (u, w):
            parts = [mid(x, top, end) for x in range(tiles)]
            sums.append(
                [
                    both
                    + (lower(x, top, end) + upper(x, top, end))
                    + (mid(x, top - 1, end - 1) + mid(x, top + 1, end + 1))
                    for x, both in enumerate(beside(parts, (0.0, 0.0)))
                ]
            )
        for x in range(tiles):
            coupled = k(x, top, end) * sums[0][x] + sums[1][x]
            value = (2.0 - JACOBI_WEIGHT) * u[1](x, top, end) + r(x, top, end) * coupled
            store(x, top, end, value)


def around(tiles, ext, mid, beyond, store):
    for top in range(0, ext, SUB):
        end = top + SUB
        parts = [mid(x, top, end) for x in range(tiles)]
        for x, both in enumerate(beside(parts, (parts[0], parts[-1]))):
            k = parts[x]
            above = pltpu.roll(k, 1, 0) if top == 0 else mid(x, top - 1, end - 1)
            below = pltpu.roll(k, SUB - 1, 0) if end == ext else mid(x, top + 1, end + 1)
            store(x, top, end, (6.0 * k + beyond(x, top, end)) + (above + below) + both)


def plane_of(held, *at):
    return lambda x, top, end: held[(*at, x, slice(top, end), slice(None))]


def put_rows(held, to, at, rows):
    for x in range(held.shape[1]):
        held[to, x, at : at + rows.shape[0], :] = rows[:, x * LANE : (x + 1) * LANE]


def repeat_sides(flags, held, at):
    end = held.shape[-2] - SUB

    @pl.when(flags[2] == 1)
    def _():
        for p in at:
            held[(*p, slice(None), slice(SUB - 1, SUB))] = held[(*p, slice(None), slice(SUB, SUB + 1))]

    @pl.when(flags[3] == 1)
    def _():
        for p in at:
            held[(*p, slice(None), slice(end, end + 1))] = held[
                (*p, slice(None), slice(end - 1, end))
            ]


def put_block(fine, held, to, source, row, cells, length):
    if fine:
        put_rows(held, to, SUB, source[row : row + cells, :])
    else:
        half = cells // 2
        put_rows(held, to, SUB, source[row : row + half, :length])
        put_rows(held, to, SUB + half, source[row : row + half, length:])


def layout_kernel(sizes, *rest):
    away, outs, near, sems = rest[:6], rest[6:10], rest[10:16], rest[16]
    for copy in load(list(zip(away, near)), sems):
        copy.wait()
    source, coarse_source, *edges = near
    sides = edges[2:]
    for fine, inner, outer in ((True, *outs[:2]), (False, *outs[2:])):
        planes, cells, length = sizes if fine else [n // 2 for n in sizes]
        f = source if fine else coarse_source
        source_row = 0 if fine else SUB

        def plane(held, to, p):
            put_rows(held, to, SUB, f[p].astype(jnp.float32))
            for side, row in zip(sides, (SUB - 1, SUB + cells)):
                at = source_row + p
                put_rows(held, to, row, side[at : at + 1, :length])

        for p in range(1, planes - 1):
            plane(inner, p - 1, p)
        for group, p in enumerate((0, planes - 1)):
            row = 0 if fine else 2 * cells
            put_block(fine, outer.at[group], 0, edges[group], row, cells, length)
            plane(outer.at[group], 1, p)


def inner_level(sizes, ks, fs, us, ws, rs):
    planes, _, length = sizes
    tiles, ext = ks.shape[1:3]

    def first(p, carry):
        def store(x, top, end, u, w, r):
            at = (p - 1, x, slice(top, end))
            us[at], ws[at], rs[at] = u, w, r

        near = [plane_of(ks, p + i) for i in (0, -1, 1)]
        first_sweep(tiles, ext, *near, plane_of(fs, p - 1), store)
        return carry

    lax.fori_loop(1, planes - 1, first, 0)


def prepare(ks, us, ws, rs, sums, ready):
    planes, tiles, ext, _ = ks.shape

    def end_of(group, carry):
        inwards = lambda i, count: jnp.where(group == 0, i, count - 1 - i)

        def store_sum(x, top, end, value):
            sums[group, x, top:end, :] = value

        own = [plane_of(ks, inwards(i, planes)) for i in range(2)]
        around(tiles, ext, *own, store_sum)

        def store(x, top, end, value):
            ready[group, x, top:end, :] = value

        nothing = lambda x, top, end: 0.0
        u, w = (
            [nothing] + [plane_of(held, inwards(i, planes - 2)) for i in range(2)]
            for held in (us, ws)
        )
        scale = plane_of(rs, inwards(0, planes - 2))
        second_sweep(tiles, ext, own[1], u, w, scale, store)
        return carry

    lax.fori_loop(0, 2, end_of, 0)


def inner_kernel(sizes, shares, flags, b, eh_hbm, el_hbm, edges, cks, cols, fs, cfs, *rest):
    out_hbm, us, ws, rs, cus, cws, crs, sums, ready, csums, cready, *rest = rest
    ks, eh, el, lh, ll, out, sems = rest
    planes, cells, length = sizes
    tiles, ext = ks.shape[1:3]
    copies = load([(eh_hbm, eh), (el_hbm, el)], sems)
    middle = range(2, planes - 2)
    gather_modes(b, middle, shares, lh, ll)
    for i, p in enumerate((0, 1, planes - 2, planes - 1)):
        ks[p] = edges[i]
    for h in range(HALO):
        for p in middle:
            at = h * planes + p
            put_rows(ks, p, halo_row(h, cells), cols[at : at + 1, :])
    for copy in copies:
        copy.wait()
    for p in range(2, planes - 2, 2):
        inverse_pair(p - 2, lh, ll, eh, el, ks, p, cells)
    repeat_sides(flags, ks, [(p,) for p in middle])
    inner_level(sizes, ks, fs, us, ws, rs)

    def second(p, carry):
        def store(x, top, end, value):
            out[p - 2, top - SUB : end - SUB, x * LANE : (x + 1) * LANE] = value

        u, w = ([plane_of(held, p - 1 + i) for i in (-1, 0, 1)] for held in (us, ws))
        second_sweep(tiles, ext, plane_of(ks, p), u, w, plane_of(rs, p - 1), store)
        return carry

    lax.fori_loop(2, planes - 2, second, 0)
    copies = send([(out, out_hbm.at[2 : planes - 2])], sems, 0)
    prepare(ks, us, ws, rs, sums, ready)
    inner_level([n // 2 for n in sizes], cks, cfs, cus, cws, crs)
    prepare(cks, cus, cws, crs, csums, cready)
    for copy in copies:
        copy.wait()


def outer_kernel(sizes, flags, *rest):
    kept, coarse_kept, (k_far, k_near, _, out, coarse_out), rest = (
        rest[:7],
        rest[7:14],
        rest[14:19],
        rest[19:],
    )
    scratch = (rest[:6], rest[6:])
    levels = (sizes, tuple(n // 2 for n in sizes))
    start = 0
    sent = []
    for size, held, given, target in zip(
        levels, scratch, (kept, coarse_kept), (out, coarse_out)
    ):
        planes = size[0]
        ks, fs, inner_us, inner_ws, inner_rs, sums, ready = given
        halo, us, ws, rs, done, sems = held
        tiles, ext = ks.shape[1:3]
        rows = size[1]
        for group, edge in ((flags[4], k_far), (1 - flags[4], k_near)):
            at = start
            for place in range(2 * tiles):
                to = place * ext + SUB
                halo[group, to : to + rows, :] = edge[at : at + rows, :]
                at += rows
            for x in range(tiles):
                to = (tiles + x) * ext
                halo[group, to + SUB - 1 : to + SUB, :] = edge[at + x : at + x + 1, :]
                to += SUB + rows
                halo[group, to : to + 1, :] = edge[at + tiles + x : at + tiles + x + 1, :]
        start = at + SUB
        for group in range(2):

            @pl.when(flags[group] == 1)
            def _():
                for x in range(tiles):
                    at = (tiles + x) * ext
                    halo[group, at : at + ext, :] = ks[3 * group, x]

        def both_ends(group, carry):
            def halo_plane(slot):
                def get(x, top, end):
                    at = (slot * tiles + x) * ext
                    return halo[group, at + top : at + end, :]

                return get

            inwards = lambda i, count: jnp.where(group == 0, i, count - 1 - i)
            own = [plane_of(ks, inwards(i, 4)) for i in range(2)]
            def store_outer(x, top, end, u, w, r):
                at = (group, 0, x, slice(top, end))
                us[at], ws[at] = u, w

            beyond = halo_plane(1)
            first_sweep(
                tiles, ext, beyond, halo_plane(0), own[0], plane_of(fs, group, 0), store_outer
            )
            for top in range(0, ext, SUB):
                for x in range(tiles):
                    at = (x, slice(top, top + SUB))
                    near_sum = sums[(group, *at)] + beyond(x, top, top + SUB)
                    scale = JACOBI_WEIGHT / near_sum
                    u = fs[(group, 1, *at)] * (2.0 * scale)
                    us[(group, 1, *at)] = u
                    ws[(group, 1, *at)] = own[0](x, top, top + SUB) * u
                    rs[(group, *at)] = scale
            u, w = (
                [plane_of(new, group, i) for i in range(2)]
                + [plane_of(old, inwards(0, planes - 2))]
                for new, old in ((us, inner_us), (ws, inner_ws))
            )

            def store(x, top, end, value):
                done[group, 0, top - SUB : end - SUB, x * LANE : (x + 1) * LANE] = value

            second_sweep(tiles, ext, own[0], u, w, plane_of(rs, group), store)
            scale = plane_of(inner_rs, inwards(0, planes - 2))
            for top in range(SUB, ext - SUB, SUB):
                for x in range(tiles):
                    at = (x, top, top + SUB)
                    coupled = own[1](*at) * u[1](*at) + w[1](*at)
                    value = ready[group, x, top : top + SUB, :] + scale(*at) * coupled
                    done[group, 1, top - SUB : top, x * LANE : (x + 1) * LANE] = value
            for i in range(2):
                pltpu.make_async_copy(
                    done.at[group, i], target.at[inwards(i, planes)], sems.at[2 * group + i]
                ).start()
            return carry

        lax.fori_loop(0, 2, both_ends, 0)
        for group, at in enumerate(((0, 1), (planes - 1, planes - 2))):
            for i, p in enumerate(at):
                sent.append(
                    pltpu.make_async_copy(
                        done.at[group, i], target.at[p], sems.at[2 * group + i]
                    )
                )
    for copy in sent:
        copy.wait()


SMEM = pl.BlockSpec(memory_space=pltpu.SMEM)
VMEM = pl.BlockSpec(memory_space=pltpu.VMEM)
AWAY = pl.BlockSpec(memory_space=pltpu.HBM)
ANY = pl.BlockSpec(memory_space=pl.ANY)


def call(kernel, outs, operands, scratch, flops, specs, limit, out_specs=None, aliases=None):
    many = isinstance(outs, (list, tuple))
    written = outs if many else [outs]
    moved = sum(math.prod(x.shape) * x.dtype.itemsize for x in (*operands, *written))
    operands = [
        pltpu.with_memory_space_constraint(x, pltpu.HBM) if spec is AWAY else x
        for x, spec in zip(operands, specs)
    ]
    out_specs = out_specs or [
        VMEM if isinstance(x, jax.ShapeDtypeStruct) else AWAY for x in written
    ]
    return pl.pallas_call(
        kernel,
        out_shape=outs,
        in_specs=specs,
        out_specs=out_specs if many else out_specs[0],
        scratch_shapes=scratch,
        input_output_aliases=aliases or {},
        compiler_params=pltpu.CompilerParams(vmem_limit_bytes=limit * MIB),
        cost_estimate=pl.CostEstimate(flops=flops, bytes_accessed=moved, transcendentals=0),
    )(*operands)


def f32(*shape):
    return jax.ShapeDtypeStruct(shape, jnp.float32)


def room(*arrays):
    return [pltpu.VMEM(x.shape, x.dtype) for x in arrays]


def chain(axis):
    up = [(i, i + 1) for i in range(lax.axis_size(axis) - 1)]
    return up, [(j, i) for i, j in up]


def swap(lo, hi, axis):
    up, down = chain(axis)
    return lax.ppermute(hi, axis, up), lax.ppermute(lo, axis, down)


def held_planes(size, *count):
    planes, cells, length = size
    return f32(*count, length // LANE, cells + 2 * SUB, LANE)


def outer_scratch(size):
    planes, cells, length = size
    return room(
        f32(2, 2 * (length // LANE) * (cells + 2 * SUB), LANE),
        held_planes(size, 2, 2),
        held_planes(size, 2, 2),
        held_planes(size, 2),
        f32(2, 2, cells, length),
    ) + [pltpu.SemaphoreType.DMA((4,))]


def fused_body(noise, source):
    rows, groups = lax.axis_size("row"), lax.axis_size(PLANE)
    devices = rows * groups
    planes, cells, length = noise.shape
    first, second = planes * rows, cells * groups
    bf16 = jnp.bfloat16
    held = length // 2 // devices
    js = list(range(held))
    low = held // 2
    me = lax.axis_index(EVERY)
    row_at, group_at = lax.axis_index("row"), lax.axis_index(PLANE)
    flags = jnp.stack(
        [
            row_at == 0,
            row_at == rows - 1,
            group_at == 0,
            group_at == groups - 1,
            row_at % 2 == 1,
        ]
    ).astype(jnp.int32)
    norm = FIELD_SCALE * (float(first) * float(second) * float(length)) ** (-0.5)
    flat = (planes * cells, length)

    pieces = 4
    table = [x.reshape(pieces, -1, length) for x in two_parts(forward_third(length, devices, js))]
    table = np.concatenate(table, axis=1)
    shape = (length * SUB, LANE)
    sent = call(
        functools.partial(forward_kernel, planes),
        pltpu.HBM(shape, jnp.float32),
        (table, noise.reshape(flat)),
        room(table)
        + [
            pltpu.VMEM(flat, bf16),
            pltpu.VMEM(shape, jnp.float32),
            pltpu.SemaphoreType.DMA((2 * pieces + planes // 2,)),
        ],
        4 * length * length * planes * cells,
        [AWAY] * 2,
        12,
    )
    sent, source = lax.optimization_barrier((sent, source))
    sent = sent.reshape(devices, 2 * held, SUB, LANE)
    arrived = lax.all_to_all(sent, EVERY, split_axis=0, concat_axis=0, tiled=True)

    pairs = np.zeros((length, length // 2), np.float32)
    pairs[np.arange(length), np.arange(length) // 2] = 0.125
    level = f32(cells + cells // 4, length)
    side = f32(2 * SUB, length)
    coarse_source, *edges = call(
        functools.partial(source_kernel, planes),
        [f32(planes * cells // 4, length // 2), level, level, side, side],
        (pairs.astype(bf16), source.reshape(flat)),
        [
            pltpu.VMEM((planes * cells, length // 2), jnp.float32),
            pltpu.VMEM((cells, LANE), jnp.float32),
        ],
        planes * cells * length * length,
        [VMEM] * 2,
        12,
    )
    coarse_source = coarse_source.reshape(planes // 2, cells // 2, length // 2)
    edges = (*swap(*edges[:2], "row"), *swap(*edges[2:], PLANE))
    arrived, edges, coarse_source = lax.optimization_barrier((arrived, edges, coarse_source))

    constants = (
        two_parts(second_table(second))
        + (
            stacked(forward_first(first)),
            stacked(inverse_first(first)),
            stacked(inverse_first_coarse(first // 2, rows)),
        )
        + two_parts(second_coarse(second // 2, groups))
        + two_parts(second_table(second).transpose(0, 2, 1))
    )
    tiles = 2 * held + low // 2 + 1
    modes = (me + devices * np.array(js)).astype(jnp.float32)
    weight = jnp.where(modes == 0.0, norm, 2.0 * norm).astype(jnp.float32)
    scale = jnp.stack([DECAY * modes * modes, weight], axis=1)
    block = (2, 2 * held * first, second // 2)
    shape = (devices, tiles, SUB, LANE)
    out = call(
        functools.partial(middle_kernel, (first, second, rows, groups, held, low)),
        pltpu.HBM(shape, jnp.float32),
        (scale, arrived, *constants),
        room(*constants)
        + [
            pltpu.VMEM(shape, jnp.float32),
            pltpu.SemaphoreType.DMA((len(constants),)),
            pltpu.VMEM(block, bf16),
            pltpu.VMEM(block, bf16),
            pltpu.VMEM(block, jnp.float32),
            pltpu.VMEM(block, bf16),
            pltpu.VMEM(block, bf16),
            pltpu.VMEM((low // 2 * first, second), bf16),
            pltpu.VMEM((low // 2 * first, second), bf16),
        ],
        6 * 2 * 2 * held * first * second * (second + 2 * first),
        [SMEM, VMEM] + [AWAY] * len(constants),
        22,
    )
    out, source, coarse_source, edges = lax.optimization_barrier(
        (out, source, coarse_source, edges)
    )
    got = lax.all_to_all(out, EVERY, split_axis=0, concat_axis=0, tiled=True)
    size, coarse_size = noise.shape, coarse_source.shape
    sizes = (size, coarse_size)
    sources = (source, coarse_source, *edges)
    laid = call(
        functools.partial(layout_kernel, size),
        [
            held_planes(s, *count)
            for s in sizes
            for count in ((s[0] - 2,), (2, 2))
        ],
        sources,
        room(*sources) + [pltpu.SemaphoreType.DMA((6,))],
        source.size,
        [AWAY] * 6,
        12,
    )
    got, laid = lax.optimization_barrier((got, laid))

    third = inverse_third(length, devices, js)
    constants = (
        two_parts(third)
        + two_parts(third_coarse(length // 2, devices, js[:low]))
        + (lane_order(2 * held, low).astype(bf16),)
        + two_parts(third_coarse_halo(length // 2, devices, js[:low]))
    )
    edge = f32(sum(2 * (s[2] // LANE) * s[1] + SUB for s in sizes), LANE)
    shares = (devices, 2 * held, tiles)
    got = got.reshape(devices * tiles * SUB, LANE)
    ks, coarse_ks, cols, far, near = call(
        functools.partial(edge_kernel, (devices, 2 * held, low, tiles, planes, length)),
        [held_planes(s, 4) for s in sizes] + [f32(HALO * planes, length), edge, edge],
        (flags, got, *constants),
        room(*constants)
        + [pltpu.VMEM((2, 4 * cells, devices * held), bf16)] * 2
        + [pltpu.VMEM((planes // 2 * LANE, devices * low), bf16)] * 2
        + [pltpu.SemaphoreType.DMA((7,))],
        3 * planes * cells * length * length,
        [SMEM, VMEM] + [AWAY] * 7,
        16,
    )
    k_far, k_near = (
        lax.ppermute(
            x, "row", [p for i in range(at, rows - 1, 2) for p in ((i, i + 1), (i + 1, i))]
        )
        for x, at in ((far, 1), (near, 0))
    )
    inner_f, outer_f, coarse_inner_f, coarse_outer_f = laid
    inner, *kept = call(
        functools.partial(inner_kernel, size, shares),
        [pltpu.HBM(size, jnp.float32)]
        + [held_planes(s, s[0] - 2) for s in sizes for _ in range(3)]
        + [held_planes(s, 2) for s in sizes for _ in range(2)],
        (flags, got, *constants[:2], ks, coarse_ks, cols, inner_f, coarse_inner_f),
        room(held_planes(size, planes), *constants[:2])
        + [pltpu.VMEM((2, (planes - 4) * cells, devices * held), bf16)] * 2
        + room(f32(planes - 4, cells, length))
        + [pltpu.SemaphoreType.DMA((2,))],
        3 * planes * cells * length * length,
        [SMEM, VMEM] + [AWAY] * 2 + [VMEM] * 5,
        18,
    )
    return call(
        functools.partial(outer_kernel, size),
        [pltpu.HBM(s, jnp.float32) for s in sizes],
        (
            flags,
            *(ks, outer_f, *kept[:3], *kept[6:8]),
            *(coarse_ks, coarse_outer_f, *kept[3:6], *kept[8:]),
            *(k_far, k_near, inner),
        ),
        outer_scratch(size) + outer_scratch(coarse_size),
        30 * source.size,
        [SMEM] + [VMEM] * 16 + [AWAY],
        18,
        None,
        {17: 0},
    )


NEIGHBOUR_STEPS = ((1, 0, 0), (-1, 0, 0), (0, 1, 0), (0, -1, 0), (0, 0, 1), (0, 0, -1))


def padded(x, sides, width):
    for axis, dim in sides:
        peers, length = (lax.axis_size(axis), x.shape[dim])
        up = [(i, (i + 1) % peers) for i in range(peers - 1)]
        down = [(j, i) for i, j in up]
        last = lax.slice_in_dim(x, length - width, length, axis=dim)
        leading = lax.slice_in_dim(x, 0, width, axis=dim)
        before = lax.ppermute(last, axis, up)
        after = lax.ppermute(leading, axis, down)
        x = jnp.concatenate([before, x, after], axis=dim)
    return x


def signed_modes(index, length):
    return jnp.where(index < length // 2, index, index - length).astype(jnp.float32)


def amplitude(first_modes, second_modes, third_modes, first_edge, second_edge, third_edge):
    squared = first_modes * first_modes + second_modes * second_modes + third_modes * third_modes
    value = FIELD_SCALE / (1.0 + (2.0 * math.pi * CORRELATION) ** 2 * squared)
    edge = (
        (jnp.abs(first_modes) == first_edge)
        | (jnp.abs(second_modes) == second_edge)
        | (jnp.abs(third_modes) == third_edge)
    )
    return jnp.where(edge, 0.0, value)


def phase_table(count_rows, count_cols, modulus, sign):
    left_index = jnp.arange(count_rows, dtype=jnp.int32)[:, None]
    right_index = jnp.arange(count_cols, dtype=jnp.int32)[None, :]
    angle = 2.0 * math.pi / modulus * (left_index * right_index % modulus).astype(jnp.float32)
    return (jnp.cos(angle), sign * jnp.sin(angle))


def split_length(length):
    outer_len = 2 ** ((length.bit_length() - 1) // 2)
    return (outer_len, length // outer_len)


def real_form(form, left_value, right_value):
    return jnp.einsum(form, left_value, right_value, precision=lax.Precision.HIGHEST)


def complex_form(form, left_real, left_imag, right_real, right_imag):
    real_part = real_form(form, left_real, right_real) - real_form(form, left_imag, right_imag)
    imag_part = real_form(form, left_real, right_imag) + real_form(form, left_imag, right_real)
    return (real_part, imag_part)


def merge_pair(values, out_form, first_letter):
    merge_at = out_form.index(first_letter)
    out_dims = list(values.shape)
    merged = (
        out_dims[:merge_at]
        + [out_dims[merge_at] * out_dims[merge_at + 1]]
        + out_dims[merge_at + 2 :]
    )
    return values.reshape(merged)


def forward_axis(real_part, imag_part, lead_form, out_form, kept_modes):
    length = real_part.shape[-1]
    outer_len, inner_len = split_length(length)
    split_shape = real_part.shape[:-1] + (outer_len, inner_len)
    outer_real, outer_imag = phase_table(outer_len, outer_len, outer_len, -1.0)
    twist_real, twist_imag = phase_table(outer_len, inner_len, length, -1.0)
    inner_real, inner_imag = phase_table(inner_len, kept_modes // outer_len, inner_len, -1.0)
    first_form = lead_form + "ab,ai->" + lead_form + "ib"
    split_real = real_part.reshape(split_shape)
    if imag_part is None:
        section_real = real_form(first_form, split_real, outer_real)
        section_imag = real_form(first_form, split_real, outer_imag)
    else:
        section_real, section_imag = complex_form(
            first_form, split_real, imag_part.reshape(split_shape), outer_real, outer_imag
        )
    turned_real = section_real * twist_real - section_imag * twist_imag
    turned_imag = section_real * twist_imag + section_imag * twist_real
    result_real, result_imag = complex_form(
        lead_form + "ib,bj->" + out_form, turned_real, turned_imag, inner_real, inner_imag
    )
    return (merge_pair(result_real, out_form, "j"), merge_pair(result_imag, out_form, "j"))


def inverse_axis(real_part, imag_part, length, lead_form, out_form, real_only):
    kept_modes = real_part.shape[-1]
    outer_len, inner_len = split_length(length)
    split_shape = real_part.shape[:-1] + (kept_modes // outer_len, outer_len)
    inner_real, inner_imag = phase_table(kept_modes // outer_len, inner_len, inner_len, 1.0)
    twist_real, twist_imag = phase_table(outer_len, inner_len, length, 1.0)
    outer_real, outer_imag = phase_table(outer_len, outer_len, outer_len, 1.0)
    section_real, section_imag = complex_form(
        lead_form + "ji,jb->" + lead_form + "ib",
        real_part.reshape(split_shape),
        imag_part.reshape(split_shape),
        inner_real,
        inner_imag,
    )
    turned_real = section_real * twist_real - section_imag * twist_imag
    turned_imag = section_real * twist_imag + section_imag * twist_real
    second_form = lead_form + "ib,ia->" + out_form
    if real_only:
        result = real_form(second_form, turned_real, outer_real) - real_form(
            second_form, turned_imag, outer_imag
        )
        return merge_pair(result, out_form, "a")
    result_real, result_imag = complex_form(
        second_form, turned_real, turned_imag, outer_real, outer_imag
    )
    return (merge_pair(result_real, out_form, "a"), merge_pair(result_imag, out_form, "a"))


def low_band(values, half_coarse, fine_len):
    return jnp.concatenate(
        [values[:, :, :half_coarse], values[:, :, fine_len - half_coarse :]], axis=2
    )


def window(values, margin, offset):
    return values[
        margin + offset[0] : values.shape[0] - margin + offset[0],
        margin + offset[1] : values.shape[1] - margin + offset[1],
        margin + offset[2] : values.shape[2] - margin + offset[2],
    ]


def face_weight(center, beside):
    return jnp.where(beside > 0.0, 0.5 * (center + beside), center)


def smooth_twice(kappa, source):
    no_shift = (0, 0, 0)
    center = window(kappa, 1, no_shift)
    faces = [face_weight(center, window(kappa, 1, offset)) for offset in NEIGHBOUR_STEPS]
    diagonal = faces[0] + faces[1] + faces[2] + faces[3] + faces[4] + faces[5]
    guarded = jnp.where(center > 0.0, diagonal, 1.0)
    first_sweep = JACOBI_WEIGHT * window(source, 1, no_shift) / guarded
    inner_first = window(first_sweep, 1, no_shift)
    inner_diagonal = window(diagonal, 1, no_shift)
    coupled = jnp.zeros_like(inner_first)
    for face_value, offset in zip(faces, NEIGHBOUR_STEPS):
        coupled = coupled + window(face_value, 1, no_shift) * window(first_sweep, 1, offset)
    residual = window(source, 2, no_shift) - inner_diagonal * inner_first + coupled
    return inner_first + JACOBI_WEIGHT * residual / inner_diagonal


def pad_depth(values):
    return jnp.pad(values, ((0, 0), (0, 0), (2, 2)))


def plain_body(noise, source):
    row_at = lax.axis_index("row")
    group_at = lax.axis_index(("level", "col"))
    fine_field = noise.astype(jnp.float32)
    fine_len = fine_field.shape[-1]
    coarse_len = fine_len // 2
    half_coarse = coarse_len // 2
    kept_modes = fine_len // 2
    real_part, imag_part = forward_axis(fine_field, None, "pq", "pjiq", kept_modes)
    real_part, imag_part = (
        lax.all_to_all(real_part, ("level", "col"), split_axis=1, concat_axis=2, tiled=True),
        lax.all_to_all(imag_part, ("level", "col"), split_axis=1, concat_axis=2, tiled=True),
    )
    real_part, imag_part = forward_axis(real_part, imag_part, "pq", "jiqp", fine_len)
    real_part, imag_part = (
        lax.all_to_all(real_part, "row", split_axis=0, concat_axis=2, tiled=True),
        lax.all_to_all(imag_part, "row", split_axis=0, concat_axis=2, tiled=True),
    )
    slab_len = real_part.shape[-1]
    coarse_slab = slab_len // 2
    half_slab = coarse_slab // 2
    real_part, imag_part = forward_axis(real_part, imag_part, "pq", "pqji", slab_len)
    second_count = real_part.shape[0]
    third_count = real_part.shape[1]
    wave_second = signed_modes(
        row_at * second_count + jnp.arange(second_count, dtype=jnp.int32), fine_len
    )[:, None, None]
    third_index = group_at * third_count + jnp.arange(third_count, dtype=jnp.int32)
    wave_third = signed_modes(third_index, fine_len)[None, :, None]
    spread = 2.0
    mirror_weight = jnp.where(third_index == 0, 1.0, spread).astype(jnp.float32)[None, :, None]
    norm_factor = (float(slab_len) * float(fine_len) * float(fine_len)) ** (-0.5)
    wave_first = signed_modes(jnp.arange(slab_len, dtype=jnp.int32), slab_len)[None, None, :]
    fine_scale = (
        amplitude(
            wave_second, wave_third, wave_first, fine_len / 2.0, fine_len / 2.0, slab_len / 2.0
        )
        * mirror_weight
        * norm_factor
    )
    coarse_first = signed_modes(jnp.arange(coarse_slab, dtype=jnp.int32), coarse_slab)[
        None, None, :
    ]
    coarse_scale = (
        amplitude(
            wave_second,
            wave_third,
            coarse_first,
            coarse_len / 2.0,
            coarse_len / 2.0,
            coarse_slab / 2.0,
        )
        * mirror_weight
        * norm_factor
    )
    coarse_real = low_band(real_part, half_slab, slab_len) * coarse_scale
    coarse_imag = low_band(imag_part, half_slab, slab_len) * coarse_scale
    fine_real, fine_imag = inverse_axis(
        real_part * fine_scale, imag_part * fine_scale, slab_len, "pq", "abqp", False
    )
    coarse_real, coarse_imag = inverse_axis(
        coarse_real, coarse_imag, coarse_slab, "pq", "abqp", False
    )
    fine_real, fine_imag, coarse_real, coarse_imag = (
        lax.all_to_all(fine_real, "row", split_axis=0, concat_axis=2, tiled=True),
        lax.all_to_all(fine_imag, "row", split_axis=0, concat_axis=2, tiled=True),
        lax.all_to_all(coarse_real, "row", split_axis=0, concat_axis=2, tiled=True),
        lax.all_to_all(coarse_imag, "row", split_axis=0, concat_axis=2, tiled=True),
    )
    coarse_real = low_band(coarse_real, half_coarse, fine_len)
    coarse_imag = low_band(coarse_imag, half_coarse, fine_len)
    fine_real, fine_imag = inverse_axis(fine_real, fine_imag, fine_len, "pq", "pabq", False)
    coarse_real, coarse_imag = inverse_axis(
        coarse_real, coarse_imag, coarse_len, "pq", "pabq", False
    )
    fine_real, fine_imag, coarse_real, coarse_imag = (
        lax.all_to_all(fine_real, ("level", "col"), split_axis=1, concat_axis=2, tiled=True),
        lax.all_to_all(fine_imag, ("level", "col"), split_axis=1, concat_axis=2, tiled=True),
        lax.all_to_all(coarse_real, ("level", "col"), split_axis=1, concat_axis=2, tiled=True),
        lax.all_to_all(coarse_imag, ("level", "col"), split_axis=1, concat_axis=2, tiled=True),
    )
    coarse_real = coarse_real[:, :, :half_coarse]
    coarse_imag = coarse_imag[:, :, :half_coarse]
    fine_log = inverse_axis(fine_real, fine_imag, fine_len, "pq", "pqab", True)
    coarse_log = inverse_axis(coarse_real, coarse_imag, coarse_len, "pq", "pqab", True)
    fine_kappa = jnp.exp(fine_log)
    coarse_kappa = jnp.exp(coarse_log)
    fine_source = source.astype(jnp.float32)
    coarse_rows = coarse_log.shape[0]
    coarse_cols = coarse_log.shape[1]
    coarse_source = fine_source.reshape(coarse_rows, 2, coarse_cols, 2, coarse_len, 2).mean(
        axis=(1, 3, 5)
    )
    fine_kappa, fine_source, coarse_kappa, coarse_source = (
        padded(fine_kappa, (("row", 0), (("level", "col"), 1)), 2),
        padded(fine_source, (("row", 0), (("level", "col"), 1)), 2),
        padded(coarse_kappa, (("row", 0), (("level", "col"), 1)), 2),
        padded(coarse_source, (("row", 0), (("level", "col"), 1)), 2),
    )
    fine_pressure = smooth_twice(pad_depth(fine_kappa), pad_depth(fine_source))
    coarse_pressure = smooth_twice(pad_depth(coarse_kappa), pad_depth(coarse_source))
    return (fine_pressure, coarse_pressure)


def body(noise, source):
    planes, cells, length = noise.shape
    rows, groups = lax.axis_size("row"), lax.axis_size(PLANE)
    modes = length // 2 // (rows * groups)
    fills = planes == SUB and cells == LANE and 2 * HALO * modes == LANE // 2
    if fills and length % (4 * LANE) == 0 and rows % 2 == 0 and groups % 4 == 0:
        return fused_body(noise, source)
    return plain_body(noise, source)


def solution(mesh):
    return jax.shard_map(
        body,
        mesh=mesh,
        in_specs=(P("row", ("level", "col"), None), P("row", ("level", "col"), None)),
        out_specs=(P("row", ("level", "col"), None), P("row", ("level", "col"), None)),
        check_vma=False,
    )
```

```python
import functools
import math

import jax
import jax.numpy as jnp
import numpy as np
from jax import lax
from jax.experimental import pallas as pl
from jax.experimental.pallas import tpu as pltpu
from jax.sharding import PartitionSpec as P

JACOBI_WEIGHT = 2.0 / 3.0
CORRELATION = 0.2
FIELD_SCALE = 0.3
DECAY = (2.0 * math.pi * CORRELATION) ** 2
EVERY = ("row", "level", "col")
PLANE = ("level", "col")
MIB = 1 << 20
SUB, LANE = 8, 128
HALO = 4


def two_parts(matrix):
    high = matrix.astype(jnp.bfloat16)
    low = (matrix - high.astype(np.float64)).astype(jnp.bfloat16)
    return high, low


def angles(rows, cols, length):
    return 2.0 * np.pi * (np.outer(rows, cols) % length) / length


def third_modes(devices, js):
    return np.array([[d + devices * j for j in js] for d in range(devices)])


def forward_third(length, devices, js):
    theta = angles(third_modes(devices, js).reshape(-1), np.arange(length), length)
    return np.stack([np.cos(theta), -np.sin(theta)], axis=1).reshape(-1, length)


def inverse_third(length, devices, js):
    modes = third_modes(devices, js).reshape(devices // 2, 2, len(js)).transpose(1, 0, 2)
    theta = 2.0 * np.pi * (modes[..., None] * np.arange(length // 2) % length) / length
    both = np.stack([np.cos(theta), -np.sin(theta)], axis=3)
    return both.reshape(2, -1, length // 2)


def second_modes(length):
    return np.arange(length // 2).reshape(-1, 2).T


def second_table(length):
    theta = second_modes(length)[:, None, :] * np.arange(length // 2)[None, :, None]
    theta = 2.0 * np.pi * (theta % length) / length
    return np.concatenate([np.cos(theta), np.sin(theta)], axis=2)


def forward_first(length):
    theta = angles(np.arange(length), np.arange(length), length)
    cos, sin = np.cos(theta), np.sin(theta)
    return np.block([[cos, sin], [-sin, cos]])


def inverse_first(length):
    theta = angles(np.arange(length), np.arange(length), length)
    cos, sin = np.cos(theta), np.sin(theta)
    cos[:, length // 2] = 0.0
    sin[:, length // 2] = 0.0
    return np.block([[cos, -sin], [sin, cos]])


def inverse_first_coarse(length, rows):
    full = inverse_first(length)
    value = full.reshape(2, rows, length // rows, 2 * length)
    turned = np.concatenate([-full[length:], full[:length]]).reshape(value.shape)
    order = lambda x: x.transpose(1, 0, 2, 3).reshape(2 * length, 2 * length)
    return np.concatenate([order(value), order(turned)])


def second_coarse(length, groups):
    theta = angles(second_modes(length).reshape(-1), np.arange(length), length)
    table = np.concatenate([np.cos(theta), np.sin(theta)])
    span = length // groups
    out = np.zeros((2, length, groups, 2, span))
    for pair in range(2):
        out[pair, :, :, pair, :] = table.reshape(length, groups, span)
    return out.reshape(2 * length, 2 * length)


def third_coarse(length, devices, js):
    modes = third_modes(devices, js).reshape(devices, len(js) // 2, 2)
    theta = 2.0 * np.pi * (modes[..., None] * np.arange(length) % length) / length
    both = np.stack([np.cos(theta), -np.sin(theta)])
    return both.transpose(0, 2, 1, 3, 4).reshape(2 * (len(js) // 2) * devices, 2 * length)


def third_coarse_halo(length, devices, js):
    theta = angles(third_modes(devices, js).reshape(-1), np.arange(length), length)
    return np.concatenate([np.cos(theta), -np.sin(theta)], axis=1)


def lane_order(parts, coarse_parts):
    out = np.zeros((LANE, LANE))
    for h in range(HALO):
        for q in range(parts):
            out[HALO * q + h, parts * h + q] = 1.0
        for j in range(coarse_parts):
            out[LANE // 2 + HALO * j + h, LANE // 2 + coarse_parts * h + j] = 1.0
    return out


def split(x):
    high = x.astype(jnp.bfloat16)
    return high, (x - high.astype(jnp.float32)).astype(jnp.bfloat16)


def dot(a, b):
    return lax.dot_general(a, b, (((1,), (0,)), ((), ())), preferred_element_type=jnp.float32)


def dot_t(a, b):
    return lax.dot_general(a, b, (((1,), (1,)), ((), ())), preferred_element_type=jnp.float32)


def stacked(matrix):
    high, low = two_parts(matrix)
    return np.block([[high, high], [low, np.zeros_like(low)]])


def dot_left(stack, x):
    value = dot(stack, jnp.concatenate(split(x), axis=0))
    rows = stack.shape[0] // 2
    return value[:rows] + value[rows:]


def dot3(a, b):
    (ah, al), (bh, bl) = a, b
    return dot(ah, bh) + (dot(ah, bl) + dot(al, bh))


def load(pairs, sems):
    copies = [pltpu.make_async_copy(a, b, sems.at[i]) for i, (a, b) in enumerate(pairs)]
    for copy in copies:
        copy.start()
    return copies


def send(pairs, sems, first):
    copies = [pltpu.make_async_copy(a, b, sems.at[first + i]) for i, (a, b) in enumerate(pairs)]
    for copy in copies:
        copy.start()
    return copies


def forward_kernel(planes, d_hbm, x_hbm, out_hbm, d, x, out, sems):
    pieces, rows = d.shape[0], d.shape[1] // 2
    parts = [slice(p * LANE, (p + 2) * LANE) for p in range(0, planes, 2)]
    pairs = [(x_hbm.at[at, :], x.at[at, :]) for at in parts]
    copies = load([(d_hbm.at[0], d.at[0])] + pairs + [(d_hbm.at[i], d.at[i]) for i in range(1, pieces)], sems)
    sent = []
    copies[0].wait()
    for piece in range(pieces):
        if piece:
            copies[len(parts) + piece].wait()
        for i, at in enumerate(parts):
            if piece == 0:
                copies[i + 1].wait()
            value = dot_t(d[piece], x[at, :])
            value = value[:rows] + value[rows:]
            for h in range(2):
                out[pl.ds(piece * rows * SUB + 2 * i + h, rows, stride=SUB), :] = value[
                    :, h * LANE : (h + 1) * LANE
                ]
        tall = slice(piece * rows * SUB, (piece + 1) * rows * SUB)
        sent += send([(out.at[tall, :], out_hbm.at[tall, :])], sems, len(copies) + piece)
    for copy in sent:
        copy.wait()


def middle_kernel(sizes, scale, b, *rest):
    (first, second, rows, groups, js, low) = sizes
    count = 9
    away, out_hbm, near, rest = (
        rest[:count],
        rest[count],
        rest[count + 1 : 2 * count + 1],
        rest[2 * count + 1 :],
    )
    out, sems, zh, zl, y, oh, ol, qh, ql = rest
    copies = load(list(zip(away, near))[:5], sems)
    csh, csl, forward, inverse, coarse_inverse, cch, ccl, ch, cl = near
    q_count = 2 * js
    half, quarter = second // 2, second // 4
    for q in range(q_count):
        for g in range(groups // 2):
            for r in range(0, rows, 2):
                at = r * groups + g
                near_half = jnp.concatenate([b[at, q], b[at + groups, q]], axis=0)
                at += groups // 2
                far_half = jnp.concatenate([b[at, q], b[at + groups, q]], axis=0)
                at = slice(q * first + r * SUB, q * first + (r + 2) * SUB)
                lanes = slice(g * LANE, (g + 1) * LANE)
                zh[0, at, lanes], zl[0, at, lanes] = split(near_half + far_half)
                zh[1, at, lanes], zl[1, at, lanes] = split(near_half - far_half)
    for copy in copies:
        copy.wait()
    copies = send(list(zip(away, near))[5:], sems, 5)
    wide = 16 * first
    for top in range(0, q_count * first, wide):
        at = slice(top, top + wide)
        for parity in range(2):
            y[parity, at, :] = dot3(
                (zh[parity, at, :], zl[parity, at, :]), (csh[parity], csl[parity])
            )
    mode0 = lax.broadcasted_iota(jnp.int32, (first, second), 0)
    mode0 = jnp.where(mode0 < first // 2, mode0, mode0 - first).astype(jnp.float32)
    lane = lax.broadcasted_iota(jnp.int32, (first, second), 1)
    mode1 = jnp.where(lane < half, lane, lane - half)
    mode1 = jnp.where(mode1 < quarter, 2 * mode1, 2 * (mode1 - quarter) + 1).astype(jnp.float32)
    base = 1.0 + DECAY * (mode0 * mode0 + mode1 * mode1)
    for j in range(js):
        top = j * 2 * first
        re, im = slice(top, top + first), slice(top + first, top + 2 * first)
        cos, sin = slice(0, quarter), slice(quarter, half)
        whole = lambda part, lanes: jnp.concatenate(
            [y[0, part, lanes], y[1, part, lanes]], axis=1
        )
        rc, rs, ic, isn = whole(re, cos), whole(re, sin), whole(im, cos), whole(im, sin)
        wave = jnp.concatenate(
            [
                jnp.concatenate([rc + isn, rc - isn], axis=1),
                jnp.concatenate([ic - rs, ic + rs], axis=1),
            ],
            axis=0,
        )
        spectrum = dot_left(forward[...], wave)
        amp = jnp.where(lane == half, 0.0, scale[j, 1] / (base + scale[j, 0]))
        scaled = spectrum * jnp.concatenate([amp, amp], axis=0)
        field = dot_left(inverse[...], scaled)
        plus, minus = field[:, :half], field[:, half:]
        even, odd = plus + minus, plus - minus
        odd = jnp.concatenate([-odd[first:], odd[:first]], axis=0)
        at = slice(top, top + 2 * first)
        for parity, lanes in enumerate((cos, sin)):
            operand = jnp.concatenate([even[:, lanes], odd[:, lanes]], axis=1)
            oh[parity, at, :], ol[parity, at, :] = split(operand)
        if j < low:
            keep = first // 4
            kept = [
                scaled[at : at + keep, :]
                for at in (0, first - keep, first, 2 * first - keep)
            ]
            band = jnp.concatenate(kept, axis=0)
            low_lane = lax.broadcasted_iota(jnp.int32, (first, quarter), 1) < quarter // 2
            pieces = []
            for at in (0, half):
                upper = pltpu.roll(band[:, at + quarter : at + half], quarter // 2, 1)
                pieces.append(jnp.where(low_lane, band[:, at : at + quarter], upper))
            band = jnp.concatenate(pieces, axis=1)
            field = dot_left(coarse_inverse[...], band)
            value, turned = field[:first], field[first:]
            operand = jnp.concatenate(
                [
                    value[:, :quarter] + value[:, quarter:],
                    turned[:, :quarter] - turned[:, quarter:],
                ],
                axis=1,
            )
            at = slice(j // 2 * first, (j // 2 + 1) * first)
            lanes = slice(j % 2 * half, (j % 2 + 1) * half)
            qh[at, lanes], ql[at, lanes] = split(operand)
    for copy in copies:
        copy.wait()
    copies = []
    wide = 4 * first
    lane = lax.broadcasted_iota(jnp.int32, (SUB, LANE), 1)
    extra = q_count + low // 2

    def leave(start, stop):
        at = slice(start, stop)
        copies.extend(send([(out.at[:, at], out_hbm.at[:, at])], sems, len(copies)))

    def give(value, start):
        tiles = value.shape[0] // first
        for q in range(tiles):
            for r in range(rows):
                for g in range(groups):
                    at = q * first + r * SUB
                    out[r * groups + g, start + q] = value[
                        at : at + SUB, g * LANE : (g + 1) * LANE
                    ]
        leave(start, start + tiles)

    def halo_columns(value, start, held):
        tiles = value.shape[0] // first
        for r in range(rows):
            for g in range(groups):
                total = held[r, g]
                left = max(g - 1, 0) * LANE
                right = min(g + 1, groups - 1) * LANE
                for q in range(tiles):
                    at = slice(q * first + r * SUB, q * first + (r + 1) * SUB)
                    both = jnp.where(
                        lane < LANE // 2,
                        value[at, right : right + LANE],
                        value[at, left : left + LANE],
                    )
                    to = HALO * (start + q)
                    both = pltpu.roll(both, (to + 2) % LANE, 1)
                    total = jnp.where((lane >= to) & (lane < to + HALO), both, total)
                held[r, g] = total

    def coarse_columns(value, held):
        half_lane = LANE // 2
        for j in range(low):
            for r in range(rows):
                at = slice(j // 2 * first + r * SUB, j // 2 * first + (r + 1) * SUB)
                shift = HALO * j + 2 - j % 2 * half_lane
                to = half_lane + HALO * j
                for g in range(groups):
                    left = max(g - 1, 0) * LANE
                    right = min(g + 1, groups - 1) * LANE
                    left = pltpu.roll(value[at, left : left + LANE], shift % LANE, 1)
                    right = pltpu.roll(
                        value[at, right : right + LANE], (shift + half_lane) % LANE, 1
                    )
                    total = jnp.where((lane >= to) & (lane < to + 2), left, held[r, g])
                    held[r, g] = jnp.where(
                        (lane >= to + 2) & (lane < to + HALO), right, total
                    )

    columns = {
        (r, g): jnp.zeros((SUB, LANE), jnp.float32) for r in range(rows) for g in range(groups)
    }
    coarse = dot3((qh[...], ql[...]), (cch[...], ccl[...]))
    give(coarse, q_count)
    coarse_columns(coarse, columns)
    for top in range(0, q_count * first, wide):
        at = slice(top, top + wide)
        even, odd = (
            dot3((oh[parity, at, :], ol[parity, at, :]), (ch[parity], cl[parity]))
            for parity in range(2)
        )
        value = jnp.concatenate([even + odd, even - odd], axis=1)
        give(value, top // first)
        halo_columns(value, top // first, columns)
    for (r, g), total in columns.items():
        out[r * groups + g, extra] = total
    leave(extra, extra + 1)
    for copy in copies:
        copy.wait()


def gather_modes(b, at, sizes, lh, ll):
    devices, q_count, tiles = sizes
    for i, n in enumerate(at):
        for parity in range(2):
            rows = jnp.concatenate(
                [
                    b[pl.ds(s * tiles * SUB + n, q_count, stride=SUB), :]
                    for s in range(parity, devices, 2)
                ],
                axis=0,
            )
            to = slice(i * LANE, (i + 1) * LANE)
            lh[parity, to, :], ll[parity, to, :] = split(jnp.transpose(rows))


def inverse_pair(i, lh, ll, eh, el, ks, to, cells):
    at = slice(i * cells, (i + 2) * cells)
    even, odd = (
        dot3((lh[parity, at, :], ll[parity, at, :]), (eh[parity], el[parity]))
        for parity in range(2)
    )
    value = jnp.exp(jnp.concatenate([even + odd, even - odd], axis=1))
    for n in range(2):
        put_rows(ks, to + n, SUB, value[n * cells : (n + 1) * cells])


def edge_kernel(sizes, flags, b, *rest):
    (devices, q_count, low, tiles, planes, length) = sizes
    away, (ks, cks, cols, far, near_edge), rest = rest[:7], rest[7:12], rest[12:]
    near, (lh, ll, mh, ml, sems) = rest[:7], rest[7:]
    copies = load(list(zip(away, near))[:4], sems)
    eh, el, ceh, cel, order, cwh, cwl = near
    cells, short = LANE, length // 2
    halves, coarse_planes = low // 2, planes // 2
    half = cells // 2
    gather_modes(b, (0, 1, planes - 2, planes - 1), (devices, q_count, tiles), lh, ll)
    for n in range(coarse_planes):
        rows = jnp.concatenate(
            [
                b[pl.ds((q_count + h) * SUB + c * coarse_planes + n, devices, stride=tiles * SUB), :]
                for c in range(2)
                for h in range(halves)
            ],
            axis=0,
        )
        at = slice(n * LANE, (n + 1) * LANE)
        mh[at, :], ml[at, :] = split(jnp.transpose(rows))

    for copy in copies:
        copy.wait()
    copies = send(list(zip(away, near))[4:], sems, 4)

    for i in range(0, 4, 2):
        inverse_pair(i, lh, ll, eh, el, ks, i, cells)
    value = dot3((mh[...], ml[...]), (ceh[...], cel[...]))
    for n in range(coarse_planes):
        top = n * cells
        part = value[top : top + half, :short] + value[top + half : top + cells, short:]
        part = jnp.exp(part)
        put_rows(cks, n, SUB, part)

    for copy in copies:
        copy.wait()
    lane = lax.broadcasted_iota(jnp.int32, (SUB, LANE), 1)
    tile_rows = [b[(s * tiles + tiles - 1) * SUB : (s + 1) * tiles * SUB, :] for s in range(devices)]
    high, rest_part = split(jnp.concatenate(tile_rows, axis=0))
    ordered = dot(high, order[...]) + dot(rest_part, order[...])

    def joined(of, width, start):
        fit = LANE // width
        cells_of = []
        for h in range(HALO):
            parts = []
            for i, s in enumerate(of):
                moved = ordered[s * SUB : (s + 1) * SUB]
                shift = (i % fit * width - start - h * width) % LANE
                moved = pltpu.roll(moved, shift, 1) if shift else moved
                if i % fit == 0:
                    parts.append(moved)
                else:
                    parts[-1] = jnp.where(lane >= i % fit * width, moved, parts[-1])
            cells_of.append(jnp.concatenate(parts, axis=1))
        return split(jnp.concatenate(cells_of, axis=0))

    even, odd = (
        dot3(joined(range(parity, devices, 2), q_count, 0), (eh[parity], el[parity]))
        for parity in range(2)
    )
    value = jnp.exp(jnp.concatenate([even + odd, even - odd], axis=1))
    cols[...] = value
    for h in range(HALO):
        for i, n in enumerate((0, 1, planes - 2, planes - 1)):
            at = h * planes + n
            put_rows(ks, i, halo_row(h, cells), value[at : at + 1, :])
    whole = dot3(joined(range(devices), low, LANE // 2), (cwh[...], cwl[...]))
    for h in range(HALO):
        top = h * SUB
        part = whole[top : top + coarse_planes, :short] + whole[top + coarse_planes : top + SUB, short:]
        part = jnp.exp(part)
        for n in range(coarse_planes):
            put_rows(cks, n, halo_row(h, half), part[n : n + 1, :])
    for held in (ks, cks):
        repeat_sides(flags, held, [(n,) for n in range(4)])
    odd_row = flags[4] == 1
    low_end = (jnp.where(odd_row, 2, 1), jnp.where(odd_row, 3, 0))
    high_end = (jnp.where(odd_row, 1, 2), jnp.where(odd_row, 0, 3))
    for edge, of in ((far, low_end), (near_edge, high_end)):
        at = 0
        for held in (ks, cks):
            count, end = held.shape[1], held.shape[2] - SUB
            for n in of:
                for x in range(count):
                    edge[at : at + end - SUB, :] = held[n, x, SUB:end, :]
                    at += end - SUB
            for x in range(count):
                edge[at + x : at + x + 1, :] = held[of[1], x, SUB - 1 : SUB, :]
                edge[at + count + x : at + count + x + 1, :] = held[of[1], x, end : end + 1, :]
            at += SUB


def halo_row(h, cells):
    return SUB - 2 + h if h < 2 else SUB + cells + h - 2


def source_kernel(planes, pairs, x, out, lo, hi, left, right, held, summed):
    cells = x.shape[0] // planes
    length = x.shape[1]
    half, fourth = cells // 2, cells // 4
    held[...] = dot(x[...], pairs[...])
    for n in range(planes // 2):
        top = 2 * n * cells
        for at in range(0, out.shape[1], LANE):
            lanes = slice(at, at + LANE)
            summed[...] = held[top : top + cells, lanes] + held[top + cells : top + 2 * cells, lanes]
            out[n * half : (n + 1) * half, lanes] = (
                summed[pl.ds(0, half, stride=2), :] + summed[pl.ds(1, half, stride=2), :]
            )
    for edge, plane in ((lo, 0), (hi, planes - 1)):
        edge[:cells, :] = x[plane * cells : (plane + 1) * cells, :].astype(jnp.float32)
        at = plane // 2 * half
        edge[cells:, : length // 2] = out[at : at + fourth, :]
        edge[cells:, length // 2 :] = out[at + fourth : at + half, :]
    for edge, row in ((left, 0), (right, cells - 1)):
        edge[...] = jnp.zeros_like(edge)
        for n in range(planes):
            at = n * cells + (row // SUB * SUB)
            edge[n : n + 1, :] = x[at : at + SUB, :].astype(jnp.float32)[row % SUB : row % SUB + 1]
        for n in range(planes // 2):
            at = n * half + row // 2
            edge[SUB + n : SUB + n + 1, : length // 2] = out[at : at + 1, :]


def beside(parts, ends):
    lane = lax.broadcasted_iota(jnp.int32, parts[0].shape, 1)
    ahead = [pltpu.roll(x, 1, 1) for x in parts]
    behind = [pltpu.roll(x, LANE - 1, 1) for x in parts]
    sums = []
    for i in range(len(parts)):
        left = jnp.where(lane == 0, ahead[i - 1] if i else ends[0], ahead[i])
        right = jnp.where(
            lane == LANE - 1, behind[i + 1] if i + 1 < len(parts) else ends[1], behind[i]
        )
        sums.append(left + right)
    return sums


def first_sweep(tiles, ext, mid, lower, upper, f, store):
    for top in range(0, ext, SUB):
        end = top + SUB
        parts = [mid(x, top, end) for x in range(tiles)]
        for x, both in enumerate(beside(parts, (parts[0], parts[-1]))):
            k = parts[x]
            above = pltpu.roll(k, 1, 0) if top == 0 else mid(x, top - 1, end - 1)
            below = pltpu.roll(k, SUB - 1, 0) if end == ext else mid(x, top + 1, end + 1)
            total = (lower(x, top, end) + upper(x, top, end)) + (above + below) + both
            scale = JACOBI_WEIGHT / (6.0 * k + total)
            u = f(x, top, end) * (2.0 * scale)
            store(x, top, end, u, k * u, scale)


def second_sweep(tiles, ext, k, u, w, r, store):
    for top in range(SUB, ext - SUB, SUB):
        end = top + SUB
        sums = []
        for lower, mid, upper in (u, w):
            parts = [mid(x, top, end) for x in range(tiles)]
            sums.append(
                [
                    both
                    + (lower(x, top, end) + upper(x, top, end))
                    + (mid(x, top - 1, end - 1) + mid(x, top + 1, end + 1))
                    for x, both in enumerate(beside(parts, (0.0, 0.0)))
                ]
            )
        for x in range(tiles):
            coupled = k(x, top, end) * sums[0][x] + sums[1][x]
            value = (2.0 - JACOBI_WEIGHT) * u[1](x, top, end) + r(x, top, end) * coupled
            store(x, top, end, value)


def around(tiles, ext, mid, beyond, store):
    for top in range(0, ext, SUB):
        end = top + SUB
        parts = [mid(x, top, end) for x in range(tiles)]
        for x, both in enumerate(beside(parts, (parts[0], parts[-1]))):
            k = parts[x]
            above = pltpu.roll(k, 1, 0) if top == 0 else mid(x, top - 1, end - 1)
            below = pltpu.roll(k, SUB - 1, 0) if end == ext else mid(x, top + 1, end + 1)
            store(x, top, end, (6.0 * k + beyond(x, top, end)) + (above + below) + both)


def plane_of(held, *at):
    return lambda x, top, end: held[(*at, x, slice(top, end), slice(None))]


def put_rows(held, to, at, rows):
    for x in range(held.shape[1]):
        held[to, x, at : at + rows.shape[0], :] = rows[:, x * LANE : (x + 1) * LANE]


def repeat_sides(flags, held, at):
    end = held.shape[-2] - SUB

    @pl.when(flags[2] == 1)
    def _():
        for p in at:
            held[(*p, slice(None), slice(SUB - 1, SUB))] = held[(*p, slice(None), slice(SUB, SUB + 1))]

    @pl.when(flags[3] == 1)
    def _():
        for p in at:
            held[(*p, slice(None), slice(end, end + 1))] = held[
                (*p, slice(None), slice(end - 1, end))
            ]


def put_block(fine, held, to, source, row, cells, length):
    if fine:
        put_rows(held, to, SUB, source[row : row + cells, :])
    else:
        half = cells // 2
        put_rows(held, to, SUB, source[row : row + half, :length])
        put_rows(held, to, SUB + half, source[row : row + half, length:])


def layout_kernel(sizes, *rest):
    away, outs, near, sems = rest[:6], rest[6:10], rest[10:16], rest[16]
    for copy in load(list(zip(away, near)), sems):
        copy.wait()
    source, coarse_source, *edges = near
    sides = edges[2:]
    for fine, inner, outer in ((True, *outs[:2]), (False, *outs[2:])):
        planes, cells, length = sizes if fine else [n // 2 for n in sizes]
        f = source if fine else coarse_source
        source_row = 0 if fine else SUB

        def plane(held, to, p):
            put_rows(held, to, SUB, f[p].astype(jnp.float32))
            for side, row in zip(sides, (SUB - 1, SUB + cells)):
                at = source_row + p
                put_rows(held, to, row, side[at : at + 1, :length])

        for p in range(1, planes - 1):
            plane(inner, p - 1, p)
        for group, p in enumerate((0, planes - 1)):
            row = 0 if fine else 2 * cells
            put_block(fine, outer.at[group], 0, edges[group], row, cells, length)
            plane(outer.at[group], 1, p)


def inner_level(sizes, ks, fs, us, ws, rs):
    planes, _, length = sizes
    tiles, ext = ks.shape[1:3]

    def first(p, carry):
        def store(x, top, end, u, w, r):
            at = (p - 1, x, slice(top, end))
            us[at], ws[at], rs[at] = u, w, r

        near = [plane_of(ks, p + i) for i in (0, -1, 1)]
        first_sweep(tiles, ext, *near, plane_of(fs, p - 1), store)
        return carry

    lax.fori_loop(1, planes - 1, first, 0)


def prepare(ks, us, ws, rs, sums, ready):
    planes, tiles, ext, _ = ks.shape

    def end_of(group, carry):
        inwards = lambda i, count: jnp.where(group == 0, i, count - 1 - i)

        def store_sum(x, top, end, value):
            sums[group, x, top:end, :] = value

        own = [plane_of(ks, inwards(i, planes)) for i in range(2)]
        around(tiles, ext, *own, store_sum)

        def store(x, top, end, value):
            ready[group, x, top:end, :] = value

        nothing = lambda x, top, end: 0.0
        u, w = (
            [nothing] + [plane_of(held, inwards(i, planes - 2)) for i in range(2)]
            for held in (us, ws)
        )
        scale = plane_of(rs, inwards(0, planes - 2))
        second_sweep(tiles, ext, own[1], u, w, scale, store)
        return carry

    lax.fori_loop(0, 2, end_of, 0)


def inner_kernel(sizes, shares, flags, b, eh_hbm, el_hbm, edges, cks, cols, fs, cfs, *rest):
    out_hbm, us, ws, rs, cus, cws, crs, sums, ready, csums, cready, *rest = rest
    ks, eh, el, lh, ll, out, sems = rest
    planes, cells, length = sizes
    tiles, ext = ks.shape[1:3]
    copies = load([(eh_hbm, eh), (el_hbm, el)], sems)
    middle = range(2, planes - 2)
    gather_modes(b, middle, shares, lh, ll)
    for i, p in enumerate((0, 1, planes - 2, planes - 1)):
        ks[p] = edges[i]
    for h in range(HALO):
        for p in middle:
            at = h * planes + p
            put_rows(ks, p, halo_row(h, cells), cols[at : at + 1, :])
    for copy in copies:
        copy.wait()
    for p in range(2, planes - 2, 2):
        inverse_pair(p - 2, lh, ll, eh, el, ks, p, cells)
    repeat_sides(flags, ks, [(p,) for p in middle])
    inner_level(sizes, ks, fs, us, ws, rs)

    def second(p, carry):
        def store(x, top, end, value):
            out[p - 2, top - SUB : end - SUB, x * LANE : (x + 1) * LANE] = value

        u, w = ([plane_of(held, p - 1 + i) for i in (-1, 0, 1)] for held in (us, ws))
        second_sweep(tiles, ext, plane_of(ks, p), u, w, plane_of(rs, p - 1), store)
        return carry

    lax.fori_loop(2, planes - 2, second, 0)
    copies = send([(out, out_hbm.at[2 : planes - 2])], sems, 0)
    prepare(ks, us, ws, rs, sums, ready)
    inner_level([n // 2 for n in sizes], cks, cfs, cus, cws, crs)
    prepare(cks, cus, cws, crs, csums, cready)
    for copy in copies:
        copy.wait()


def outer_kernel(sizes, flags, *rest):
    kept, coarse_kept, (k_far, k_near, _, out, coarse_out), rest = (
        rest[:7],
        rest[7:14],
        rest[14:19],
        rest[19:],
    )
    scratch = (rest[:6], rest[6:])
    levels = (sizes, tuple(n // 2 for n in sizes))
    start = 0
    sent = []
    for size, held, given, target in zip(
        levels, scratch, (kept, coarse_kept), (out, coarse_out)
    ):
        planes = size[0]
        ks, fs, inner_us, inner_ws, inner_rs, sums, ready = given
        halo, us, ws, rs, done, sems = held
        tiles, ext = ks.shape[1:3]
        rows = size[1]
        for group, edge in ((flags[4], k_far), (1 - flags[4], k_near)):
            at = start
            for place in range(2 * tiles):
                to = place * ext + SUB
                halo[group, to : to + rows, :] = edge[at : at + rows, :]
                at += rows
            for x in range(tiles):
                to = (tiles + x) * ext
                halo[group, to + SUB - 1 : to + SUB, :] = edge[at + x : at + x + 1, :]
                to += SUB + rows
                halo[group, to : to + 1, :] = edge[at + tiles + x : at + tiles + x + 1, :]
        start = at + SUB
        for group in range(2):

            @pl.when(flags[group] == 1)
            def _():
                for x in range(tiles):
                    at = (tiles + x) * ext
                    halo[group, at : at + ext, :] = ks[3 * group, x]

        def both_ends(group, carry):
            def halo_plane(slot):
                def get(x, top, end):
                    at = (slot * tiles + x) * ext
                    return halo[group, at + top : at + end, :]

                return get

            inwards = lambda i, count: jnp.where(group == 0, i, count - 1 - i)
            own = [plane_of(ks, inwards(i, 4)) for i in range(2)]
            def store_outer(x, top, end, u, w, r):
                at = (group, 0, x, slice(top, end))
                us[at], ws[at] = u, w

            beyond = halo_plane(1)
            first_sweep(
                tiles, ext, beyond, halo_plane(0), own[0], plane_of(fs, group, 0), store_outer
            )
            for top in range(0, ext, SUB):
                for x in range(tiles):
                    at = (x, slice(top, top + SUB))
                    near_sum = sums[(group, *at)] + beyond(x, top, top + SUB)
                    scale = JACOBI_WEIGHT / near_sum
                    u = fs[(group, 1, *at)] * (2.0 * scale)
                    us[(group, 1, *at)] = u
                    ws[(group, 1, *at)] = own[0](x, top, top + SUB) * u
                    rs[(group, *at)] = scale
            u, w = (
                [plane_of(new, group, i) for i in range(2)]
                + [plane_of(old, inwards(0, planes - 2))]
                for new, old in ((us, inner_us), (ws, inner_ws))
            )

            def store(x, top, end, value):
                done[group, 0, top - SUB : end - SUB, x * LANE : (x + 1) * LANE] = value

            second_sweep(tiles, ext, own[0], u, w, plane_of(rs, group), store)
            scale = plane_of(inner_rs, inwards(0, planes - 2))
            for top in range(SUB, ext - SUB, SUB):
                for x in range(tiles):
                    at = (x, top, top + SUB)
                    coupled = own[1](*at) * u[1](*at) + w[1](*at)
                    value = ready[group, x, top : top + SUB, :] + scale(*at) * coupled
                    done[group, 1, top - SUB : top, x * LANE : (x + 1) * LANE] = value
            for i in range(2):
                pltpu.make_async_copy(
                    done.at[group, i], target.at[inwards(i, planes)], sems.at[2 * group + i]
                ).start()
            return carry

        lax.fori_loop(0, 2, both_ends, 0)
        for group, at in enumerate(((0, 1), (planes - 1, planes - 2))):
            for i, p in enumerate(at):
                sent.append(
                    pltpu.make_async_copy(
                        done.at[group, i], target.at[p], sems.at[2 * group + i]
                    )
                )
    for copy in sent:
        copy.wait()


SMEM = pl.BlockSpec(memory_space=pltpu.SMEM)
VMEM = pl.BlockSpec(memory_space=pltpu.VMEM)
AWAY = pl.BlockSpec(memory_space=pltpu.HBM)
ANY = pl.BlockSpec(memory_space=pl.ANY)


def call(kernel, outs, operands, scratch, flops, specs, limit, out_specs=None, aliases=None):
    many = isinstance(outs, (list, tuple))
    written = outs if many else [outs]
    moved = sum(math.prod(x.shape) * x.dtype.itemsize for x in (*operands, *written))
    operands = [
        pltpu.with_memory_space_constraint(x, pltpu.HBM) if spec is AWAY else x
        for x, spec in zip(operands, specs)
    ]
    out_specs = out_specs or [
        VMEM if isinstance(x, jax.ShapeDtypeStruct) else AWAY for x in written
    ]
    return pl.pallas_call(
        kernel,
        out_shape=outs,
        in_specs=specs,
        out_specs=out_specs if many else out_specs[0],
        scratch_shapes=scratch,
        input_output_aliases=aliases or {},
        compiler_params=pltpu.CompilerParams(vmem_limit_bytes=limit * MIB),
        cost_estimate=pl.CostEstimate(flops=flops, bytes_accessed=moved, transcendentals=0),
    )(*operands)


def f32(*shape):
    return jax.ShapeDtypeStruct(shape, jnp.float32)


def room(*arrays):
    return [pltpu.VMEM(x.shape, x.dtype) for x in arrays]


def chain(axis):
    up = [(i, i + 1) for i in range(lax.axis_size(axis) - 1)]
    return up, [(j, i) for i, j in up]


def swap(lo, hi, axis):
    up, down = chain(axis)
    return lax.ppermute(hi, axis, up), lax.ppermute(lo, axis, down)


def held_planes(size, *count):
    planes, cells, length = size
    return f32(*count, length // LANE, cells + 2 * SUB, LANE)


def outer_scratch(size):
    planes, cells, length = size
    return room(
        f32(2, 2 * (length // LANE) * (cells + 2 * SUB), LANE),
        held_planes(size, 2, 2),
        held_planes(size, 2, 2),
        held_planes(size, 2),
        f32(2, 2, cells, length),
    ) + [pltpu.SemaphoreType.DMA((4,))]


def fused_body(noise, source):
    rows, groups = lax.axis_size("row"), lax.axis_size(PLANE)
    devices = rows * groups
    planes, cells, length = noise.shape
    first, second = planes * rows, cells * groups
    bf16 = jnp.bfloat16
    held = length // 2 // devices
    js = list(range(held))
    low = held // 2
    me = lax.axis_index(EVERY)
    row_at, group_at = lax.axis_index("row"), lax.axis_index(PLANE)
    flags = jnp.stack(
        [
            row_at == 0,
            row_at == rows - 1,
            group_at == 0,
            group_at == groups - 1,
            row_at % 2 == 1,
        ]
    ).astype(jnp.int32)
    norm = FIELD_SCALE * (float(first) * float(second) * float(length)) ** (-0.5)
    flat = (planes * cells, length)

    pieces = 4
    table = [x.reshape(pieces, -1, length) for x in two_parts(forward_third(length, devices, js))]
    table = np.concatenate(table, axis=1)
    shape = (length * SUB, LANE)
    sent = call(
        functools.partial(forward_kernel, planes),
        pltpu.HBM(shape, jnp.float32),
        (table, noise.reshape(flat)),
        room(table)
        + [
            pltpu.VMEM(flat, bf16),
            pltpu.VMEM(shape, jnp.float32),
            pltpu.SemaphoreType.DMA((2 * pieces + planes // 2,)),
        ],
        4 * length * length * planes * cells,
        [AWAY] * 2,
        12,
    )
    sent, source = lax.optimization_barrier((sent, source))
    sent = sent.reshape(devices, 2 * held, SUB, LANE)
    arrived = lax.all_to_all(sent, EVERY, split_axis=0, concat_axis=0, tiled=True)

    pairs = np.zeros((length, length // 2), np.float32)
    pairs[np.arange(length), np.arange(length) // 2] = 0.125
    level = f32(cells + cells // 4, length)
    side = f32(2 * SUB, length)
    coarse_source, *edges = call(
        functools.partial(source_kernel, planes),
        [f32(planes * cells // 4, length // 2), level, level, side, side],
        (pairs.astype(bf16), source.reshape(flat)),
        [
            pltpu.VMEM((planes * cells, length // 2), jnp.float32),
            pltpu.VMEM((cells, LANE), jnp.float32),
        ],
        planes * cells * length * length,
        [VMEM] * 2,
        12,
    )
    coarse_source = coarse_source.reshape(planes // 2, cells // 2, length // 2)
    edges = (*swap(*edges[:2], "row"), *swap(*edges[2:], PLANE))
    arrived, edges, coarse_source = lax.optimization_barrier((arrived, edges, coarse_source))

    constants = (
        two_parts(second_table(second))
        + (
            stacked(forward_first(first)),
            stacked(inverse_first(first)),
            stacked(inverse_first_coarse(first // 2, rows)),
        )
        + two_parts(second_coarse(second // 2, groups))
        + two_parts(second_table(second).transpose(0, 2, 1))
    )
    tiles = 2 * held + low // 2 + 1
    modes = (me + devices * np.array(js)).astype(jnp.float32)
    weight = jnp.where(modes == 0.0, norm, 2.0 * norm).astype(jnp.float32)
    scale = jnp.stack([DECAY * modes * modes, weight], axis=1)
    block = (2, 2 * held * first, second // 2)
    shape = (devices, tiles, SUB, LANE)
    out = call(
        functools.partial(middle_kernel, (first, second, rows, groups, held, low)),
        pltpu.HBM(shape, jnp.float32),
        (scale, arrived, *constants),
        room(*constants)
        + [
            pltpu.VMEM(shape, jnp.float32),
            pltpu.SemaphoreType.DMA((len(constants),)),
            pltpu.VMEM(block, bf16),
            pltpu.VMEM(block, bf16),
            pltpu.VMEM(block, jnp.float32),
            pltpu.VMEM(block, bf16),
            pltpu.VMEM(block, bf16),
            pltpu.VMEM((low // 2 * first, second), bf16),
            pltpu.VMEM((low // 2 * first, second), bf16),
        ],
        6 * 2 * 2 * held * first * second * (second + 2 * first),
        [SMEM, VMEM] + [AWAY] * len(constants),
        22,
    )
    out, source, coarse_source, edges = lax.optimization_barrier(
        (out, source, coarse_source, edges)
    )
    got = lax.all_to_all(out, EVERY, split_axis=0, concat_axis=0, tiled=True)
    size, coarse_size = noise.shape, coarse_source.shape
    sizes = (size, coarse_size)
    sources = (source, coarse_source, *edges)
    laid = call(
        functools.partial(layout_kernel, size),
        [
            held_planes(s, *count)
            for s in sizes
            for count in ((s[0] - 2,), (2, 2))
        ],
        sources,
        room(*sources) + [pltpu.SemaphoreType.DMA((6,))],
        source.size,
        [AWAY] * 6,
        12,
    )
    got, laid = lax.optimization_barrier((got, laid))

    third = inverse_third(length, devices, js)
    constants = (
        two_parts(third)
        + two_parts(third_coarse(length // 2, devices, js[:low]))
        + (lane_order(2 * held, low).astype(bf16),)
        + two_parts(third_coarse_halo(length // 2, devices, js[:low]))
    )
    edge = f32(sum(2 * (s[2] // LANE) * s[1] + SUB for s in sizes), LANE)
    shares = (devices, 2 * held, tiles)
    got = got.reshape(devices * tiles * SUB, LANE)
    ks, coarse_ks, cols, far, near = call(
        functools.partial(edge_kernel, (devices, 2 * held, low, tiles, planes, length)),
        [held_planes(s, 4) for s in sizes] + [f32(HALO * planes, length), edge, edge],
        (flags, got, *constants),
        room(*constants)
        + [pltpu.VMEM((2, 4 * cells, devices * held), bf16)] * 2
        + [pltpu.VMEM((planes // 2 * LANE, devices * low), bf16)] * 2
        + [pltpu.SemaphoreType.DMA((7,))],
        3 * planes * cells * length * length,
        [SMEM, VMEM] + [AWAY] * 7,
        16,
    )
    k_far, k_near = (
        lax.ppermute(
            x, "row", [p for i in range(at, rows - 1, 2) for p in ((i, i + 1), (i + 1, i))]
        )
        for x, at in ((far, 1), (near, 0))
    )
    inner_f, outer_f, coarse_inner_f, coarse_outer_f = laid
    inner, *kept = call(
        functools.partial(inner_kernel, size, shares),
        [pltpu.HBM(size, jnp.float32)]
        + [held_planes(s, s[0] - 2) for s in sizes for _ in range(3)]
        + [held_planes(s, 2) for s in sizes for _ in range(2)],
        (flags, got, *constants[:2], ks, coarse_ks, cols, inner_f, coarse_inner_f),
        room(held_planes(size, planes), *constants[:2])
        + [pltpu.VMEM((2, (planes - 4) * cells, devices * held), bf16)] * 2
        + room(f32(planes - 4, cells, length))
        + [pltpu.SemaphoreType.DMA((2,))],
        3 * planes * cells * length * length,
        [SMEM, VMEM] + [AWAY] * 2 + [VMEM] * 5,
        18,
    )
    return call(
        functools.partial(outer_kernel, size),
        [pltpu.HBM(s, jnp.float32) for s in sizes],
        (
            flags,
            *(ks, outer_f, *kept[:3], *kept[6:8]),
            *(coarse_ks, coarse_outer_f, *kept[3:6], *kept[8:]),
            *(k_far, k_near, inner),
        ),
        outer_scratch(size) + outer_scratch(coarse_size),
        30 * source.size,
        [SMEM] + [VMEM] * 16 + [AWAY],
        18,
        None,
        {17: 0},
    )


NEIGHBOUR_STEPS = ((1, 0, 0), (-1, 0, 0), (0, 1, 0), (0, -1, 0), (0, 0, 1), (0, 0, -1))


def padded(x, sides, width):
    for axis, dim in sides:
        peers, length = (lax.axis_size(axis), x.shape[dim])
        up = [(i, (i + 1) % peers) for i in range(peers - 1)]
        down = [(j, i) for i, j in up]
        last = lax.slice_in_dim(x, length - width, length, axis=dim)
        leading = lax.slice_in_dim(x, 0, width, axis=dim)
        before = lax.ppermute(last, axis, up)
        after = lax.ppermute(leading, axis, down)
        x = jnp.concatenate([before, x, after], axis=dim)
    return x


def signed_modes(index, length):
    return jnp.where(index < length // 2, index, index - length).astype(jnp.float32)


def amplitude(first_modes, second_modes, third_modes, first_edge, second_edge, third_edge):
    squared = first_modes * first_modes + second_modes * second_modes + third_modes * third_modes
    value = FIELD_SCALE / (1.0 + (2.0 * math.pi * CORRELATION) ** 2 * squared)
    edge = (
        (jnp.abs(first_modes) == first_edge)
        | (jnp.abs(second_modes) == second_edge)
        | (jnp.abs(third_modes) == third_edge)
    )
    return jnp.where(edge, 0.0, value)


def phase_table(count_rows, count_cols, modulus, sign):
    left_index = jnp.arange(count_rows, dtype=jnp.int32)[:, None]
    right_index = jnp.arange(count_cols, dtype=jnp.int32)[None, :]
    angle = 2.0 * math.pi / modulus * (left_index * right_index % modulus).astype(jnp.float32)
    return (jnp.cos(angle), sign * jnp.sin(angle))


def split_length(length):
    outer_len = 2 ** ((length.bit_length() - 1) // 2)
    return (outer_len, length // outer_len)


def real_form(form, left_value, right_value):
    return jnp.einsum(form, left_value, right_value, precision=lax.Precision.HIGHEST)


def complex_form(form, left_real, left_imag, right_real, right_imag):
    real_part = real_form(form, left_real, right_real) - real_form(form, left_imag, right_imag)
    imag_part = real_form(form, left_real, right_imag) + real_form(form, left_imag, right_real)
    return (real_part, imag_part)


def merge_pair(values, out_form, first_letter):
    merge_at = out_form.index(first_letter)
    out_dims = list(values.shape)
    merged = (
        out_dims[:merge_at]
        + [out_dims[merge_at] * out_dims[merge_at + 1]]
        + out_dims[merge_at + 2 :]
    )
    return values.reshape(merged)


def forward_axis(real_part, imag_part, lead_form, out_form, kept_modes):
    length = real_part.shape[-1]
    outer_len, inner_len = split_length(length)
    split_shape = real_part.shape[:-1] + (outer_len, inner_len)
    outer_real, outer_imag = phase_table(outer_len, outer_len, outer_len, -1.0)
    twist_real, twist_imag = phase_table(outer_len, inner_len, length, -1.0)
    inner_real, inner_imag = phase_table(inner_len, kept_modes // outer_len, inner_len, -1.0)
    first_form = lead_form + "ab,ai->" + lead_form + "ib"
    split_real = real_part.reshape(split_shape)
    if imag_part is None:
        section_real = real_form(first_form, split_real, outer_real)
        section_imag = real_form(first_form, split_real, outer_imag)
    else:
        section_real, section_imag = complex_form(
            first_form, split_real, imag_part.reshape(split_shape), outer_real, outer_imag
        )
    turned_real = section_real * twist_real - section_imag * twist_imag
    turned_imag = section_real * twist_imag + section_imag * twist_real
    result_real, result_imag = complex_form(
        lead_form + "ib,bj->" + out_form, turned_real, turned_imag, inner_real, inner_imag
    )
    return (merge_pair(result_real, out_form, "j"), merge_pair(result_imag, out_form, "j"))


def inverse_axis(real_part, imag_part, length, lead_form, out_form, real_only):
    kept_modes = real_part.shape[-1]
    outer_len, inner_len = split_length(length)
    split_shape = real_part.shape[:-1] + (kept_modes // outer_len, outer_len)
    inner_real, inner_imag = phase_table(kept_modes // outer_len, inner_len, inner_len, 1.0)
    twist_real, twist_imag = phase_table(outer_len, inner_len, length, 1.0)
    outer_real, outer_imag = phase_table(outer_len, outer_len, outer_len, 1.0)
    section_real, section_imag = complex_form(
        lead_form + "ji,jb->" + lead_form + "ib",
        real_part.reshape(split_shape),
        imag_part.reshape(split_shape),
        inner_real,
        inner_imag,
    )
    turned_real = section_real * twist_real - section_imag * twist_imag
    turned_imag = section_real * twist_imag + section_imag * twist_real
    second_form = lead_form + "ib,ia->" + out_form
    if real_only:
        result = real_form(second_form, turned_real, outer_real) - real_form(
            second_form, turned_imag, outer_imag
        )
        return merge_pair(result, out_form, "a")
    result_real, result_imag = complex_form(
        second_form, turned_real, turned_imag, outer_real, outer_imag
    )
    return (merge_pair(result_real, out_form, "a"), merge_pair(result_imag, out_form, "a"))


def low_band(values, half_coarse, fine_len):
    return jnp.concatenate(
        [values[:, :, :half_coarse], values[:, :, fine_len - half_coarse :]], axis=2
    )


def window(values, margin, offset):
    return values[
        margin + offset[0] : values.shape[0] - margin + offset[0],
        margin + offset[1] : values.shape[1] - margin + offset[1],
        margin + offset[2] : values.shape[2] - margin + offset[2],
    ]


def face_weight(center, beside):
    return jnp.where(beside > 0.0, 0.5 * (center + beside), center)


def smooth_twice(kappa, source):
    no_shift = (0, 0, 0)
    center = window(kappa, 1, no_shift)
    faces = [face_weight(center, window(kappa, 1, offset)) for offset in NEIGHBOUR_STEPS]
    diagonal = faces[0] + faces[1] + faces[2] + faces[3] + faces[4] + faces[5]
    guarded = jnp.where(center > 0.0, diagonal, 1.0)
    first_sweep = JACOBI_WEIGHT * window(source, 1, no_shift) / guarded
    inner_first = window(first_sweep, 1, no_shift)
    inner_diagonal = window(diagonal, 1, no_shift)
    coupled = jnp.zeros_like(inner_first)
    for face_value, offset in zip(faces, NEIGHBOUR_STEPS):
        coupled = coupled + window(face_value, 1, no_shift) * window(first_sweep, 1, offset)
    residual = window(source, 2, no_shift) - inner_diagonal * inner_first + coupled
    return inner_first + JACOBI_WEIGHT * residual / inner_diagonal


def pad_depth(values):
    return jnp.pad(values, ((0, 0), (0, 0), (2, 2)))


def plain_body(noise, source):
    row_at = lax.axis_index("row")
    group_at = lax.axis_index(("level", "col"))
    fine_field = noise.astype(jnp.float32)
    fine_len = fine_field.shape[-1]
    coarse_len = fine_len // 2
    half_coarse = coarse_len // 2
    kept_modes = fine_len // 2
    real_part, imag_part = forward_axis(fine_field, None, "pq", "pjiq", kept_modes)
    real_part, imag_part = (
        lax.all_to_all(real_part, ("level", "col"), split_axis=1, concat_axis=2, tiled=True),
        lax.all_to_all(imag_part, ("level", "col"), split_axis=1, concat_axis=2, tiled=True),
    )
    real_part, imag_part = forward_axis(real_part, imag_part, "pq", "jiqp", fine_len)
    real_part, imag_part = (
        lax.all_to_all(real_part, "row", split_axis=0, concat_axis=2, tiled=True),
        lax.all_to_all(imag_part, "row", split_axis=0, concat_axis=2, tiled=True),
    )
    slab_len = real_part.shape[-1]
    coarse_slab = slab_len // 2
    half_slab = coarse_slab // 2
    real_part, imag_part = forward_axis(real_part, imag_part, "pq", "pqji", slab_len)
    second_count = real_part.shape[0]
    third_count = real_part.shape[1]
    wave_second = signed_modes(
        row_at * second_count + jnp.arange(second_count, dtype=jnp.int32), fine_len
    )[:, None, None]
    third_index = group_at * third_count + jnp.arange(third_count, dtype=jnp.int32)
    wave_third = signed_modes(third_index, fine_len)[None, :, None]
    spread = 2.0
    mirror_weight = jnp.where(third_index == 0, 1.0, spread).astype(jnp.float32)[None, :, None]
    norm_factor = (float(slab_len) * float(fine_len) * float(fine_len)) ** (-0.5)
    wave_first = signed_modes(jnp.arange(slab_len, dtype=jnp.int32), slab_len)[None, None, :]
    fine_scale = (
        amplitude(
            wave_second, wave_third, wave_first, fine_len / 2.0, fine_len / 2.0, slab_len / 2.0
        )
        * mirror_weight
        * norm_factor
    )
    coarse_first = signed_modes(jnp.arange(coarse_slab, dtype=jnp.int32), coarse_slab)[
        None, None, :
    ]
    coarse_scale = (
        amplitude(
            wave_second,
            wave_third,
            coarse_first,
            coarse_len / 2.0,
            coarse_len / 2.0,
            coarse_slab / 2.0,
        )
        * mirror_weight
        * norm_factor
    )
    coarse_real = low_band(real_part, half_slab, slab_len) * coarse_scale
    coarse_imag = low_band(imag_part, half_slab, slab_len) * coarse_scale
    fine_real, fine_imag = inverse_axis(
        real_part * fine_scale, imag_part * fine_scale, slab_len, "pq", "abqp", False
    )
    coarse_real, coarse_imag = inverse_axis(
        coarse_real, coarse_imag, coarse_slab, "pq", "abqp", False
    )
    fine_real, fine_imag, coarse_real, coarse_imag = (
        lax.all_to_all(fine_real, "row", split_axis=0, concat_axis=2, tiled=True),
        lax.all_to_all(fine_imag, "row", split_axis=0, concat_axis=2, tiled=True),
        lax.all_to_all(coarse_real, "row", split_axis=0, concat_axis=2, tiled=True),
        lax.all_to_all(coarse_imag, "row", split_axis=0, concat_axis=2, tiled=True),
    )
    coarse_real = low_band(coarse_real, half_coarse, fine_len)
    coarse_imag = low_band(coarse_imag, half_coarse, fine_len)
    fine_real, fine_imag = inverse_axis(fine_real, fine_imag, fine_len, "pq", "pabq", False)
    coarse_real, coarse_imag = inverse_axis(
        coarse_real, coarse_imag, coarse_len, "pq", "pabq", False
    )
    fine_real, fine_imag, coarse_real, coarse_imag = (
        lax.all_to_all(fine_real, ("level", "col"), split_axis=1, concat_axis=2, tiled=True),
        lax.all_to_all(fine_imag, ("level", "col"), split_axis=1, concat_axis=2, tiled=True),
        lax.all_to_all(coarse_real, ("level", "col"), split_axis=1, concat_axis=2, tiled=True),
        lax.all_to_all(coarse_imag, ("level", "col"), split_axis=1, concat_axis=2, tiled=True),
    )
    coarse_real = coarse_real[:, :, :half_coarse]
    coarse_imag = coarse_imag[:, :, :half_coarse]
    fine_log = inverse_axis(fine_real, fine_imag, fine_len, "pq", "pqab", True)
    coarse_log = inverse_axis(coarse_real, coarse_imag, coarse_len, "pq", "pqab", True)
    fine_kappa = jnp.exp(fine_log)
    coarse_kappa = jnp.exp(coarse_log)
    fine_source = source.astype(jnp.float32)
    coarse_rows = coarse_log.shape[0]
    coarse_cols = coarse_log.shape[1]
    coarse_source = fine_source.reshape(coarse_rows, 2, coarse_cols, 2, coarse_len, 2).mean(
        axis=(1, 3, 5)
    )
    fine_kappa, fine_source, coarse_kappa, coarse_source = (
        padded(fine_kappa, (("row", 0), (("level", "col"), 1)), 2),
        padded(fine_source, (("row", 0), (("level", "col"), 1)), 2),
        padded(coarse_kappa, (("row", 0), (("level", "col"), 1)), 2),
        padded(coarse_source, (("row", 0), (("level", "col"), 1)), 2),
    )
    fine_pressure = smooth_twice(pad_depth(fine_kappa), pad_depth(fine_source))
    coarse_pressure = smooth_twice(pad_depth(coarse_kappa), pad_depth(coarse_source))
    return (fine_pressure, coarse_pressure)


def body(noise, source):
    planes, cells, length = noise.shape
    rows, groups = lax.axis_size("row"), lax.axis_size(PLANE)
    modes = length // 2 // (rows * groups)
    fills = planes == SUB and cells == LANE and 2 * HALO * modes == LANE // 2
    if fills and length % (4 * LANE) == 0 and rows % 2 == 0 and groups % 4 == 0:
        return fused_body(noise, source)
    return plain_body(noise, source)


def solution(mesh):
    return jax.shard_map(
        body,
        mesh=mesh,
        in_specs=(P("row", ("level", "col"), None), P("row", ("level", "col"), None)),
        out_specs=(P("row", ("level", "col"), None), P("row", ("level", "col"), None)),
        check_vma=False,
    )
```
